32 devices in a mesh: groups: 2 (over y), cells: 4 (over z), slots: 2 (over x), mp: 2 (over core).
Axes of the slice: x: 2, y: 2, z: 4, core: 2. Of those that a mesh axis runs over, the one named last changes fastest.
Arguments:
- obs_feat: bfloat16 [16384, 768], P(('groups', 'cells', 'slots', 'mp')), parts along dimension 0, may hold values from -6 to 6
- obs_cell: int32 [16384], P(('groups', 'cells', 'slots', 'mp')), parts along dimension 0, may hold values from 0 to 1023, as said below
- obs_slot: int32 [16384], P(('groups', 'cells', 'slots', 'mp')), parts along dimension 0, may hold values from 0 to 3
- obs_count: int32 [32], P(('groups', 'cells', 'slots', 'mp')), parts along dimension 0, may hold values from 256 to 512
- time_embed: bfloat16 [8, 768], replicated, may hold values from -6 to 6
- w_qkv: bfloat16 [768, 3, 768], P('cells', None, 'mp'), may hold values from -0.21875 to 0.21875
- w_out: bfloat16 [768, 768], P('mp', 'cells'), may hold values from -0.21875 to 0.21875
- w_gate_up: bfloat16 [768, 2, 3072], P('cells', None, 'mp'), may hold values from -0.21875 to 0.21875
- w_down: bfloat16 [3072, 768], P('mp', 'cells'), may hold values from -0.109375 to 0.109375
Outputs:
- mixed: bfloat16 [2048, 8, 768], P(('groups', 'cells', 'slots', 'mp')), parts along dimension 0
The draws below stay inside these ranges and needn't reach their ends.
There are 2 independent parts, one for each index of `groups`. The reference program is written for one: setup_inputs(seed, part) draws one part's arguments, and reference() takes and returns one part's arrays. A program takes and returns all parts, laid end to end along the dimension named above; an argument that names none is the same for every part. Nothing has to cross between parts.
Inputs may be any that keep to these rules, and one draw needn't show every extreme that they name: `obs_cell`: call the block of cell g the pair (g // 256, (g // 64) % 2). Among the live rows of one device at most 192 lie in any one block, and one block, the same for all devices of a part, gets exactly 192 live rows from every device.
All inputs are finite; a program needn't handle non-finite values.
Results may differ from the reference program's by a relative error of at most 0.0057.
Values may be sent and summed in bfloat16 or wider, within the bound.
No kernel may reach another device: no remote copies, remote signals or barrier semaphores. Data moves between devices by JAX's collectives and lax.ppermute only.
A program may use at most 128 MiB of HBM per device.

```python
import jax
import jax.numpy as jnp
from jax import lax

D = 768
HD = 64
FF = 3072
TSTEPS = 8
CB = 128
OBS_DEV = 512
SLOT_DEV = 4
CELLS = 1024
OBS = 8192
N_CELLS = 4
N_SLOTS = 2
N_MP = 2


def shuffled_places(device_key, places):
    return jax.random.permutation(device_key, places)


def draw_obs_cell(key, part):
    key = jax.random.fold_in(key, 5)
    owners = N_CELLS * N_MP
    devices = N_CELLS * N_SLOTS * N_MP
    capacity = 3 * OBS_DEV // owners
    places = owners * capacity
    swath_owner = jax.random.randint(jax.random.fold_in(key, 1), (), 0, owners)
    device_keys = jax.random.split(jax.random.fold_in(key, 2), devices)
    orders = jax.vmap(shuffled_places, in_axes=(0, None))(device_keys, places)
    place_ids = jnp.arange(places, dtype=jnp.int32)
    scores = jnp.where((place_ids // capacity == swath_owner)[None, :], place_ids[None, :] - places, orders)
    chosen = jnp.argsort(scores, axis=1, stable=True)[:, :OBS_DEV]
    owner_idx = chosen // capacity
    local_idx = jax.random.randint(jax.random.fold_in(key, 3), (devices, OBS_DEV), 0, CB)
    quarter = CB // N_SLOTS
    cell_part = owner_idx // N_MP
    mp_part = owner_idx % N_MP
    slot_part = local_idx // quarter
    local_part = local_idx % quarter
    cell_ids = ((cell_part * N_SLOTS + slot_part) * N_MP + mp_part) * quarter + local_part
    return cell_ids.reshape(-1).astype(jnp.int32)


def draw_obs_count(key, part):
    key = jax.random.fold_in(key, 7)
    devices = N_CELLS * N_SLOTS * N_MP
    counts = jax.random.randint(jax.random.fold_in(key, 1), (devices,), OBS_DEV // 2, OBS_DEV + 1)
    full_device = jax.random.randint(jax.random.fold_in(key, 2), (), 0, devices)
    return jnp.where(jnp.arange(devices) == full_device, OBS_DEV, counts).astype(jnp.int32)


def set_ends(entries, key, smallest, largest):
    extent = entries.shape
    place = [jax.random.randint(jax.random.fold_in(key, axis), (), 0, extent[axis]) for axis in range(len(extent))]
    entries = entries.at[tuple(place)].set(smallest)
    longest = extent.index(max(extent))
    place[longest] = (place[longest] + 1) % extent[longest]
    return entries.at[tuple(place)].set(largest)


def block_scale(key, shape, cuts, smallest, top_value):
    def one(axis_at, shards_of):
        steps = jax.random.uniform(jax.random.fold_in(jax.random.fold_in(key, 6), axis_at), (shards_of,), jnp.float32, smallest / len(cuts), top_value / len(cuts))
        return jnp.repeat(jnp.exp(steps), shape[axis_at] // shards_of).reshape((-1,) + (1,) * (len(shape) - axis_at - 1))

    loudness = one(*cuts[0])
    for cut in cuts[1:]:
        loudness = loudness * one(*cut)
    return loudness


def bell_draw(own_key, extent, deviation, most, shards=(), kind=jnp.bfloat16):
    result = deviation * jax.random.normal(own_key, extent, jnp.float32)
    if shards:
        result = result * block_scale(own_key, extent, shards, -0.22, 0.18)
    return jnp.clip(result, -most, most).astype(kind)


def setup_inputs(seed: int = 0, part: int = 0) -> dict:
    key_list = jax.random.split(jax.random.key(seed), 10)
    part_splits = jax.random.split(jax.random.fold_in(key_list[9], part), 10)
    return {
        "obs_feat": bell_draw(part_splits[0], (OBS, D), 1.0, 6.0, ((0, 16),)),
        "obs_cell": draw_obs_cell(jax.random.fold_in(jax.random.fold_in(key_list[9], part), 71), part),
        "obs_slot": set_ends(jax.random.randint(part_splits[2], (OBS,), 0, SLOT_DEV), jax.random.fold_in(part_splits[2], 1), 0, SLOT_DEV - 1).astype(jnp.int32),
        "obs_count": draw_obs_count(jax.random.fold_in(jax.random.fold_in(key_list[9], part), 71), part),
        "time_embed": bell_draw(key_list[4], (TSTEPS, D), 1.0, 6.0),
        "w_qkv": bell_draw(key_list[5], (D, 3, D), D ** -0.5, 0.21875, ((0, 4), (2, 2))),
        "w_out": bell_draw(key_list[6], (D, D), D ** -0.5, 0.21875, ((0, 2), (1, 4))),
        "w_gate_up": bell_draw(key_list[7], (D, 2, FF), D ** -0.5, 0.21875, ((0, 4), (2, 2))),
        "w_down": bell_draw(key_list[8], (FF, D), FF ** -0.5, 0.109375, ((0, 2), (1, 4))),
    }


EPS = 1e-06

def rms_scale(values):
    return values * lax.rsqrt(lax.optimization_barrier(jnp.mean(values * values, axis=-1, keepdims=True)) + EPS)

def encoder_layer(tokens_in, w_qkv, w_out, w_gate_up, w_down):
    item_count = tokens_in.shape[0]
    feat_width = tokens_in.shape[2]
    resid = tokens_in.astype(jnp.float32)
    normed = rms_scale(resid).astype(jnp.bfloat16)
    flat_rows = normed.reshape(-1, feat_width)
    head_count = w_qkv.shape[2] // HD
    projected = jnp.dot(flat_rows, w_qkv.reshape(feat_width, -1), preferred_element_type=jnp.float32)
    projected = projected.reshape(item_count, TSTEPS, 3, head_count, HD)
    queries = rms_scale(projected[:, :, 0]).astype(jnp.bfloat16)
    keys_att = rms_scale(projected[:, :, 1]).astype(jnp.bfloat16)
    values_att = projected[:, :, 2].astype(jnp.bfloat16)
    scores = jnp.einsum('cthe,cshe->chts', queries.astype(jnp.float32), keys_att.astype(jnp.float32)) * HD ** (-0.5)
    expo = jnp.exp(scores)
    attn_probs = (expo / lax.optimization_barrier(jnp.sum(expo, axis=-1, keepdims=True))).astype(jnp.bfloat16)
    context = jnp.einsum('chts,cshe->cthe', attn_probs.astype(jnp.float32), values_att.astype(jnp.float32))
    context = context.astype(jnp.bfloat16).reshape(-1, head_count * HD)
    attn_out = jnp.dot(context, w_out, preferred_element_type=jnp.float32)
    gate_up = jnp.dot(flat_rows, w_gate_up.reshape(feat_width, -1), preferred_element_type=jnp.float32)
    gate_up = gate_up.reshape(flat_rows.shape[0], 2, -1)
    hidden = (jax.nn.silu(gate_up[:, 0]) * gate_up[:, 1]).astype(jnp.bfloat16)
    mlp_out = jnp.dot(hidden, w_down, preferred_element_type=jnp.float32)
    summed = (attn_out + mlp_out).reshape(item_count, TSTEPS, feat_width)
    return (resid + summed).astype(jnp.bfloat16)

def reference(obs_feat, obs_cell, obs_slot, obs_count, time_embed, w_qkv, w_out, w_gate_up, w_down):
    row_ids = jnp.arange(OBS, dtype=jnp.int32)
    device_ids = row_ids // OBS_DEV
    valid_row = row_ids % OBS_DEV < obs_count[device_ids]
    slot_group = device_ids // N_MP % N_SLOTS
    time_step = slot_group * SLOT_DEV + obs_slot
    segment = jnp.where(valid_row, obs_cell * TSTEPS + time_step, CELLS * TSTEPS).astype(jnp.int32)
    pooled_sum = jax.ops.segment_sum(obs_feat.astype(jnp.float32), segment, num_segments=CELLS * TSTEPS + 1)[:-1]
    cell_count = jax.ops.segment_sum(jnp.ones((OBS,), jnp.float32), segment, num_segments=CELLS * TSTEPS + 1)[:-1]
    pooled = pooled_sum / jnp.maximum(cell_count, 1.0)[:, None]
    tokens = (pooled.reshape(CELLS, TSTEPS, D) + time_embed.astype(jnp.float32)[None]).astype(jnp.bfloat16)
    blocks = tokens.reshape(CELLS // CB, CB, TSTEPS, D)

    def apply_block(block_in):
        return encoder_layer(block_in, w_qkv, w_out, w_gate_up, w_down)
    mixed = lax.map(apply_block, blocks)
    return mixed.reshape(CELLS, TSTEPS, D)
```

```python
import jax
import jax.numpy as jnp
from jax import lax
from jax.sharding import PartitionSpec as P

HD = 64
TSTEPS = 8
CB = 128


EPS = 1e-06


def rms_scale(values):
    return values * lax.rsqrt(jnp.mean(values * values, axis=-1, keepdims=True) + EPS)


def gather_weights(local_rows):
    n_share = lax.axis_size("groups") * lax.axis_size("slots")
    share = local_rows.shape[0] // n_share
    which = lax.axis_index("groups") * lax.axis_size("slots") + lax.axis_index("slots")
    mine = lax.dynamic_slice_in_dim(local_rows, which * share, share, 0)
    mine = mine.reshape(share, -1)
    return lax.all_gather(mine, ("mp", "cells", "groups", "slots"), axis=0, tiled=True)


def on_device(obs_feat, obs_cell, obs_slot, obs_count, time_embed, w_qkv, w_out, w_gate_up, w_down):
    n_cells = lax.axis_size("cells")
    n_slots = lax.axis_size("slots")
    n_mp = lax.axis_size("mp")
    n_owners = n_cells * n_mp
    obs_rows = obs_feat.shape[0]
    feat_width = obs_feat.shape[1]
    capacity = 3 * obs_rows // n_owners
    quarter = CB // n_slots
    slot_dev = TSTEPS // n_slots
    my_owner = lax.axis_index("cells") * n_mp + lax.axis_index("mp")
    my_slot = lax.axis_index("slots")
    full_qkv = gather_weights(w_qkv)
    full_out = gather_weights(w_out.T)
    full_gate_up = gather_weights(w_gate_up)
    full_down = gather_weights(w_down.T)

    row_ids = jnp.arange(obs_rows, dtype=jnp.int32)
    valid_row = row_ids < obs_count[0]
    local_part = obs_cell % quarter
    mp_part = obs_cell // quarter % n_mp
    slot_part = obs_cell // (quarter * n_mp) % n_slots
    cell_part = obs_cell // (quarter * n_mp * n_slots)
    ahead = jnp.where(
        valid_row, (cell_part * n_mp + mp_part - my_owner + n_owners) % n_owners, n_owners
    )
    position = (slot_part * quarter + local_part) * slot_dev + obs_slot
    owner_hot = (ahead[:, None] == jnp.arange(n_owners, dtype=jnp.int32)[None, :]).astype(
        jnp.bfloat16
    )
    lower_tri = (row_ids[None, :] <= row_ids[:, None]).astype(jnp.bfloat16)
    running = jnp.dot(lower_tri, owner_hot, preferred_element_type=jnp.float32)
    slot_rank = jnp.sum(running * owner_hot.astype(jnp.float32), axis=1).astype(jnp.int32) - 1
    place = jnp.where(valid_row, ahead * capacity + slot_rank, n_owners * capacity)
    place_ids = jnp.arange(n_owners * capacity, dtype=jnp.int32)
    taken = place_ids[:, None] == place[None, :]
    send_pos = jnp.sum(jnp.where(taken, position[None, :] + 1, 0), axis=1) - 1
    send_pos = send_pos.reshape(n_owners, capacity)

    def shift(values, step):
        pairs = [(j, (j + step) % n_owners) for j in range(n_owners)]
        return lax.ppermute(values, ("cells", "mp"), pairs)

    got_feat, got_pos = [], []
    for step in range(n_owners):
        hot = taken[step * capacity : (step + 1) * capacity].astype(jnp.bfloat16)
        block = jnp.dot(hot, obs_feat, preferred_element_type=jnp.float32).astype(jnp.bfloat16)
        got_feat.append(shift(block, step) if step else block)
        got_pos.append(shift(send_pos[step], step) if step else send_pos[step])
    got_feat = jnp.concatenate(got_feat, axis=0)
    got_pos = jnp.concatenate(got_pos, axis=0)
    onehot_tab = (jnp.arange(CB * slot_dev, dtype=jnp.int32)[:, None] == got_pos[None, :]).astype(
        jnp.bfloat16
    )
    pooled_sum = jnp.dot(onehot_tab, got_feat, preferred_element_type=jnp.float32)
    cell_count = jnp.sum(onehot_tab.astype(jnp.float32), axis=1)
    pooled = pooled_sum / jnp.maximum(cell_count, 1.0)[:, None]
    slot_embed = lax.dynamic_slice_in_dim(time_embed, my_slot * slot_dev, slot_dev, 0)
    tokens = (
        pooled.reshape(CB, slot_dev, feat_width) + slot_embed.astype(jnp.float32)[None]
    ).astype(jnp.bfloat16)
    token_grid = tokens.reshape(n_slots, quarter, slot_dev, feat_width)
    token_block = lax.all_to_all(token_grid, "slots", split_axis=0, concat_axis=2, tiled=True)
    resid = token_block.reshape(quarter, TSTEPS, feat_width).astype(jnp.float32)
    normed = rms_scale(resid).astype(jnp.bfloat16)
    flat_rows = normed.reshape(-1, feat_width)
    n_rows = flat_rows.shape[0]
    head_count = w_qkv.shape[2] // HD

    total = resid.reshape(n_rows, feat_width)
    for part in range(n_mp):
        rows = slice(part * feat_width, (part + 1) * feat_width)
        projected = jnp.dot(flat_rows, full_qkv[rows], preferred_element_type=jnp.float32)
        projected = projected.reshape(quarter, TSTEPS, 3, head_count, HD)
        queries = rms_scale(projected[:, :, 0]).astype(jnp.bfloat16)
        keys_att = rms_scale(projected[:, :, 1]).astype(jnp.bfloat16)
        values_att = projected[:, :, 2].astype(jnp.bfloat16)
        scores = jnp.einsum(
            "cthe,cshe->chts", queries, keys_att, preferred_element_type=jnp.float32
        ) * HD ** (-0.5)
        expo = jnp.exp(scores)
        attn_probs = (expo / jnp.sum(expo, axis=-1, keepdims=True)).astype(jnp.bfloat16)
        context = jnp.einsum(
            "chts,cshe->cthe", attn_probs, values_att, preferred_element_type=jnp.float32
        )
        context = context.astype(jnp.bfloat16).reshape(n_rows, head_count * HD)
        total += jnp.dot(context, full_out[rows].T, preferred_element_type=jnp.float32)
        gate_up = jnp.dot(flat_rows, full_gate_up[rows], preferred_element_type=jnp.float32)
        hidden_width = gate_up.shape[1] // 2
        hidden = jax.nn.silu(gate_up[:, :hidden_width]) * gate_up[:, hidden_width:]
        total += jnp.dot(
            hidden.astype(jnp.bfloat16), full_down[rows].T, preferred_element_type=jnp.float32
        )
    return total.astype(jnp.bfloat16).reshape(quarter, TSTEPS, feat_width)


def solution(mesh):
    placed = (
        P(("groups", "cells", "slots", "mp"), None),
        P(("groups", "cells", "slots", "mp")),
        P(("groups", "cells", "slots", "mp")),
        P(("groups", "cells", "slots", "mp")),
        P(),
        P("cells", None, "mp"),
        P("mp", "cells"),
        P("cells", None, "mp"),
        P("mp", "cells"),
    )
    return jax.shard_map(
        on_device,
        mesh=mesh,
        in_specs=placed,
        out_specs=P(("groups", "cells", "slots", "mp"), None, None),
        check_vma=False,
    )
```

```python
import functools

import jax
import jax.numpy as jnp
from jax import lax
from jax.experimental import pallas as pl
from jax.experimental.pallas import tpu as pltpu
from jax.sharding import PartitionSpec as P

HD = 64
TSTEPS = 8
CB = 128
EPS = 1e-06

META_ROWS = 16
CODE = 32
LANES = 128
VMEM_LIMIT = 48 * 1024 * 1024
F32 = jnp.float32
BF16 = jnp.bfloat16
WHOLE = pl.BlockSpec(memory_space=pltpu.VMEM)
SCALARS = pl.BlockSpec(memory_space=pltpu.SMEM)


def iota(shape, axis):
    return lax.broadcasted_iota(jnp.int32, shape, axis)


def dot(left, right):
    return jnp.dot(left, right, preferred_element_type=F32)


def dot_t(left, right):
    return lax.dot_general(left, right, (((1,), (1,)), ((), ())), preferred_element_type=F32)


def params(**extra):
    return pltpu.CompilerParams(vmem_limit_bytes=VMEM_LIMIT, **extra)


def place_kernel(n_owners, capacity, ahead_ref, position_ref, feat_ref, *out_refs):
    rows = feat_ref.shape[0]
    ahead = ahead_ref[...]
    owner_hot = (iota((n_owners, rows), 0) == ahead).astype(F32)
    upper = (iota((rows, rows), 0) <= iota((rows, rows), 1)).astype(BF16)
    running = dot(owner_hot.astype(BF16), upper)
    rank = jnp.sum(running * owner_hot, axis=0, keepdims=True).astype(jnp.int32) - 1
    code = position_ref[...] + 1
    line = iota((META_ROWS, rows), 0)
    meta = jnp.where(line == 0, code // CODE, jnp.where(line == 1, code % CODE, 0))
    meta = meta.astype(F32).astype(BF16)
    feat = feat_ref[...]
    for block in range(n_owners):
        place = jnp.where(ahead == block, rank, -1)
        taken = (iota((capacity, rows), 0) == place).astype(F32).astype(BF16)
        out = out_refs[block]
        out[:capacity, :] = dot(taken, feat).astype(BF16)
        out[capacity:, :] = jnp.zeros((META_ROWS, out.shape[1]), BF16)
        out[capacity:, :capacity] = dot_t(meta, taken).astype(BF16)


def place_rows(ahead, position, obs_feat, n_owners, capacity):
    rows, width = obs_feat.shape
    block = jax.ShapeDtypeStruct((capacity + META_ROWS, width), BF16)
    return pl.pallas_call(
        functools.partial(place_kernel, n_owners, capacity),
        out_shape=[block] * n_owners,
        in_specs=[WHOLE] * 3,
        out_specs=[WHOLE] * n_owners,
        compiler_params=params(),
        cost_estimate=pl.CostEstimate(
            flops=2 * rows * width * n_owners * capacity,
            bytes_accessed=2 * width * (rows + n_owners * capacity),
            transcendentals=0,
        ),
        name="place_rows",
    )(ahead.reshape(1, rows), position.reshape(1, rows), obs_feat)


def pool_kernel(capacity, slot_dev, slot_ref, embed_ref, *refs):
    block_refs, (keep_ref, send_ref) = refs[:-2], refs[-2:]
    half = keep_ref.shape[0]
    places = 2 * half
    mine = slot_ref[0]
    total = jnp.zeros((places, keep_ref.shape[1]), F32)
    seen = jnp.zeros((places, capacity), F32)
    for block in block_refs:
        meta = block[capacity:, :capacity].astype(F32)
        code = (meta[0:1] * CODE + meta[1:2]).astype(jnp.int32) - 1
        turned = jnp.where(code >= half, code - half, code + half)
        code = jnp.where((code >= 0) & (mine == 1), turned, code)
        hot = (iota((places, capacity), 0) == code).astype(F32)
        seen += hot
        total += dot(hot.astype(BF16), block[:capacity, :])
    count = jnp.sum(seen, axis=1, keepdims=True)
    steps = embed_ref.shape[0]
    step_hot = iota((places, steps), 1) == iota((places, steps), 0) % slot_dev + mine * slot_dev
    embed = dot(step_hot.astype(F32).astype(BF16), embed_ref[...])
    tokens = (total / jnp.maximum(count, 1.0) + embed).astype(BF16)
    keep_ref[...] = tokens[:half]
    send_ref[...] = tokens[half:]


def pool_rows(my_slot, time_embed, blocks, capacity, slot_dev):
    width = time_embed.shape[1]
    half = jax.ShapeDtypeStruct((CB * slot_dev // 2, width), BF16)
    return pl.pallas_call(
        functools.partial(pool_kernel, capacity, slot_dev),
        out_shape=[half, half],
        in_specs=[SCALARS] + [WHOLE] * (1 + len(blocks)),
        out_specs=[WHOLE] * 2,
        compiler_params=params(),
        cost_estimate=pl.CostEstimate(
            flops=2 * CB * slot_dev * width * len(blocks) * capacity,
            bytes_accessed=2 * width * (CB * slot_dev + len(blocks) * capacity),
            transcendentals=0,
        ),
        name="pool_rows",
    )(my_slot, time_embed, *blocks)


def weave_kernel(slot_dev, slot_ref, keep_ref, got_ref, out_ref):
    rows, half = out_ref.shape[0], keep_ref.shape[0]
    mine = slot_ref[0]
    row, col = iota((rows, half), 0), iota((rows, half), 1)
    source = col == row // TSTEPS * slot_dev + row % slot_dev
    own = row % TSTEPS // slot_dev == mine
    from_keep = (source & own).astype(F32).astype(BF16)
    from_got = (source & jnp.logical_not(own)).astype(F32).astype(BF16)
    out_ref[...] = (dot(from_keep, keep_ref[...]) + dot(from_got, got_ref[...])).astype(BF16)


def weave_steps(my_slot, keep, got, slot_dev):
    rows, width = 2 * keep.shape[0], keep.shape[1]
    return pl.pallas_call(
        functools.partial(weave_kernel, slot_dev),
        out_shape=jax.ShapeDtypeStruct((rows, width), BF16),
        in_specs=[SCALARS, WHOLE, WHOLE],
        out_specs=WHOLE,
        compiler_params=params(),
        cost_estimate=pl.CostEstimate(
            flops=2 * rows * rows * width, bytes_accessed=4 * rows * width, transcendentals=0
        ),
        name="weave_steps",
    )(my_slot, keep, got)


def head_scale(values, ones):
    square = values * values
    high = square.astype(BF16)
    low = (square - high.astype(F32)).astype(BF16)
    sums = dot(high, ones) + dot(low, ones)
    return (values * lax.rsqrt(sums * (1.0 / HD) + EPS)).astype(BF16)


def layer_kernel(
    heads_width, tok_ref, qkv_ref, out_w_ref, gate_ref, up_ref, down_ref, out_ref, norm_ref, acc_ref, ctx_ref
):
    step = pl.program_id(0)
    rows = tok_ref.shape[0]

    @pl.when(step == 0)
    def attention():
        tokens = tok_ref[...].astype(F32)
        scale = lax.rsqrt(jnp.mean(tokens * tokens, axis=1, keepdims=True) + EPS)
        normed = (tokens * scale).astype(BF16)
        norm_ref[...] = normed
        projected = dot(normed, qkv_ref[...])
        same_head = iota((LANES, LANES), 0) // HD == iota((LANES, LANES), 1) // HD
        ones = same_head.astype(F32).astype(BF16)
        group = LANES
        first = iota((group, LANES), 1) < HD
        row, col = iota((2 * group, group), 0), iota((2 * group, group), 1)
        same_cell = row % group // TSTEPS == col // TSTEPS
        for pair in range(heads_width // LANES):
            at = pair * LANES
            query = head_scale(projected[:, at : at + LANES], ones)
            key = head_scale(projected[:, heads_width + at : heads_width + at + LANES], ones)
            value = projected[:, 2 * heads_width + at : 2 * heads_width + at + LANES].astype(BF16)
            for begin in range(0, rows, group):
                q = query[begin : begin + group]
                k = key[begin : begin + group]
                v = value[begin : begin + group]
                both = jnp.concatenate(
                    [jnp.where(first, q, jnp.zeros_like(q)), jnp.where(first, jnp.zeros_like(q), q)], axis=0
                )
                scores = dot_t(both, k) * HD ** (-0.5)
                expo = jnp.where(same_cell, jnp.exp(scores), 0.0)
                probs = (expo / jnp.sum(expo, axis=1, keepdims=True)).astype(BF16)
                mixed = dot(probs, v)
                ctx = jnp.where(first, mixed[:group], mixed[group:])
                ctx_ref[begin : begin + group, at : at + LANES] = ctx.astype(BF16)
        acc_ref[...] = dot_t(ctx_ref[...], out_w_ref[...])

    @pl.when(step > 0)
    def gated():
        normed = norm_ref[...]
        gate = dot(normed, gate_ref[...])
        up = dot(normed, up_ref[...])
        hidden = (gate / (1.0 + jnp.exp(-gate)) * up).astype(BF16)
        acc_ref[...] += dot_t(hidden, down_ref[...])

    @pl.when(step == pl.num_programs(0) - 1)
    def finish():
        out_ref[...] = acc_ref[...].astype(out_ref.dtype)


def layer(tokens, weights, heads_width, hidden_width, out_type):
    rows, width = tokens.shape
    chunk = heads_width
    steps = hidden_width // chunk
    gate_at = 3
    up_at = gate_at + steps
    out_at = up_at + steps
    down_at = out_at + 1

    def chunk_spec(at):
        return pl.BlockSpec((width, chunk), lambda i: (0, at + jnp.maximum(i - 1, 0)))

    flops = 2 * rows * width * weights.shape[1]
    return pl.pallas_call(
        functools.partial(layer_kernel, heads_width),
        out_shape=jax.ShapeDtypeStruct((rows, width), out_type),
        grid=(1 + steps,),
        in_specs=[
            pl.BlockSpec((rows, width), lambda i: (0, 0)),
            pl.BlockSpec((width, 3 * chunk), lambda i: (0, 0)),
            pl.BlockSpec((width, chunk), lambda i: (0, out_at)),
            chunk_spec(gate_at),
            chunk_spec(up_at),
            chunk_spec(down_at),
        ],
        out_specs=pl.BlockSpec((rows, width), lambda i: (0, 0)),
        scratch_shapes=[
            pltpu.VMEM((rows, width), BF16),
            pltpu.VMEM((rows, width), F32),
            pltpu.VMEM((rows, heads_width), BF16),
        ],
        compiler_params=params(dimension_semantics=("arbitrary",)),
        cost_estimate=pl.CostEstimate(
            flops=flops, bytes_accessed=2 * weights.size + 4 * rows * width, transcendentals=rows * hidden_width
        ),
        name="layer",
    )(tokens, weights, weights, weights, weights, weights)


def gather_weights(w_qkv, w_out, w_gate_up, w_down):
    n_share = lax.axis_size("groups") * lax.axis_size("slots")
    which = lax.axis_index("groups") * lax.axis_size("slots") + lax.axis_index("slots")
    parts = []
    for weight in (w_qkv, w_gate_up, w_out.T, w_down.T):
        share = weight.shape[0] // n_share
        mine = lax.dynamic_slice_in_dim(weight, which * share, share, 0)
        parts.append(mine.reshape(share, -1))
    mine = jnp.concatenate(parts, axis=1)
    return lax.all_gather(mine, ("cells", "groups", "slots"), axis=0, tiled=True)


def tokens_by_permutes(ahead, position, obs_feat, time_embed, my_slot, capacity, slot_dev):
    n_owners = lax.axis_size("cells") * lax.axis_size("mp")
    blocks = place_rows(ahead, position, obs_feat, n_owners, capacity)

    def shift(values, step):
        pairs = [(j, (j + step) % n_owners) for j in range(n_owners)]
        return lax.ppermute(values, ("cells", "mp"), pairs)

    got = [blocks[0]] + [shift(blocks[step], step) for step in range(1, n_owners)]
    keep, send = pool_rows(my_slot.reshape(1), time_embed, got, capacity, slot_dev)
    other = lax.ppermute(send, "slots", [(0, 1), (1, 0)])
    return weave_steps(my_slot.reshape(1), keep, other, slot_dev)


def tokens_by_exchanges(ahead, position, obs_feat, time_embed, my_slot, capacity, slot_dev):
    n_slots = lax.axis_size("slots")
    n_owners = lax.axis_size("cells") * lax.axis_size("mp")
    my_owner = lax.axis_index("cells") * lax.axis_size("mp") + lax.axis_index("mp")
    rows, width = obs_feat.shape
    owners = jnp.arange(n_owners, dtype=jnp.int32)
    owner = jnp.where(ahead < n_owners, (ahead + my_owner) % n_owners, n_owners)
    owner_hot = (owner[:, None] == owners[None, :]).astype(F32)
    row_ids = jnp.arange(rows, dtype=jnp.int32)
    lower = (row_ids[None, :] <= row_ids[:, None]).astype(BF16)
    running = dot(lower, owner_hot.astype(BF16))
    rank = jnp.sum(running * owner_hot, axis=1).astype(jnp.int32) - 1
    place = jnp.where(owner < n_owners, owner * capacity + rank, n_owners * capacity)
    place_ids = jnp.arange(n_owners * capacity, dtype=jnp.int32)
    taken = place_ids[:, None] == place[None, :]
    send_feat = dot(taken.astype(BF16), obs_feat).astype(BF16).reshape(n_owners, capacity, width)
    send_code = jnp.sum(jnp.where(taken, position[None, :] + 1, 0), axis=1).reshape(n_owners, capacity)
    axes = ("cells", "mp")
    got_feat = lax.all_to_all(send_feat, axes, split_axis=0, concat_axis=0, tiled=True).reshape(-1, width)
    got_code = lax.all_to_all(send_code, axes, split_axis=0, concat_axis=0, tiled=True).reshape(-1) - 1
    hot = (jnp.arange(CB * slot_dev, dtype=jnp.int32)[:, None] == got_code[None, :]).astype(BF16)
    count = jnp.sum(hot.astype(F32), axis=1)
    pooled = dot(hot, got_feat) / jnp.maximum(count, 1.0)[:, None]
    embed = lax.dynamic_slice_in_dim(time_embed, my_slot * slot_dev, slot_dev, 0).astype(F32)
    tokens = (pooled.reshape(CB, slot_dev, width) + embed[None]).astype(BF16)
    grid = tokens.reshape(n_slots, CB // n_slots, slot_dev, width)
    grid = lax.all_to_all(grid, "slots", split_axis=0, concat_axis=2, tiled=True)
    return grid.reshape(-1, width)


def on_device(obs_feat, obs_cell, obs_slot, obs_count, time_embed, w_qkv, w_out, w_gate_up, w_down):
    n_cells = lax.axis_size("cells")
    n_slots = lax.axis_size("slots")
    n_mp = lax.axis_size("mp")
    n_owners = n_cells * n_mp
    rows, width = obs_feat.shape
    capacity = 3 * rows // n_owners
    quarter = CB // n_slots
    slot_dev = TSTEPS // n_slots
    my_owner = lax.axis_index("cells") * n_mp + lax.axis_index("mp")
    my_slot = lax.axis_index("slots")
    weights = gather_weights(w_qkv, w_out, w_gate_up, w_down)

    valid = jnp.arange(rows, dtype=jnp.int32) < obs_count[0]
    owner = obs_cell // (quarter * n_mp * n_slots) * n_mp + obs_cell // quarter % n_mp
    ahead = jnp.where(valid, (owner - my_owner + n_owners) % n_owners, n_owners)
    local = obs_cell // (quarter * n_mp) % n_slots * quarter + obs_cell % quarter
    position = local * slot_dev + obs_slot
    route = tokens_by_permutes if n_slots == 2 and capacity % 16 == 0 else tokens_by_exchanges
    tokens = route(ahead, position, obs_feat, time_embed, my_slot, capacity, slot_dev)

    swap = [(0, 1), (1, 0)]
    heads_width, hidden_width = w_qkv.shape[2], w_gate_up.shape[2]
    partner = lax.ppermute(tokens, "mp", swap)
    for_partner = layer(partner, weights, heads_width, hidden_width, BF16)
    from_partner = lax.ppermute(for_partner, "mp", swap)
    own = layer(tokens, weights, heads_width, hidden_width, F32)
    mixed = tokens.astype(F32) + own + from_partner.astype(F32)
    return mixed.astype(BF16).reshape(quarter, TSTEPS, width)


def solution(mesh):
    placed = (
        P(("groups", "cells", "slots", "mp"), None),
        P(("groups", "cells", "slots", "mp")),
        P(("groups", "cells", "slots", "mp")),
        P(("groups", "cells", "slots", "mp")),
        P(),
        P("cells", None, "mp"),
        P("mp", "cells"),
        P("cells", None, "mp"),
        P("mp", "cells"),
    )
    return jax.shard_map(
        on_device,
        mesh=mesh,
        in_specs=placed,
        out_specs=P(("groups", "cells", "slots", "mp"), None, None),
        check_vma=False,
    )
```

```python
import functools

import jax
import jax.numpy as jnp
from jax import lax
from jax.experimental import pallas as pl
from jax.experimental.pallas import tpu as pltpu
from jax.sharding import PartitionSpec as P

HD = 64
TSTEPS = 8
CB = 128
EPS = 1e-06

META_ROWS = 16
CODE = 32
LANES = 128
VMEM_LIMIT = 48 * 1024 * 1024
F32 = jnp.float32
BF16 = jnp.bfloat16
WHOLE = pl.BlockSpec(memory_space=pltpu.VMEM)
SCALARS = pl.BlockSpec(memory_space=pltpu.SMEM)


def iota(shape, axis):
    return lax.broadcasted_iota(jnp.int32, shape, axis)


def dot(left, right):
    return jnp.dot(left, right, preferred_element_type=F32)


def dot_t(left, right):
    return lax.dot_general(left, right, (((1,), (1,)), ((), ())), preferred_element_type=F32)


def params():
    return pltpu.CompilerParams(vmem_limit_bytes=VMEM_LIMIT)


def place_kernel(capacity, owner_ref, position_ref, feat_ref, out_ref):
    n_owners, rows = out_ref.shape[0], feat_ref.shape[0]
    owner = owner_ref[...]
    owner_hot = (iota((n_owners, rows), 0) == owner).astype(F32)
    upper = (iota((rows, rows), 0) <= iota((rows, rows), 1)).astype(BF16)
    running = dot(owner_hot.astype(BF16), upper)
    rank = jnp.sum(running * owner_hot, axis=0, keepdims=True).astype(jnp.int32) - 1
    code = position_ref[...] + 1
    line = iota((META_ROWS, rows), 0)
    meta = jnp.where(line == 0, code // CODE, jnp.where(line == 1, code % CODE, 0))
    meta = meta.astype(F32).astype(BF16)
    feat = feat_ref[...]
    for block in range(n_owners):
        place = jnp.where(owner == block, rank, -1)
        taken = (iota((capacity, rows), 0) == place).astype(F32).astype(BF16)
        out_ref[block, :capacity, :] = dot(taken, feat).astype(BF16)
        out_ref[block, capacity:, :] = jnp.zeros((META_ROWS, feat.shape[1]), BF16)
        out_ref[block, capacity:, :capacity] = dot_t(meta, taken).astype(BF16)


def place_rows(owner, position, obs_feat, n_owners, capacity):
    rows, width = obs_feat.shape
    return pl.pallas_call(
        functools.partial(place_kernel, capacity),
        out_shape=jax.ShapeDtypeStruct((n_owners, capacity + META_ROWS, width), BF16),
        in_specs=[WHOLE] * 3,
        out_specs=WHOLE,
        compiler_params=params(),
        cost_estimate=pl.CostEstimate(
            flops=2 * rows * width * n_owners * capacity,
            bytes_accessed=2 * width * (rows + n_owners * capacity),
            transcendentals=0,
        ),
        name="place_rows",
    )(owner.reshape(1, rows), position.reshape(1, rows), obs_feat)


def pool_kernel(capacity, slot_dev, slot_ref, embed_ref, got_ref, keep_ref, send_ref):
    half = keep_ref.shape[0]
    places = 2 * half
    mine = slot_ref[0]
    total = jnp.zeros((places, keep_ref.shape[1]), F32)
    seen = jnp.zeros((places, capacity), F32)
    for block in range(got_ref.shape[0]):
        meta = got_ref[block, capacity:, :capacity].astype(F32)
        code = (meta[0:1] * CODE + meta[1:2]).astype(jnp.int32) - 1
        turned = jnp.where(code >= half, code - half, code + half)
        code = jnp.where((code >= 0) & (mine == 1), turned, code)
        hot = (iota((places, capacity), 0) == code).astype(F32)
        seen += hot
        total += dot(hot.astype(BF16), got_ref[block, :capacity, :])
    count = jnp.sum(seen, axis=1, keepdims=True)
    steps = embed_ref.shape[0]
    step_hot = iota((places, steps), 1) == iota((places, steps), 0) % slot_dev + mine * slot_dev
    embed = dot(step_hot.astype(F32).astype(BF16), embed_ref[...])
    tokens = (total / jnp.maximum(count, 1.0) + embed).astype(BF16)
    keep_ref[...] = tokens[:half]
    send_ref[...] = tokens[half:]


def pool_rows(my_slot, time_embed, got, capacity, slot_dev):
    width = time_embed.shape[1]
    half = jax.ShapeDtypeStruct((CB * slot_dev // 2, width), BF16)
    return pl.pallas_call(
        functools.partial(pool_kernel, capacity, slot_dev),
        out_shape=[half, half],
        in_specs=[SCALARS, WHOLE, WHOLE],
        out_specs=[WHOLE] * 2,
        compiler_params=params(),
        cost_estimate=pl.CostEstimate(
            flops=2 * CB * slot_dev * got.size, bytes_accessed=2 * got.size, transcendentals=0
        ),
        name="pool_rows",
    )(my_slot, time_embed, got)


def weave_kernel(slot_dev, slot_ref, order_ref, keep_ref, got_ref, out_ref):
    rows, width = out_ref.shape
    half = keep_ref.shape[0]
    mine = slot_ref[0]
    row, col = iota((rows, half), 0), iota((rows, half), 1)
    source = col == row // TSTEPS * slot_dev + row % slot_dev
    own = row % TSTEPS // slot_dev == mine
    from_keep = (source & own).astype(F32).astype(BF16)
    from_got = (source & jnp.logical_not(own)).astype(F32).astype(BF16)
    tokens = (dot(from_keep, keep_ref[...]) + dot(from_got, got_ref[...])).astype(BF16)
    move = (iota((width, width), 0) == order_ref[...]).astype(F32).astype(BF16)
    out_ref[...] = dot(tokens, move).astype(BF16)


def weave_steps(my_slot, order, keep, got, slot_dev):
    rows, width = 2 * keep.shape[0], keep.shape[1]
    return pl.pallas_call(
        functools.partial(weave_kernel, slot_dev),
        out_shape=jax.ShapeDtypeStruct((rows, width), BF16),
        in_specs=[SCALARS] + [WHOLE] * 3,
        out_specs=WHOLE,
        compiler_params=params(),
        cost_estimate=pl.CostEstimate(
            flops=2 * rows * width * (rows + width), bytes_accessed=4 * rows * width, transcendentals=0
        ),
        name="weave_steps",
    )(my_slot, order.reshape(1, width), keep, got)


def head_scale(values, ones):
    square = values * values
    high = square.astype(BF16)
    low = (square - high.astype(F32)).astype(BF16)
    sums = dot(high, ones) + dot(low, ones)
    return (values * lax.rsqrt(sums * (1.0 / HD) + EPS)).astype(BF16)


def attention(normed, weight, heads_width, ctx_ref):
    rows = normed.shape[0]
    projected = dot(normed, weight)
    same_head = iota((LANES, LANES), 0) // HD == iota((LANES, LANES), 1) // HD
    ones = same_head.astype(F32).astype(BF16)
    group = LANES
    first = iota((group, LANES), 1) < HD
    row, col = iota((2 * group, group), 0), iota((2 * group, group), 1)
    same_cell = row % group // TSTEPS == col // TSTEPS
    for pair in range(heads_width // LANES):
        at = pair * LANES
        query = head_scale(projected[:, at : at + LANES], ones)
        key = head_scale(projected[:, heads_width + at : heads_width + at + LANES], ones)
        value = projected[:, 2 * heads_width + at : 2 * heads_width + at + LANES].astype(BF16)
        for begin in range(0, rows, group):
            q = query[begin : begin + group]
            k = key[begin : begin + group]
            v = value[begin : begin + group]
            none = jnp.zeros_like(q)
            both = jnp.concatenate([jnp.where(first, q, none), jnp.where(first, none, q)], axis=0)
            scores = dot_t(both, k) * HD ** (-0.5)
            expo = jnp.where(same_cell, jnp.exp(scores), 0.0)
            probs = (expo / jnp.sum(expo, axis=1, keepdims=True)).astype(BF16)
            mixed = dot(probs, v)
            ctx = jnp.where(first, mixed[:group], mixed[group:])
            ctx_ref[begin : begin + group, at : at + LANES] = ctx.astype(BF16)


def gated(normed, gate_w, up_w, down_w):
    gate = dot(normed, gate_w)
    up = dot(normed, up_w)
    hidden = (gate / (1.0 + jnp.exp(-gate)) * up).astype(BF16)
    return dot_t(hidden, down_w)


def chunk_kernel(plan, unit, n_units, with_heads, n_sets, n_pieces, *refs):
    refs = list(refs)
    take = lambda count: [refs.pop(0) for _ in range(count)]
    rows_in = take(n_sets)
    sums_in = [None] * n_sets if with_heads else take(n_sets)
    pieces = take(n_pieces)
    norm_out = take(n_sets) if with_heads else rows_in
    sums_out = take(n_sets)
    w_ref, ctx_ref, sems = take(3)
    width = w_ref.shape[0]
    copies = {}
    for number, (section, piece, source_col, row, col, size) in enumerate(plan):
        copy = pltpu.make_async_copy(
            pieces[piece].at[:, pl.ds(source_col, size)],
            w_ref.at[pl.ds(row, pieces[piece].shape[0]), pl.ds(col, size)],
            sems.at[number],
        )
        copy.start()
        copies.setdefault(section, []).append(copy)

    def ready(sections):
        for section in sections:
            for copy in copies.pop(section, []):
                copy.wait()

    def columns(first, count):
        return w_ref[:, first * unit : (first + count) * unit]

    begin = 0
    sums = sums_in
    if with_heads:
        for rows_ref, norm_ref in zip(rows_in, norm_out):
            tokens = rows_ref[...].astype(F32)
            scale = lax.rsqrt(jnp.mean(tokens * tokens, axis=1, keepdims=True) + EPS)
            norm_ref[...] = (tokens * scale).astype(BF16)
        ready(range(4))
        for norm_ref, sum_ref in zip(norm_out, sums_out):
            attention(norm_ref[...], columns(0, 3), unit, ctx_ref)
            sum_ref[...] = dot_t(ctx_ref[...], columns(3, 1))
        begin, sums = 4, sums_out
    for number in range(n_units):
        at = begin + 3 * number
        ready(range(at, at + 3))
        for norm_ref, sum_ref, out_ref in zip(norm_out, sums, sums_out):
            add = gated(norm_ref[...], columns(at, 1), columns(at + 1, 1), columns(at + 2, 1))
            out_ref[...] = (sum_ref[...] + add).astype(out_ref.dtype)
        sums = sums_out


def layer_chunk(rows_in, sums_in, pieces, unit, with_heads, out_type):
    n_sets = len(rows_in)
    rows, width = rows_in[0].shape
    columns = max(at + array.shape[1] for array, _, at in pieces)
    n_units = (columns // unit - 4 * with_heads) // 3
    plan = []
    for section in range(columns // unit):
        left, right = section * unit, (section + 1) * unit
        for number, (array, row, at) in enumerate(pieces):
            low, high = max(left, at), min(right, at + array.shape[1])
            if low < high:
                plan.append((section, number, low - at, row, low, high - low))
    like = lambda kind: jax.ShapeDtypeStruct((rows, width), kind)
    outs = [like(BF16)] * (n_sets * with_heads) + [like(out_type)] * n_sets
    results = pl.pallas_call(
        functools.partial(chunk_kernel, plan, unit, n_units, with_heads, n_sets, len(pieces)),
        out_shape=outs,
        in_specs=[WHOLE] * (len(rows_in) + len(sums_in)) + [pl.BlockSpec(memory_space=pl.ANY)] * len(pieces),
        out_specs=[WHOLE] * len(outs),
        scratch_shapes=[
            pltpu.VMEM((width, columns), BF16),
            pltpu.VMEM((rows, unit), BF16),
            pltpu.SemaphoreType.DMA((len(plan),)),
        ],
        compiler_params=params(),
        cost_estimate=pl.CostEstimate(
            flops=2 * n_sets * rows * width * columns,
            bytes_accessed=2 * width * columns + 8 * n_sets * rows * width,
            transcendentals=n_sets * n_units * rows * unit,
        ),
        name="layer_heads" if with_heads else "layer_gated",
    )(*rows_in, *sums_in, *[array for array, _, _ in pieces])
    return results[: -n_sets] if with_heads else rows_in, results[-n_sets:]


def finish_kernel(tok_ref, sum_ref, got_ref, order_ref, out_ref):
    width = out_ref.shape[1]
    mixed = (tok_ref[...].astype(F32) + sum_ref[...] + got_ref[...].astype(F32)).astype(BF16)
    move = (iota((width, width), 0) == order_ref[...]).astype(F32).astype(BF16)
    out_ref[...] = dot_t(mixed, move).astype(BF16)


def finish(tokens, sums, got, order):
    rows, width = tokens.shape
    return pl.pallas_call(
        finish_kernel,
        out_shape=jax.ShapeDtypeStruct((rows, width), BF16),
        in_specs=[WHOLE] * 4,
        out_specs=WHOLE,
        compiler_params=params(),
        cost_estimate=pl.CostEstimate(
            flops=2 * rows * width * width, bytes_accessed=10 * rows * width, transcendentals=0
        ),
        name="finish",
    )(tokens, sums, got, order.reshape(1, width))


def chunk_columns(w_qkv, w_out, w_gate_up, w_down, units):
    unit = w_qkv.shape[2]
    parts = []
    for number in units:
        if number < 0:
            parts += [w_qkv[:, 0], w_qkv[:, 1], w_qkv[:, 2], w_out]
        else:
            cols = slice(number * unit, (number + 1) * unit)
            parts += [w_gate_up[:, 0, cols], w_gate_up[:, 1, cols], w_down[:, cols]]
    return jnp.concatenate(parts, axis=1)


def chunk_pieces(shard, share_rows):
    n_cells = lax.axis_size("cells")
    rows = shard.shape[0]
    share = share_rows.shape[0]
    mine = lax.axis_index("cells")
    lines = lax.all_gather(share_rows, "cells", axis=0, tiled=True)
    others = jnp.concatenate(
        [
            lax.dynamic_slice_in_dim(lines, (mine + ahead) % n_cells * share, share, 0)
            for ahead in range(1, n_cells)
        ],
        axis=0,
    )
    swap = [(0, 1), (1, 0)]
    by_slot = lax.ppermute(others, "slots", swap)
    by_group = lax.ppermute(others, "groups", swap)
    cut = shard.shape[1] // (2 * LANES) * LANES
    far_a = lax.ppermute(by_slot[:, :cut], "groups", swap)
    far_b = lax.ppermute(by_group[:, cut:], "slots", swap)
    step = others.shape[0]
    return [
        (shard, 0, 0),
        (others, rows, 0),
        (by_slot, rows + step, 0),
        (by_group, rows + 2 * step, 0),
        (far_a, rows + 3 * step, 0),
        (far_b, rows + 3 * step, cut),
    ]


def arrival_order(width, n_cells, n_share):
    mine = lax.axis_index("cells")
    share_id = lax.axis_index("groups") * lax.axis_size("slots") + lax.axis_index("slots")
    rows = width // n_cells
    share = rows // n_share
    step = (n_cells - 1) * share
    place = jnp.arange(width, dtype=jnp.int32)
    past = jnp.maximum(place - rows, 0)
    which = past // step
    cell = (mine + 1 + past % step // share) % n_cells
    far = cell * rows + (which ^ share_id) * share + past % share
    return jnp.where(place < rows, mine * rows + place, far)


def tokens_by_blocks(owner, position, obs_feat, time_embed, my_slot, capacity, slot_dev, order):
    n_owners = lax.axis_size("cells") * lax.axis_size("mp")
    blocks = place_rows(owner, position, obs_feat, n_owners, capacity)
    got = lax.all_to_all(blocks, ("cells", "mp"), split_axis=0, concat_axis=0, tiled=True)
    keep, send = pool_rows(my_slot.reshape(1), time_embed, got, capacity, slot_dev)
    other = lax.ppermute(send, "slots", [(0, 1), (1, 0)])
    return weave_steps(my_slot.reshape(1), order, keep, other, slot_dev)


def tokens_by_exchanges(owner, position, obs_feat, time_embed, my_slot, capacity, slot_dev):
    n_slots = lax.axis_size("slots")
    n_owners = lax.axis_size("cells") * lax.axis_size("mp")
    rows, width = obs_feat.shape
    owners = jnp.arange(n_owners, dtype=jnp.int32)
    owner_hot = (owner[:, None] == owners[None, :]).astype(F32)
    row_ids = jnp.arange(rows, dtype=jnp.int32)
    lower = (row_ids[None, :] <= row_ids[:, None]).astype(BF16)
    running = dot(lower, owner_hot.astype(BF16))
    rank = jnp.sum(running * owner_hot, axis=1).astype(jnp.int32) - 1
    place = jnp.where(owner < n_owners, owner * capacity + rank, n_owners * capacity)
    place_ids = jnp.arange(n_owners * capacity, dtype=jnp.int32)
    taken = place_ids[:, None] == place[None, :]
    send_feat = dot(taken.astype(BF16), obs_feat).astype(BF16).reshape(n_owners, capacity, width)
    send_code = jnp.sum(jnp.where(taken, position[None, :] + 1, 0), axis=1).reshape(n_owners, capacity)
    axes = ("cells", "mp")
    got_feat = lax.all_to_all(send_feat, axes, split_axis=0, concat_axis=0, tiled=True).reshape(-1, width)
    got_code = lax.all_to_all(send_code, axes, split_axis=0, concat_axis=0, tiled=True).reshape(-1) - 1
    hot = (jnp.arange(CB * slot_dev, dtype=jnp.int32)[:, None] == got_code[None, :]).astype(BF16)
    count = jnp.sum(hot.astype(F32), axis=1)
    pooled = dot(hot, got_feat) / jnp.maximum(count, 1.0)[:, None]
    embed = lax.dynamic_slice_in_dim(time_embed, my_slot * slot_dev, slot_dev, 0).astype(F32)
    tokens = (pooled.reshape(CB, slot_dev, width) + embed[None]).astype(BF16)
    grid = tokens.reshape(n_slots, CB // n_slots, slot_dev, width)
    grid = lax.all_to_all(grid, "slots", split_axis=0, concat_axis=2, tiled=True)
    return grid.reshape(-1, width)


def on_device(obs_feat, obs_cell, obs_slot, obs_count, time_embed, w_qkv, w_out, w_gate_up, w_down):
    n_cells = lax.axis_size("cells")
    n_slots = lax.axis_size("slots")
    n_groups = lax.axis_size("groups")
    n_mp = lax.axis_size("mp")
    n_owners = n_cells * n_mp
    rows, width = obs_feat.shape
    capacity = 3 * rows // n_owners
    quarter = CB // n_slots
    slot_dev = TSTEPS // n_slots
    my_slot = lax.axis_index("slots")
    n_share = n_groups * n_slots
    share = w_qkv.shape[0] // n_share
    unit = w_qkv.shape[2]
    n_units = w_gate_up.shape[2] // unit

    valid = jnp.arange(rows, dtype=jnp.int32) < obs_count[0]
    owner = obs_cell // (quarter * n_mp * n_slots) * n_mp + obs_cell // quarter % n_mp
    owner = jnp.where(valid, owner, n_owners)
    local = obs_cell // (quarter * n_mp) % n_slots * quarter + obs_cell % quarter
    position = local * slot_dev + obs_slot

    local_weights = (w_qkv, w_out.T, w_gate_up, w_down.T)
    which = lax.axis_index("groups") * n_slots + my_slot
    share_weights = [lax.dynamic_slice_in_dim(w, which * share, share, 0) for w in local_weights]
    chunks = [[-1, 0], list(range(1, n_units - 1)), [n_units - 1]]
    if n_slots == 2 and n_groups == 2 and share % 16 == 0 and capacity % 16 == 0:
        order = arrival_order(width, n_cells, n_share)
        gathered = [
            chunk_pieces(chunk_columns(*local_weights, units), chunk_columns(*share_weights, units))
            for units in chunks
        ]
        tokens = tokens_by_blocks(owner, position, obs_feat, time_embed, my_slot, capacity, slot_dev, order)
    else:
        order = jnp.arange(width, dtype=jnp.int32)
        axes = ("cells", "groups", "slots")
        gathered = [
            [(lax.all_gather(chunk_columns(*share_weights, units), axes, axis=0, tiled=True), 0, 0)]
            for units in chunks
        ]
        tokens = tokens_by_exchanges(owner, position, obs_feat, time_embed, my_slot, capacity, slot_dev)

    swap = [(0, 1), (1, 0)]
    partner = lax.ppermute(tokens, "mp", swap)
    normed, sums = layer_chunk([partner, tokens], [], gathered[0], unit, True, F32)
    for pieces in gathered[1:-1]:
        _, sums = layer_chunk(normed, sums, pieces, unit, False, F32)
    _, (for_partner,) = layer_chunk(normed[:1], sums[:1], gathered[-1], unit, False, BF16)
    from_partner = lax.ppermute(for_partner, "mp", swap)
    _, (own,) = layer_chunk(normed[1:], sums[1:], gathered[-1], unit, False, F32)
    return finish(tokens, own, from_partner, order).reshape(quarter, TSTEPS, width)


def solution(mesh):
    placed = (
        P(("groups", "cells", "slots", "mp"), None),
        P(("groups", "cells", "slots", "mp")),
        P(("groups", "cells", "slots", "mp")),
        P(("groups", "cells", "slots", "mp")),
        P(),
        P("cells", None, "mp"),
        P("mp", "cells"),
        P("cells", None, "mp"),
        P("mp", "cells"),
    )
    return jax.shard_map(
        on_device,
        mesh=mesh,
        in_specs=placed,
        out_specs=P(("groups", "cells", "slots", "mp"), None, None),
        check_vma=False,
    )
```

```python
import functools

import jax
import jax.numpy as jnp
from jax import lax
from jax.experimental import pallas as pl
from jax.experimental.pallas import tpu as pltpu
from jax.sharding import PartitionSpec as P

HD = 64
TSTEPS = 8
CB = 128
EPS = 1e-06

META_ROWS = 16
CODE = 32
LANES = 128
VMEM_LIMIT = 48 * 1024 * 1024
F32 = jnp.float32
BF16 = jnp.bfloat16
WHOLE = pl.BlockSpec(memory_space=pltpu.VMEM)
SCALARS = pl.BlockSpec(memory_space=pltpu.SMEM)


def iota(shape, axis):
    return lax.broadcasted_iota(jnp.int32, shape, axis)


def dot(left, right):
    return jnp.dot(left, right, preferred_element_type=F32)


def dot_t(left, right):
    return lax.dot_general(left, right, (((1,), (1,)), ((), ())), preferred_element_type=F32)


def params():
    return pltpu.CompilerParams(vmem_limit_bytes=VMEM_LIMIT)


def place_kernel(capacity, owner_ref, position_ref, feat_ref, out_ref):
    n_owners, rows = out_ref.shape[0], feat_ref.shape[0]
    owner = owner_ref[...]
    owner_hot = (iota((n_owners, rows), 0) == owner).astype(F32)
    upper = (iota((rows, rows), 0) <= iota((rows, rows), 1)).astype(BF16)
    running = dot(owner_hot.astype(BF16), upper)
    rank = jnp.sum(running * owner_hot, axis=0, keepdims=True).astype(jnp.int32) - 1
    code = position_ref[...] + 1
    line = iota((META_ROWS, rows), 0)
    meta = jnp.where(line == 0, code // CODE, jnp.where(line == 1, code % CODE, 0))
    meta = meta.astype(F32).astype(BF16)
    feat = feat_ref[...]
    for block in range(n_owners):
        place = jnp.where(owner == block, rank, -1)
        taken = (iota((capacity, rows), 0) == place).astype(F32).astype(BF16)
        out_ref[block, :capacity, :] = dot(taken, feat).astype(BF16)
        out_ref[block, capacity:, :] = jnp.zeros((META_ROWS, feat.shape[1]), BF16)
        out_ref[block, capacity:, :capacity] = dot_t(meta, taken).astype(BF16)


def place_rows(owner, position, obs_feat, n_owners, capacity):
    rows, width = obs_feat.shape
    return pl.pallas_call(
        functools.partial(place_kernel, capacity),
        out_shape=jax.ShapeDtypeStruct((n_owners, capacity + META_ROWS, width), BF16),
        in_specs=[WHOLE] * 3,
        out_specs=WHOLE,
        compiler_params=params(),
        cost_estimate=pl.CostEstimate(
            flops=2 * rows * width * n_owners * capacity,
            bytes_accessed=2 * width * (rows + n_owners * capacity),
            transcendentals=0,
        ),
        name="place_rows",
    )(owner.reshape(1, rows), position.reshape(1, rows), obs_feat)


def pool_kernel(capacity, slot_dev, slot_ref, embed_ref, got_ref, keep_ref, send_ref):
    half = keep_ref.shape[0]
    places = 2 * half
    mine = slot_ref[0]
    total = jnp.zeros((places, keep_ref.shape[1]), F32)
    seen = jnp.zeros((places, capacity), F32)
    for block in range(got_ref.shape[0]):
        meta = got_ref[block, capacity:, :capacity].astype(F32)
        code = (meta[0:1] * CODE + meta[1:2]).astype(jnp.int32) - 1
        turned = jnp.where(code >= half, code - half, code + half)
        code = jnp.where((code >= 0) & (mine == 1), turned, code)
        hot = (iota((places, capacity), 0) == code).astype(F32)
        seen += hot
        total += dot(hot.astype(BF16), got_ref[block, :capacity, :])
    count = jnp.sum(seen, axis=1, keepdims=True)
    steps = embed_ref.shape[0]
    step_hot = iota((places, steps), 1) == iota((places, steps), 0) % slot_dev + mine * slot_dev
    embed = dot(step_hot.astype(F32).astype(BF16), embed_ref[...])
    tokens = (total / jnp.maximum(count, 1.0) + embed).astype(BF16)
    keep_ref[...] = tokens[:half]
    send_ref[...] = tokens[half:]


def pool_rows(my_slot, time_embed, got, capacity, slot_dev):
    width = time_embed.shape[1]
    half = jax.ShapeDtypeStruct((CB * slot_dev // 2, width), BF16)
    return pl.pallas_call(
        functools.partial(pool_kernel, capacity, slot_dev),
        out_shape=[half, half],
        in_specs=[SCALARS, WHOLE, WHOLE],
        out_specs=[WHOLE] * 2,
        compiler_params=params(),
        cost_estimate=pl.CostEstimate(
            flops=2 * CB * slot_dev * got.size, bytes_accessed=2 * got.size, transcendentals=0
        ),
        name="pool_rows",
    )(my_slot, time_embed, got)


def weave_kernel(slot_dev, slot_ref, order_ref, keep_ref, got_ref, out_ref):
    rows, width = out_ref.shape
    half = keep_ref.shape[0]
    mine = slot_ref[0]
    row, col = iota((rows, half), 0), iota((rows, half), 1)
    source = col == row // TSTEPS * slot_dev + row % slot_dev
    own = row % TSTEPS // slot_dev == mine
    from_keep = (source & own).astype(F32).astype(BF16)
    from_got = (source & jnp.logical_not(own)).astype(F32).astype(BF16)
    tokens = (dot(from_keep, keep_ref[...]) + dot(from_got, got_ref[...])).astype(BF16)
    move = (iota((width, width), 0) == order_ref[...]).astype(F32).astype(BF16)
    out_ref[...] = dot(tokens, move).astype(BF16)


def weave_steps(my_slot, order, keep, got, slot_dev):
    rows, width = 2 * keep.shape[0], keep.shape[1]
    return pl.pallas_call(
        functools.partial(weave_kernel, slot_dev),
        out_shape=jax.ShapeDtypeStruct((rows, width), BF16),
        in_specs=[SCALARS] + [WHOLE] * 3,
        out_specs=WHOLE,
        compiler_params=params(),
        cost_estimate=pl.CostEstimate(
            flops=2 * rows * width * (rows + width), bytes_accessed=4 * rows * width, transcendentals=0
        ),
        name="weave_steps",
    )(my_slot, order.reshape(1, width), keep, got)


def head_scale(values, ones):
    square = values * values
    high = square.astype(BF16)
    low = (square - high.astype(F32)).astype(BF16)
    sums = dot(high, ones) + dot(low, ones)
    return (values * lax.rsqrt(sums * (1.0 / HD) + EPS)).astype(BF16)


def attention(normed, weight, heads_width, ctx_ref):
    rows = normed.shape[0]
    projected = dot(normed, weight)
    same_head = iota((LANES, LANES), 0) // HD == iota((LANES, LANES), 1) // HD
    ones = same_head.astype(F32).astype(BF16)
    group = LANES
    first = iota((group, LANES), 1) < HD
    row, col = iota((2 * group, group), 0), iota((2 * group, group), 1)
    same_cell = row % group // TSTEPS == col // TSTEPS
    for pair in range(heads_width // LANES):
        at = pair * LANES
        query = head_scale(projected[:, at : at + LANES], ones)
        key = head_scale(projected[:, heads_width + at : heads_width + at + LANES], ones)
        value = projected[:, 2 * heads_width + at : 2 * heads_width + at + LANES].astype(BF16)
        for begin in range(0, rows, group):
            q = query[begin : begin + group]
            k = key[begin : begin + group]
            v = value[begin : begin + group]
            none = jnp.zeros_like(q)
            both = jnp.concatenate([jnp.where(first, q, none), jnp.where(first, none, q)], axis=0)
            scores = dot_t(both, k) * HD ** (-0.5)
            expo = jnp.where(same_cell, jnp.exp(scores), 0.0)
            probs = (expo / jnp.sum(expo, axis=1, keepdims=True)).astype(BF16)
            mixed = dot(probs, v)
            ctx = jnp.where(first, mixed[:group], mixed[group:])
            ctx_ref[begin : begin + group, at : at + LANES] = ctx.astype(BF16)


def gated(normed, gate_w, up_w, down_w):
    gate = dot(normed, gate_w)
    up = dot(normed, up_w)
    hidden = (gate / (1.0 + jnp.exp(-gate)) * up).astype(BF16)
    return dot_t(hidden, down_w)


def chunk_kernel(plan, unit, n_units, with_heads, n_sets, n_pieces, *refs):
    refs = list(refs)
    take = lambda count: [refs.pop(0) for _ in range(count)]
    rows_in = take(n_sets)
    sums_in = [None] * n_sets if with_heads else take(n_sets)
    pieces = take(n_pieces)
    norm_out = take(n_sets) if with_heads else rows_in
    sums_out = take(n_sets)
    w_ref, ctx_ref, sems = take(3)
    width = w_ref.shape[0]
    copies = {}
    for number, (section, piece, source_col, row, col, size) in enumerate(plan):
        copy = pltpu.make_async_copy(
            pieces[piece].at[:, pl.ds(source_col, size)],
            w_ref.at[pl.ds(row, pieces[piece].shape[0]), pl.ds(col, size)],
            sems.at[number],
        )
        copy.start()
        copies.setdefault(section, []).append(copy)

    def ready(sections):
        for section in sections:
            for copy in copies.pop(section, []):
                copy.wait()

    def columns(first, count):
        return w_ref[:, first * unit : (first + count) * unit]

    begin = 0
    sums = sums_in
    if with_heads:
        for rows_ref, norm_ref in zip(rows_in, norm_out):
            tokens = rows_ref[...].astype(F32)
            scale = lax.rsqrt(jnp.mean(tokens * tokens, axis=1, keepdims=True) + EPS)
            norm_ref[...] = (tokens * scale).astype(BF16)
        ready(range(4))
        for norm_ref, sum_ref in zip(norm_out, sums_out):
            attention(norm_ref[...], columns(0, 3), unit, ctx_ref)
            sum_ref[...] = dot_t(ctx_ref[...], columns(3, 1))
        begin, sums = 4, sums_out
    for number in range(n_units):
        at = begin + 3 * number
        ready(range(at, at + 3))
        for norm_ref, sum_ref, out_ref in zip(norm_out, sums, sums_out):
            add = gated(norm_ref[...], columns(at, 1), columns(at + 1, 1), columns(at + 2, 1))
            out_ref[...] = (sum_ref[...] + add).astype(out_ref.dtype)
        sums = sums_out


def layer_chunk(rows_in, sums_in, pieces, unit, with_heads, out_type):
    n_sets = len(rows_in)
    rows, width = rows_in[0].shape
    columns = max(at + array.shape[1] for array, _, at in pieces)
    n_units = (columns // unit - 4 * with_heads) // 3
    plan = []
    for section in range(columns // unit):
        left, right = section * unit, (section + 1) * unit
        for number, (array, row, at) in enumerate(pieces):
            low, high = max(left, at), min(right, at + array.shape[1])
            if low < high:
                plan.append((section, number, low - at, row, low, high - low))
    like = lambda kind: jax.ShapeDtypeStruct((rows, width), kind)
    outs = [like(BF16)] * (n_sets * with_heads) + [like(out_type)] * n_sets
    results = pl.pallas_call(
        functools.partial(chunk_kernel, plan, unit, n_units, with_heads, n_sets, len(pieces)),
        out_shape=outs,
        in_specs=[WHOLE] * (len(rows_in) + len(sums_in)) + [pl.BlockSpec(memory_space=pl.ANY)] * len(pieces),
        out_specs=[WHOLE] * len(outs),
        scratch_shapes=[
            pltpu.VMEM((width, columns), BF16),
            pltpu.VMEM((rows, unit), BF16),
            pltpu.SemaphoreType.DMA((len(plan),)),
        ],
        compiler_params=params(),
        cost_estimate=pl.CostEstimate(
            flops=2 * n_sets * rows * width * columns,
            bytes_accessed=2 * width * columns + 8 * n_sets * rows * width,
            transcendentals=n_sets * n_units * rows * unit,
        ),
        name="layer_heads" if with_heads else "layer_gated",
    )(*rows_in, *sums_in, *[array for array, _, _ in pieces])
    return results[: -n_sets] if with_heads else rows_in, results[-n_sets:]


def finish_kernel(tok_ref, sum_ref, got_ref, order_ref, out_ref):
    width = out_ref.shape[1]
    mixed = (tok_ref[...].astype(F32) + sum_ref[...] + got_ref[...].astype(F32)).astype(BF16)
    move = (iota((width, width), 0) == order_ref[...]).astype(F32).astype(BF16)
    out_ref[...] = dot_t(mixed, move).astype(BF16)


def finish(tokens, sums, got, order):
    rows, width = tokens.shape
    return pl.pallas_call(
        finish_kernel,
        out_shape=jax.ShapeDtypeStruct((rows, width), BF16),
        in_specs=[WHOLE] * 4,
        out_specs=WHOLE,
        compiler_params=params(),
        cost_estimate=pl.CostEstimate(
            flops=2 * rows * width * width, bytes_accessed=10 * rows * width, transcendentals=0
        ),
        name="finish",
    )(tokens, sums, got, order.reshape(1, width))


def chunk_columns(w_qkv, w_out, w_gate_up, w_down, units):
    unit = w_qkv.shape[2]
    parts = []
    for number in units:
        if number < 0:
            parts += [w_qkv[:, 0], w_qkv[:, 1], w_qkv[:, 2], w_out]
        else:
            cols = slice(number * unit, (number + 1) * unit)
            parts += [w_gate_up[:, 0, cols], w_gate_up[:, 1, cols], w_down[:, cols]]
    return jnp.concatenate(parts, axis=1)


def chunk_pieces(shard, share_rows):
    n_cells = lax.axis_size("cells")
    rows = shard.shape[0]
    up = [(j, (j + 1) % n_cells) for j in range(n_cells)]
    down = [(j, (j - 1) % n_cells) for j in range(n_cells)]
    below = [lax.ppermute(share_rows, "cells", up)]
    above = [lax.ppermute(share_rows, "cells", down)]
    while len(below) + len(above) < n_cells - 1:
        line, way = (below, up) if len(below) <= len(above) else (above, down)
        line.append(lax.ppermute(line[-1], "cells", way))
    others = jnp.concatenate(above + below[::-1], axis=0)
    swap = [(0, 1), (1, 0)]
    by_slot = lax.ppermute(others, "slots", swap)
    by_group = lax.ppermute(others, "groups", swap)
    cut = shard.shape[1] // (2 * LANES) * LANES
    far_a = lax.ppermute(by_slot[:, :cut], "groups", swap)
    far_b = lax.ppermute(by_group[:, cut:], "slots", swap)
    step = others.shape[0]
    return [
        (shard, 0, 0),
        (others, rows, 0),
        (by_slot, rows + step, 0),
        (by_group, rows + 2 * step, 0),
        (far_a, rows + 3 * step, 0),
        (far_b, rows + 3 * step, cut),
    ]


def arrival_order(width, n_cells, n_share):
    mine = lax.axis_index("cells")
    share_id = lax.axis_index("groups") * lax.axis_size("slots") + lax.axis_index("slots")
    rows = width // n_cells
    share = rows // n_share
    step = (n_cells - 1) * share
    place = jnp.arange(width, dtype=jnp.int32)
    past = jnp.maximum(place - rows, 0)
    which = past // step
    cell = (mine + 1 + past % step // share) % n_cells
    far = cell * rows + (which ^ share_id) * share + past % share
    return jnp.where(place < rows, mine * rows + place, far)


def tokens_by_blocks(owner, position, obs_feat, time_embed, my_slot, capacity, slot_dev, order):
    n_owners = lax.axis_size("cells") * lax.axis_size("mp")
    blocks = place_rows(owner, position, obs_feat, n_owners, capacity)
    got = lax.all_to_all(blocks, ("cells", "mp"), split_axis=0, concat_axis=0, tiled=True)
    keep, send = pool_rows(my_slot.reshape(1), time_embed, got, capacity, slot_dev)
    other = lax.ppermute(send, "slots", [(0, 1), (1, 0)])
    return weave_steps(my_slot.reshape(1), order, keep, other, slot_dev)


def tokens_by_exchanges(owner, position, obs_feat, time_embed, my_slot, capacity, slot_dev):
    n_slots = lax.axis_size("slots")
    n_owners = lax.axis_size("cells") * lax.axis_size("mp")
    rows, width = obs_feat.shape
    owners = jnp.arange(n_owners, dtype=jnp.int32)
    owner_hot = (owner[:, None] == owners[None, :]).astype(F32)
    row_ids = jnp.arange(rows, dtype=jnp.int32)
    lower = (row_ids[None, :] <= row_ids[:, None]).astype(BF16)
    running = dot(lower, owner_hot.astype(BF16))
    rank = jnp.sum(running * owner_hot, axis=1).astype(jnp.int32) - 1
    place = jnp.where(owner < n_owners, owner * capacity + rank, n_owners * capacity)
    place_ids = jnp.arange(n_owners * capacity, dtype=jnp.int32)
    taken = place_ids[:, None] == place[None, :]
    send_feat = dot(taken.astype(BF16), obs_feat).astype(BF16).reshape(n_owners, capacity, width)
    send_code = jnp.sum(jnp.where(taken, position[None, :] + 1, 0), axis=1).reshape(n_owners, capacity)
    axes = ("cells", "mp")
    got_feat = lax.all_to_all(send_feat, axes, split_axis=0, concat_axis=0, tiled=True).reshape(-1, width)
    got_code = lax.all_to_all(send_code, axes, split_axis=0, concat_axis=0, tiled=True).reshape(-1) - 1
    hot = (jnp.arange(CB * slot_dev, dtype=jnp.int32)[:, None] == got_code[None, :]).astype(BF16)
    count = jnp.sum(hot.astype(F32), axis=1)
    pooled = dot(hot, got_feat) / jnp.maximum(count, 1.0)[:, None]
    embed = lax.dynamic_slice_in_dim(time_embed, my_slot * slot_dev, slot_dev, 0).astype(F32)
    tokens = (pooled.reshape(CB, slot_dev, width) + embed[None]).astype(BF16)
    grid = tokens.reshape(n_slots, CB // n_slots, slot_dev, width)
    grid = lax.all_to_all(grid, "slots", split_axis=0, concat_axis=2, tiled=True)
    return grid.reshape(-1, width)


def on_device(obs_feat, obs_cell, obs_slot, obs_count, time_embed, w_qkv, w_out, w_gate_up, w_down):
    n_cells = lax.axis_size("cells")
    n_slots = lax.axis_size("slots")
    n_groups = lax.axis_size("groups")
    n_mp = lax.axis_size("mp")
    n_owners = n_cells * n_mp
    rows, width = obs_feat.shape
    capacity = 3 * rows // n_owners
    quarter = CB // n_slots
    slot_dev = TSTEPS // n_slots
    my_slot = lax.axis_index("slots")
    n_share = n_groups * n_slots
    share = w_qkv.shape[0] // n_share
    unit = w_qkv.shape[2]
    n_units = w_gate_up.shape[2] // unit

    valid = jnp.arange(rows, dtype=jnp.int32) < obs_count[0]
    owner = obs_cell // (quarter * n_mp * n_slots) * n_mp + obs_cell // quarter % n_mp
    owner = jnp.where(valid, owner, n_owners)
    local = obs_cell // (quarter * n_mp) % n_slots * quarter + obs_cell % quarter
    position = local * slot_dev + obs_slot

    local_weights = (w_qkv, w_out.T, w_gate_up, w_down.T)
    which = lax.axis_index("groups") * n_slots + my_slot
    share_weights = [lax.dynamic_slice_in_dim(w, which * share, share, 0) for w in local_weights]
    chunks = [[-1, 0], list(range(1, n_units - 1)), [n_units - 1]]
    if n_slots == 2 and n_groups == 2 and share % 16 == 0 and capacity % 16 == 0:
        order = arrival_order(width, n_cells, n_share)
        gathered = [
            chunk_pieces(chunk_columns(*local_weights, units), chunk_columns(*share_weights, units))
            for units in chunks
        ]
        tokens = tokens_by_blocks(owner, position, obs_feat, time_embed, my_slot, capacity, slot_dev, order)
    else:
        order = jnp.arange(width, dtype=jnp.int32)
        axes = ("cells", "groups", "slots")
        gathered = [
            [(lax.all_gather(chunk_columns(*share_weights, units), axes, axis=0, tiled=True), 0, 0)]
            for units in chunks
        ]
        tokens = tokens_by_exchanges(owner, position, obs_feat, time_embed, my_slot, capacity, slot_dev)

    swap = [(0, 1), (1, 0)]
    partner = lax.ppermute(tokens, "mp", swap)
    normed, sums = layer_chunk([partner, tokens], [], gathered[0], unit, True, F32)
    for pieces in gathered[1:-1]:
        _, sums = layer_chunk(normed, sums, pieces, unit, False, F32)
    _, (for_partner,) = layer_chunk(normed[:1], sums[:1], gathered[-1], unit, False, BF16)
    from_partner = lax.ppermute(for_partner, "mp", swap)
    _, (own,) = layer_chunk(normed[1:], sums[1:], gathered[-1], unit, False, F32)
    return finish(tokens, own, from_partner, order).reshape(quarter, TSTEPS, width)


def solution(mesh):
    placed = (
        P(("groups", "cells", "slots", "mp"), None),
        P(("groups", "cells", "slots", "mp")),
        P(("groups", "cells", "slots", "mp")),
        P(("groups", "cells", "slots", "mp")),
        P(),
        P("cells", None, "mp"),
        P("mp", "cells"),
        P("cells", None, "mp"),
        P("mp", "cells"),
    )
    return jax.shard_map(
        on_device,
        mesh=mesh,
        in_specs=placed,
        out_specs=P(("groups", "cells", "slots", "mp"), None, None),
        check_vma=False,
    )
```

```python
import functools

import jax
import jax.numpy as jnp
from jax import lax
from jax.experimental import pallas as pl
from jax.experimental.pallas import tpu as pltpu
from jax.sharding import PartitionSpec as P

HD = 64
TSTEPS = 8
CB = 128
EPS = 1e-06

CODE = 32
UNIT = 512
LANES = 128
VMEM_LIMIT = 48 * 1024 * 1024
F32 = jnp.float32
BF16 = jnp.bfloat16
WHOLE = pl.BlockSpec(memory_space=pltpu.VMEM)
SCALARS = pl.BlockSpec(memory_space=pltpu.SMEM)


def iota(shape, axis):
    return lax.broadcasted_iota(jnp.int32, shape, axis)


def dot(left, right):
    return jnp.dot(left, right, preferred_element_type=F32)


def dot_t(left, right):
    return lax.dot_general(left, right, (((1,), (1,)), ((), ())), preferred_element_type=F32)


def params():
    return pltpu.CompilerParams(vmem_limit_bytes=VMEM_LIMIT)


def place_kernel(capacity, owner_ref, position_ref, feat_ref, out_ref, code_ref):
    n_owners, rows = out_ref.shape[0], feat_ref.shape[0]
    owner = owner_ref[...]
    owner_hot = (iota((n_owners, rows), 0) == owner).astype(F32)
    upper = (iota((rows, rows), 0) <= iota((rows, rows), 1)).astype(BF16)
    running = dot(owner_hot.astype(BF16), upper)
    rank = jnp.sum(running * owner_hot, axis=0, keepdims=True).astype(jnp.int32) - 1
    code = position_ref[...] + 1
    line = iota((8, rows), 0)
    digits = jnp.where(line == 0, code // CODE, jnp.where(line == 1, code % CODE, 0))
    digits = digits.astype(F32).astype(BF16)
    feat = feat_ref[...]
    for block in range(n_owners):
        place = jnp.where(owner == block, rank, -1)
        taken = (iota((capacity, rows), 0) == place).astype(F32).astype(BF16)
        out_ref[block] = dot(taken, feat).astype(BF16)
        sent = dot_t(digits, taken)
        code_ref[block] = (sent[0:1] * CODE + sent[1:2]).astype(jnp.int32) - 1


def place_rows(owner, position, obs_feat, n_owners, capacity):
    rows, width = obs_feat.shape
    return pl.pallas_call(
        functools.partial(place_kernel, capacity),
        out_shape=[
            jax.ShapeDtypeStruct((n_owners, capacity, width), BF16),
            jax.ShapeDtypeStruct((n_owners, 1, capacity), jnp.int32),
        ],
        in_specs=[WHOLE] * 3,
        out_specs=[WHOLE] * 2,
        compiler_params=params(),
        cost_estimate=pl.CostEstimate(
            flops=2 * rows * width * n_owners * capacity,
            bytes_accessed=2 * width * (rows + n_owners * capacity),
            transcendentals=0,
        ),
        name="place_rows",
    )(owner.reshape(1, rows), position.reshape(1, rows), obs_feat)


def pool_kernel(capacity, slot_dev, slot_ref, embed_ref, code_ref, got_ref, keep_ref, send_ref):
    half = keep_ref.shape[0]
    places = 2 * half
    mine = slot_ref[0]
    total = jnp.zeros((places, keep_ref.shape[1]), F32)
    seen = jnp.zeros((places, capacity), F32)
    for block in range(got_ref.shape[0]):
        code = code_ref[block]
        turned = jnp.where(code >= half, code - half, code + half)
        code = jnp.where((code >= 0) & (mine == 1), turned, code)
        hot = (iota((places, capacity), 0) == code).astype(F32)
        seen += hot
        total += dot(hot.astype(BF16), got_ref[block])
    count = jnp.sum(seen, axis=1, keepdims=True)
    steps = embed_ref.shape[0]
    step_hot = iota((places, steps), 1) == iota((places, steps), 0) % slot_dev + mine * slot_dev
    embed = dot(step_hot.astype(F32).astype(BF16), embed_ref[...])
    tokens = (total / jnp.maximum(count, 1.0) + embed).astype(BF16)
    keep_ref[...] = tokens[:half]
    send_ref[...] = tokens[half:]


def pool_rows(my_slot, time_embed, codes, got, capacity, slot_dev):
    width = time_embed.shape[1]
    half = jax.ShapeDtypeStruct((CB * slot_dev // 2, width), BF16)
    return pl.pallas_call(
        functools.partial(pool_kernel, capacity, slot_dev),
        out_shape=[half, half],
        in_specs=[SCALARS] + [WHOLE] * 3,
        out_specs=[WHOLE] * 2,
        compiler_params=params(),
        cost_estimate=pl.CostEstimate(
            flops=2 * CB * slot_dev * got.size, bytes_accessed=2 * got.size, transcendentals=0
        ),
        name="pool_rows",
    )(my_slot, time_embed, codes, got)


def weave_kernel(slot_dev, slot_ref, order_ref, keep_ref, got_ref, out_ref):
    rows, width = out_ref.shape
    half = keep_ref.shape[0]
    mine = slot_ref[0]
    row, col = iota((rows, half), 0), iota((rows, half), 1)
    source = col == row // TSTEPS * slot_dev + row % slot_dev
    own = row % TSTEPS // slot_dev == mine
    from_keep = (source & own).astype(F32).astype(BF16)
    from_got = (source & jnp.logical_not(own)).astype(F32).astype(BF16)
    tokens = (dot(from_keep, keep_ref[...]) + dot(from_got, got_ref[...])).astype(BF16)
    move = (iota((width, width), 0) == order_ref[...]).astype(F32).astype(BF16)
    out_ref[...] = dot(tokens, move).astype(BF16)


def weave_steps(my_slot, order, keep, got, slot_dev):
    rows, width = 2 * keep.shape[0], keep.shape[1]
    return pl.pallas_call(
        functools.partial(weave_kernel, slot_dev),
        out_shape=jax.ShapeDtypeStruct((rows, width), BF16),
        in_specs=[SCALARS] + [WHOLE] * 3,
        out_specs=WHOLE,
        compiler_params=params(),
        cost_estimate=pl.CostEstimate(
            flops=2 * rows * width * (rows + width), bytes_accessed=4 * rows * width, transcendentals=0
        ),
        name="weave_steps",
    )(my_slot, order.reshape(1, width), keep, got)


def head_scale(values, ones):
    sums = dot((values * values).astype(BF16), ones)
    return values * lax.rsqrt(sums * (1.0 / HD) + EPS)


def attention(normed, weight, heads_width, ctx_ref):
    rows = normed.shape[0]
    projected = dot(normed, weight)
    same_head = iota((LANES, LANES), 0) // HD == iota((LANES, LANES), 1) // HD
    ones = same_head.astype(F32).astype(BF16)
    group = LANES
    first = iota((group, LANES), 1) < HD
    row, col = iota((2 * group, group), 0), iota((2 * group, group), 1)
    same_cell = row % group // TSTEPS == col // TSTEPS
    count = jnp.ones((group, LANES), BF16)
    for pair in range(heads_width // LANES):
        at = pair * LANES
        query = (head_scale(projected[:, at : at + LANES], ones) * HD ** (-0.5)).astype(BF16)
        key = head_scale(projected[:, heads_width + at : heads_width + at + LANES], ones).astype(BF16)
        value = projected[:, 2 * heads_width + at : 2 * heads_width + at + LANES].astype(BF16)
        for begin in range(0, rows, group):
            q = query[begin : begin + group]
            k = key[begin : begin + group]
            v = value[begin : begin + group]
            none = jnp.zeros_like(q)
            both = jnp.concatenate([jnp.where(first, q, none), jnp.where(first, none, q)], axis=0)
            expo = jnp.where(same_cell, jnp.exp(dot_t(both, k)), 0.0).astype(BF16)
            mixed = dot(expo, jnp.concatenate([v, count], axis=1))
            top, low = mixed[:group], mixed[group:]
            over = jnp.where(first, top[:, :LANES], low[:, :LANES])
            under = jnp.where(first, top[:, LANES:], low[:, LANES:])
            ctx_ref[begin : begin + group, at : at + LANES] = (over / under).astype(BF16)


def gated(normed, gate_w, up_w, down_w):
    gate = dot(normed, gate_w)
    up = dot(normed, up_w)
    hidden = (gate * (0.5 * jnp.tanh(0.5 * gate) + 0.5) * up).astype(BF16)
    return dot_t(hidden, down_w)


def layer_kernel(plan, sections, tok_ref, *refs):
    pieces, (out_ref, w_ref, norm_ref, ctx_ref, acc_ref, sems) = refs[:-6], refs[-6:]
    copies = {}
    for number, (section, piece, source_col, row, col, size) in enumerate(plan):
        copy = pltpu.make_async_copy(
            pieces[piece].at[:, pl.ds(source_col, size)],
            w_ref.at[pl.ds(row, pieces[piece].shape[0]), pl.ds(col, size)],
            sems.at[number],
        )
        copy.start()
        copies.setdefault(section, []).append(copy)

    def columns(section):
        for copy in copies[section]:
            copy.wait()
        begin, end = sections[section]
        return w_ref[:, begin:end]

    tokens = tok_ref[...].astype(F32)
    scale = lax.rsqrt(jnp.mean(tokens * tokens, axis=1, keepdims=True) + EPS)
    norm_ref[...] = (tokens * scale).astype(BF16)
    attention(norm_ref[...], columns(0), ctx_ref.shape[1], ctx_ref)
    acc_ref[...] = dot_t(ctx_ref[...], columns(1))
    for at in range(2, len(sections), 3):
        add = gated(norm_ref[...], columns(at), columns(at + 1), columns(at + 2))
        if at + 3 < len(sections):
            acc_ref[...] += add
        else:
            out_ref[...] = (acc_ref[...] + add).astype(out_ref.dtype)


def layer(tokens, pieces, heads_width, hidden_width, out_type):
    rows, width = tokens.shape
    gate_at = 3 * heads_width
    up_at = gate_at + hidden_width
    out_at = up_at + hidden_width
    down_at = out_at + heads_width
    columns = down_at + hidden_width
    unit = min(UNIT, hidden_width)
    sections = [(0, gate_at), (out_at, down_at)]
    for begin in range(0, hidden_width, unit):
        sections += [(at + begin, at + begin + unit) for at in (gate_at, up_at, down_at)]
    plan = []
    for section, (left, right) in enumerate(sections):
        for number, (array, row, at) in enumerate(pieces):
            low, high = max(left, at), min(right, at + array.shape[1])
            if low < high:
                plan.append((section, number, low - at, row, low, high - low))
    return pl.pallas_call(
        functools.partial(layer_kernel, plan, sections),
        out_shape=jax.ShapeDtypeStruct((rows, width), out_type),
        in_specs=[WHOLE] + [pl.BlockSpec(memory_space=pl.ANY)] * len(pieces),
        out_specs=WHOLE,
        scratch_shapes=[
            pltpu.VMEM((width, columns), BF16),
            pltpu.VMEM((rows, width), BF16),
            pltpu.VMEM((rows, heads_width), BF16),
            pltpu.VMEM((rows, width), F32),
            pltpu.SemaphoreType.DMA((len(plan),)),
        ],
        compiler_params=params(),
        cost_estimate=pl.CostEstimate(
            flops=2 * rows * width * columns,
            bytes_accessed=2 * width * columns + 6 * rows * width,
            transcendentals=rows * hidden_width,
        ),
        name="layer",
    )(tokens, *[array for array, _, _ in pieces])


def finish_kernel(tok_ref, sum_ref, got_ref, order_ref, out_ref):
    width = out_ref.shape[1]
    mixed = (tok_ref[...].astype(F32) + sum_ref[...] + got_ref[...].astype(F32)).astype(BF16)
    move = (iota((width, width), 0) == order_ref[...]).astype(F32).astype(BF16)
    out_ref[...] = dot_t(mixed, move).astype(BF16)


def finish(tokens, sums, got, order):
    rows, width = tokens.shape
    return pl.pallas_call(
        finish_kernel,
        out_shape=jax.ShapeDtypeStruct((rows, width), BF16),
        in_specs=[WHOLE] * 4,
        out_specs=WHOLE,
        compiler_params=params(),
        cost_estimate=pl.CostEstimate(
            flops=2 * rows * width * width, bytes_accessed=10 * rows * width, transcendentals=0
        ),
        name="finish",
    )(tokens, sums, got, order.reshape(1, width))


def side_by_side(w_qkv, w_out, w_gate_up, w_down):
    rows = w_qkv.shape[0]
    return jnp.concatenate([w_qkv.reshape(rows, -1), w_gate_up.reshape(rows, -1), w_out, w_down], axis=1)


def shares_along_cells(share_rows):
    n_cells = lax.axis_size("cells")
    up = [(j, (j + 1) % n_cells) for j in range(n_cells)]
    down = [(j, (j - 1) % n_cells) for j in range(n_cells)]
    below = [lax.ppermute(share_rows, "cells", up)]
    above = [lax.ppermute(share_rows, "cells", down)]
    while len(below) + len(above) < n_cells - 1:
        line, way = (below, up) if len(below) <= len(above) else (above, down)
        line.append(lax.ppermute(line[-1], "cells", way))
    return above + below[::-1]


def pieces_of_all(shard, shares):
    rows = shard.shape[0]
    others = jnp.concatenate(shares, axis=0)
    swap = [(0, 1), (1, 0)]
    by_slot = lax.ppermute(others, "slots", swap)
    by_group = lax.ppermute(others, "groups", swap)
    cut = shard.shape[1] // (2 * LANES) * LANES
    far_a = lax.ppermute(by_slot[:, :cut], "groups", swap)
    far_b = lax.ppermute(by_group[:, cut:], "slots", swap)
    step = others.shape[0]
    return [
        (shard, 0, 0),
        (others, rows, 0),
        (by_slot, rows + step, 0),
        (by_group, rows + 2 * step, 0),
        (far_a, rows + 3 * step, 0),
        (far_b, rows + 3 * step, cut),
    ]


def arrival_order(width, n_cells, n_share):
    mine = lax.axis_index("cells")
    share_id = lax.axis_index("groups") * lax.axis_size("slots") + lax.axis_index("slots")
    rows = width // n_cells
    share = rows // n_share
    step = (n_cells - 1) * share
    place = jnp.arange(width, dtype=jnp.int32)
    past = jnp.maximum(place - rows, 0)
    which = past // step
    cell = (mine + 1 + past % step // share) % n_cells
    far = cell * rows + (which ^ share_id) * share + past % share
    return jnp.where(place < rows, mine * rows + place, far)


def tokens_by_blocks(owner, position, obs_feat, time_embed, my_slot, capacity, slot_dev, order, shares):
    n_owners = lax.axis_size("cells") * lax.axis_size("mp")
    blocks, codes = place_rows(owner, position, obs_feat, n_owners, capacity)
    codes = lax.all_to_all(codes, ("cells", "mp"), split_axis=0, concat_axis=0, tiled=True)
    blocks, *shares = lax.optimization_barrier((blocks, *shares))
    got = lax.all_to_all(blocks, ("cells", "mp"), split_axis=0, concat_axis=0, tiled=True)
    keep, send = pool_rows(my_slot.reshape(1), time_embed, codes, got, capacity, slot_dev)
    other = lax.ppermute(send, "slots", [(0, 1), (1, 0)])
    return weave_steps(my_slot.reshape(1), order, keep, other, slot_dev), shares


def tokens_by_exchanges(owner, position, obs_feat, time_embed, my_slot, capacity, slot_dev):
    n_slots = lax.axis_size("slots")
    n_owners = lax.axis_size("cells") * lax.axis_size("mp")
    rows, width = obs_feat.shape
    owners = jnp.arange(n_owners, dtype=jnp.int32)
    owner_hot = (owner[:, None] == owners[None, :]).astype(F32)
    row_ids = jnp.arange(rows, dtype=jnp.int32)
    lower = (row_ids[None, :] <= row_ids[:, None]).astype(BF16)
    running = dot(lower, owner_hot.astype(BF16))
    rank = jnp.sum(running * owner_hot, axis=1).astype(jnp.int32) - 1
    place = jnp.where(owner < n_owners, owner * capacity + rank, n_owners * capacity)
    place_ids = jnp.arange(n_owners * capacity, dtype=jnp.int32)
    taken = place_ids[:, None] == place[None, :]
    send_feat = dot(taken.astype(BF16), obs_feat).astype(BF16).reshape(n_owners, capacity, width)
    send_code = jnp.sum(jnp.where(taken, position[None, :] + 1, 0), axis=1).reshape(n_owners, capacity)
    axes = ("cells", "mp")
    got_feat = lax.all_to_all(send_feat, axes, split_axis=0, concat_axis=0, tiled=True).reshape(-1, width)
    got_code = lax.all_to_all(send_code, axes, split_axis=0, concat_axis=0, tiled=True).reshape(-1) - 1
    hot = (jnp.arange(CB * slot_dev, dtype=jnp.int32)[:, None] == got_code[None, :]).astype(BF16)
    count = jnp.sum(hot.astype(F32), axis=1)
    pooled = dot(hot, got_feat) / jnp.maximum(count, 1.0)[:, None]
    embed = lax.dynamic_slice_in_dim(time_embed, my_slot * slot_dev, slot_dev, 0).astype(F32)
    tokens = (pooled.reshape(CB, slot_dev, width) + embed[None]).astype(BF16)
    grid = tokens.reshape(n_slots, CB // n_slots, slot_dev, width)
    grid = lax.all_to_all(grid, "slots", split_axis=0, concat_axis=2, tiled=True)
    return grid.reshape(-1, width)


def on_device(obs_feat, obs_cell, obs_slot, obs_count, time_embed, w_qkv, w_out, w_gate_up, w_down):
    n_cells = lax.axis_size("cells")
    n_slots = lax.axis_size("slots")
    n_groups = lax.axis_size("groups")
    n_mp = lax.axis_size("mp")
    n_owners = n_cells * n_mp
    rows, width = obs_feat.shape
    capacity = 3 * rows // n_owners
    quarter = CB // n_slots
    slot_dev = TSTEPS // n_slots
    my_slot = lax.axis_index("slots")
    n_share = n_groups * n_slots
    share = w_qkv.shape[0] // n_share
    valid = jnp.arange(rows, dtype=jnp.int32) < obs_count[0]
    owner = obs_cell // (quarter * n_mp * n_slots) * n_mp + obs_cell // quarter % n_mp
    owner = jnp.where(valid, owner, n_owners)
    local = obs_cell // (quarter * n_mp) % n_slots * quarter + obs_cell % quarter
    position = local * slot_dev + obs_slot

    local_weights = (w_qkv, w_out.T, w_gate_up, w_down.T)
    which = lax.axis_index("groups") * n_slots + my_slot
    share_rows = side_by_side(*[lax.dynamic_slice_in_dim(w, which * share, share, 0) for w in local_weights])
    if n_slots == 2 and n_groups == 2 and share % 16 == 0 and capacity % 16 == 0:
        order = arrival_order(width, n_cells, n_share)
        shares = shares_along_cells(share_rows)
        tokens, shares = tokens_by_blocks(
            owner, position, obs_feat, time_embed, my_slot, capacity, slot_dev, order, shares
        )
        pieces = pieces_of_all(side_by_side(*local_weights), shares)
    else:
        order = jnp.arange(width, dtype=jnp.int32)
        pieces = [(lax.all_gather(share_rows, ("cells", "groups", "slots"), axis=0, tiled=True), 0, 0)]
        tokens = tokens_by_exchanges(owner, position, obs_feat, time_embed, my_slot, capacity, slot_dev)

    swap = [(0, 1), (1, 0)]
    heads_width, hidden_width = w_qkv.shape[2], w_gate_up.shape[2]
    partner = lax.ppermute(tokens, "mp", swap)
    for_partner = layer(partner, pieces, heads_width, hidden_width, BF16)
    from_partner = lax.ppermute(for_partner, "mp", swap)
    own = layer(tokens, pieces, heads_width, hidden_width, F32)
    return finish(tokens, own, from_partner, order).reshape(quarter, TSTEPS, width)


def solution(mesh):
    placed = (
        P(("groups", "cells", "slots", "mp"), None),
        P(("groups", "cells", "slots", "mp")),
        P(("groups", "cells", "slots", "mp")),
        P(("groups", "cells", "slots", "mp")),
        P(),
        P("cells", None, "mp"),
        P("mp", "cells"),
        P("cells", None, "mp"),
        P("mp", "cells"),
    )
    return jax.shard_map(
        on_device,
        mesh=mesh,
        in_specs=placed,
        out_specs=P(("groups", "cells", "slots", "mp"), None, None),
        check_vma=False,
    )
```

```python
import functools

import jax
import jax.numpy as jnp
from jax import lax
from jax.experimental import pallas as pl
from jax.experimental.pallas import tpu as pltpu
from jax.sharding import PartitionSpec as P

HD = 64
TSTEPS = 8
CB = 128
EPS = 1e-06

CODE = 32
UNIT = 512
LANES = 128
VMEM_LIMIT = 48 * 1024 * 1024
F32 = jnp.float32
BF16 = jnp.bfloat16
WHOLE = pl.BlockSpec(memory_space=pltpu.VMEM)
SCALARS = pl.BlockSpec(memory_space=pltpu.SMEM)


def iota(shape, axis):
    return lax.broadcasted_iota(jnp.int32, shape, axis)


def dot(left, right):
    return jnp.dot(left, right, preferred_element_type=F32)


def dot_t(left, right):
    return lax.dot_general(left, right, (((1,), (1,)), ((), ())), preferred_element_type=F32)


def params():
    return pltpu.CompilerParams(vmem_limit_bytes=VMEM_LIMIT)


def place_kernel(capacity, owner_ref, position_ref, feat_ref, out_ref, code_ref):
    n_owners, rows = out_ref.shape[0], feat_ref.shape[0]
    owner = owner_ref[...]
    owner_hot = (iota((n_owners, rows), 0) == owner).astype(F32)
    upper = (iota((rows, rows), 0) <= iota((rows, rows), 1)).astype(BF16)
    running = dot(owner_hot.astype(BF16), upper)
    rank = jnp.sum(running * owner_hot, axis=0, keepdims=True).astype(jnp.int32) - 1
    code = position_ref[...] + 1
    line = iota((8, rows), 0)
    digits = jnp.where(line == 0, code // CODE, jnp.where(line == 1, code % CODE, 0))
    digits = digits.astype(F32).astype(BF16)
    feat = feat_ref[...]
    for block in range(n_owners):
        place = jnp.where(owner == block, rank, -1)
        taken = (iota((capacity, rows), 0) == place).astype(F32).astype(BF16)
        out_ref[block] = dot(taken, feat).astype(BF16)
        sent = dot_t(digits, taken)
        code_ref[block] = (sent[0:1] * CODE + sent[1:2]).astype(jnp.int32) - 1


def place_rows(owner, position, obs_feat, n_owners, capacity):
    rows, width = obs_feat.shape
    return pl.pallas_call(
        functools.partial(place_kernel, capacity),
        out_shape=[
            jax.ShapeDtypeStruct((n_owners, capacity, width), BF16),
            jax.ShapeDtypeStruct((n_owners, 1, capacity), jnp.int32),
        ],
        in_specs=[WHOLE] * 3,
        out_specs=[WHOLE] * 2,
        compiler_params=params(),
        cost_estimate=pl.CostEstimate(
            flops=2 * rows * width * n_owners * capacity,
            bytes_accessed=2 * width * (rows + n_owners * capacity),
            transcendentals=0,
        ),
        name="place_rows",
    )(owner.reshape(1, rows), position.reshape(1, rows), obs_feat)


def pool_kernel(capacity, slot_dev, slot_ref, embed_ref, code_ref, got_ref, keep_ref, send_ref):
    half = keep_ref.shape[0]
    places = 2 * half
    mine = slot_ref[0]
    total = jnp.zeros((places, keep_ref.shape[1]), F32)
    seen = jnp.zeros((places, capacity), F32)
    for block in range(got_ref.shape[0]):
        code = code_ref[block]
        turned = jnp.where(code >= half, code - half, code + half)
        code = jnp.where((code >= 0) & (mine == 1), turned, code)
        hot = (iota((places, capacity), 0) == code).astype(F32)
        seen += hot
        total += dot(hot.astype(BF16), got_ref[block])
    count = jnp.sum(seen, axis=1, keepdims=True)
    steps = embed_ref.shape[0]
    step_hot = iota((places, steps), 1) == iota((places, steps), 0) % slot_dev + mine * slot_dev
    embed = dot(step_hot.astype(F32).astype(BF16), embed_ref[...])
    tokens = (total / jnp.maximum(count, 1.0) + embed).astype(BF16)
    keep_ref[...] = tokens[:half]
    send_ref[...] = tokens[half:]


def pool_rows(my_slot, time_embed, codes, got, capacity, slot_dev):
    width = time_embed.shape[1]
    half = jax.ShapeDtypeStruct((CB * slot_dev // 2, width), BF16)
    return pl.pallas_call(
        functools.partial(pool_kernel, capacity, slot_dev),
        out_shape=[half, half],
        in_specs=[SCALARS] + [WHOLE] * 3,
        out_specs=[WHOLE] * 2,
        compiler_params=params(),
        cost_estimate=pl.CostEstimate(
            flops=2 * CB * slot_dev * got.size, bytes_accessed=2 * got.size, transcendentals=0
        ),
        name="pool_rows",
    )(my_slot, time_embed, codes, got)


def weave_kernel(slot_dev, slot_ref, order_ref, keep_ref, got_ref, out_ref):
    rows, width = out_ref.shape
    half = keep_ref.shape[0]
    mine = slot_ref[0]
    row, col = iota((rows, half), 0), iota((rows, half), 1)
    source = col == row // TSTEPS * slot_dev + row % slot_dev
    own = row % TSTEPS // slot_dev == mine
    from_keep = (source & own).astype(F32).astype(BF16)
    from_got = (source & jnp.logical_not(own)).astype(F32).astype(BF16)
    tokens = (dot(from_keep, keep_ref[...]) + dot(from_got, got_ref[...])).astype(BF16)
    move = (iota((width, width), 0) == order_ref[...]).astype(F32).astype(BF16)
    out_ref[...] = dot(tokens, move).astype(BF16)


def weave_steps(my_slot, order, keep, got, slot_dev):
    rows, width = 2 * keep.shape[0], keep.shape[1]
    return pl.pallas_call(
        functools.partial(weave_kernel, slot_dev),
        out_shape=jax.ShapeDtypeStruct((rows, width), BF16),
        in_specs=[SCALARS] + [WHOLE] * 3,
        out_specs=WHOLE,
        compiler_params=params(),
        cost_estimate=pl.CostEstimate(
            flops=2 * rows * width * (rows + width), bytes_accessed=4 * rows * width, transcendentals=0
        ),
        name="weave_steps",
    )(my_slot, order.reshape(1, width), keep, got)


def head_scale(values, ones):
    sums = dot((values * values).astype(BF16), ones)
    return values * lax.rsqrt(sums * (1.0 / HD) + EPS)


def attention(normed, weight, heads_width, ctx_ref):
    rows = normed.shape[0]
    projected = dot(normed, weight)
    same_head = iota((LANES, LANES), 0) // HD == iota((LANES, LANES), 1) // HD
    ones = same_head.astype(F32).astype(BF16)
    group = LANES
    first = iota((group, LANES), 1) < HD
    row, col = iota((2 * group, group), 0), iota((2 * group, group), 1)
    same_cell = row % group // TSTEPS == col // TSTEPS
    count = jnp.ones((group, LANES), BF16)
    for pair in range(heads_width // LANES):
        at = pair * LANES
        query = (head_scale(projected[:, at : at + LANES], ones) * HD ** (-0.5)).astype(BF16)
        key = head_scale(projected[:, heads_width + at : heads_width + at + LANES], ones).astype(BF16)
        value = projected[:, 2 * heads_width + at : 2 * heads_width + at + LANES].astype(BF16)
        for begin in range(0, rows, group):
            q = query[begin : begin + group]
            k = key[begin : begin + group]
            v = value[begin : begin + group]
            none = jnp.zeros_like(q)
            both = jnp.concatenate([jnp.where(first, q, none), jnp.where(first, none, q)], axis=0)
            expo = jnp.where(same_cell, jnp.exp(dot_t(both, k)), 0.0).astype(BF16)
            mixed = dot(expo, jnp.concatenate([v, count], axis=1))
            top, low = mixed[:group], mixed[group:]
            over = jnp.where(first, top[:, :LANES], low[:, :LANES])
            under = jnp.where(first, top[:, LANES:], low[:, LANES:])
            ctx_ref[begin : begin + group, at : at + LANES] = (over / under).astype(BF16)


def gated(normed, gate_w, up_w, down_w):
    gate = dot(normed, gate_w)
    up = dot(normed, up_w)
    hidden = (gate * (0.5 * jnp.tanh(0.5 * gate) + 0.5) * up).astype(BF16)
    return dot_t(hidden, down_w)


def layer_kernel(plan, sections, with_heads, n_sets, n_pieces, places, *refs):
    refs = list(refs)
    take = lambda count: [refs.pop(0) for _ in range(count)]
    tokens = take(n_sets)
    sums = take(0 if with_heads else n_sets)
    pieces = take(n_pieces)
    outs = take(n_sets)
    w_ref, norm_ref, ctx_ref, acc_ref, sems = refs
    copies = {}
    for number, (section, piece, slot, n_rows, source_col, row, col, size) in enumerate(plan):
        source_row = 0 if slot is None else pl.multiple_of(places[slot], 16)
        copy = pltpu.make_async_copy(
            pieces[piece].at[pl.ds(source_row, n_rows), pl.ds(source_col, size)],
            w_ref.at[pl.ds(row, n_rows), pl.ds(col, size)],
            sems.at[number],
        )
        copy.start()
        copies.setdefault(section, []).append(copy)

    def columns(section):
        for copy in copies.pop(section, []):
            copy.wait()
        begin, end = sections[section]
        return w_ref[:, begin:end]

    for number in range(n_sets):
        rows = tokens[number][...].astype(F32)
        scale = lax.rsqrt(jnp.mean(rows * rows, axis=1, keepdims=True) + EPS)
        norm_ref[number] = (rows * scale).astype(BF16)
    first = 0
    if with_heads:
        for number in range(n_sets):
            attention(norm_ref[number], columns(0), ctx_ref.shape[1], ctx_ref)
            acc_ref[number] = dot_t(ctx_ref[...], columns(1))
        first = 2
    for at in range(first, len(sections), 3):
        for number in range(n_sets):
            add = gated(norm_ref[number], columns(at), columns(at + 1), columns(at + 2))
            so_far = sums[number][...] if at == 0 else acc_ref[number]
            if at + 3 < len(sections):
                acc_ref[number] = so_far + add
            else:
                outs[number][...] = (so_far + add).astype(outs[number].dtype)


def layer(places, tokens, sums, pieces, heads_width, n_units, out_type):
    n_sets = len(tokens)
    rows, width = tokens[0].shape
    gate_at = 3 * heads_width
    up_at = gate_at + n_units * UNIT
    out_at = up_at + n_units * UNIT
    down_at = out_at + heads_width
    columns = down_at + n_units * UNIT
    sections = [(0, gate_at), (out_at, down_at)] if heads_width else []
    for begin in range(0, n_units * UNIT, UNIT):
        sections += [(at + begin, at + begin + UNIT) for at in (gate_at, up_at, down_at)]
    plan = []
    for section, (left, right) in enumerate(sections):
        for number, (array, slot, row, n_rows, at) in enumerate(pieces):
            low, high = max(left, at), min(right, at + array.shape[1])
            if low < high:
                plan.append((section, number, slot, n_rows, low - at, row, low, high - low))
    return pl.pallas_call(
        functools.partial(layer_kernel, plan, sections, heads_width > 0, n_sets, len(pieces)),
        out_shape=[jax.ShapeDtypeStruct((rows, width), out_type)] * n_sets,
        in_specs=[SCALARS] + [WHOLE] * (n_sets + len(sums)) + [pl.BlockSpec(memory_space=pl.ANY)] * len(pieces),
        out_specs=[WHOLE] * n_sets,
        scratch_shapes=[
            pltpu.VMEM((width, columns), BF16),
            pltpu.VMEM((n_sets, rows, width), BF16),
            pltpu.VMEM((rows, max(heads_width, LANES)), BF16),
            pltpu.VMEM((n_sets, rows, width), F32),
            pltpu.SemaphoreType.DMA((len(plan),)),
        ],
        compiler_params=params(),
        cost_estimate=pl.CostEstimate(
            flops=2 * n_sets * rows * width * columns,
            bytes_accessed=2 * width * columns + 6 * n_sets * rows * width,
            transcendentals=n_sets * n_units * rows * UNIT,
        ),
        name="layer_heads" if heads_width else "layer_gated",
    )(places, *tokens, *sums, *[piece[0] for piece in pieces])


def finish_kernel(tok_ref, sum_ref, got_ref, order_ref, out_ref):
    width = out_ref.shape[1]
    mixed = (tok_ref[...].astype(F32) + sum_ref[...] + got_ref[...].astype(F32)).astype(BF16)
    move = (iota((width, width), 0) == order_ref[...]).astype(F32).astype(BF16)
    out_ref[...] = dot_t(mixed, move).astype(BF16)


def finish(tokens, sums, got, order):
    rows, width = tokens.shape
    return pl.pallas_call(
        finish_kernel,
        out_shape=jax.ShapeDtypeStruct((rows, width), BF16),
        in_specs=[WHOLE] * 4,
        out_specs=WHOLE,
        compiler_params=params(),
        cost_estimate=pl.CostEstimate(
            flops=2 * rows * width * width, bytes_accessed=10 * rows * width, transcendentals=0
        ),
        name="finish",
    )(tokens, sums, got, order.reshape(1, width))


def side_by_side(w_qkv, w_out, w_gate_up, w_down, first, last, with_heads):
    rows = w_qkv.shape[0]
    gate_up = w_gate_up[:, :, first:last].reshape(rows, -1)
    down = w_down[:, first:last]
    parts = [w_qkv.reshape(rows, -1), gate_up, w_out, down] if with_heads else [gate_up, down]
    return jnp.concatenate(parts, axis=1)


def shares_along_cells(share_rows):
    n_cells = lax.axis_size("cells")
    up = [(j, (j + 1) % n_cells) for j in range(n_cells)]
    down = [(j, (j - 1) % n_cells) for j in range(n_cells)]
    below = [lax.ppermute(share_rows, "cells", up)]
    above = [lax.ppermute(share_rows, "cells", down)]
    while len(below) + len(above) < n_cells - 1:
        line, way = (below, up) if len(below) <= len(above) else (above, down)
        line.append(lax.ppermute(line[-1], "cells", way))
    return above + below[::-1]


def pieces_by_gather(shard, others, n_share):
    rows, step = shard.shape[0], others.shape[0]
    shares = lax.all_gather(others, ("groups", "slots"), axis=0, tiled=True)
    return [(shard, None, 0, rows, 0)] + [(shares, far, rows + far * step, step, 0) for far in range(n_share)]


def pieces_by_permutes(shard, others):
    rows, step = shard.shape[0], others.shape[0]
    swap = [(0, 1), (1, 0)]
    by_slot = lax.ppermute(others, "slots", swap)
    by_group = lax.ppermute(others, "groups", swap)
    cut = shard.shape[1] // (2 * LANES) * LANES
    far_a = lax.ppermute(by_slot[:, :cut], "groups", swap)
    far_b = lax.ppermute(by_group[:, cut:], "slots", swap)
    return [
        (shard, None, 0, rows, 0),
        (others, None, rows, step, 0),
        (by_slot, None, rows + step, step, 0),
        (by_group, None, rows + 2 * step, step, 0),
        (far_a, None, rows + 3 * step, step, 0),
        (far_b, None, rows + 3 * step, step, cut),
    ]


def arrival_order(width, n_cells, n_share):
    mine = lax.axis_index("cells")
    share_id = lax.axis_index("groups") * lax.axis_size("slots") + lax.axis_index("slots")
    rows = width // n_cells
    share = rows // n_share
    step = (n_cells - 1) * share
    place = jnp.arange(width, dtype=jnp.int32)
    past = jnp.maximum(place - rows, 0)
    which = past // step
    cell = (mine + 1 + past % step // share) % n_cells
    far = cell * rows + (which ^ share_id) * share + past % share
    return jnp.where(place < rows, mine * rows + place, far)


def tokens_by_blocks(blocks, codes, time_embed, my_slot, slot_dev, order, shares, later):
    blocks, codes, *shares = lax.optimization_barrier((blocks, codes, *shares))
    got = lax.all_to_all(blocks, ("cells", "mp"), split_axis=0, concat_axis=0, tiled=True)
    got, later = lax.optimization_barrier((got, later))
    keep, send = pool_rows(my_slot.reshape(1), time_embed, codes, got, blocks.shape[1], slot_dev)
    other = lax.ppermute(send, "slots", [(0, 1), (1, 0)])
    return weave_steps(my_slot.reshape(1), order, keep, other, slot_dev), shares, later


def tokens_by_exchanges(owner, position, obs_feat, time_embed, my_slot, capacity, slot_dev):
    n_slots = lax.axis_size("slots")
    n_owners = lax.axis_size("cells") * lax.axis_size("mp")
    rows, width = obs_feat.shape
    owners = jnp.arange(n_owners, dtype=jnp.int32)
    owner_hot = (owner[:, None] == owners[None, :]).astype(F32)
    row_ids = jnp.arange(rows, dtype=jnp.int32)
    lower = (row_ids[None, :] <= row_ids[:, None]).astype(BF16)
    running = dot(lower, owner_hot.astype(BF16))
    rank = jnp.sum(running * owner_hot, axis=1).astype(jnp.int32) - 1
    place = jnp.where(owner < n_owners, owner * capacity + rank, n_owners * capacity)
    place_ids = jnp.arange(n_owners * capacity, dtype=jnp.int32)
    taken = place_ids[:, None] == place[None, :]
    send_feat = dot(taken.astype(BF16), obs_feat).astype(BF16).reshape(n_owners, capacity, width)
    send_code = jnp.sum(jnp.where(taken, position[None, :] + 1, 0), axis=1).reshape(n_owners, capacity)
    axes = ("cells", "mp")
    got_feat = lax.all_to_all(send_feat, axes, split_axis=0, concat_axis=0, tiled=True).reshape(-1, width)
    got_code = lax.all_to_all(send_code, axes, split_axis=0, concat_axis=0, tiled=True).reshape(-1) - 1
    hot = (jnp.arange(CB * slot_dev, dtype=jnp.int32)[:, None] == got_code[None, :]).astype(BF16)
    count = jnp.sum(hot.astype(F32), axis=1)
    pooled = dot(hot, got_feat) / jnp.maximum(count, 1.0)[:, None]
    embed = lax.dynamic_slice_in_dim(time_embed, my_slot * slot_dev, slot_dev, 0).astype(F32)
    tokens = (pooled.reshape(CB, slot_dev, width) + embed[None]).astype(BF16)
    grid = tokens.reshape(n_slots, CB // n_slots, slot_dev, width)
    grid = lax.all_to_all(grid, "slots", split_axis=0, concat_axis=2, tiled=True)
    return grid.reshape(-1, width)


def on_device(obs_feat, obs_cell, obs_slot, obs_count, time_embed, w_qkv, w_out, w_gate_up, w_down):
    n_cells = lax.axis_size("cells")
    n_slots = lax.axis_size("slots")
    n_groups = lax.axis_size("groups")
    n_mp = lax.axis_size("mp")
    n_owners = n_cells * n_mp
    rows, width = obs_feat.shape
    capacity = 3 * rows // n_owners
    quarter = CB // n_slots
    slot_dev = TSTEPS // n_slots
    my_slot = lax.axis_index("slots")
    n_share = n_groups * n_slots
    share = w_qkv.shape[0] // n_share
    valid = jnp.arange(rows, dtype=jnp.int32) < obs_count[0]
    owner = obs_cell // (quarter * n_mp * n_slots) * n_mp + obs_cell // quarter % n_mp
    owner = jnp.where(valid, owner, n_owners)
    local = obs_cell // (quarter * n_mp) % n_slots * quarter + obs_cell % quarter
    position = local * slot_dev + obs_slot

    local_weights = (w_qkv, w_out.T, w_gate_up, w_down.T)
    which = lax.axis_index("groups") * n_slots + my_slot
    share_weights = [lax.dynamic_slice_in_dim(w, which * share, share, 0) for w in local_weights]
    heads_width, hidden_width = w_qkv.shape[2], w_gate_up.shape[2]
    early = hidden_width - UNIT
    part_a, part_b = (0, early, True), (early, hidden_width, False)
    share_a, share_b = side_by_side(*share_weights, *part_a), side_by_side(*share_weights, *part_b)
    if n_slots == 2 and n_groups == 2 and share % 16 == 0 and capacity % 16 == 0:
        order = arrival_order(width, n_cells, n_share)
        shares = shares_along_cells(share_a)
        blocks, codes = place_rows(owner, position, obs_feat, n_owners, capacity)
        codes = lax.all_to_all(codes, ("cells", "mp"), split_axis=0, concat_axis=0, tiled=True)
        tokens, shares, share_b = tokens_by_blocks(
            blocks, codes, time_embed, my_slot, slot_dev, order, shares, share_b
        )
        others_a = jnp.concatenate(shares, axis=0)
        pieces_a = pieces_by_gather(side_by_side(*local_weights, *part_a), others_a, n_share)
        places = (jnp.arange(n_share, dtype=jnp.int32) ^ which) * others_a.shape[0]
        others_b = jnp.concatenate(shares_along_cells(share_b), axis=0)
        pieces_b = pieces_by_permutes(side_by_side(*local_weights, *part_b), others_b)
    else:
        order = jnp.arange(width, dtype=jnp.int32)
        axes = ("cells", "groups", "slots")
        pieces_a, pieces_b = [
            [(lax.all_gather(mine, axes, axis=0, tiled=True), None, 0, width, 0)] for mine in (share_a, share_b)
        ]
        places = jnp.zeros((n_share,), jnp.int32)
        tokens = tokens_by_exchanges(owner, position, obs_feat, time_embed, my_slot, capacity, slot_dev)

    swap = [(0, 1), (1, 0)]
    partner = lax.ppermute(tokens, "mp", swap)
    sums = layer(places, [partner, tokens], [], pieces_a, heads_width, early // UNIT, F32)
    (for_partner,) = layer(places, [partner], sums[:1], pieces_b, 0, 1, BF16)
    from_partner = lax.ppermute(for_partner, "mp", swap)
    (own,) = layer(places, [tokens], sums[1:], pieces_b, 0, 1, F32)
    return finish(tokens, own, from_partner, order).reshape(quarter, TSTEPS, width)


def solution(mesh):
    placed = (
        P(("groups", "cells", "slots", "mp"), None),
        P(("groups", "cells", "slots", "mp")),
        P(("groups", "cells", "slots", "mp")),
        P(("groups", "cells", "slots", "mp")),
        P(),
        P("cells", None, "mp"),
        P("mp", "cells"),
        P("cells", None, "mp"),
        P("mp", "cells"),
    )
    return jax.shard_map(
        on_device,
        mesh=mesh,
        in_specs=placed,
        out_specs=P(("groups", "cells", "slots", "mp"), None, None),
        check_vma=False,
    )
```

```python
import functools

import jax
import jax.numpy as jnp
from jax import lax
from jax.experimental import pallas as pl
from jax.experimental.pallas import tpu as pltpu
from jax.sharding import PartitionSpec as P

HD = 64
TSTEPS = 8
CB = 128
EPS = 1e-06

CODE = 32
UNIT = 512
LANES = 128
VMEM_LIMIT = 48 * 1024 * 1024
F32 = jnp.float32
BF16 = jnp.bfloat16
WHOLE = pl.BlockSpec(memory_space=pltpu.VMEM)
SCALARS = pl.BlockSpec(memory_space=pltpu.SMEM)


def iota(shape, axis):
    return lax.broadcasted_iota(jnp.int32, shape, axis)


def dot(left, right):
    return jnp.dot(left, right, preferred_element_type=F32)


def dot_t(left, right):
    return lax.dot_general(left, right, (((1,), (1,)), ((), ())), preferred_element_type=F32)


def params():
    return pltpu.CompilerParams(vmem_limit_bytes=VMEM_LIMIT)


def place_kernel(capacity, owner_ref, position_ref, feat_ref, out_ref, code_ref):
    n_owners, rows = out_ref.shape[0], feat_ref.shape[0]
    owner = owner_ref[...]
    owner_hot = (iota((n_owners, rows), 0) == owner).astype(F32)
    upper = (iota((rows, rows), 0) <= iota((rows, rows), 1)).astype(BF16)
    running = dot(owner_hot.astype(BF16), upper)
    rank = jnp.sum(running * owner_hot, axis=0, keepdims=True).astype(jnp.int32) - 1
    code = position_ref[...] + 1
    line = iota((8, rows), 0)
    digits = jnp.where(line == 0, code // CODE, jnp.where(line == 1, code % CODE, 0))
    digits = digits.astype(F32).astype(BF16)
    feat = feat_ref[...]
    for block in range(n_owners):
        place = jnp.where(owner == block, rank, -1)
        taken = (iota((capacity, rows), 0) == place).astype(F32).astype(BF16)
        out_ref[block] = dot(taken, feat).astype(BF16)
        sent = dot_t(digits, taken)
        code_ref[block] = (sent[0:1] * CODE + sent[1:2]).astype(jnp.int32) - 1


def place_rows(owner, position, obs_feat, n_owners, capacity):
    rows, width = obs_feat.shape
    return pl.pallas_call(
        functools.partial(place_kernel, capacity),
        out_shape=[
            jax.ShapeDtypeStruct((n_owners, capacity, width), BF16),
            jax.ShapeDtypeStruct((n_owners, 1, capacity), jnp.int32),
        ],
        in_specs=[WHOLE] * 3,
        out_specs=[WHOLE] * 2,
        compiler_params=params(),
        cost_estimate=pl.CostEstimate(
            flops=2 * rows * width * n_owners * capacity,
            bytes_accessed=2 * width * (rows + n_owners * capacity),
            transcendentals=0,
        ),
        name="place_rows",
    )(owner.reshape(1, rows), position.reshape(1, rows), obs_feat)


def pool_kernel(capacity, slot_dev, slot_ref, embed_ref, code_ref, got_ref, keep_ref, send_ref):
    half = keep_ref.shape[0]
    places = 2 * half
    mine = slot_ref[0]
    total = jnp.zeros((places, keep_ref.shape[1]), F32)
    seen = jnp.zeros((places, capacity), F32)
    for block in range(got_ref.shape[0]):
        code = code_ref[block]
        turned = jnp.where(code >= half, code - half, code + half)
        code = jnp.where((code >= 0) & (mine == 1), turned, code)
        hot = (iota((places, capacity), 0) == code).astype(F32)
        seen += hot
        total += dot(hot.astype(BF16), got_ref[block])
    count = jnp.sum(seen, axis=1, keepdims=True)
    steps = embed_ref.shape[0]
    step_hot = iota((places, steps), 1) == iota((places, steps), 0) % slot_dev + mine * slot_dev
    embed = dot(step_hot.astype(F32).astype(BF16), embed_ref[...])
    tokens = (total / jnp.maximum(count, 1.0) + embed).astype(BF16)
    keep_ref[...] = tokens[:half]
    send_ref[...] = tokens[half:]


def pool_rows(my_slot, time_embed, codes, got, capacity, slot_dev):
    width = time_embed.shape[1]
    half = jax.ShapeDtypeStruct((CB * slot_dev // 2, width), BF16)
    return pl.pallas_call(
        functools.partial(pool_kernel, capacity, slot_dev),
        out_shape=[half, half],
        in_specs=[SCALARS] + [WHOLE] * 3,
        out_specs=[WHOLE] * 2,
        compiler_params=params(),
        cost_estimate=pl.CostEstimate(
            flops=2 * CB * slot_dev * got.size, bytes_accessed=2 * got.size, transcendentals=0
        ),
        name="pool_rows",
    )(my_slot, time_embed, codes, got)


def weave_kernel(slot_dev, slot_ref, order_ref, keep_ref, got_ref, out_ref):
    rows, width = out_ref.shape
    half = keep_ref.shape[0]
    mine = slot_ref[0]
    row, col = iota((rows, half), 0), iota((rows, half), 1)
    source = col == row // TSTEPS * slot_dev + row % slot_dev
    own = row % TSTEPS // slot_dev == mine
    from_keep = (source & own).astype(F32).astype(BF16)
    from_got = (source & jnp.logical_not(own)).astype(F32).astype(BF16)
    tokens = (dot(from_keep, keep_ref[...]) + dot(from_got, got_ref[...])).astype(BF16)
    move = (iota((width, width), 0) == order_ref[...]).astype(F32).astype(BF16)
    out_ref[...] = dot(tokens, move).astype(BF16)


def weave_steps(my_slot, order, keep, got, slot_dev):
    rows, width = 2 * keep.shape[0], keep.shape[1]
    return pl.pallas_call(
        functools.partial(weave_kernel, slot_dev),
        out_shape=jax.ShapeDtypeStruct((rows, width), BF16),
        in_specs=[SCALARS] + [WHOLE] * 3,
        out_specs=WHOLE,
        compiler_params=params(),
        cost_estimate=pl.CostEstimate(
            flops=2 * rows * width * (rows + width), bytes_accessed=4 * rows * width, transcendentals=0
        ),
        name="weave_steps",
    )(my_slot, order.reshape(1, width), keep, got)


def head_scale(values, ones):
    sums = dot((values * values).astype(BF16), ones)
    return values * lax.rsqrt(sums * (1.0 / HD) + EPS)


def attention(normed, weight, heads_width, ctx_ref):
    rows = normed.shape[0]
    projected = dot(normed, weight)
    same_head = iota((LANES, LANES), 0) // HD == iota((LANES, LANES), 1) // HD
    ones = same_head.astype(F32).astype(BF16)
    group = LANES
    first = iota((group, LANES), 1) < HD
    row, col = iota((2 * group, group), 0), iota((2 * group, group), 1)
    same_cell = row % group // TSTEPS == col // TSTEPS
    count = jnp.ones((group, LANES), BF16)
    begins = range(0, rows, group)
    for pair in range(heads_width // LANES):
        at = pair * LANES
        query = (head_scale(projected[:, at : at + LANES], ones) * HD ** (-0.5)).astype(BF16)
        key = head_scale(projected[:, heads_width + at : heads_width + at + LANES], ones).astype(BF16)
        value = projected[:, 2 * heads_width + at : 2 * heads_width + at + LANES].astype(BF16)
        none = jnp.zeros_like(query)
        first_rows = iota((rows, LANES), 1) < HD
        left, right = jnp.where(first_rows, query, none), jnp.where(first_rows, none, query)
        scores = [
            dot_t(jnp.concatenate([left[at : at + group], right[at : at + group]], axis=0), key[at : at + group])
            for at in begins
        ]
        expos = [jnp.where(same_cell, jnp.exp(score), 0.0).astype(BF16) for score in scores]
        mixed = [
            dot(expo, jnp.concatenate([value[at : at + group], count], axis=1)) for at, expo in zip(begins, expos)
        ]
        for begin, both in zip(begins, mixed):
            top, low = both[:group], both[group:]
            over = jnp.where(first, top[:, :LANES], low[:, :LANES])
            under = jnp.where(first, top[:, LANES:], low[:, LANES:])
            ctx_ref[begin : begin + group, at : at + LANES] = (over / under).astype(BF16)


def gated(normed, gate_w, up_w, down_w):
    gate = dot(normed, gate_w)
    up = dot(normed, up_w)
    hidden = (gate * (0.5 * jnp.tanh(0.5 * gate) + 0.5) * up).astype(BF16)
    return dot_t(hidden, down_w)


def layer_kernel(plan, sections, with_heads, n_sets, n_pieces, *refs):
    refs = list(refs)
    take = lambda count: [refs.pop(0) for _ in range(count)]
    tokens = take(n_sets)
    sums = take(0 if with_heads else n_sets)
    pieces = take(n_pieces)
    outs = take(n_sets)
    w_ref, norm_ref, ctx_ref, acc_ref, sems = refs
    copies = {}
    for number, (section, piece, source_col, row, col, size) in enumerate(plan):
        copy = pltpu.make_async_copy(
            pieces[piece].at[:, pl.ds(source_col, size)],
            w_ref.at[pl.ds(row, pieces[piece].shape[0]), pl.ds(col, size)],
            sems.at[number],
        )
        copy.start()
        copies.setdefault(section, []).append(copy)

    def columns(section):
        for copy in copies.pop(section, []):
            copy.wait()
        begin, end = sections[section]
        return w_ref[:, begin:end]

    for number in range(n_sets):
        rows = tokens[number][...].astype(F32)
        scale = lax.rsqrt(jnp.mean(rows * rows, axis=1, keepdims=True) + EPS)
        norm_ref[number] = (rows * scale).astype(BF16)
    first = 0
    if with_heads:
        for number in range(n_sets):
            attention(norm_ref[number], columns(0), ctx_ref.shape[1], ctx_ref)
            acc_ref[number] = dot_t(ctx_ref[...], columns(1))
        first = 2
    for at in range(first, len(sections), 3):
        for number in range(n_sets):
            add = gated(norm_ref[number], columns(at), columns(at + 1), columns(at + 2))
            so_far = sums[number][...] if at == 0 else acc_ref[number]
            if at + 3 < len(sections):
                acc_ref[number] = so_far + add
            else:
                outs[number][...] = (so_far + add).astype(outs[number].dtype)


def layer(tokens, sums, pieces, heads_width, n_units, out_type):
    n_sets = len(tokens)
    rows, width = tokens[0].shape
    gate_at = 3 * heads_width
    up_at = gate_at + n_units * UNIT
    out_at = up_at + n_units * UNIT
    down_at = out_at + heads_width
    columns = down_at + n_units * UNIT
    sections = [(0, gate_at), (out_at, down_at)] if heads_width else []
    for begin in range(0, n_units * UNIT, UNIT):
        sections += [(at + begin, at + begin + UNIT) for at in (gate_at, up_at, down_at)]
    plan = []
    for section, (left, right) in enumerate(sections):
        for number, (array, row, at) in enumerate(pieces):
            low, high = max(left, at), min(right, at + array.shape[1])
            if low < high:
                plan.append((section, number, low - at, row, low, high - low))
    return pl.pallas_call(
        functools.partial(layer_kernel, plan, sections, heads_width > 0, n_sets, len(pieces)),
        out_shape=[jax.ShapeDtypeStruct((rows, width), out_type)] * n_sets,
        in_specs=[WHOLE] * (n_sets + len(sums)) + [pl.BlockSpec(memory_space=pl.ANY)] * len(pieces),
        out_specs=[WHOLE] * n_sets,
        scratch_shapes=[
            pltpu.VMEM((width, columns), BF16),
            pltpu.VMEM((n_sets, rows, width), BF16),
            pltpu.VMEM((rows, max(heads_width, LANES)), BF16),
            pltpu.VMEM((n_sets, rows, width), F32),
            pltpu.SemaphoreType.DMA((len(plan),)),
        ],
        compiler_params=params(),
        cost_estimate=pl.CostEstimate(
            flops=2 * n_sets * rows * width * columns,
            bytes_accessed=2 * width * columns + 6 * n_sets * rows * width,
            transcendentals=n_sets * n_units * rows * UNIT,
        ),
        name="layer_heads" if heads_width else "layer_gated",
    )(*tokens, *sums, *[piece[0] for piece in pieces])


def finish_kernel(tok_ref, sum_ref, got_ref, order_ref, out_ref):
    width = out_ref.shape[1]
    mixed = (tok_ref[...].astype(F32) + sum_ref[...] + got_ref[...].astype(F32)).astype(BF16)
    move = (iota((width, width), 0) == order_ref[...]).astype(F32).astype(BF16)
    out_ref[...] = dot_t(mixed, move).astype(BF16)


def finish(tokens, sums, got, order):
    rows, width = tokens.shape
    return pl.pallas_call(
        finish_kernel,
        out_shape=jax.ShapeDtypeStruct((rows, width), BF16),
        in_specs=[WHOLE] * 4,
        out_specs=WHOLE,
        compiler_params=params(),
        cost_estimate=pl.CostEstimate(
            flops=2 * rows * width * width, bytes_accessed=10 * rows * width, transcendentals=0
        ),
        name="finish",
    )(tokens, sums, got, order.reshape(1, width))


def side_by_side(w_qkv, w_out, w_gate_up, w_down, first, last, with_heads):
    rows = w_qkv.shape[0]
    gate_up = w_gate_up[:, :, first:last].reshape(rows, -1)
    down = w_down[:, first:last]
    parts = [w_qkv.reshape(rows, -1), gate_up, w_out, down] if with_heads else [gate_up, down]
    return jnp.concatenate(parts, axis=1)


def along_cells(values, distance):
    n_cells = lax.axis_size("cells")
    return lax.ppermute(values, "cells", [(j, (j - distance) % n_cells) for j in range(n_cells)])


def from_neighbours(share_rows):
    return along_cells(share_rows, 1), along_cells(share_rows, -1)


def from_all_cells(above, below):
    above, below = [above], [below]
    while len(above) + len(below) < lax.axis_size("cells") - 1:
        line, way = (below, -1) if len(below) <= len(above) else (above, 1)
        line.append(along_cells(line[-1], way))
    return above + below[::-1]


def pieces_of_all(shard, shares):
    rows = shard.shape[0]
    others = jnp.concatenate(shares, axis=0)
    step = others.shape[0]
    n_slots = lax.axis_size("slots")
    n_share = lax.axis_size("groups") * n_slots
    pieces = [(shard, 0, 0), (others, rows, 0)]
    for far in range(1, n_share):
        pairs = [(place, place ^ far) for place in range(n_share)]
        pieces.append((lax.ppermute(others, ("groups", "slots"), pairs), rows + far * step, 0))
    return pieces


def arrival_order(width, n_cells, n_share):
    mine = lax.axis_index("cells")
    share_id = lax.axis_index("groups") * lax.axis_size("slots") + lax.axis_index("slots")
    rows = width // n_cells
    share = rows // n_share
    step = (n_cells - 1) * share
    place = jnp.arange(width, dtype=jnp.int32)
    past = jnp.maximum(place - rows, 0)
    which = past // step
    cell = (mine + 1 + past % step // share) % n_cells
    far = cell * rows + (which ^ share_id) * share + past % share
    return jnp.where(place < rows, mine * rows + place, far)


def pooled_blocks(blocks, codes, time_embed, my_slot, slot_dev):
    got = lax.all_to_all(blocks, ("cells", "mp"), split_axis=0, concat_axis=0, tiled=True)
    return pool_rows(my_slot.reshape(1), time_embed, codes, got, blocks.shape[1], slot_dev)


def tokens_by_exchanges(owner, position, obs_feat, time_embed, my_slot, capacity, slot_dev):
    n_slots = lax.axis_size("slots")
    n_owners = lax.axis_size("cells") * lax.axis_size("mp")
    rows, width = obs_feat.shape
    owners = jnp.arange(n_owners, dtype=jnp.int32)
    owner_hot = (owner[:, None] == owners[None, :]).astype(F32)
    row_ids = jnp.arange(rows, dtype=jnp.int32)
    lower = (row_ids[None, :] <= row_ids[:, None]).astype(BF16)
    running = dot(lower, owner_hot.astype(BF16))
    rank = jnp.sum(running * owner_hot, axis=1).astype(jnp.int32) - 1
    place = jnp.where(owner < n_owners, owner * capacity + rank, n_owners * capacity)
    place_ids = jnp.arange(n_owners * capacity, dtype=jnp.int32)
    taken = place_ids[:, None] == place[None, :]
    send_feat = dot(taken.astype(BF16), obs_feat).astype(BF16).reshape(n_owners, capacity, width)
    send_code = jnp.sum(jnp.where(taken, position[None, :] + 1, 0), axis=1).reshape(n_owners, capacity)
    axes = ("cells", "mp")
    got_feat = lax.all_to_all(send_feat, axes, split_axis=0, concat_axis=0, tiled=True).reshape(-1, width)
    got_code = lax.all_to_all(send_code, axes, split_axis=0, concat_axis=0, tiled=True).reshape(-1) - 1
    hot = (jnp.arange(CB * slot_dev, dtype=jnp.int32)[:, None] == got_code[None, :]).astype(BF16)
    count = jnp.sum(hot.astype(F32), axis=1)
    pooled = dot(hot, got_feat) / jnp.maximum(count, 1.0)[:, None]
    embed = lax.dynamic_slice_in_dim(time_embed, my_slot * slot_dev, slot_dev, 0).astype(F32)
    tokens = (pooled.reshape(CB, slot_dev, width) + embed[None]).astype(BF16)
    grid = tokens.reshape(n_slots, CB // n_slots, slot_dev, width)
    grid = lax.all_to_all(grid, "slots", split_axis=0, concat_axis=2, tiled=True)
    return grid.reshape(-1, width)


def on_device(obs_feat, obs_cell, obs_slot, obs_count, time_embed, w_qkv, w_out, w_gate_up, w_down):
    n_cells = lax.axis_size("cells")
    n_slots = lax.axis_size("slots")
    n_groups = lax.axis_size("groups")
    n_mp = lax.axis_size("mp")
    n_owners = n_cells * n_mp
    rows, width = obs_feat.shape
    capacity = 3 * rows // n_owners
    quarter = CB // n_slots
    slot_dev = TSTEPS // n_slots
    my_slot = lax.axis_index("slots")
    n_share = n_groups * n_slots
    share = w_qkv.shape[0] // n_share
    valid = jnp.arange(rows, dtype=jnp.int32) < obs_count[0]
    owner = obs_cell // (quarter * n_mp * n_slots) * n_mp + obs_cell // quarter % n_mp
    owner = jnp.where(valid, owner, n_owners)
    local = obs_cell // (quarter * n_mp) % n_slots * quarter + obs_cell % quarter
    position = local * slot_dev + obs_slot

    local_weights = (w_qkv, w_out.T, w_gate_up, w_down.T)
    which = lax.axis_index("groups") * n_slots + my_slot
    share_weights = [lax.dynamic_slice_in_dim(w, which * share, share, 0) for w in local_weights]
    heads_width, hidden_width = w_qkv.shape[2], w_gate_up.shape[2]
    early = hidden_width - UNIT
    part_a, part_b = (0, early, True), (early, hidden_width, False)
    share_a, share_b = side_by_side(*share_weights, *part_a), side_by_side(*share_weights, *part_b)
    if n_slots == 2 and n_groups == 2 and share % 16 == 0 and capacity % 16 == 0:
        order = arrival_order(width, n_cells, n_share)
        shares = from_all_cells(*from_neighbours(share_a))
        blocks, codes = place_rows(owner, position, obs_feat, n_owners, capacity)
        codes = lax.all_to_all(codes, ("cells", "mp"), split_axis=0, concat_axis=0, tiled=True)
        blocks, codes, *shares = lax.optimization_barrier((blocks, codes, *shares))
        pieces_a = pieces_of_all(side_by_side(*local_weights, *part_a), shares)
        keep, send = pooled_blocks(blocks, codes, time_embed, my_slot, slot_dev)
        arrays, share_b, send = lax.optimization_barrier(([piece[0] for piece in pieces_a], share_b, send))
        pieces_a = [(array, *place) for array, (_, *place) in zip(arrays, pieces_a)]
        other = lax.ppermute(send, "slots", [(0, 1), (1, 0)])
        near_b = from_neighbours(share_b)
        other, near_b = lax.optimization_barrier((other, near_b))
        pieces_b = pieces_of_all(side_by_side(*local_weights, *part_b), from_all_cells(*near_b))
        tokens = weave_steps(my_slot.reshape(1), order, keep, other, slot_dev)
    else:
        order = jnp.arange(width, dtype=jnp.int32)
        axes = ("cells", "groups", "slots")
        pieces_a, pieces_b = [
            [(lax.all_gather(mine, axes, axis=0, tiled=True), 0, 0)] for mine in (share_a, share_b)
        ]
        tokens = tokens_by_exchanges(owner, position, obs_feat, time_embed, my_slot, capacity, slot_dev)

    swap = [(0, 1), (1, 0)]
    partner = lax.ppermute(tokens, "mp", swap)
    sums = layer([partner, tokens], [], pieces_a, heads_width, early // UNIT, F32)
    (for_partner,) = layer([partner], sums[:1], pieces_b, 0, 1, BF16)
    from_partner = lax.ppermute(for_partner, "mp", swap)
    (own,) = layer([tokens], sums[1:], pieces_b, 0, 1, F32)
    return finish(tokens, own, from_partner, order).reshape(quarter, TSTEPS, width)


def solution(mesh):
    placed = (
        P(("groups", "cells", "slots", "mp"), None),
        P(("groups", "cells", "slots", "mp")),
        P(("groups", "cells", "slots", "mp")),
        P(("groups", "cells", "slots", "mp")),
        P(),
        P("cells", None, "mp"),
        P("mp", "cells"),
        P("cells", None, "mp"),
        P("mp", "cells"),
    )
    return jax.shard_map(
        on_device,
        mesh=mesh,
        in_specs=placed,
        out_specs=P(("groups", "cells", "slots", "mp"), None, None),
        check_vma=False,
    )
```

```python
import functools

import jax
import jax.numpy as jnp
from jax import lax
from jax.experimental import pallas as pl
from jax.experimental.pallas import tpu as pltpu
from jax.sharding import PartitionSpec as P

HD = 64
TSTEPS = 8
CB = 128
EPS = 1e-06

CODE = 32
UNIT = 512
LANES = 128
VMEM_LIMIT = 48 * 1024 * 1024
F32 = jnp.float32
BF16 = jnp.bfloat16
WHOLE = pl.BlockSpec(memory_space=pltpu.VMEM)
SCALARS = pl.BlockSpec(memory_space=pltpu.SMEM)


def iota(shape, axis):
    return lax.broadcasted_iota(jnp.int32, shape, axis)


def dot(left, right):
    return jnp.dot(left, right, preferred_element_type=F32)


def dot_t(left, right):
    return lax.dot_general(left, right, (((1,), (1,)), ((), ())), preferred_element_type=F32)


def params():
    return pltpu.CompilerParams(vmem_limit_bytes=VMEM_LIMIT)


def place_kernel(capacity, owner_ref, position_ref, feat_ref, out_ref, code_ref):
    n_owners, rows = out_ref.shape[0], feat_ref.shape[0]
    owner = owner_ref[...]
    owner_hot = (iota((n_owners, rows), 0) == owner).astype(F32)
    upper = (iota((rows, rows), 0) <= iota((rows, rows), 1)).astype(BF16)
    running = dot(owner_hot.astype(BF16), upper)
    rank = jnp.sum(running * owner_hot, axis=0, keepdims=True).astype(jnp.int32) - 1
    code = position_ref[...] + 1
    line = iota((8, rows), 0)
    digits = jnp.where(line == 0, code // CODE, jnp.where(line == 1, code % CODE, 0))
    digits = digits.astype(F32).astype(BF16)
    feat = feat_ref[...]
    for block in range(n_owners):
        place = jnp.where(owner == block, rank, -1)
        taken = (iota((capacity, rows), 0) == place).astype(F32).astype(BF16)
        out_ref[block] = dot(taken, feat).astype(BF16)
        sent = dot_t(digits, taken)
        code_ref[block] = (sent[0:1] * CODE + sent[1:2]).astype(jnp.int32) - 1


def place_rows(owner, position, obs_feat, n_owners, capacity):
    rows, width = obs_feat.shape
    return pl.pallas_call(
        functools.partial(place_kernel, capacity),
        out_shape=[
            jax.ShapeDtypeStruct((n_owners, capacity, width), BF16),
            jax.ShapeDtypeStruct((n_owners, 1, capacity), jnp.int32),
        ],
        in_specs=[WHOLE] * 3,
        out_specs=[WHOLE] * 2,
        compiler_params=params(),
        cost_estimate=pl.CostEstimate(
            flops=2 * rows * width * n_owners * capacity,
            bytes_accessed=2 * width * (rows + n_owners * capacity),
            transcendentals=0,
        ),
        name="place_rows",
    )(owner.reshape(1, rows), position.reshape(1, rows), obs_feat)


def pool_kernel(capacity, slot_dev, slot_ref, embed_ref, code_ref, got_ref, keep_ref, send_ref):
    half = keep_ref.shape[0]
    places = 2 * half
    mine = slot_ref[0]
    total = jnp.zeros((places, keep_ref.shape[1]), F32)
    seen = jnp.zeros((places, capacity), F32)
    for block in range(got_ref.shape[0]):
        code = code_ref[block]
        turned = jnp.where(code >= half, code - half, code + half)
        code = jnp.where((code >= 0) & (mine == 1), turned, code)
        hot = (iota((places, capacity), 0) == code).astype(F32)
        seen += hot
        total += dot(hot.astype(BF16), got_ref[block])
    count = jnp.sum(seen, axis=1, keepdims=True)
    steps = embed_ref.shape[0]
    step_hot = iota((places, steps), 1) == iota((places, steps), 0) % slot_dev + mine * slot_dev
    embed = dot(step_hot.astype(F32).astype(BF16), embed_ref[...])
    tokens = (total / jnp.maximum(count, 1.0) + embed).astype(BF16)
    keep_ref[...] = tokens[:half]
    send_ref[...] = tokens[half:]


def pool_rows(my_slot, time_embed, codes, got, capacity, slot_dev):
    width = time_embed.shape[1]
    half = jax.ShapeDtypeStruct((CB * slot_dev // 2, width), BF16)
    return pl.pallas_call(
        functools.partial(pool_kernel, capacity, slot_dev),
        out_shape=[half, half],
        in_specs=[SCALARS] + [WHOLE] * 3,
        out_specs=[WHOLE] * 2,
        compiler_params=params(),
        cost_estimate=pl.CostEstimate(
            flops=2 * CB * slot_dev * got.size, bytes_accessed=2 * got.size, transcendentals=0
        ),
        name="pool_rows",
    )(my_slot, time_embed, codes, got)


def weave_kernel(slot_dev, slot_ref, order_ref, keep_ref, got_ref, out_ref):
    rows, width = out_ref.shape
    half = keep_ref.shape[0]
    mine = slot_ref[0]
    row, col = iota((rows, half), 0), iota((rows, half), 1)
    source = col == row // TSTEPS * slot_dev + row % slot_dev
    own = row % TSTEPS // slot_dev == mine
    from_keep = (source & own).astype(F32).astype(BF16)
    from_got = (source & jnp.logical_not(own)).astype(F32).astype(BF16)
    tokens = (dot(from_keep, keep_ref[...]) + dot(from_got, got_ref[...])).astype(BF16)
    move = (iota((width, width), 0) == order_ref[...]).astype(F32).astype(BF16)
    out_ref[...] = dot(tokens, move).astype(BF16)


def weave_steps(my_slot, order, keep, got, slot_dev):
    rows, width = 2 * keep.shape[0], keep.shape[1]
    return pl.pallas_call(
        functools.partial(weave_kernel, slot_dev),
        out_shape=jax.ShapeDtypeStruct((rows, width), BF16),
        in_specs=[SCALARS] + [WHOLE] * 3,
        out_specs=WHOLE,
        compiler_params=params(),
        cost_estimate=pl.CostEstimate(
            flops=2 * rows * width * (rows + width), bytes_accessed=4 * rows * width, transcendentals=0
        ),
        name="weave_steps",
    )(my_slot, order.reshape(1, width), keep, got)


def attention(normed, weight, heads_width, ctx_ref):
    rows = normed.shape[0]
    group = LANES
    lane = iota((1, LANES), 1)
    first = iota((group, LANES), 1) < HD
    masks = [(lane < HD).astype(F32).astype(BF16), (lane >= HD).astype(F32).astype(BF16)]
    ones = (iota((LANES, LANES), 0) // HD == iota((LANES, LANES), 1) // HD).astype(F32)
    mean = (ones * (1.0 / HD)).astype(BF16)
    ones = ones.astype(BF16)
    same_cell = iota((2 * group, group), 0) % group // TSTEPS == iota((2 * group, group), 1) // TSTEPS
    same_cell = same_cell.astype(F32).astype(BF16)
    count = jnp.ones((group, LANES), BF16)
    projected = dot(normed, weight)
    begins = range(0, rows, group)
    for at in range(0, heads_width, LANES):
        query = projected[:, at : at + LANES]
        key = projected[:, heads_width + at : heads_width + at + LANES]
        value = projected[:, 2 * heads_width + at : 2 * heads_width + at + LANES].astype(BF16)
        query_bf, key_bf = query.astype(BF16), key.astype(BF16)
        query = (query * lax.rsqrt(dot(query_bf * query_bf, ones) + HD * EPS)).astype(BF16)
        key = (key * lax.rsqrt(dot(key_bf * key_bf, mean) + EPS)).astype(BF16)
        left, right = query * masks[0], query * masks[1]
        scores = [
            dot_t(jnp.concatenate([left[at : at + group], right[at : at + group]], axis=0), key[at : at + group])
            for at in begins
        ]
        expos = [jnp.exp(score).astype(BF16) * same_cell for score in scores]
        mixed = [
            dot(expo, jnp.concatenate([value[at : at + group], count], axis=1)) for at, expo in zip(begins, expos)
        ]
        for begin, both in zip(begins, mixed):
            top, low = both[:group], both[group:]
            over = jnp.where(first, top[:, :LANES], low[:, :LANES])
            under = jnp.where(first, top[:, LANES:], low[:, LANES:])
            ctx_ref[begin : begin + group, at : at + LANES] = (over / under).astype(BF16)


def gated(normed, gate_w, up_w, down_w):
    gate = dot(normed, gate_w)
    up = dot(normed, up_w)
    hidden = (gate * (0.5 * jnp.tanh(0.5 * gate) + 0.5) * up).astype(BF16)
    return dot_t(hidden, down_w)


def layer_kernel(plan, sections, tok_ref, *refs):
    pieces, (out_ref, w_ref, norm_ref, ctx_ref, acc_ref, sems) = refs[:-6], refs[-6:]
    copies = {}
    for number, (section, piece, row, col, size) in enumerate(plan):
        copy = pltpu.make_async_copy(
            pieces[piece].at[:, pl.ds(col, size)],
            w_ref.at[pl.ds(row, pieces[piece].shape[0]), pl.ds(col, size)],
            sems.at[number],
        )
        copy.start()
        copies.setdefault(section, []).append(copy)

    def columns(section):
        for copy in copies[section]:
            copy.wait()
        begin, end = sections[section]
        return w_ref[:, begin:end]

    tokens = tok_ref[...].astype(F32)
    scale = lax.rsqrt(jnp.mean(tokens * tokens, axis=1, keepdims=True) + EPS)
    norm_ref[...] = (tokens * scale).astype(BF16)
    attention(norm_ref[...], columns(0), ctx_ref.shape[1], ctx_ref)
    acc_ref[...] = dot_t(ctx_ref[...], columns(1))
    for at in range(2, len(sections), 3):
        add = gated(norm_ref[...], columns(at), columns(at + 1), columns(at + 2))
        if at + 3 < len(sections):
            acc_ref[...] += add
        else:
            out_ref[...] = (acc_ref[...] + add).astype(out_ref.dtype)


def layer(tokens, pieces, heads_width, hidden_width, out_type):
    rows, width = tokens.shape
    gate_at = 3 * heads_width
    up_at = gate_at + hidden_width
    out_at = up_at + hidden_width
    down_at = out_at + heads_width
    columns = down_at + hidden_width
    sections = [(0, gate_at), (out_at, down_at)]
    for begin in range(0, hidden_width, UNIT):
        sections += [(at + begin, at + begin + UNIT) for at in (gate_at, up_at, down_at)]
    plan = [
        (section, number, row, left, right - left)
        for section, (left, right) in enumerate(sections)
        for number, (_, row) in enumerate(pieces)
    ]
    return pl.pallas_call(
        functools.partial(layer_kernel, plan, sections),
        out_shape=jax.ShapeDtypeStruct((rows, width), out_type),
        in_specs=[WHOLE] + [pl.BlockSpec(memory_space=pl.ANY)] * len(pieces),
        out_specs=WHOLE,
        scratch_shapes=[
            pltpu.VMEM((width, columns), BF16),
            pltpu.VMEM((rows, width), BF16),
            pltpu.VMEM((rows, heads_width), BF16),
            pltpu.VMEM((rows, width), F32),
            pltpu.SemaphoreType.DMA((len(plan),)),
        ],
        compiler_params=params(),
        cost_estimate=pl.CostEstimate(
            flops=2 * rows * width * columns,
            bytes_accessed=2 * width * columns + 6 * rows * width,
            transcendentals=rows * hidden_width,
        ),
        name="layer",
    )(tokens, *[array for array, _ in pieces])


def finish_kernel(tok_ref, sum_ref, got_ref, order_ref, out_ref):
    width = out_ref.shape[1]
    mixed = (tok_ref[...].astype(F32) + sum_ref[...] + got_ref[...].astype(F32)).astype(BF16)
    move = (iota((width, width), 0) == order_ref[...]).astype(F32).astype(BF16)
    out_ref[...] = dot_t(mixed, move).astype(BF16)


def finish(tokens, sums, got, order):
    rows, width = tokens.shape
    return pl.pallas_call(
        finish_kernel,
        out_shape=jax.ShapeDtypeStruct((rows, width), BF16),
        in_specs=[WHOLE] * 4,
        out_specs=WHOLE,
        compiler_params=params(),
        cost_estimate=pl.CostEstimate(
            flops=2 * rows * width * width, bytes_accessed=10 * rows * width, transcendentals=0
        ),
        name="finish",
    )(tokens, sums, got, order.reshape(1, width))


def side_by_side(w_qkv, w_out, w_gate_up, w_down):
    rows = w_qkv.shape[0]
    return jnp.concatenate([w_qkv.reshape(rows, -1), w_gate_up.reshape(rows, -1), w_out, w_down], axis=1)


def along_cells(values, distance):
    n_cells = lax.axis_size("cells")
    return lax.ppermute(values, "cells", [(j, (j - distance) % n_cells) for j in range(n_cells)])


def to_other_places(shares):
    n_slots = lax.axis_size("slots")
    n_share = lax.axis_size("groups") * n_slots
    places = [shares]
    for far in range(1, n_share):
        pairs = [(place, place ^ far) for place in range(n_share)]
        places.append(lax.ppermute(shares, ("groups", "slots"), pairs))
    return places


def arrival_order(width, n_share):
    n_cells = lax.axis_size("cells")
    mine = lax.axis_index("cells")
    place = lax.axis_index("groups") * lax.axis_size("slots") + lax.axis_index("slots")
    rows = width // n_cells
    share = rows // n_share
    row = jnp.arange(width, dtype=jnp.int32)
    past = row - 2 * rows
    far = jnp.where(past < 0, row // share % n_share, past // (2 * share))
    distance = jnp.where(past < 0, n_cells - 1, 1 + past // share % 2)
    other = (mine + distance) % n_cells * rows + (far ^ place) * share + row % share
    return jnp.where(row < rows, mine * rows + row, other)


def pooled_blocks(blocks, codes, time_embed, my_slot, slot_dev):
    got = lax.all_to_all(blocks, ("cells", "mp"), split_axis=0, concat_axis=0, tiled=True)
    return pool_rows(my_slot.reshape(1), time_embed, codes, got, blocks.shape[1], slot_dev)


def tokens_by_exchanges(owner, position, obs_feat, time_embed, my_slot, capacity, slot_dev):
    n_slots = lax.axis_size("slots")
    n_owners = lax.axis_size("cells") * lax.axis_size("mp")
    rows, width = obs_feat.shape
    owners = jnp.arange(n_owners, dtype=jnp.int32)
    owner_hot = (owner[:, None] == owners[None, :]).astype(F32)
    row_ids = jnp.arange(rows, dtype=jnp.int32)
    lower = (row_ids[None, :] <= row_ids[:, None]).astype(BF16)
    running = dot(lower, owner_hot.astype(BF16))
    rank = jnp.sum(running * owner_hot, axis=1).astype(jnp.int32) - 1
    place = jnp.where(owner < n_owners, owner * capacity + rank, n_owners * capacity)
    place_ids = jnp.arange(n_owners * capacity, dtype=jnp.int32)
    taken = place_ids[:, None] == place[None, :]
    send_feat = dot(taken.astype(BF16), obs_feat).astype(BF16).reshape(n_owners, capacity, width)
    send_code = jnp.sum(jnp.where(taken, position[None, :] + 1, 0), axis=1).reshape(n_owners, capacity)
    axes = ("cells", "mp")
    got_feat = lax.all_to_all(send_feat, axes, split_axis=0, concat_axis=0, tiled=True).reshape(-1, width)
    got_code = lax.all_to_all(send_code, axes, split_axis=0, concat_axis=0, tiled=True).reshape(-1) - 1
    hot = (jnp.arange(CB * slot_dev, dtype=jnp.int32)[:, None] == got_code[None, :]).astype(BF16)
    count = jnp.sum(hot.astype(F32), axis=1)
    pooled = dot(hot, got_feat) / jnp.maximum(count, 1.0)[:, None]
    embed = lax.dynamic_slice_in_dim(time_embed, my_slot * slot_dev, slot_dev, 0).astype(F32)
    tokens = (pooled.reshape(CB, slot_dev, width) + embed[None]).astype(BF16)
    grid = tokens.reshape(n_slots, CB // n_slots, slot_dev, width)
    grid = lax.all_to_all(grid, "slots", split_axis=0, concat_axis=2, tiled=True)
    return grid.reshape(-1, width)


def on_device(obs_feat, obs_cell, obs_slot, obs_count, time_embed, w_qkv, w_out, w_gate_up, w_down):
    n_cells = lax.axis_size("cells")
    n_slots = lax.axis_size("slots")
    n_groups = lax.axis_size("groups")
    n_mp = lax.axis_size("mp")
    n_owners = n_cells * n_mp
    rows, width = obs_feat.shape
    capacity = 3 * rows // n_owners
    quarter = CB // n_slots
    slot_dev = TSTEPS // n_slots
    my_slot = lax.axis_index("slots")
    n_share = n_groups * n_slots
    share = w_qkv.shape[0] // n_share
    valid = jnp.arange(rows, dtype=jnp.int32) < obs_count[0]
    owner = obs_cell // (quarter * n_mp * n_slots) * n_mp + obs_cell // quarter % n_mp
    owner = jnp.where(valid, owner, n_owners)
    local = obs_cell // (quarter * n_mp) % n_slots * quarter + obs_cell % quarter
    position = local * slot_dev + obs_slot

    local_weights = (w_qkv, w_out.T, w_gate_up, w_down.T)
    which = lax.axis_index("groups") * n_slots + my_slot
    share_weights = [lax.dynamic_slice_in_dim(w, which * share, share, 0) for w in local_weights]
    share_rows = side_by_side(*share_weights)
    if n_slots == 2 and n_groups == 2 and n_cells == 4 and share % 16 == 0 and capacity % 16 == 0:
        order = arrival_order(width, n_share)
        below = along_cells(share_rows, -1)
        blocks, codes = place_rows(owner, position, obs_feat, n_owners, capacity)
        codes = lax.all_to_all(codes, ("cells", "mp"), split_axis=0, concat_axis=0, tiled=True)
        below, codes, share_rows = lax.optimization_barrier((below, codes, share_rows))
        first = to_other_places(below)
        above, opposite = along_cells(share_rows, 1), along_cells(below, -1)
        blocks, above, opposite, first = lax.optimization_barrier((blocks, above, opposite, first))
        second = to_other_places(jnp.concatenate([above, opposite], axis=0))
        keep, send = pooled_blocks(blocks, codes, time_embed, my_slot, slot_dev)
        send, second = lax.optimization_barrier((send, second))
        other = lax.ppermute(send, "slots", [(0, 1), (1, 0)])
        tokens = weave_steps(my_slot.reshape(1), order, keep, other, slot_dev)
        pieces, row = [], 0
        for array in [side_by_side(*local_weights)] + first + second:
            pieces.append((array, row))
            row += array.shape[0]
    else:
        order = jnp.arange(width, dtype=jnp.int32)
        pieces = [(lax.all_gather(share_rows, ("cells", "groups", "slots"), axis=0, tiled=True), 0)]
        tokens = tokens_by_exchanges(owner, position, obs_feat, time_embed, my_slot, capacity, slot_dev)

    swap = [(0, 1), (1, 0)]
    heads_width, hidden_width = w_qkv.shape[2], w_gate_up.shape[2]
    partner = lax.ppermute(tokens, "mp", swap)
    for_partner = layer(partner, pieces, heads_width, hidden_width, BF16)
    from_partner = lax.ppermute(for_partner, "mp", swap)
    own = layer(tokens, pieces, heads_width, hidden_width, F32)
    return finish(tokens, own, from_partner, order).reshape(quarter, TSTEPS, width)


def solution(mesh):
    placed = (
        P(("groups", "cells", "slots", "mp"), None),
        P(("groups", "cells", "slots", "mp")),
        P(("groups", "cells", "slots", "mp")),
        P(("groups", "cells", "slots", "mp")),
        P(),
        P("cells", None, "mp"),
        P("mp", "cells"),
        P("cells", None, "mp"),
        P("mp", "cells"),
    )
    return jax.shard_map(
        on_device,
        mesh=mesh,
        in_specs=placed,
        out_specs=P(("groups", "cells", "slots", "mp"), None, None),
        check_vma=False,
    )
```

```python
import functools

import jax
import jax.numpy as jnp
from jax import lax
from jax.experimental import pallas as pl
from jax.experimental.pallas import tpu as pltpu
from jax.sharding import PartitionSpec as P

HD = 64
TSTEPS = 8
CB = 128
EPS = 1e-06

CODE = 32
UNIT = 512
LANES = 128
MIB = 1024 * 1024
F32 = jnp.float32
BF16 = jnp.bfloat16
WHOLE = pl.BlockSpec(memory_space=pltpu.VMEM)
SCALARS = pl.BlockSpec(memory_space=pltpu.SMEM)


def iota(shape, axis):
    return lax.broadcasted_iota(jnp.int32, shape, axis)


def dot(left, right):
    return jnp.dot(left, right, preferred_element_type=F32)


def dot_t(left, right):
    return lax.dot_general(left, right, (((1,), (1,)), ((), ())), preferred_element_type=F32)


def params(mib):
    return pltpu.CompilerParams(vmem_limit_bytes=mib * MIB)


def place_kernel(capacity, owner_ref, position_ref, feat_ref, out_ref, code_ref):
    n_owners, rows = out_ref.shape[0], feat_ref.shape[0]
    owner = owner_ref[...]
    owner_hot = (iota((n_owners, rows), 0) == owner).astype(F32)
    upper = (iota((rows, rows), 0) <= iota((rows, rows), 1)).astype(BF16)
    running = dot(owner_hot.astype(BF16), upper)
    rank = jnp.sum(running * owner_hot, axis=0, keepdims=True).astype(jnp.int32) - 1
    code = position_ref[...] + 1
    line = iota((8, rows), 0)
    digits = jnp.where(line == 0, code // CODE, jnp.where(line == 1, code % CODE, 0))
    digits = digits.astype(F32).astype(BF16)
    feat = feat_ref[...]
    for block in range(n_owners):
        place = jnp.where(owner == block, rank, -1)
        taken = (iota((capacity, rows), 0) == place).astype(F32).astype(BF16)
        out_ref[block] = dot(taken, feat).astype(BF16)
        sent = dot_t(digits, taken)
        code_ref[block] = (sent[0:1] * CODE + sent[1:2]).astype(jnp.int32) - 1


def place_rows(owner, position, obs_feat, n_owners, capacity):
    rows, width = obs_feat.shape
    return pl.pallas_call(
        functools.partial(place_kernel, capacity),
        out_shape=[
            jax.ShapeDtypeStruct((n_owners, capacity, width), BF16),
            jax.ShapeDtypeStruct((n_owners, 1, capacity), jnp.int32),
        ],
        in_specs=[WHOLE] * 3,
        out_specs=[WHOLE] * 2,
        compiler_params=params(24),
        cost_estimate=pl.CostEstimate(
            flops=2 * rows * width * n_owners * capacity,
            bytes_accessed=2 * width * (rows + n_owners * capacity),
            transcendentals=0,
        ),
        name="place_rows",
    )(owner.reshape(1, rows), position.reshape(1, rows), obs_feat)


def pool_kernel(capacity, slot_dev, slot_ref, embed_ref, code_ref, got_ref, keep_ref, send_ref):
    half = keep_ref.shape[0]
    places = 2 * half
    mine = slot_ref[0]
    total = jnp.zeros((places, keep_ref.shape[1]), F32)
    seen = jnp.zeros((places, capacity), F32)
    for block in range(got_ref.shape[0]):
        code = code_ref[block]
        turned = jnp.where(code >= half, code - half, code + half)
        code = jnp.where((code >= 0) & (mine == 1), turned, code)
        hot = (iota((places, capacity), 0) == code).astype(F32)
        seen += hot
        total += dot(hot.astype(BF16), got_ref[block])
    count = jnp.sum(seen, axis=1, keepdims=True)
    steps = embed_ref.shape[0]
    step_hot = iota((places, steps), 1) == iota((places, steps), 0) % slot_dev + mine * slot_dev
    embed = dot(step_hot.astype(F32).astype(BF16), embed_ref[...])
    tokens = (total / jnp.maximum(count, 1.0) + embed).astype(BF16)
    keep_ref[...] = tokens[:half]
    send_ref[...] = tokens[half:]


def pool_rows(my_slot, time_embed, codes, got, capacity, slot_dev):
    width = time_embed.shape[1]
    half = jax.ShapeDtypeStruct((CB * slot_dev // 2, width), BF16)
    return pl.pallas_call(
        functools.partial(pool_kernel, capacity, slot_dev),
        out_shape=[half, half],
        in_specs=[SCALARS] + [WHOLE] * 3,
        out_specs=[WHOLE] * 2,
        compiler_params=params(24),
        cost_estimate=pl.CostEstimate(
            flops=2 * CB * slot_dev * got.size, bytes_accessed=2 * got.size, transcendentals=0
        ),
        name="pool_rows",
    )(my_slot, time_embed, codes, got)


def weave_kernel(slot_dev, slot_ref, order_ref, keep_ref, got_ref, out_ref):
    rows, width = out_ref.shape
    half = keep_ref.shape[0]
    mine = slot_ref[0]
    row, col = iota((rows, half), 0), iota((rows, half), 1)
    source = col == row // TSTEPS * slot_dev + row % slot_dev
    own = row % TSTEPS // slot_dev == mine
    from_keep = (source & own).astype(F32).astype(BF16)
    from_got = (source & jnp.logical_not(own)).astype(F32).astype(BF16)
    tokens = (dot(from_keep, keep_ref[...]) + dot(from_got, got_ref[...])).astype(BF16)
    move = (iota((width, width), 0) == order_ref[...]).astype(F32).astype(BF16)
    out_ref[...] = dot(tokens, move).astype(BF16)


def weave_steps(my_slot, order, keep, got, slot_dev):
    rows, width = 2 * keep.shape[0], keep.shape[1]
    return pl.pallas_call(
        functools.partial(weave_kernel, slot_dev),
        out_shape=jax.ShapeDtypeStruct((rows, width), BF16),
        in_specs=[SCALARS] + [WHOLE] * 3,
        out_specs=WHOLE,
        compiler_params=params(16),
        cost_estimate=pl.CostEstimate(
            flops=2 * rows * width * (rows + width), bytes_accessed=4 * rows * width, transcendentals=0
        ),
        name="weave_steps",
    )(my_slot, order.reshape(1, width), keep, got)


def attention(normed, weight, heads_width, ctx_ref):
    rows = normed.shape[0]
    group = LANES
    lane = iota((1, LANES), 1)
    first = iota((group, LANES), 1) < HD
    masks = [(lane < HD).astype(F32).astype(BF16), (lane >= HD).astype(F32).astype(BF16)]
    ones = (iota((LANES, LANES), 0) // HD == iota((LANES, LANES), 1) // HD).astype(F32)
    mean = (ones * (1.0 / HD)).astype(BF16)
    ones = ones.astype(BF16)
    same_cell = iota((2 * group, group), 0) % group // TSTEPS == iota((2 * group, group), 1) // TSTEPS
    same_cell = same_cell.astype(F32).astype(BF16)
    count = jnp.ones((group, LANES), BF16)
    projected = dot(normed, weight)
    begins = range(0, rows, group)
    for at in range(0, heads_width, LANES):
        query = projected[:, at : at + LANES]
        key = projected[:, heads_width + at : heads_width + at + LANES]
        value = projected[:, 2 * heads_width + at : 2 * heads_width + at + LANES].astype(BF16)
        query_bf, key_bf = query.astype(BF16), key.astype(BF16)
        query = (query * lax.rsqrt(dot(query_bf * query_bf, ones) + HD * EPS)).astype(BF16)
        key = (key * lax.rsqrt(dot(key_bf * key_bf, mean) + EPS)).astype(BF16)
        left, right = query * masks[0], query * masks[1]
        scores = [
            dot_t(jnp.concatenate([left[at : at + group], right[at : at + group]], axis=0), key[at : at + group])
            for at in begins
        ]
        expos = [jnp.exp(score).astype(BF16) * same_cell for score in scores]
        mixed = [
            dot(expo, jnp.concatenate([value[at : at + group], count], axis=1)) for at, expo in zip(begins, expos)
        ]
        for begin, both in zip(begins, mixed):
            top, low = both[:group], both[group:]
            over = jnp.where(first, top[:, :LANES], low[:, :LANES])
            under = jnp.where(first, top[:, LANES:], low[:, LANES:])
            ctx_ref[begin : begin + group, at : at + LANES] = (over / under).astype(BF16)


def gated(normed, gate_w, up_w, down_w):
    gate = dot(normed, gate_w)
    up = dot(normed, up_w)
    hidden = (gate * (0.5 * jnp.tanh(0.5 * gate) + 0.5) * up).astype(BF16)
    return dot_t(hidden, down_w)


def put_rows_kernel(firsts, *refs):
    pieces, (out_ref, sems) = refs[: len(firsts)], refs[-2:]
    copies = [
        pltpu.make_async_copy(piece, out_ref.at[pl.ds(first, piece.shape[0]), :], sems.at[number])
        for number, (first, piece) in enumerate(zip(firsts, pieces))
    ]
    for copy in copies:
        copy.start()
    for copy in copies:
        copy.wait()


def put_rows(pieces, rows, first, into=None):
    firsts = [first + sum(piece.shape[0] for piece in pieces[:number]) for number in range(len(pieces))]
    operands = pieces if into is None else pieces + [into]
    return pl.pallas_call(
        functools.partial(put_rows_kernel, firsts),
        out_shape=jax.ShapeDtypeStruct((rows, pieces[0].shape[1]), BF16),
        in_specs=[pl.BlockSpec(memory_space=pl.ANY)] * len(operands),
        out_specs=pl.BlockSpec(memory_space=pl.ANY),
        scratch_shapes=[pltpu.SemaphoreType.DMA((len(pieces),))],
        input_output_aliases={} if into is None else {len(pieces): 0},
        compiler_params=params(2),
        cost_estimate=pl.CostEstimate(
            flops=0, bytes_accessed=4 * sum(piece.size for piece in pieces), transcendentals=0
        ),
        name="put_rows",
    )(*operands)


def layer_kernel(hidden_width, tok_ref, w_ref, out_ref, norm_ref, ctx_ref, acc_ref):
    heads_width = ctx_ref.shape[1]
    gate_at = 3 * heads_width
    up_at = gate_at + hidden_width
    out_at = up_at + hidden_width
    down_at = out_at + heads_width
    tokens = tok_ref[...].astype(F32)
    scale = lax.rsqrt(jnp.mean(tokens * tokens, axis=1, keepdims=True) + EPS)
    norm_ref[...] = (tokens * scale).astype(BF16)
    attention(norm_ref[...], w_ref[:, :gate_at], heads_width, ctx_ref)
    acc_ref[...] = dot_t(ctx_ref[...], w_ref[:, out_at:down_at])
    for begin in range(0, hidden_width, UNIT):
        gate_w, up_w, down_w = [w_ref[:, at + begin : at + begin + UNIT] for at in (gate_at, up_at, down_at)]
        add = gated(norm_ref[...], gate_w, up_w, down_w)
        if begin + UNIT < hidden_width:
            acc_ref[...] += add
        else:
            out_ref[...] = (acc_ref[...] + add).astype(out_ref.dtype)


def layer(tokens, weights, heads_width, hidden_width, out_type):
    rows, width = tokens.shape
    return pl.pallas_call(
        functools.partial(layer_kernel, hidden_width),
        out_shape=jax.ShapeDtypeStruct((rows, width), out_type),
        in_specs=[WHOLE] * 2,
        out_specs=WHOLE,
        scratch_shapes=[
            pltpu.VMEM((rows, width), BF16),
            pltpu.VMEM((rows, heads_width), BF16),
            pltpu.VMEM((rows, width), F32),
        ],
        compiler_params=params(36),
        cost_estimate=pl.CostEstimate(
            flops=2 * rows * width * weights.shape[1],
            bytes_accessed=2 * weights.size + 6 * rows * width,
            transcendentals=rows * hidden_width,
        ),
        name="layer",
    )(tokens, weights)


def finish_kernel(tok_ref, sum_ref, got_ref, order_ref, out_ref):
    width = out_ref.shape[1]
    mixed = (tok_ref[...].astype(F32) + sum_ref[...] + got_ref[...].astype(F32)).astype(BF16)
    move = (iota((width, width), 0) == order_ref[...]).astype(F32).astype(BF16)
    out_ref[...] = dot_t(mixed, move).astype(BF16)


def finish(tokens, sums, got, order):
    rows, width = tokens.shape
    return pl.pallas_call(
        finish_kernel,
        out_shape=jax.ShapeDtypeStruct((rows, width), BF16),
        in_specs=[WHOLE] * 4,
        out_specs=WHOLE,
        compiler_params=params(16),
        cost_estimate=pl.CostEstimate(
            flops=2 * rows * width * width, bytes_accessed=10 * rows * width, transcendentals=0
        ),
        name="finish",
    )(tokens, sums, got, order.reshape(1, width))


def side_by_side(w_qkv, w_out, w_gate_up, w_down):
    rows = w_qkv.shape[0]
    return jnp.concatenate([w_qkv.reshape(rows, -1), w_gate_up.reshape(rows, -1), w_out, w_down], axis=1)


def along_cells(values, distance):
    n_cells = lax.axis_size("cells")
    return lax.ppermute(values, "cells", [(j, (j - distance) % n_cells) for j in range(n_cells)])


def to_other_places(shares):
    n_slots = lax.axis_size("slots")
    n_share = lax.axis_size("groups") * n_slots
    places = [shares]
    for far in range(1, n_share):
        pairs = [(place, place ^ far) for place in range(n_share)]
        places.append(lax.ppermute(shares, ("groups", "slots"), pairs))
    return places


def arrival_order(width, n_share):
    n_cells = lax.axis_size("cells")
    mine = lax.axis_index("cells")
    place = lax.axis_index("groups") * lax.axis_size("slots") + lax.axis_index("slots")
    rows = width // n_cells
    share = rows // n_share
    row = jnp.arange(width, dtype=jnp.int32)
    past = row - 2 * rows
    far = jnp.where(past < 0, row // share % n_share, past // (2 * share))
    distance = jnp.where(past < 0, n_cells - 1, 1 + past // share % 2)
    other = (mine + distance) % n_cells * rows + (far ^ place) * share + row % share
    return jnp.where(row < rows, mine * rows + row, other)


def tokens_by_exchanges(owner, position, obs_feat, time_embed, my_slot, capacity, slot_dev):
    n_slots = lax.axis_size("slots")
    n_owners = lax.axis_size("cells") * lax.axis_size("mp")
    rows, width = obs_feat.shape
    owners = jnp.arange(n_owners, dtype=jnp.int32)
    owner_hot = (owner[:, None] == owners[None, :]).astype(F32)
    row_ids = jnp.arange(rows, dtype=jnp.int32)
    lower = (row_ids[None, :] <= row_ids[:, None]).astype(BF16)
    running = dot(lower, owner_hot.astype(BF16))
    rank = jnp.sum(running * owner_hot, axis=1).astype(jnp.int32) - 1
    place = jnp.where(owner < n_owners, owner * capacity + rank, n_owners * capacity)
    place_ids = jnp.arange(n_owners * capacity, dtype=jnp.int32)
    taken = place_ids[:, None] == place[None, :]
    send_feat = dot(taken.astype(BF16), obs_feat).astype(BF16).reshape(n_owners, capacity, width)
    send_code = jnp.sum(jnp.where(taken, position[None, :] + 1, 0), axis=1).reshape(n_owners, capacity)
    axes = ("cells", "mp")
    got_feat = lax.all_to_all(send_feat, axes, split_axis=0, concat_axis=0, tiled=True).reshape(-1, width)
    got_code = lax.all_to_all(send_code, axes, split_axis=0, concat_axis=0, tiled=True).reshape(-1) - 1
    hot = (jnp.arange(CB * slot_dev, dtype=jnp.int32)[:, None] == got_code[None, :]).astype(BF16)
    count = jnp.sum(hot.astype(F32), axis=1)
    pooled = dot(hot, got_feat) / jnp.maximum(count, 1.0)[:, None]
    embed = lax.dynamic_slice_in_dim(time_embed, my_slot * slot_dev, slot_dev, 0).astype(F32)
    tokens = (pooled.reshape(CB, slot_dev, width) + embed[None]).astype(BF16)
    grid = tokens.reshape(n_slots, CB // n_slots, slot_dev, width)
    grid = lax.all_to_all(grid, "slots", split_axis=0, concat_axis=2, tiled=True)
    return grid.reshape(-1, width)


def on_device(obs_feat, obs_cell, obs_slot, obs_count, time_embed, w_qkv, w_out, w_gate_up, w_down):
    n_cells = lax.axis_size("cells")
    n_slots = lax.axis_size("slots")
    n_groups = lax.axis_size("groups")
    n_mp = lax.axis_size("mp")
    n_owners = n_cells * n_mp
    rows, width = obs_feat.shape
    capacity = 3 * rows // n_owners
    quarter = CB // n_slots
    slot_dev = TSTEPS // n_slots
    my_slot = lax.axis_index("slots")
    n_share = n_groups * n_slots
    share = w_qkv.shape[0] // n_share
    valid = jnp.arange(rows, dtype=jnp.int32) < obs_count[0]
    owner = obs_cell // (quarter * n_mp * n_slots) * n_mp + obs_cell // quarter % n_mp
    owner = jnp.where(valid, owner, n_owners)
    local = obs_cell // (quarter * n_mp) % n_slots * quarter + obs_cell % quarter
    position = local * slot_dev + obs_slot

    local_weights = (w_qkv, w_out.T, w_gate_up, w_down.T)
    which = lax.axis_index("groups") * n_slots + my_slot
    share_weights = [lax.dynamic_slice_in_dim(w, which * share, share, 0) for w in local_weights]
    share_rows = side_by_side(*share_weights)
    if n_slots == 2 and n_groups == 2 and n_cells == 4 and share % 16 == 0 and capacity % 16 == 0:
        order = arrival_order(width, n_share)
        below = along_cells(share_rows, -1)
        blocks, codes = place_rows(owner, position, obs_feat, n_owners, capacity)
        codes = lax.all_to_all(codes, ("cells", "mp"), split_axis=0, concat_axis=0, tiled=True)
        below, codes, share_rows = lax.optimization_barrier((below, codes, share_rows))
        first = to_other_places(below)
        above, opposite = along_cells(share_rows, 1), along_cells(below, -1)
        blocks, above, opposite, first = lax.optimization_barrier((blocks, above, opposite, first))
        second = to_other_places(jnp.concatenate([above, opposite], axis=0))
        weights = put_rows([side_by_side(*local_weights)] + first, width, 0)
        got = lax.all_to_all(blocks, ("cells", "mp"), split_axis=0, concat_axis=0, tiled=True)
        got, weights = lax.optimization_barrier((got, weights))
        keep, send = pool_rows(my_slot.reshape(1), time_embed, codes, got, capacity, slot_dev)
        send, second = lax.optimization_barrier((send, second))
        other = lax.ppermute(send, "slots", [(0, 1), (1, 0)])
        weights = put_rows(second, width, width // 2, weights)
        other, weights = lax.optimization_barrier((other, weights))
        tokens = weave_steps(my_slot.reshape(1), order, keep, other, slot_dev)
    else:
        order = jnp.arange(width, dtype=jnp.int32)
        weights = lax.all_gather(share_rows, ("cells", "groups", "slots"), axis=0, tiled=True)
        tokens = tokens_by_exchanges(owner, position, obs_feat, time_embed, my_slot, capacity, slot_dev)

    swap = [(0, 1), (1, 0)]
    heads_width, hidden_width = w_qkv.shape[2], w_gate_up.shape[2]
    partner = lax.ppermute(tokens, "mp", swap)
    for_partner = layer(partner, weights, heads_width, hidden_width, BF16)
    from_partner = lax.ppermute(for_partner, "mp", swap)
    own = layer(tokens, weights, heads_width, hidden_width, F32)
    return finish(tokens, own, from_partner, order).reshape(quarter, TSTEPS, width)


def solution(mesh):
    placed = (
        P(("groups", "cells", "slots", "mp"), None),
        P(("groups", "cells", "slots", "mp")),
        P(("groups", "cells", "slots", "mp")),
        P(("groups", "cells", "slots", "mp")),
        P(),
        P("cells", None, "mp"),
        P("mp", "cells"),
        P("cells", None, "mp"),
        P("mp", "cells"),
    )
    return jax.shard_map(
        on_device,
        mesh=mesh,
        in_specs=placed,
        out_specs=P(("groups", "cells", "slots", "mp"), None, None),
        check_vma=False,
    )
```

```python
import functools

import jax
import jax.numpy as jnp
from jax import lax
from jax.experimental import pallas as pl
from jax.experimental.pallas import tpu as pltpu
from jax.sharding import PartitionSpec as P

HD = 64
TSTEPS = 8
CB = 128
EPS = 1e-06

CODE = 32
UNIT = 512
LANES = 128
MIB = 1024 * 1024
F32 = jnp.float32
BF16 = jnp.bfloat16
WHOLE = pl.BlockSpec(memory_space=pltpu.VMEM)
SCALARS = pl.BlockSpec(memory_space=pltpu.SMEM)


def iota(shape, axis):
    return lax.broadcasted_iota(jnp.int32, shape, axis)


def dot(left, right):
    return jnp.dot(left, right, preferred_element_type=F32)


def dot_t(left, right):
    return lax.dot_general(left, right, (((1,), (1,)), ((), ())), preferred_element_type=F32)


def params(mib):
    return pltpu.CompilerParams(vmem_limit_bytes=mib * MIB)


def block_places(owner, n_owners):
    rows = owner.shape[1]
    owner_hot = (iota((n_owners, rows), 0) == owner).astype(F32)
    upper = (iota((rows, rows), 0) <= iota((rows, rows), 1)).astype(BF16)
    running = dot(owner_hot.astype(BF16), upper)
    return jnp.sum(running * owner_hot, axis=0, keepdims=True).astype(jnp.int32) - 1


def one_hot_rows(owner, rank, block, capacity):
    place = jnp.where(owner == block, rank, -1)
    return (iota((capacity, owner.shape[1]), 0) == place).astype(F32).astype(BF16)


def code_kernel(owner_ref, position_ref, time_ref, code_ref, embed_ref):
    n_owners, _, capacity = code_ref.shape
    embed_ref[...] = time_ref[...]
    owner = owner_ref[...]
    rank = block_places(owner, n_owners)
    code = position_ref[...] + 1
    line = iota((8, owner.shape[1]), 0)
    digits = jnp.where(line == 0, code // CODE, jnp.where(line == 1, code % CODE, 0))
    digits = digits.astype(F32).astype(BF16)
    for block in range(n_owners):
        sent = dot_t(digits, one_hot_rows(owner, rank, block, capacity))
        code_ref[block] = (sent[0:1] * CODE + sent[1:2]).astype(jnp.int32) - 1


def place_codes(owner, position, time_embed, n_owners, capacity):
    rows = owner.shape[0]
    return pl.pallas_call(
        code_kernel,
        out_shape=[
            jax.ShapeDtypeStruct((n_owners, 1, capacity), jnp.int32),
            jax.ShapeDtypeStruct(time_embed.shape, BF16),
        ],
        in_specs=[WHOLE] * 3,
        out_specs=[WHOLE] * 2,
        compiler_params=params(6),
        cost_estimate=pl.CostEstimate(
            flops=16 * rows * n_owners * capacity, bytes_accessed=8 * rows, transcendentals=0
        ),
        name="place_codes",
    )(owner.reshape(1, rows), position.reshape(1, rows), time_embed)


def place_kernel(owner_ref, feat_ref, out_ref):
    n_owners, capacity, _ = out_ref.shape
    owner = owner_ref[...]
    rank = block_places(owner, n_owners)
    feat = feat_ref[...]
    for block in range(n_owners):
        out_ref[block] = dot(one_hot_rows(owner, rank, block, capacity), feat).astype(BF16)


def place_rows(owner, obs_feat, n_owners, capacity):
    rows, width = obs_feat.shape
    return pl.pallas_call(
        place_kernel,
        out_shape=jax.ShapeDtypeStruct((n_owners, capacity, width), BF16),
        in_specs=[WHOLE] * 2,
        out_specs=WHOLE,
        compiler_params=params(12),
        cost_estimate=pl.CostEstimate(
            flops=2 * rows * width * n_owners * capacity,
            bytes_accessed=2 * width * (rows + n_owners * capacity),
            transcendentals=0,
        ),
        name="place_rows",
    )(owner.reshape(1, rows), obs_feat)


def pool_kernel(capacity, slot_dev, slot_ref, embed_ref, code_ref, got_ref, keep_ref, send_ref):
    half = keep_ref.shape[0]
    places = 2 * half
    mine = slot_ref[0]
    total = jnp.zeros((places, keep_ref.shape[1]), F32)
    seen = jnp.zeros((places, capacity), F32)
    for block in range(got_ref.shape[0]):
        code = code_ref[block]
        turned = jnp.where(code >= half, code - half, code + half)
        code = jnp.where((code >= 0) & (mine == 1), turned, code)
        hot = (iota((places, capacity), 0) == code).astype(F32)
        seen += hot
        total += dot(hot.astype(BF16), got_ref[block])
    count = jnp.sum(seen, axis=1, keepdims=True)
    steps = embed_ref.shape[0]
    step_hot = iota((places, steps), 1) == iota((places, steps), 0) % slot_dev + mine * slot_dev
    embed = dot(step_hot.astype(F32).astype(BF16), embed_ref[...])
    tokens = (total / jnp.maximum(count, 1.0) + embed).astype(BF16)
    keep_ref[...] = tokens[:half]
    send_ref[...] = tokens[half:]


def pool_rows(my_slot, time_embed, codes, got, capacity, slot_dev):
    width = time_embed.shape[1]
    half = jax.ShapeDtypeStruct((CB * slot_dev // 2, width), BF16)
    return pl.pallas_call(
        functools.partial(pool_kernel, capacity, slot_dev),
        out_shape=[half, half],
        in_specs=[SCALARS] + [WHOLE] * 3,
        out_specs=[WHOLE] * 2,
        compiler_params=params(12),
        cost_estimate=pl.CostEstimate(
            flops=2 * CB * slot_dev * got.size, bytes_accessed=2 * got.size, transcendentals=0
        ),
        name="pool_rows",
    )(my_slot, time_embed, codes, got)


def weave_kernel(slot_dev, slot_ref, order_ref, keep_ref, got_ref, out_ref):
    rows, width = out_ref.shape
    half = keep_ref.shape[0]
    mine = slot_ref[0]
    row, col = iota((rows, half), 0), iota((rows, half), 1)
    source = col == row // TSTEPS * slot_dev + row % slot_dev
    own = row % TSTEPS // slot_dev == mine
    from_keep = (source & own).astype(F32).astype(BF16)
    from_got = (source & jnp.logical_not(own)).astype(F32).astype(BF16)
    tokens = (dot(from_keep, keep_ref[...]) + dot(from_got, got_ref[...])).astype(BF16)
    move = (iota((width, width), 0) == order_ref[...]).astype(F32).astype(BF16)
    out_ref[...] = dot(tokens, move).astype(BF16)


def weave_steps(my_slot, order, keep, got, slot_dev):
    rows, width = 2 * keep.shape[0], keep.shape[1]
    return pl.pallas_call(
        functools.partial(weave_kernel, slot_dev),
        out_shape=jax.ShapeDtypeStruct((rows, width), BF16),
        in_specs=[SCALARS] + [WHOLE] * 3,
        out_specs=WHOLE,
        compiler_params=params(10),
        cost_estimate=pl.CostEstimate(
            flops=2 * rows * width * (rows + width), bytes_accessed=4 * rows * width, transcendentals=0
        ),
        name="weave_steps",
    )(my_slot, order.reshape(1, width), keep, got)


def attention(normed, weight, heads_width, ctx_ref):
    rows = normed.shape[0]
    group = LANES
    lane = iota((1, LANES), 1)
    first = iota((group, LANES), 1) < HD
    masks = [(lane < HD).astype(F32).astype(BF16), (lane >= HD).astype(F32).astype(BF16)]
    ones = (iota((LANES, LANES), 0) // HD == iota((LANES, LANES), 1) // HD).astype(F32)
    mean = (ones * (1.0 / HD)).astype(BF16)
    ones = ones.astype(BF16)
    same_cell = iota((2 * group, group), 0) % group // TSTEPS == iota((2 * group, group), 1) // TSTEPS
    same_cell = same_cell.astype(F32).astype(BF16)
    count = jnp.ones((group, LANES), BF16)
    projected = dot(normed, weight)
    begins = range(0, rows, group)
    for at in range(0, heads_width, LANES):
        query = projected[:, at : at + LANES]
        key = projected[:, heads_width + at : heads_width + at + LANES]
        value = projected[:, 2 * heads_width + at : 2 * heads_width + at + LANES].astype(BF16)
        query_bf, key_bf = query.astype(BF16), key.astype(BF16)
        query = (query * lax.rsqrt(dot(query_bf * query_bf, ones) + HD * EPS)).astype(BF16)
        key = (key * lax.rsqrt(dot(key_bf * key_bf, mean) + EPS)).astype(BF16)
        left, right = query * masks[0], query * masks[1]
        scores = [
            dot_t(jnp.concatenate([left[at : at + group], right[at : at + group]], axis=0), key[at : at + group])
            for at in begins
        ]
        expos = [jnp.exp(score).astype(BF16) * same_cell for score in scores]
        mixed = [
            dot(expo, jnp.concatenate([value[at : at + group], count], axis=1)) for at, expo in zip(begins, expos)
        ]
        for begin, both in zip(begins, mixed):
            top, low = both[:group], both[group:]
            over = jnp.where(first, top[:, :LANES], low[:, :LANES])
            under = jnp.where(first, top[:, LANES:], low[:, LANES:])
            ctx_ref[begin : begin + group, at : at + LANES] = (over / under).astype(BF16)


def gated(normed, gate_w, up_w, down_w):
    gate = dot(normed, gate_w)
    up = dot(normed, up_w)
    hidden = (gate * (0.5 * jnp.tanh(0.5 * gate) + 0.5) * up).astype(BF16)
    return dot_t(hidden, down_w)


def put_rows_kernel(firsts, *refs):
    pieces, (out_ref, sems) = refs[: len(firsts)], refs[-2:]
    copies = [
        pltpu.make_async_copy(piece, out_ref.at[pl.ds(first, piece.shape[0]), :], sems.at[number])
        for number, (first, piece) in enumerate(zip(firsts, pieces))
    ]
    for copy in copies:
        copy.start()
    for copy in copies:
        copy.wait()


def put_rows(pieces, rows, first, into=None):
    firsts = [first + sum(piece.shape[0] for piece in pieces[:number]) for number in range(len(pieces))]
    operands = pieces if into is None else pieces + [into]
    return pl.pallas_call(
        functools.partial(put_rows_kernel, firsts),
        out_shape=jax.ShapeDtypeStruct((rows, pieces[0].shape[1]), BF16),
        in_specs=[pl.BlockSpec(memory_space=pl.ANY)] * len(operands),
        out_specs=pl.BlockSpec(memory_space=pl.ANY),
        scratch_shapes=[pltpu.SemaphoreType.DMA((len(pieces),))],
        input_output_aliases={} if into is None else {len(pieces): 0},
        compiler_params=params(2),
        cost_estimate=pl.CostEstimate(
            flops=0, bytes_accessed=4 * sum(piece.size for piece in pieces), transcendentals=0
        ),
        name="put_rows",
    )(*operands)


def layer_kernel(hidden_width, tok_ref, w_ref, out_ref, norm_ref, ctx_ref, acc_ref):
    heads_width = ctx_ref.shape[1]
    gate_at = 3 * heads_width
    up_at = gate_at + hidden_width
    out_at = up_at + hidden_width
    down_at = out_at + heads_width
    tokens = tok_ref[...].astype(F32)
    scale = lax.rsqrt(jnp.mean(tokens * tokens, axis=1, keepdims=True) + EPS)
    norm_ref[...] = (tokens * scale).astype(BF16)
    attention(norm_ref[...], w_ref[:, :gate_at], heads_width, ctx_ref)
    acc_ref[...] = dot_t(ctx_ref[...], w_ref[:, out_at:down_at])
    for begin in range(0, hidden_width, UNIT):
        gate_w, up_w, down_w = [w_ref[:, at + begin : at + begin + UNIT] for at in (gate_at, up_at, down_at)]
        add = gated(norm_ref[...], gate_w, up_w, down_w)
        if begin + UNIT < hidden_width:
            acc_ref[...] += add
        else:
            out_ref[...] = (acc_ref[...] + add).astype(out_ref.dtype)


def layer(tokens, weights, heads_width, hidden_width, out_type):
    rows, width = tokens.shape
    return pl.pallas_call(
        functools.partial(layer_kernel, hidden_width),
        out_shape=jax.ShapeDtypeStruct((rows, width), out_type),
        in_specs=[WHOLE] * 2,
        out_specs=WHOLE,
        scratch_shapes=[
            pltpu.VMEM((rows, width), BF16),
            pltpu.VMEM((rows, heads_width), BF16),
            pltpu.VMEM((rows, width), F32),
        ],
        compiler_params=params(26),
        cost_estimate=pl.CostEstimate(
            flops=2 * rows * width * weights.shape[1],
            bytes_accessed=2 * weights.size + 6 * rows * width,
            transcendentals=rows * hidden_width,
        ),
        name="layer",
    )(tokens, weights)


def finish_kernel(tok_ref, sum_ref, got_ref, order_ref, out_ref):
    width = out_ref.shape[1]
    mixed = (tok_ref[...].astype(F32) + sum_ref[...] + got_ref[...].astype(F32)).astype(BF16)
    move = (iota((width, width), 0) == order_ref[...]).astype(F32).astype(BF16)
    out_ref[...] = dot_t(mixed, move).astype(BF16)


def finish(tokens, sums, got, order):
    rows, width = tokens.shape
    return pl.pallas_call(
        finish_kernel,
        out_shape=jax.ShapeDtypeStruct((rows, width), BF16),
        in_specs=[WHOLE] * 4,
        out_specs=WHOLE,
        compiler_params=params(10),
        cost_estimate=pl.CostEstimate(
            flops=2 * rows * width * width, bytes_accessed=10 * rows * width, transcendentals=0
        ),
        name="finish",
    )(tokens, sums, got, order.reshape(1, width))


def side_by_side(w_qkv, w_out, w_gate_up, w_down):
    rows = w_qkv.shape[0]
    return jnp.concatenate([w_qkv.reshape(rows, -1), w_gate_up.reshape(rows, -1), w_out, w_down], axis=1)


def along_cells(values, distance):
    n_cells = lax.axis_size("cells")
    return lax.ppermute(values, "cells", [(j, (j - distance) % n_cells) for j in range(n_cells)])


def to_other_places(shares):
    n_slots = lax.axis_size("slots")
    n_share = lax.axis_size("groups") * n_slots
    places = [shares]
    for far in range(1, n_share):
        pairs = [(place, place ^ far) for place in range(n_share)]
        places.append(lax.ppermute(shares, ("groups", "slots"), pairs))
    return places


def arrival_order(width, n_share):
    n_cells = lax.axis_size("cells")
    mine = lax.axis_index("cells")
    place = lax.axis_index("groups") * lax.axis_size("slots") + lax.axis_index("slots")
    rows = width // n_cells
    share = rows // n_share
    row = jnp.arange(width, dtype=jnp.int32)
    past = row - 2 * rows
    far = jnp.where(past < 0, row // share % n_share, past // (2 * share))
    distance = jnp.where(past < 0, n_cells - 1, 1 + past // share % 2)
    other = (mine + distance) % n_cells * rows + (far ^ place) * share + row % share
    return jnp.where(row < rows, mine * rows + row, other)


def tokens_by_exchanges(owner, position, obs_feat, time_embed, my_slot, capacity, slot_dev):
    n_slots = lax.axis_size("slots")
    n_owners = lax.axis_size("cells") * lax.axis_size("mp")
    rows, width = obs_feat.shape
    owners = jnp.arange(n_owners, dtype=jnp.int32)
    owner_hot = (owner[:, None] == owners[None, :]).astype(F32)
    row_ids = jnp.arange(rows, dtype=jnp.int32)
    lower = (row_ids[None, :] <= row_ids[:, None]).astype(BF16)
    running = dot(lower, owner_hot.astype(BF16))
    rank = jnp.sum(running * owner_hot, axis=1).astype(jnp.int32) - 1
    place = jnp.where(owner < n_owners, owner * capacity + rank, n_owners * capacity)
    place_ids = jnp.arange(n_owners * capacity, dtype=jnp.int32)
    taken = place_ids[:, None] == place[None, :]
    send_feat = dot(taken.astype(BF16), obs_feat).astype(BF16).reshape(n_owners, capacity, width)
    send_code = jnp.sum(jnp.where(taken, position[None, :] + 1, 0), axis=1).reshape(n_owners, capacity)
    axes = ("cells", "mp")
    got_feat = lax.all_to_all(send_feat, axes, split_axis=0, concat_axis=0, tiled=True).reshape(-1, width)
    got_code = lax.all_to_all(send_code, axes, split_axis=0, concat_axis=0, tiled=True).reshape(-1) - 1
    hot = (jnp.arange(CB * slot_dev, dtype=jnp.int32)[:, None] == got_code[None, :]).astype(BF16)
    count = jnp.sum(hot.astype(F32), axis=1)
    pooled = dot(hot, got_feat) / jnp.maximum(count, 1.0)[:, None]
    embed = lax.dynamic_slice_in_dim(time_embed, my_slot * slot_dev, slot_dev, 0).astype(F32)
    tokens = (pooled.reshape(CB, slot_dev, width) + embed[None]).astype(BF16)
    grid = tokens.reshape(n_slots, CB // n_slots, slot_dev, width)
    grid = lax.all_to_all(grid, "slots", split_axis=0, concat_axis=2, tiled=True)
    return grid.reshape(-1, width)


def on_device(obs_feat, obs_cell, obs_slot, obs_count, time_embed, w_qkv, w_out, w_gate_up, w_down):
    n_cells = lax.axis_size("cells")
    n_slots = lax.axis_size("slots")
    n_groups = lax.axis_size("groups")
    n_mp = lax.axis_size("mp")
    n_owners = n_cells * n_mp
    rows, width = obs_feat.shape
    capacity = 3 * rows // n_owners
    quarter = CB // n_slots
    slot_dev = TSTEPS // n_slots
    my_slot = lax.axis_index("slots")
    n_share = n_groups * n_slots
    share = w_qkv.shape[0] // n_share
    valid = jnp.arange(rows, dtype=jnp.int32) < obs_count[0]
    owner = obs_cell // (quarter * n_mp * n_slots) * n_mp + obs_cell // quarter % n_mp
    owner = jnp.where(valid, owner, n_owners)
    local = obs_cell // (quarter * n_mp) % n_slots * quarter + obs_cell % quarter
    position = local * slot_dev + obs_slot

    local_weights = (w_qkv, w_out.T, w_gate_up, w_down.T)
    which = lax.axis_index("groups") * n_slots + my_slot
    share_weights = [lax.dynamic_slice_in_dim(w, which * share, share, 0) for w in local_weights]
    share_rows = side_by_side(*share_weights)
    if n_slots == 2 and n_groups == 2 and n_cells == 4 and share % 16 == 0 and capacity % 16 == 0:
        order = arrival_order(width, n_share)
        below = along_cells(share_rows, -1)
        codes, embed = place_codes(owner, position, time_embed, n_owners, capacity)
        codes = lax.all_to_all(codes, ("cells", "mp"), split_axis=0, concat_axis=0, tiled=True)
        below, codes, share_rows = lax.optimization_barrier((below, codes, share_rows))
        first = to_other_places(below)
        blocks = place_rows(owner, obs_feat, n_owners, capacity)
        above, opposite = along_cells(share_rows, 1), along_cells(below, -1)
        blocks, above, opposite, first = lax.optimization_barrier((blocks, above, opposite, first))
        second = to_other_places(jnp.concatenate([above, opposite], axis=0))
        weights = put_rows([side_by_side(*local_weights)] + first, width, 0)
        got = lax.all_to_all(blocks, ("cells", "mp"), split_axis=0, concat_axis=0, tiled=True)
        got, weights = lax.optimization_barrier((got, weights))
        keep, send = pool_rows(my_slot.reshape(1), embed, codes, got, capacity, slot_dev)
        send, second = lax.optimization_barrier((send, second))
        other = lax.ppermute(send, "slots", [(0, 1), (1, 0)])
        weights = put_rows(second, width, width // 2, weights)
        other, weights = lax.optimization_barrier((other, weights))
        tokens = weave_steps(my_slot.reshape(1), order, keep, other, slot_dev)
    else:
        order = jnp.arange(width, dtype=jnp.int32)
        weights = lax.all_gather(share_rows, ("cells", "groups", "slots"), axis=0, tiled=True)
        tokens = tokens_by_exchanges(owner, position, obs_feat, time_embed, my_slot, capacity, slot_dev)

    swap = [(0, 1), (1, 0)]
    heads_width, hidden_width = w_qkv.shape[2], w_gate_up.shape[2]
    partner = lax.ppermute(tokens, "mp", swap)
    for_partner = layer(partner, weights, heads_width, hidden_width, BF16)
    from_partner = lax.ppermute(for_partner, "mp", swap)
    own = layer(tokens, weights, heads_width, hidden_width, F32)
    return finish(tokens, own, from_partner, order).reshape(quarter, TSTEPS, width)


def solution(mesh):
    placed = (
        P(("groups", "cells", "slots", "mp"), None),
        P(("groups", "cells", "slots", "mp")),
        P(("groups", "cells", "slots", "mp")),
        P(("groups", "cells", "slots", "mp")),
        P(),
        P("cells", None, "mp"),
        P("mp", "cells"),
        P("cells", None, "mp"),
        P("mp", "cells"),
    )
    return jax.shard_map(
        on_device,
        mesh=mesh,
        in_specs=placed,
        out_specs=P(("groups", "cells", "slots", "mp"), None, None),
        check_vma=False,
    )
```

```python
import functools

import jax
import jax.numpy as jnp
from jax import lax
from jax.experimental import pallas as pl
from jax.experimental.pallas import tpu as pltpu
from jax.sharding import PartitionSpec as P

HD = 64
TSTEPS = 8
CB = 128
EPS = 1e-06

CODE = 32
UNIT = 512
LANES = 128
MIB = 1024 * 1024
F32 = jnp.float32
BF16 = jnp.bfloat16
WHOLE = pl.BlockSpec(memory_space=pltpu.VMEM)
SCALARS = pl.BlockSpec(memory_space=pltpu.SMEM)


def iota(shape, axis):
    return lax.broadcasted_iota(jnp.int32, shape, axis)


def dot(left, right):
    return jnp.dot(left, right, preferred_element_type=F32)


def dot_t(left, right):
    return lax.dot_general(left, right, (((1,), (1,)), ((), ())), preferred_element_type=F32)


def params(mib):
    return pltpu.CompilerParams(vmem_limit_bytes=mib * MIB)


def block_places(owner, n_owners):
    rows = owner.shape[1]
    owner_hot = (iota((n_owners, rows), 0) == owner).astype(F32)
    upper = (iota((rows, rows), 0) <= iota((rows, rows), 1)).astype(BF16)
    running = dot(owner_hot.astype(BF16), upper)
    return jnp.sum(running * owner_hot, axis=0, keepdims=True).astype(jnp.int32) - 1


def one_hot_rows(owner, rank, block, capacity):
    place = jnp.where(owner == block, rank, -1)
    return (iota((capacity, owner.shape[1]), 0) == place).astype(F32).astype(BF16)


def code_kernel(owner_ref, position_ref, time_ref, code_ref, embed_ref):
    n_owners, _, capacity = code_ref.shape
    embed_ref[...] = time_ref[...]
    owner = owner_ref[...]
    rank = block_places(owner, n_owners)
    code = position_ref[...] + 1
    line = iota((8, owner.shape[1]), 0)
    digits = jnp.where(line == 0, code // CODE, jnp.where(line == 1, code % CODE, 0))
    digits = digits.astype(F32).astype(BF16)
    for block in range(n_owners):
        sent = dot_t(digits, one_hot_rows(owner, rank, block, capacity))
        code_ref[block] = (sent[0:1] * CODE + sent[1:2]).astype(jnp.int32) - 1


def place_codes(owner, position, time_embed, n_owners, capacity):
    rows = owner.shape[0]
    return pl.pallas_call(
        code_kernel,
        out_shape=[
            jax.ShapeDtypeStruct((n_owners, 1, capacity), jnp.int32),
            jax.ShapeDtypeStruct(time_embed.shape, BF16),
        ],
        in_specs=[WHOLE] * 3,
        out_specs=[WHOLE] * 2,
        compiler_params=params(6),
        cost_estimate=pl.CostEstimate(
            flops=16 * rows * n_owners * capacity, bytes_accessed=8 * rows, transcendentals=0
        ),
        name="place_codes",
    )(owner.reshape(1, rows), position.reshape(1, rows), time_embed)


def place_kernel(owner_ref, feat_ref, out_ref):
    n_owners, capacity, _ = out_ref.shape
    owner = owner_ref[...]
    rank = block_places(owner, n_owners)
    feat = feat_ref[...]
    for block in range(n_owners):
        out_ref[block] = dot(one_hot_rows(owner, rank, block, capacity), feat).astype(BF16)


def place_rows(owner, obs_feat, n_owners, capacity):
    rows, width = obs_feat.shape
    return pl.pallas_call(
        place_kernel,
        out_shape=jax.ShapeDtypeStruct((n_owners, capacity, width), BF16),
        in_specs=[WHOLE] * 2,
        out_specs=WHOLE,
        compiler_params=params(12),
        cost_estimate=pl.CostEstimate(
            flops=2 * rows * width * n_owners * capacity,
            bytes_accessed=2 * width * (rows + n_owners * capacity),
            transcendentals=0,
        ),
        name="place_rows",
    )(owner.reshape(1, rows), obs_feat)


def pool_kernel(capacity, slot_dev, slot_ref, embed_ref, code_ref, got_ref, keep_ref, send_ref):
    half = keep_ref.shape[0]
    places = 2 * half
    mine = slot_ref[0]
    total = jnp.zeros((places, keep_ref.shape[1]), F32)
    seen = jnp.zeros((places, capacity), F32)
    for block in range(got_ref.shape[0]):
        code = code_ref[block]
        turned = jnp.where(code >= half, code - half, code + half)
        code = jnp.where((code >= 0) & (mine == 1), turned, code)
        hot = (iota((places, capacity), 0) == code).astype(F32)
        seen += hot
        total += dot(hot.astype(BF16), got_ref[block])
    count = jnp.sum(seen, axis=1, keepdims=True)
    steps = embed_ref.shape[0]
    step_hot = iota((places, steps), 1) == iota((places, steps), 0) % slot_dev + mine * slot_dev
    embed = dot(step_hot.astype(F32).astype(BF16), embed_ref[...])
    tokens = (total / jnp.maximum(count, 1.0) + embed).astype(BF16)
    keep_ref[...] = tokens[:half]
    send_ref[...] = tokens[half:]


def pool_rows(my_slot, time_embed, codes, got, capacity, slot_dev):
    width = time_embed.shape[1]
    half = jax.ShapeDtypeStruct((CB * slot_dev // 2, width), BF16)
    return pl.pallas_call(
        functools.partial(pool_kernel, capacity, slot_dev),
        out_shape=[half, half],
        in_specs=[SCALARS] + [WHOLE] * 3,
        out_specs=[WHOLE] * 2,
        compiler_params=params(12),
        cost_estimate=pl.CostEstimate(
            flops=2 * CB * slot_dev * got.size, bytes_accessed=2 * got.size, transcendentals=0
        ),
        name="pool_rows",
    )(my_slot, time_embed, codes, got)


def weave_kernel(slot_dev, slot_ref, order_ref, keep_ref, got_ref, out_ref):
    rows, width = out_ref.shape
    half = keep_ref.shape[0]
    mine = slot_ref[0]
    row, col = iota((rows, half), 0), iota((rows, half), 1)
    source = col == row // TSTEPS * slot_dev + row % slot_dev
    own = row % TSTEPS // slot_dev == mine
    from_keep = (source & own).astype(F32).astype(BF16)
    from_got = (source & jnp.logical_not(own)).astype(F32).astype(BF16)
    tokens = (dot(from_keep, keep_ref[...]) + dot(from_got, got_ref[...])).astype(BF16)
    move = (iota((width, width), 0) == order_ref[...]).astype(F32).astype(BF16)
    out_ref[...] = dot(tokens, move).astype(BF16)


def weave_steps(my_slot, order, keep, got, slot_dev):
    rows, width = 2 * keep.shape[0], keep.shape[1]
    return pl.pallas_call(
        functools.partial(weave_kernel, slot_dev),
        out_shape=jax.ShapeDtypeStruct((rows, width), BF16),
        in_specs=[SCALARS] + [WHOLE] * 3,
        out_specs=WHOLE,
        compiler_params=params(10),
        cost_estimate=pl.CostEstimate(
            flops=2 * rows * width * (rows + width), bytes_accessed=4 * rows * width, transcendentals=0
        ),
        name="weave_steps",
    )(my_slot, order.reshape(1, width), keep, got)


def attention(normed, weight, heads_width, ctx_ref):
    rows = normed.shape[0]
    group = LANES
    lane = iota((1, LANES), 1)
    first = iota((group, LANES), 1) < HD
    masks = [(lane < HD).astype(F32).astype(BF16), (lane >= HD).astype(F32).astype(BF16)]
    ones = (iota((LANES, LANES), 0) // HD == iota((LANES, LANES), 1) // HD).astype(F32)
    mean = (ones * (1.0 / HD)).astype(BF16)
    ones = ones.astype(BF16)
    same_cell = iota((2 * group, group), 0) % group // TSTEPS == iota((2 * group, group), 1) // TSTEPS
    same_cell = same_cell.astype(F32).astype(BF16)
    count = jnp.ones((group, LANES), BF16)
    projected = dot(normed, weight)
    begins = range(0, rows, group)
    for at in range(0, heads_width, LANES):
        query = projected[:, at : at + LANES]
        key = projected[:, heads_width + at : heads_width + at + LANES]
        value = projected[:, 2 * heads_width + at : 2 * heads_width + at + LANES].astype(BF16)
        query_bf, key_bf = query.astype(BF16), key.astype(BF16)
        query = (query * lax.rsqrt(dot(query_bf * query_bf, ones) + HD * EPS)).astype(BF16)
        key = (key * lax.rsqrt(dot(key_bf * key_bf, mean) + EPS)).astype(BF16)
        left, right = query * masks[0], query * masks[1]
        scores = [
            dot_t(jnp.concatenate([left[at : at + group], right[at : at + group]], axis=0), key[at : at + group])
            for at in begins
        ]
        expos = [jnp.exp(score).astype(BF16) * same_cell for score in scores]
        mixed = [
            dot(expo, jnp.concatenate([value[at : at + group], count], axis=1)) for at, expo in zip(begins, expos)
        ]
        for begin, both in zip(begins, mixed):
            top, low = both[:group], both[group:]
            over = jnp.where(first, top[:, :LANES], low[:, :LANES])
            under = jnp.where(first, top[:, LANES:], low[:, LANES:])
            ctx_ref[begin : begin + group, at : at + LANES] = (over / under).astype(BF16)


def gated(normed, gate_w, up_w, down_w):
    gate = dot(normed, gate_w)
    up = dot(normed, up_w)
    hidden = (gate * (0.5 * jnp.tanh(0.5 * gate) + 0.5) * up).astype(BF16)
    return dot_t(hidden, down_w)


def put_rows_kernel(firsts, *refs):
    pieces, (out_ref, sems) = refs[: len(firsts)], refs[-2:]
    copies = [
        pltpu.make_async_copy(piece, out_ref.at[pl.ds(first, piece.shape[0]), :], sems.at[number])
        for number, (first, piece) in enumerate(zip(firsts, pieces))
    ]
    for copy in copies:
        copy.start()
    for copy in copies:
        copy.wait()


def put_rows(pieces, rows, first, into=None):
    firsts = [first + sum(piece.shape[0] for piece in pieces[:number]) for number in range(len(pieces))]
    operands = pieces if into is None else pieces + [into]
    return pl.pallas_call(
        functools.partial(put_rows_kernel, firsts),
        out_shape=jax.ShapeDtypeStruct((rows, pieces[0].shape[1]), BF16),
        in_specs=[pl.BlockSpec(memory_space=pl.ANY)] * len(operands),
        out_specs=pl.BlockSpec(memory_space=pl.ANY),
        scratch_shapes=[pltpu.SemaphoreType.DMA((len(pieces),))],
        input_output_aliases={} if into is None else {len(pieces): 0},
        compiler_params=params(56),
        cost_estimate=pl.CostEstimate(
            flops=0, bytes_accessed=4 * sum(piece.size for piece in pieces), transcendentals=0
        ),
        name="put_rows",
    )(*operands)


def layer_kernel(sections, tok_ref, far_ref, out_ref, w_ref, norm_ref, ctx_ref, acc_ref, sems):
    copies = [
        pltpu.make_async_copy(far_ref.at[:, pl.ds(at, size)], w_ref.at[:, pl.ds(at, size)], sems.at[number])
        for number, (at, size) in enumerate(sections)
    ]
    for copy in copies:
        copy.start()

    def columns(number):
        copies[number].wait()
        at, size = sections[number]
        return w_ref[:, at : at + size]

    tokens = tok_ref[...].astype(F32)
    scale = lax.rsqrt(jnp.mean(tokens * tokens, axis=1, keepdims=True) + EPS)
    norm_ref[...] = (tokens * scale).astype(BF16)
    attention(norm_ref[...], columns(0), ctx_ref.shape[1], ctx_ref)
    acc_ref[...] = dot_t(ctx_ref[...], columns(1))
    for at in range(2, len(sections), 3):
        add = gated(norm_ref[...], columns(at), columns(at + 1), columns(at + 2))
        if at + 3 < len(sections):
            acc_ref[...] += add
        else:
            out_ref[...] = (acc_ref[...] + add).astype(out_ref.dtype)


def layer(tokens, weights, heads_width, hidden_width, out_type):
    rows, width = tokens.shape
    gate_at = 3 * heads_width
    up_at = gate_at + hidden_width
    out_at = up_at + hidden_width
    down_at = out_at + heads_width
    sections = [(0, gate_at), (out_at, heads_width)]
    for begin in range(0, hidden_width, UNIT):
        sections += [(at + begin, UNIT) for at in (gate_at, up_at, down_at)]
    return pl.pallas_call(
        functools.partial(layer_kernel, sections),
        out_shape=jax.ShapeDtypeStruct((rows, width), out_type),
        in_specs=[WHOLE, pl.BlockSpec(memory_space=pl.ANY)],
        out_specs=WHOLE,
        scratch_shapes=[
            pltpu.VMEM(weights.shape, BF16),
            pltpu.VMEM((rows, width), BF16),
            pltpu.VMEM((rows, heads_width), BF16),
            pltpu.VMEM((rows, width), F32),
            pltpu.SemaphoreType.DMA((len(sections),)),
        ],
        compiler_params=params(56),
        cost_estimate=pl.CostEstimate(
            flops=2 * rows * width * weights.shape[1],
            bytes_accessed=2 * weights.size + 6 * rows * width,
            transcendentals=rows * hidden_width,
        ),
        name="layer",
    )(tokens, weights)


def finish_kernel(tok_ref, sum_ref, got_ref, order_ref, out_ref):
    width = out_ref.shape[1]
    mixed = (tok_ref[...].astype(F32) + sum_ref[...] + got_ref[...].astype(F32)).astype(BF16)
    move = (iota((width, width), 0) == order_ref[...]).astype(F32).astype(BF16)
    out_ref[...] = dot_t(mixed, move).astype(BF16)


def finish(tokens, sums, got, order):
    rows, width = tokens.shape
    return pl.pallas_call(
        finish_kernel,
        out_shape=jax.ShapeDtypeStruct((rows, width), BF16),
        in_specs=[WHOLE] * 4,
        out_specs=WHOLE,
        compiler_params=params(10),
        cost_estimate=pl.CostEstimate(
            flops=2 * rows * width * width, bytes_accessed=10 * rows * width, transcendentals=0
        ),
        name="finish",
    )(tokens, sums, got, order.reshape(1, width))


def side_by_side(w_qkv, w_out, w_gate_up, w_down):
    rows = w_qkv.shape[0]
    return jnp.concatenate([w_qkv.reshape(rows, -1), w_gate_up.reshape(rows, -1), w_out, w_down], axis=1)


def along_cells(values, distance):
    n_cells = lax.axis_size("cells")
    return lax.ppermute(values, "cells", [(j, (j - distance) % n_cells) for j in range(n_cells)])


def to_other_places(shares):
    n_slots = lax.axis_size("slots")
    n_share = lax.axis_size("groups") * n_slots
    places = [shares]
    for far in range(1, n_share):
        pairs = [(place, place ^ far) for place in range(n_share)]
        places.append(lax.ppermute(shares, ("groups", "slots"), pairs))
    return places


def arrival_order(width, n_share):
    n_cells = lax.axis_size("cells")
    mine = lax.axis_index("cells")
    place = lax.axis_index("groups") * lax.axis_size("slots") + lax.axis_index("slots")
    rows = width // n_cells
    share = rows // n_share
    row = jnp.arange(width, dtype=jnp.int32)
    past = row - 2 * rows
    far = jnp.where(past < 0, row // share % n_share, past // (2 * share))
    distance = jnp.where(past < 0, n_cells - 1, 1 + past // share % 2)
    other = (mine + distance) % n_cells * rows + (far ^ place) * share + row % share
    return jnp.where(row < rows, mine * rows + row, other)


def tokens_by_exchanges(owner, position, obs_feat, time_embed, my_slot, capacity, slot_dev):
    n_slots = lax.axis_size("slots")
    n_owners = lax.axis_size("cells") * lax.axis_size("mp")
    rows, width = obs_feat.shape
    owners = jnp.arange(n_owners, dtype=jnp.int32)
    owner_hot = (owner[:, None] == owners[None, :]).astype(F32)
    row_ids = jnp.arange(rows, dtype=jnp.int32)
    lower = (row_ids[None, :] <= row_ids[:, None]).astype(BF16)
    running = dot(lower, owner_hot.astype(BF16))
    rank = jnp.sum(running * owner_hot, axis=1).astype(jnp.int32) - 1
    place = jnp.where(owner < n_owners, owner * capacity + rank, n_owners * capacity)
    place_ids = jnp.arange(n_owners * capacity, dtype=jnp.int32)
    taken = place_ids[:, None] == place[None, :]
    send_feat = dot(taken.astype(BF16), obs_feat).astype(BF16).reshape(n_owners, capacity, width)
    send_code = jnp.sum(jnp.where(taken, position[None, :] + 1, 0), axis=1).reshape(n_owners, capacity)
    axes = ("cells", "mp")
    got_feat = lax.all_to_all(send_feat, axes, split_axis=0, concat_axis=0, tiled=True).reshape(-1, width)
    got_code = lax.all_to_all(send_code, axes, split_axis=0, concat_axis=0, tiled=True).reshape(-1) - 1
    hot = (jnp.arange(CB * slot_dev, dtype=jnp.int32)[:, None] == got_code[None, :]).astype(BF16)
    count = jnp.sum(hot.astype(F32), axis=1)
    pooled = dot(hot, got_feat) / jnp.maximum(count, 1.0)[:, None]
    embed = lax.dynamic_slice_in_dim(time_embed, my_slot * slot_dev, slot_dev, 0).astype(F32)
    tokens = (pooled.reshape(CB, slot_dev, width) + embed[None]).astype(BF16)
    grid = tokens.reshape(n_slots, CB // n_slots, slot_dev, width)
    grid = lax.all_to_all(grid, "slots", split_axis=0, concat_axis=2, tiled=True)
    return grid.reshape(-1, width)


def on_device(obs_feat, obs_cell, obs_slot, obs_count, time_embed, w_qkv, w_out, w_gate_up, w_down):
    n_cells = lax.axis_size("cells")
    n_slots = lax.axis_size("slots")
    n_groups = lax.axis_size("groups")
    n_mp = lax.axis_size("mp")
    n_owners = n_cells * n_mp
    rows, width = obs_feat.shape
    capacity = 3 * rows // n_owners
    quarter = CB // n_slots
    slot_dev = TSTEPS // n_slots
    my_slot = lax.axis_index("slots")
    n_share = n_groups * n_slots
    share = w_qkv.shape[0] // n_share
    valid = jnp.arange(rows, dtype=jnp.int32) < obs_count[0]
    owner = obs_cell // (quarter * n_mp * n_slots) * n_mp + obs_cell // quarter % n_mp
    owner = jnp.where(valid, owner, n_owners)
    local = obs_cell // (quarter * n_mp) % n_slots * quarter + obs_cell % quarter
    position = local * slot_dev + obs_slot

    local_weights = (w_qkv, w_out.T, w_gate_up, w_down.T)
    which = lax.axis_index("groups") * n_slots + my_slot
    share_weights = [lax.dynamic_slice_in_dim(w, which * share, share, 0) for w in local_weights]
    share_rows = side_by_side(*share_weights)
    if n_slots == 2 and n_groups == 2 and n_cells == 4 and share % 16 == 0 and capacity % 16 == 0:
        order = arrival_order(width, n_share)
        below = along_cells(share_rows, -1)
        codes, embed = place_codes(owner, position, time_embed, n_owners, capacity)
        codes = lax.all_to_all(codes, ("cells", "mp"), split_axis=0, concat_axis=0, tiled=True)
        below, codes, share_rows = lax.optimization_barrier((below, codes, share_rows))
        first = to_other_places(below)
        blocks = place_rows(owner, obs_feat, n_owners, capacity)
        above, opposite = along_cells(share_rows, 1), along_cells(below, -1)
        blocks, above, opposite, first = lax.optimization_barrier((blocks, above, opposite, first))
        second = to_other_places(jnp.concatenate([above, opposite], axis=0))
        weights = put_rows([side_by_side(*local_weights)] + first, width, 0)
        got = lax.all_to_all(blocks, ("cells", "mp"), split_axis=0, concat_axis=0, tiled=True)
        got, weights = lax.optimization_barrier((got, weights))
        keep, send = pool_rows(my_slot.reshape(1), embed, codes, got, capacity, slot_dev)
        send, second = lax.optimization_barrier((send, second))
        other = lax.ppermute(send, "slots", [(0, 1), (1, 0)])
        weights = put_rows(second, width, width // 2, weights)
        other, weights = lax.optimization_barrier((other, weights))
        tokens = weave_steps(my_slot.reshape(1), order, keep, other, slot_dev)
    else:
        order = jnp.arange(width, dtype=jnp.int32)
        weights = lax.all_gather(share_rows, ("cells", "groups", "slots"), axis=0, tiled=True)
        tokens = tokens_by_exchanges(owner, position, obs_feat, time_embed, my_slot, capacity, slot_dev)

    swap = [(0, 1), (1, 0)]
    heads_width, hidden_width = w_qkv.shape[2], w_gate_up.shape[2]
    partner = lax.ppermute(tokens, "mp", swap)
    for_partner = layer(partner, weights, heads_width, hidden_width, BF16)
    from_partner = lax.ppermute(for_partner, "mp", swap)
    own = layer(tokens, weights, heads_width, hidden_width, F32)
    return finish(tokens, own, from_partner, order).reshape(quarter, TSTEPS, width)


def solution(mesh):
    placed = (
        P(("groups", "cells", "slots", "mp"), None),
        P(("groups", "cells", "slots", "mp")),
        P(("groups", "cells", "slots", "mp")),
        P(("groups", "cells", "slots", "mp")),
        P(),
        P("cells", None, "mp"),
        P("mp", "cells"),
        P("cells", None, "mp"),
        P("mp", "cells"),
    )
    return jax.shard_map(
        on_device,
        mesh=mesh,
        in_specs=placed,
        out_specs=P(("groups", "cells", "slots", "mp"), None, None),
        check_vma=False,
    )
```

```python
import functools

import jax
import jax.numpy as jnp
from jax import lax
from jax.experimental import pallas as pl
from jax.experimental.pallas import tpu as pltpu
from jax.sharding import PartitionSpec as P

HD = 64
TSTEPS = 8
CB = 128
EPS = 1e-06

CODE = 32
UNIT = 512
LANES = 128
MIB = 1024 * 1024
F32 = jnp.float32
BF16 = jnp.bfloat16
WHOLE = pl.BlockSpec(memory_space=pltpu.VMEM)
SCALARS = pl.BlockSpec(memory_space=pltpu.SMEM)
FAR = pl.BlockSpec(memory_space=pl.ANY)


def iota(shape, axis):
    return lax.broadcasted_iota(jnp.int32, shape, axis)


def dot(left, right):
    return jnp.dot(left, right, preferred_element_type=F32)


def dot_t(left, right):
    return lax.dot_general(left, right, (((1,), (1,)), ((), ())), preferred_element_type=F32)


def params(mib):
    return pltpu.CompilerParams(vmem_limit_bytes=mib * MIB)


def block_places(owner, n_owners):
    rows = owner.shape[1]
    owner_hot = (iota((n_owners, rows), 0) == owner).astype(F32)
    upper = (iota((rows, rows), 0) <= iota((rows, rows), 1)).astype(BF16)
    running = dot(owner_hot.astype(BF16), upper)
    return jnp.sum(running * owner_hot, axis=0, keepdims=True).astype(jnp.int32) - 1


def one_hot_rows(owner, rank, block, capacity):
    place = jnp.where(owner == block, rank, -1)
    return (iota((capacity, owner.shape[1]), 0) == place).astype(F32).astype(BF16)


def code_kernel(owner_ref, position_ref, time_ref, code_ref, embed_ref):
    n_owners, _, capacity = code_ref.shape
    embed_ref[...] = time_ref[...]
    owner = owner_ref[...]
    rank = block_places(owner, n_owners)
    code = position_ref[...] + 1
    line = iota((8, owner.shape[1]), 0)
    digits = jnp.where(line == 0, code // CODE, jnp.where(line == 1, code % CODE, 0))
    digits = digits.astype(F32).astype(BF16)
    for block in range(n_owners):
        sent = dot_t(digits, one_hot_rows(owner, rank, block, capacity))
        code_ref[block] = (sent[0:1] * CODE + sent[1:2]).astype(jnp.int32) - 1


def place_codes(owner, position, time_embed, n_owners, capacity):
    rows = owner.shape[0]
    return pl.pallas_call(
        code_kernel,
        out_shape=[
            jax.ShapeDtypeStruct((n_owners, 1, capacity), jnp.int32),
            jax.ShapeDtypeStruct(time_embed.shape, BF16),
        ],
        in_specs=[WHOLE] * 3,
        out_specs=[WHOLE] * 2,
        compiler_params=params(12),
        cost_estimate=pl.CostEstimate(
            flops=16 * rows * n_owners * capacity, bytes_accessed=8 * rows, transcendentals=0
        ),
        name="place_codes",
    )(owner.reshape(1, rows), position.reshape(1, rows), time_embed)


def place_kernel(owner_ref, feat_ref, out_ref):
    n_owners, capacity, _ = out_ref.shape
    owner = owner_ref[...]
    rank = block_places(owner, n_owners)
    feat = feat_ref[...]
    for block in range(n_owners):
        out_ref[block] = dot(one_hot_rows(owner, rank, block, capacity), feat).astype(BF16)


def place_rows(owner, obs_feat, n_owners, capacity):
    rows, width = obs_feat.shape
    return pl.pallas_call(
        place_kernel,
        out_shape=jax.ShapeDtypeStruct((n_owners, capacity, width), BF16),
        in_specs=[WHOLE] * 2,
        out_specs=WHOLE,
        compiler_params=params(12),
        cost_estimate=pl.CostEstimate(
            flops=2 * rows * width * n_owners * capacity,
            bytes_accessed=2 * width * (rows + n_owners * capacity),
            transcendentals=0,
        ),
        name="place_rows",
    )(owner.reshape(1, rows), obs_feat)


def pool_kernel(capacity, slot_dev, slot_ref, embed_ref, code_ref, got_ref, keep_ref, send_ref):
    half = keep_ref.shape[0]
    places = 2 * half
    mine = slot_ref[0]
    total = jnp.zeros((places, keep_ref.shape[1]), F32)
    seen = jnp.zeros((places, capacity), F32)
    for block in range(got_ref.shape[0]):
        code = code_ref[block]
        turned = jnp.where(code >= half, code - half, code + half)
        code = jnp.where((code >= 0) & (mine == 1), turned, code)
        hot = (iota((places, capacity), 0) == code).astype(F32)
        seen += hot
        total += dot(hot.astype(BF16), got_ref[block])
    count = jnp.sum(seen, axis=1, keepdims=True)
    steps = embed_ref.shape[0]
    step_hot = iota((places, steps), 1) == iota((places, steps), 0) % slot_dev + mine * slot_dev
    embed = dot(step_hot.astype(F32).astype(BF16), embed_ref[...])
    tokens = (total / jnp.maximum(count, 1.0) + embed).astype(BF16)
    keep_ref[...] = tokens[:half]
    send_ref[...] = tokens[half:]


def pool_rows(my_slot, time_embed, codes, got, capacity, slot_dev):
    width = time_embed.shape[1]
    half = jax.ShapeDtypeStruct((CB * slot_dev // 2, width), BF16)
    return pl.pallas_call(
        functools.partial(pool_kernel, capacity, slot_dev),
        out_shape=[half, half],
        in_specs=[SCALARS] + [WHOLE] * 3,
        out_specs=[WHOLE] * 2,
        compiler_params=params(12),
        cost_estimate=pl.CostEstimate(
            flops=2 * CB * slot_dev * got.size, bytes_accessed=2 * got.size, transcendentals=0
        ),
        name="pool_rows",
    )(my_slot, time_embed, codes, got)


def weave_kernel(slot_dev, slot_ref, order_ref, keep_ref, got_ref, out_ref):
    rows, width = out_ref.shape
    half = keep_ref.shape[0]
    mine = slot_ref[0]
    row, col = iota((rows, half), 0), iota((rows, half), 1)
    source = col == row // TSTEPS * slot_dev + row % slot_dev
    own = row % TSTEPS // slot_dev == mine
    from_keep = (source & own).astype(F32).astype(BF16)
    from_got = (source & jnp.logical_not(own)).astype(F32).astype(BF16)
    tokens = (dot(from_keep, keep_ref[...]) + dot(from_got, got_ref[...])).astype(BF16)
    move = (iota((width, width), 0) == order_ref[...]).astype(F32).astype(BF16)
    out_ref[...] = dot(tokens, move).astype(BF16)


def weave_steps(my_slot, order, keep, got, slot_dev):
    rows, width = 2 * keep.shape[0], keep.shape[1]
    return pl.pallas_call(
        functools.partial(weave_kernel, slot_dev),
        out_shape=jax.ShapeDtypeStruct((rows, width), BF16),
        in_specs=[SCALARS] + [WHOLE] * 3,
        out_specs=WHOLE,
        compiler_params=params(12),
        cost_estimate=pl.CostEstimate(
            flops=2 * rows * width * (rows + width), bytes_accessed=4 * rows * width, transcendentals=0
        ),
        name="weave_steps",
    )(my_slot, order.reshape(1, width), keep, got)


def attention(normed, weight, heads_width, ctx_ref):
    rows = normed.shape[0]
    group = LANES
    lane = iota((1, LANES), 1)
    first = iota((group, LANES), 1) < HD
    masks = [(lane < HD).astype(F32).astype(BF16), (lane >= HD).astype(F32).astype(BF16)]
    ones = (iota((LANES, LANES), 0) // HD == iota((LANES, LANES), 1) // HD).astype(F32)
    mean = (ones * (1.0 / HD)).astype(BF16)
    ones = ones.astype(BF16)
    same_cell = iota((2 * group, group), 0) % group // TSTEPS == iota((2 * group, group), 1) // TSTEPS
    same_cell = same_cell.astype(F32).astype(BF16)
    count = jnp.ones((group, LANES), BF16)
    projected = dot(normed, weight)
    begins = range(0, rows, group)
    for at in range(0, heads_width, LANES):
        query = projected[:, at : at + LANES]
        key = projected[:, heads_width + at : heads_width + at + LANES]
        value = projected[:, 2 * heads_width + at : 2 * heads_width + at + LANES].astype(BF16)
        query_bf, key_bf = query.astype(BF16), key.astype(BF16)
        query = (query * lax.rsqrt(dot(query_bf * query_bf, ones) + HD * EPS)).astype(BF16)
        key = (key * lax.rsqrt(dot(key_bf * key_bf, mean) + EPS)).astype(BF16)
        left, right = query * masks[0], query * masks[1]
        scores = [
            dot_t(jnp.concatenate([left[at : at + group], right[at : at + group]], axis=0), key[at : at + group])
            for at in begins
        ]
        expos = [jnp.exp(score).astype(BF16) * same_cell for score in scores]
        mixed = [
            dot(expo, jnp.concatenate([value[at : at + group], count], axis=1)) for at, expo in zip(begins, expos)
        ]
        for begin, both in zip(begins, mixed):
            top, low = both[:group], both[group:]
            over = jnp.where(first, top[:, :LANES], low[:, :LANES])
            under = jnp.where(first, top[:, LANES:], low[:, LANES:])
            ctx_ref[begin : begin + group, at : at + LANES] = (over / under).astype(BF16)


def gated(normed, gate_w, up_w, down_w):
    gate = dot(normed, gate_w)
    up = dot(normed, up_w)
    hidden = (gate * (0.5 * jnp.tanh(0.5 * gate) + 0.5) * up).astype(BF16)
    return dot_t(hidden, down_w)


def layer_kernel(plan, hidden_width, tok_ref, *refs):
    pieces, (out_ref, w_ref, norm_ref, ctx_ref, acc_ref, sems) = refs[:-6], refs[-6:]
    copies = {}
    for number, (section, piece, row, at, size) in enumerate(plan):
        copy = pltpu.make_async_copy(
            pieces[piece].at[:, pl.ds(at, size)],
            w_ref.at[pl.ds(row, pieces[piece].shape[0]), pl.ds(at, size)],
            sems.at[number],
        )
        copy.start()
        copies.setdefault(section, []).append(copy)

    def ready(section):
        for copy in copies[section]:
            copy.wait()

    heads_width = ctx_ref.shape[1]
    gate_at, up_at, out_at, down_at, _ = layer_columns(heads_width, hidden_width)
    tokens = tok_ref[...].astype(F32)
    scale = lax.rsqrt(jnp.mean(tokens * tokens, axis=1, keepdims=True) + EPS)
    norm_ref[...] = (tokens * scale).astype(BF16)
    ready(0)
    attention(norm_ref[...], w_ref[:, :gate_at], heads_width, ctx_ref)
    ready(1)
    acc_ref[...] = dot_t(ctx_ref[...], w_ref[:, out_at:down_at])
    for begin in range(0, hidden_width, UNIT):
        gate_w, up_w, down_w = [w_ref[:, at + begin : at + begin + UNIT] for at in (gate_at, up_at, down_at)]
        add = gated(norm_ref[...], gate_w, up_w, down_w)
        if begin + UNIT < hidden_width:
            acc_ref[...] += add
        else:
            out_ref[...] = (acc_ref[...] + add).astype(out_ref.dtype)


def layer_columns(heads_width, hidden_width):
    gate_at = 3 * heads_width
    up_at = gate_at + hidden_width
    out_at = up_at + hidden_width
    return gate_at, up_at, out_at, out_at + heads_width, out_at + heads_width + hidden_width


def layer(tokens, pieces, heads_width, hidden_width, out_type):
    rows, width = tokens.shape
    gate_at, _, _, _, columns = layer_columns(heads_width, hidden_width)
    plan = []
    for section, (left, right) in enumerate([(0, gate_at), (gate_at, columns)]):
        row = 0
        for number, piece in enumerate(pieces):
            plan.append((section, number, row, left, right - left))
            row += piece.shape[0]
    return pl.pallas_call(
        functools.partial(layer_kernel, plan, hidden_width),
        out_shape=jax.ShapeDtypeStruct((rows, width), out_type),
        in_specs=[WHOLE] + [FAR] * len(pieces),
        out_specs=WHOLE,
        scratch_shapes=[
            pltpu.VMEM((width, columns), BF16),
            pltpu.VMEM((rows, width), BF16),
            pltpu.VMEM((rows, heads_width), BF16),
            pltpu.VMEM((rows, width), F32),
            pltpu.SemaphoreType.DMA((len(plan),)),
        ],
        compiler_params=params(54),
        cost_estimate=pl.CostEstimate(
            flops=2 * rows * width * columns,
            bytes_accessed=2 * width * columns + 6 * rows * width,
            transcendentals=rows * hidden_width,
        ),
        name="layer",
    )(tokens, *pieces)


def finish_kernel(tok_ref, sum_ref, got_ref, order_ref, out_ref):
    width = out_ref.shape[1]
    mixed = (tok_ref[...].astype(F32) + sum_ref[...] + got_ref[...].astype(F32)).astype(BF16)
    move = (iota((width, width), 0) == order_ref[...]).astype(F32).astype(BF16)
    out_ref[...] = dot_t(mixed, move).astype(BF16)


def finish(tokens, sums, got, order):
    rows, width = tokens.shape
    return pl.pallas_call(
        finish_kernel,
        out_shape=jax.ShapeDtypeStruct((rows, width), BF16),
        in_specs=[WHOLE] * 4,
        out_specs=WHOLE,
        compiler_params=params(12),
        cost_estimate=pl.CostEstimate(
            flops=2 * rows * width * width, bytes_accessed=10 * rows * width, transcendentals=0
        ),
        name="finish",
    )(tokens, sums, got, order.reshape(1, width))


def side_by_side(w_qkv, w_out, w_gate_up, w_down):
    rows = w_qkv.shape[0]
    return jnp.concatenate([w_qkv.reshape(rows, -1), w_gate_up.reshape(rows, -1), w_out, w_down], axis=1)


def along_cells(values, distance):
    n_cells = lax.axis_size("cells")
    return lax.ppermute(values, "cells", [(j, (j - distance) % n_cells) for j in range(n_cells)])


def to_other_places(shares):
    n_slots = lax.axis_size("slots")
    n_share = lax.axis_size("groups") * n_slots
    places = [shares]
    for far in range(1, n_share):
        pairs = [(place, place ^ far) for place in range(n_share)]
        places.append(lax.ppermute(shares, ("groups", "slots"), pairs))
    return places


def arrival_order(width, n_share):
    n_cells = lax.axis_size("cells")
    mine = lax.axis_index("cells")
    place = lax.axis_index("groups") * lax.axis_size("slots") + lax.axis_index("slots")
    rows = width // n_cells
    share = rows // n_share
    row = jnp.arange(width, dtype=jnp.int32)
    past = row - 2 * rows
    far = jnp.where(past < 0, row // share % n_share, past // (2 * share))
    distance = jnp.where(past < 0, n_cells - 1, 1 + past // share % 2)
    other = (mine + distance) % n_cells * rows + (far ^ place) * share + row % share
    return jnp.where(row < rows, mine * rows + row, other)


def tokens_by_exchanges(owner, position, obs_feat, time_embed, my_slot, capacity, slot_dev):
    n_slots = lax.axis_size("slots")
    n_owners = lax.axis_size("cells") * lax.axis_size("mp")
    rows, width = obs_feat.shape
    owners = jnp.arange(n_owners, dtype=jnp.int32)
    owner_hot = (owner[:, None] == owners[None, :]).astype(F32)
    row_ids = jnp.arange(rows, dtype=jnp.int32)
    lower = (row_ids[None, :] <= row_ids[:, None]).astype(BF16)
    running = dot(lower, owner_hot.astype(BF16))
    rank = jnp.sum(running * owner_hot, axis=1).astype(jnp.int32) - 1
    place = jnp.where(owner < n_owners, owner * capacity + rank, n_owners * capacity)
    place_ids = jnp.arange(n_owners * capacity, dtype=jnp.int32)
    taken = place_ids[:, None] == place[None, :]
    send_feat = dot(taken.astype(BF16), obs_feat).astype(BF16).reshape(n_owners, capacity, width)
    send_code = jnp.sum(jnp.where(taken, position[None, :] + 1, 0), axis=1).reshape(n_owners, capacity)
    axes = ("cells", "mp")
    got_feat = lax.all_to_all(send_feat, axes, split_axis=0, concat_axis=0, tiled=True).reshape(-1, width)
    got_code = lax.all_to_all(send_code, axes, split_axis=0, concat_axis=0, tiled=True).reshape(-1) - 1
    hot = (jnp.arange(CB * slot_dev, dtype=jnp.int32)[:, None] == got_code[None, :]).astype(BF16)
    count = jnp.sum(hot.astype(F32), axis=1)
    pooled = dot(hot, got_feat) / jnp.maximum(count, 1.0)[:, None]
    embed = lax.dynamic_slice_in_dim(time_embed, my_slot * slot_dev, slot_dev, 0).astype(F32)
    tokens = (pooled.reshape(CB, slot_dev, width) + embed[None]).astype(BF16)
    grid = tokens.reshape(n_slots, CB // n_slots, slot_dev, width)
    grid = lax.all_to_all(grid, "slots", split_axis=0, concat_axis=2, tiled=True)
    return grid.reshape(-1, width)


def on_device(obs_feat, obs_cell, obs_slot, obs_count, time_embed, w_qkv, w_out, w_gate_up, w_down):
    n_cells = lax.axis_size("cells")
    n_slots = lax.axis_size("slots")
    n_groups = lax.axis_size("groups")
    n_mp = lax.axis_size("mp")
    n_owners = n_cells * n_mp
    rows, width = obs_feat.shape
    capacity = 3 * rows // n_owners
    quarter = CB // n_slots
    slot_dev = TSTEPS // n_slots
    my_slot = lax.axis_index("slots")
    n_share = n_groups * n_slots
    share = w_qkv.shape[0] // n_share
    valid = jnp.arange(rows, dtype=jnp.int32) < obs_count[0]
    owner = obs_cell // (quarter * n_mp * n_slots) * n_mp + obs_cell // quarter % n_mp
    owner = jnp.where(valid, owner, n_owners)
    local = obs_cell // (quarter * n_mp) % n_slots * quarter + obs_cell % quarter
    position = local * slot_dev + obs_slot

    local_weights = (w_qkv, w_out.T, w_gate_up, w_down.T)
    which = lax.axis_index("groups") * n_slots + my_slot
    share_weights = [lax.dynamic_slice_in_dim(w, which * share, share, 0) for w in local_weights]
    share_rows = side_by_side(*share_weights)
    if n_slots == 2 and n_groups == 2 and n_cells == 4 and share % 16 == 0 and capacity % 16 == 0:
        order = arrival_order(width, n_share)
        below = along_cells(share_rows, -1)
        codes, embed = place_codes(owner, position, time_embed, n_owners, capacity)
        codes = lax.all_to_all(codes, ("cells", "mp"), split_axis=0, concat_axis=0, tiled=True)
        below, codes, share_rows = lax.optimization_barrier((below, codes, share_rows))
        first = to_other_places(below)
        blocks = place_rows(owner, obs_feat, n_owners, capacity)
        above, opposite = along_cells(share_rows, 1), along_cells(below, -1)
        blocks, above, opposite, first = lax.optimization_barrier((blocks, above, opposite, first))
        second = to_other_places(jnp.concatenate([above, opposite], axis=0))
        shard = side_by_side(*local_weights)
        got = lax.all_to_all(blocks, ("cells", "mp"), split_axis=0, concat_axis=0, tiled=True)
        got, shard = lax.optimization_barrier((got, shard))
        keep, send = pool_rows(my_slot.reshape(1), embed, codes, got, capacity, slot_dev)
        send, second = lax.optimization_barrier((send, second))
        other = lax.ppermute(send, "slots", [(0, 1), (1, 0)])
        pieces = [shard] + first + second
        tokens = weave_steps(my_slot.reshape(1), order, keep, other, slot_dev)
    else:
        order = jnp.arange(width, dtype=jnp.int32)
        pieces = [lax.all_gather(share_rows, ("cells", "groups", "slots"), axis=0, tiled=True)]
        tokens = tokens_by_exchanges(owner, position, obs_feat, time_embed, my_slot, capacity, slot_dev)

    swap = [(0, 1), (1, 0)]
    heads_width, hidden_width = w_qkv.shape[2], w_gate_up.shape[2]
    partner = lax.ppermute(tokens, "mp", swap)
    for_partner = layer(partner, pieces, heads_width, hidden_width, BF16)
    from_partner = lax.ppermute(for_partner, "mp", swap)
    own = layer(tokens, pieces, heads_width, hidden_width, F32)
    return finish(tokens, own, from_partner, order).reshape(quarter, TSTEPS, width)


def solution(mesh):
    placed = (
        P(("groups", "cells", "slots", "mp"), None),
        P(("groups", "cells", "slots", "mp")),
        P(("groups", "cells", "slots", "mp")),
        P(("groups", "cells", "slots", "mp")),
        P(),
        P("cells", None, "mp"),
        P("mp", "cells"),
        P("cells", None, "mp"),
        P("mp", "cells"),
    )
    return jax.shard_map(
        on_device,
        mesh=mesh,
        in_specs=placed,
        out_specs=P(("groups", "cells", "slots", "mp"), None, None),
        check_vma=False,
    )
```

```python
import functools

import jax
import jax.numpy as jnp
from jax import lax
from jax.experimental import pallas as pl
from jax.experimental.pallas import tpu as pltpu
from jax.sharding import PartitionSpec as P

HD = 64
TSTEPS = 8
CB = 128
EPS = 1e-06

CODE = 32
UNIT = 512
LANES = 128
MIB = 1024 * 1024
F32 = jnp.float32
BF16 = jnp.bfloat16
WHOLE = pl.BlockSpec(memory_space=pltpu.VMEM)
SCALARS = pl.BlockSpec(memory_space=pltpu.SMEM)
FAR = pl.BlockSpec(memory_space=pl.ANY)


def iota(shape, axis):
    return lax.broadcasted_iota(jnp.int32, shape, axis)


def dot(left, right):
    return jnp.dot(left, right, preferred_element_type=F32)


def dot_t(left, right):
    return lax.dot_general(left, right, (((1,), (1,)), ((), ())), preferred_element_type=F32)


def params(mib):
    return pltpu.CompilerParams(vmem_limit_bytes=mib * MIB)


def block_places(owner, n_owners):
    rows = owner.shape[1]
    owner_hot = (iota((n_owners, rows), 0) == owner).astype(F32)
    upper = (iota((rows, rows), 0) <= iota((rows, rows), 1)).astype(BF16)
    running = dot(owner_hot.astype(BF16), upper)
    return jnp.sum(running * owner_hot, axis=0, keepdims=True).astype(jnp.int32) - 1


def one_hot_rows(owner, rank, block, capacity):
    place = jnp.where(owner == block, rank, -1)
    return (iota((capacity, owner.shape[1]), 0) == place).astype(F32).astype(BF16)


def code_kernel(owner_ref, position_ref, time_ref, code_ref, embed_ref):
    n_owners, _, capacity = code_ref.shape
    embed_ref[...] = time_ref[...]
    owner = owner_ref[...]
    rank = block_places(owner, n_owners)
    code = position_ref[...] + 1
    line = iota((8, owner.shape[1]), 0)
    digits = jnp.where(line == 0, code // CODE, jnp.where(line == 1, code % CODE, 0))
    digits = digits.astype(F32).astype(BF16)
    for block in range(n_owners):
        sent = dot_t(digits, one_hot_rows(owner, rank, block, capacity))
        code_ref[block] = (sent[0:1] * CODE + sent[1:2]).astype(jnp.int32) - 1


def place_codes(owner, position, time_embed, n_owners, capacity):
    rows = owner.shape[0]
    return pl.pallas_call(
        code_kernel,
        out_shape=[
            jax.ShapeDtypeStruct((n_owners, 1, capacity), jnp.int32),
            jax.ShapeDtypeStruct(time_embed.shape, BF16),
        ],
        in_specs=[WHOLE] * 3,
        out_specs=[WHOLE] * 2,
        compiler_params=params(12),
        cost_estimate=pl.CostEstimate(
            flops=16 * rows * n_owners * capacity, bytes_accessed=8 * rows, transcendentals=0
        ),
        name="place_codes",
    )(owner.reshape(1, rows), position.reshape(1, rows), time_embed)


def place_kernel(owner_ref, feat_ref, out_ref):
    n_owners, capacity, _ = out_ref.shape
    owner = owner_ref[...]
    rank = block_places(owner, n_owners)
    feat = feat_ref[...]
    for block in range(n_owners):
        out_ref[block] = dot(one_hot_rows(owner, rank, block, capacity), feat).astype(BF16)


def place_rows(owner, obs_feat, n_owners, capacity):
    rows, width = obs_feat.shape
    return pl.pallas_call(
        place_kernel,
        out_shape=jax.ShapeDtypeStruct((n_owners, capacity, width), BF16),
        in_specs=[WHOLE] * 2,
        out_specs=WHOLE,
        compiler_params=params(12),
        cost_estimate=pl.CostEstimate(
            flops=2 * rows * width * n_owners * capacity,
            bytes_accessed=2 * width * (rows + n_owners * capacity),
            transcendentals=0,
        ),
        name="place_rows",
    )(owner.reshape(1, rows), obs_feat)


def pool_kernel(capacity, slot_dev, slot_ref, embed_ref, code_ref, got_ref, keep_ref, send_ref):
    half = keep_ref.shape[0]
    places = 2 * half
    mine = slot_ref[0]
    total = jnp.zeros((places, keep_ref.shape[1]), F32)
    seen = jnp.zeros((places, capacity), F32)
    for block in range(got_ref.shape[0]):
        code = code_ref[block]
        turned = jnp.where(code >= half, code - half, code + half)
        code = jnp.where((code >= 0) & (mine == 1), turned, code)
        hot = (iota((places, capacity), 0) == code).astype(F32)
        seen += hot
        total += dot(hot.astype(BF16), got_ref[block])
    count = jnp.sum(seen, axis=1, keepdims=True)
    steps = embed_ref.shape[0]
    step_hot = iota((places, steps), 1) == iota((places, steps), 0) % slot_dev + mine * slot_dev
    embed = dot(step_hot.astype(F32).astype(BF16), embed_ref[...])
    tokens = (total / jnp.maximum(count, 1.0) + embed).astype(BF16)
    keep_ref[...] = tokens[:half]
    send_ref[...] = tokens[half:]


def pool_rows(my_slot, time_embed, codes, got, capacity, slot_dev):
    width = time_embed.shape[1]
    half = jax.ShapeDtypeStruct((CB * slot_dev // 2, width), BF16)
    return pl.pallas_call(
        functools.partial(pool_kernel, capacity, slot_dev),
        out_shape=[half, half],
        in_specs=[SCALARS] + [WHOLE] * 3,
        out_specs=[WHOLE] * 2,
        compiler_params=params(12),
        cost_estimate=pl.CostEstimate(
            flops=2 * CB * slot_dev * got.size, bytes_accessed=2 * got.size, transcendentals=0
        ),
        name="pool_rows",
    )(my_slot, time_embed, codes, got)


def weave_kernel(slot_dev, slot_ref, order_ref, keep_ref, got_ref, out_ref):
    rows, width = out_ref.shape
    half = keep_ref.shape[0]
    mine = slot_ref[0]
    row, col = iota((rows, half), 0), iota((rows, half), 1)
    source = col == row // TSTEPS * slot_dev + row % slot_dev
    own = row % TSTEPS // slot_dev == mine
    from_keep = (source & own).astype(F32).astype(BF16)
    from_got = (source & jnp.logical_not(own)).astype(F32).astype(BF16)
    tokens = (dot(from_keep, keep_ref[...]) + dot(from_got, got_ref[...])).astype(BF16)
    move = (iota((width, width), 0) == order_ref[...]).astype(F32).astype(BF16)
    out_ref[...] = dot(tokens, move).astype(BF16)


def weave_steps(my_slot, order, keep, got, slot_dev):
    rows, width = 2 * keep.shape[0], keep.shape[1]
    return pl.pallas_call(
        functools.partial(weave_kernel, slot_dev),
        out_shape=jax.ShapeDtypeStruct((rows, width), BF16),
        in_specs=[SCALARS] + [WHOLE] * 3,
        out_specs=WHOLE,
        compiler_params=params(12),
        cost_estimate=pl.CostEstimate(
            flops=2 * rows * width * (rows + width), bytes_accessed=4 * rows * width, transcendentals=0
        ),
        name="weave_steps",
    )(my_slot, order.reshape(1, width), keep, got)


def attention(normed, weight, heads_width, ctx_ref):
    rows = normed.shape[0]
    group = LANES
    lane = iota((1, LANES), 1)
    first = iota((group, LANES), 1) < HD
    masks = [(lane < HD).astype(F32).astype(BF16), (lane >= HD).astype(F32).astype(BF16)]
    ones = (iota((LANES, LANES), 0) // HD == iota((LANES, LANES), 1) // HD).astype(F32)
    mean = (ones * (1.0 / HD)).astype(BF16)
    ones = ones.astype(BF16)
    same_cell = iota((2 * group, group), 0) % group // TSTEPS == iota((2 * group, group), 1) // TSTEPS
    same_cell = same_cell.astype(F32).astype(BF16)
    count = jnp.ones((group, LANES), BF16)
    projected = dot(normed, weight)
    begins = range(0, rows, group)
    for at in range(0, heads_width, LANES):
        query = projected[:, at : at + LANES]
        key = projected[:, heads_width + at : heads_width + at + LANES]
        value = projected[:, 2 * heads_width + at : 2 * heads_width + at + LANES].astype(BF16)
        query_bf, key_bf = query.astype(BF16), key.astype(BF16)
        query = (query * lax.rsqrt(dot(query_bf * query_bf, ones) + HD * EPS)).astype(BF16)
        key = (key * lax.rsqrt(dot(key_bf * key_bf, mean) + EPS)).astype(BF16)
        left, right = query * masks[0], query * masks[1]
        scores = [
            dot_t(jnp.concatenate([left[at : at + group], right[at : at + group]], axis=0), key[at : at + group])
            for at in begins
        ]
        expos = [jnp.exp(score).astype(BF16) * same_cell for score in scores]
        mixed = [
            dot(expo, jnp.concatenate([value[at : at + group], count], axis=1)) for at, expo in zip(begins, expos)
        ]
        for begin, both in zip(begins, mixed):
            top, low = both[:group], both[group:]
            over = jnp.where(first, top[:, :LANES], low[:, :LANES])
            under = jnp.where(first, top[:, LANES:], low[:, LANES:])
            ctx_ref[begin : begin + group, at : at + LANES] = (over / under).astype(BF16)


def gated(normed, gate_w, up_w, down_w):
    gate = dot(normed, gate_w)
    up = dot(normed, up_w)
    hidden = (gate * (0.5 * jnp.tanh(0.5 * gate) + 0.5) * up).astype(BF16)
    return dot_t(hidden, down_w)


def layer_kernel(plan, hidden_width, tok_ref, *refs):
    pieces, (out_ref, w_ref, norm_ref, ctx_ref, acc_ref, sems) = refs[:-6], refs[-6:]
    copies = {}
    for number, (section, piece, source, row, at, size) in enumerate(plan):
        copy = pltpu.make_async_copy(
            pieces[piece].at[:, pl.ds(source, size)],
            w_ref.at[pl.ds(row, pieces[piece].shape[0]), pl.ds(at, size)],
            sems.at[number],
        )
        copies.setdefault(section, []).append(copy)

    def start(section):
        for copy in copies[section]:
            copy.start()

    def ready(section):
        for copy in copies[section]:
            copy.wait()

    start(0)
    heads_width = ctx_ref.shape[1]
    gate_at, up_at, out_at, down_at, _ = layer_columns(heads_width, hidden_width)
    tokens = tok_ref[...].astype(F32)
    scale = lax.rsqrt(jnp.mean(tokens * tokens, axis=1, keepdims=True) + EPS)
    norm_ref[...] = (tokens * scale).astype(BF16)
    ready(0)
    start(1)
    attention(norm_ref[...], w_ref[:, :gate_at], heads_width, ctx_ref)
    ready(1)
    acc_ref[...] = dot_t(ctx_ref[...], w_ref[:, out_at:down_at])
    for begin in range(0, hidden_width, UNIT):
        gate_w, up_w, down_w = [w_ref[:, at + begin : at + begin + UNIT] for at in (gate_at, up_at, down_at)]
        add = gated(norm_ref[...], gate_w, up_w, down_w)
        if begin + UNIT < hidden_width:
            acc_ref[...] += add
        else:
            out_ref[...] = (acc_ref[...] + add).astype(out_ref.dtype)


def layer_columns(heads_width, hidden_width):
    gate_at = 3 * heads_width
    up_at = gate_at + hidden_width
    out_at = up_at + hidden_width
    return gate_at, up_at, out_at, out_at + heads_width, out_at + heads_width + hidden_width


def layer(tokens, pieces, heads_width, hidden_width, out_type):
    rows, width = tokens.shape
    gate_at, _, _, _, columns = layer_columns(heads_width, hidden_width)
    plan = []
    for section, (left, right) in enumerate([(0, gate_at), (gate_at, columns)]):
        for number, (array, row, at) in enumerate(pieces):
            low, high = max(left, at), min(right, at + array.shape[1])
            if low < high:
                plan.append((section, number, low - at, row, low, high - low))
    return pl.pallas_call(
        functools.partial(layer_kernel, plan, hidden_width),
        out_shape=jax.ShapeDtypeStruct((rows, width), out_type),
        in_specs=[WHOLE] + [FAR] * len(pieces),
        out_specs=WHOLE,
        scratch_shapes=[
            pltpu.VMEM((width, columns), BF16),
            pltpu.VMEM((rows, width), BF16),
            pltpu.VMEM((rows, heads_width), BF16),
            pltpu.VMEM((rows, width), F32),
            pltpu.SemaphoreType.DMA((len(plan),)),
        ],
        compiler_params=params(54),
        cost_estimate=pl.CostEstimate(
            flops=2 * rows * width * columns,
            bytes_accessed=2 * width * columns + 6 * rows * width,
            transcendentals=rows * hidden_width,
        ),
        name="layer",
    )(tokens, *[array for array, _, _ in pieces])


def finish_kernel(tok_ref, sum_ref, got_ref, order_ref, out_ref):
    width = out_ref.shape[1]
    mixed = (tok_ref[...].astype(F32) + sum_ref[...] + got_ref[...].astype(F32)).astype(BF16)
    move = (iota((width, width), 0) == order_ref[...]).astype(F32).astype(BF16)
    out_ref[...] = dot_t(mixed, move).astype(BF16)


def finish(tokens, sums, got, order):
    rows, width = tokens.shape
    return pl.pallas_call(
        finish_kernel,
        out_shape=jax.ShapeDtypeStruct((rows, width), BF16),
        in_specs=[WHOLE] * 4,
        out_specs=WHOLE,
        compiler_params=params(12),
        cost_estimate=pl.CostEstimate(
            flops=2 * rows * width * width, bytes_accessed=10 * rows * width, transcendentals=0
        ),
        name="finish",
    )(tokens, sums, got, order.reshape(1, width))


def side_by_side(w_qkv, w_out, w_gate_up, w_down):
    rows = w_qkv.shape[0]
    return jnp.concatenate([w_qkv.reshape(rows, -1), w_gate_up.reshape(rows, -1), w_out, w_down], axis=1)


def along_cells(values, distance):
    n_cells = lax.axis_size("cells")
    return lax.ppermute(values, "cells", [(j, (j - distance) % n_cells) for j in range(n_cells)])


def to_other_places(shares):
    n_slots = lax.axis_size("slots")
    n_share = lax.axis_size("groups") * n_slots
    places = [shares]
    for far in range(1, n_share):
        pairs = [(place, place ^ far) for place in range(n_share)]
        places.append(lax.ppermute(shares, ("groups", "slots"), pairs))
    return places


def to_other_places_by_halves(shares):
    swap = [(0, 1), (1, 0)]
    by_slot = lax.ppermute(shares, "slots", swap)
    by_group = lax.ppermute(shares, "groups", swap)
    cut = shares.shape[1] // 2
    left = lax.ppermute(by_slot[:, :cut], "groups", swap)
    right = lax.ppermute(by_group[:, cut:], "slots", swap)
    return [shares, by_slot, by_group, left, right]


def arrival_order(width, n_share):
    n_cells = lax.axis_size("cells")
    mine = lax.axis_index("cells")
    place = lax.axis_index("groups") * lax.axis_size("slots") + lax.axis_index("slots")
    rows = width // n_cells
    share = rows // n_share
    row = jnp.arange(width, dtype=jnp.int32)
    past = row - 2 * rows
    far = jnp.where(past < 0, row // share % n_share, past // (2 * share))
    distance = jnp.where(past < 0, n_cells - 1, 1 + past // share % 2)
    other = (mine + distance) % n_cells * rows + (far ^ place) * share + row % share
    return jnp.where(row < rows, mine * rows + row, other)


def tokens_by_exchanges(owner, position, obs_feat, time_embed, my_slot, capacity, slot_dev):
    n_slots = lax.axis_size("slots")
    n_owners = lax.axis_size("cells") * lax.axis_size("mp")
    rows, width = obs_feat.shape
    owners = jnp.arange(n_owners, dtype=jnp.int32)
    owner_hot = (owner[:, None] == owners[None, :]).astype(F32)
    row_ids = jnp.arange(rows, dtype=jnp.int32)
    lower = (row_ids[None, :] <= row_ids[:, None]).astype(BF16)
    running = dot(lower, owner_hot.astype(BF16))
    rank = jnp.sum(running * owner_hot, axis=1).astype(jnp.int32) - 1
    place = jnp.where(owner < n_owners, owner * capacity + rank, n_owners * capacity)
    place_ids = jnp.arange(n_owners * capacity, dtype=jnp.int32)
    taken = place_ids[:, None] == place[None, :]
    send_feat = dot(taken.astype(BF16), obs_feat).astype(BF16).reshape(n_owners, capacity, width)
    send_code = jnp.sum(jnp.where(taken, position[None, :] + 1, 0), axis=1).reshape(n_owners, capacity)
    axes = ("cells", "mp")
    got_feat = lax.all_to_all(send_feat, axes, split_axis=0, concat_axis=0, tiled=True).reshape(-1, width)
    got_code = lax.all_to_all(send_code, axes, split_axis=0, concat_axis=0, tiled=True).reshape(-1) - 1
    hot = (jnp.arange(CB * slot_dev, dtype=jnp.int32)[:, None] == got_code[None, :]).astype(BF16)
    count = jnp.sum(hot.astype(F32), axis=1)
    pooled = dot(hot, got_feat) / jnp.maximum(count, 1.0)[:, None]
    embed = lax.dynamic_slice_in_dim(time_embed, my_slot * slot_dev, slot_dev, 0).astype(F32)
    tokens = (pooled.reshape(CB, slot_dev, width) + embed[None]).astype(BF16)
    grid = tokens.reshape(n_slots, CB // n_slots, slot_dev, width)
    grid = lax.all_to_all(grid, "slots", split_axis=0, concat_axis=2, tiled=True)
    return grid.reshape(-1, width)


def on_device(obs_feat, obs_cell, obs_slot, obs_count, time_embed, w_qkv, w_out, w_gate_up, w_down):
    n_cells = lax.axis_size("cells")
    n_slots = lax.axis_size("slots")
    n_groups = lax.axis_size("groups")
    n_mp = lax.axis_size("mp")
    n_owners = n_cells * n_mp
    rows, width = obs_feat.shape
    capacity = 3 * rows // n_owners
    quarter = CB // n_slots
    slot_dev = TSTEPS // n_slots
    my_slot = lax.axis_index("slots")
    n_share = n_groups * n_slots
    share = w_qkv.shape[0] // n_share
    valid = jnp.arange(rows, dtype=jnp.int32) < obs_count[0]
    owner = obs_cell // (quarter * n_mp * n_slots) * n_mp + obs_cell // quarter % n_mp
    owner = jnp.where(valid, owner, n_owners)
    local = obs_cell // (quarter * n_mp) % n_slots * quarter + obs_cell % quarter
    position = local * slot_dev + obs_slot

    local_weights = (w_qkv, w_out.T, w_gate_up, w_down.T)
    which = lax.axis_index("groups") * n_slots + my_slot
    share_weights = [lax.dynamic_slice_in_dim(w, which * share, share, 0) for w in local_weights]
    share_rows = side_by_side(*share_weights)
    if n_slots == 2 and n_groups == 2 and n_cells == 4 and share % 16 == 0 and capacity % 16 == 0:
        order = arrival_order(width, n_share)
        below = along_cells(share_rows, -1)
        codes, embed = place_codes(owner, position, time_embed, n_owners, capacity)
        codes = lax.all_to_all(codes, ("cells", "mp"), split_axis=0, concat_axis=0, tiled=True)
        below, codes, share_rows = lax.optimization_barrier((below, codes, share_rows))
        first = to_other_places(below)
        blocks = place_rows(owner, obs_feat, n_owners, capacity)
        above, opposite = along_cells(share_rows, 1), along_cells(below, -1)
        blocks, above, opposite, first = lax.optimization_barrier((blocks, above, opposite, first))
        second = to_other_places_by_halves(jnp.concatenate([above, opposite], axis=0))
        shard = side_by_side(*local_weights)
        got = lax.all_to_all(blocks, ("cells", "mp"), split_axis=0, concat_axis=0, tiled=True)
        got, shard, second = lax.optimization_barrier((got, shard, second))
        keep, send = pool_rows(my_slot.reshape(1), embed, codes, got, capacity, slot_dev)
        other = lax.ppermute(send, "slots", [(0, 1), (1, 0)])
        pieces, row = [], 0
        for array in [shard] + first + second[:3]:
            pieces.append((array, row, 0))
            row += array.shape[0]
        pieces += [(second[3], row, 0), (second[4], row, second[3].shape[1])]
        tokens = weave_steps(my_slot.reshape(1), order, keep, other, slot_dev)
    else:
        order = jnp.arange(width, dtype=jnp.int32)
        pieces = [(lax.all_gather(share_rows, ("cells", "groups", "slots"), axis=0, tiled=True), 0, 0)]
        tokens = tokens_by_exchanges(owner, position, obs_feat, time_embed, my_slot, capacity, slot_dev)

    swap = [(0, 1), (1, 0)]
    heads_width, hidden_width = w_qkv.shape[2], w_gate_up.shape[2]
    partner = lax.ppermute(tokens, "mp", swap)
    for_partner = layer(partner, pieces, heads_width, hidden_width, BF16)
    from_partner = lax.ppermute(for_partner, "mp", swap)
    own = layer(tokens, pieces, heads_width, hidden_width, F32)
    return finish(tokens, own, from_partner, order).reshape(quarter, TSTEPS, width)


def solution(mesh):
    placed = (
        P(("groups", "cells", "slots", "mp"), None),
        P(("groups", "cells", "slots", "mp")),
        P(("groups", "cells", "slots", "mp")),
        P(("groups", "cells", "slots", "mp")),
        P(),
        P("cells", None, "mp"),
        P("mp", "cells"),
        P("cells", None, "mp"),
        P("mp", "cells"),
    )
    return jax.shard_map(
        on_device,
        mesh=mesh,
        in_specs=placed,
        out_specs=P(("groups", "cells", "slots", "mp"), None, None),
        check_vma=False,
    )
```

```python
import functools

import jax
import jax.numpy as jnp
from jax import lax
from jax.experimental import pallas as pl
from jax.experimental.pallas import tpu as pltpu
from jax.sharding import PartitionSpec as P

HD = 64
TSTEPS = 8
CB = 128
EPS = 1e-06

CODE = 32
UNIT = 512
LANES = 128
MIB = 1024 * 1024
F32 = jnp.float32
BF16 = jnp.bfloat16
WHOLE = pl.BlockSpec(memory_space=pltpu.VMEM)
SCALARS = pl.BlockSpec(memory_space=pltpu.SMEM)
FAR = pl.BlockSpec(memory_space=pl.ANY)


def iota(shape, axis):
    return lax.broadcasted_iota(jnp.int32, shape, axis)


def dot(left, right):
    return jnp.dot(left, right, preferred_element_type=F32)


def dot_t(left, right):
    return lax.dot_general(left, right, (((1,), (1,)), ((), ())), preferred_element_type=F32)


def params(mib):
    return pltpu.CompilerParams(vmem_limit_bytes=mib * MIB)


def block_places(owner, n_owners):
    rows = owner.shape[1]
    owner_hot = (iota((n_owners, rows), 0) == owner).astype(F32)
    upper = (iota((rows, rows), 0) <= iota((rows, rows), 1)).astype(BF16)
    running = dot(owner_hot.astype(BF16), upper)
    return jnp.sum(running * owner_hot, axis=0, keepdims=True).astype(jnp.int32) - 1


def one_hot_rows(owner, rank, block, capacity):
    place = jnp.where(owner == block, rank, -1)
    return (iota((capacity, owner.shape[1]), 0) == place).astype(F32).astype(BF16)


def code_kernel(owner_ref, position_ref, time_ref, code_ref, embed_ref):
    n_owners, _, capacity = code_ref.shape
    embed_ref[...] = time_ref[...]
    owner = owner_ref[...]
    rank = block_places(owner, n_owners)
    code = position_ref[...] + 1
    line = iota((8, owner.shape[1]), 0)
    digits = jnp.where(line == 0, code // CODE, jnp.where(line == 1, code % CODE, 0))
    digits = digits.astype(F32).astype(BF16)
    for block in range(n_owners):
        sent = dot_t(digits, one_hot_rows(owner, rank, block, capacity))
        code_ref[block] = (sent[0:1] * CODE + sent[1:2]).astype(jnp.int32) - 1


def place_codes(owner, position, time_embed, n_owners, capacity):
    rows = owner.shape[0]
    return pl.pallas_call(
        code_kernel,
        out_shape=[
            jax.ShapeDtypeStruct((n_owners, 1, capacity), jnp.int32),
            jax.ShapeDtypeStruct(time_embed.shape, BF16),
        ],
        in_specs=[WHOLE] * 3,
        out_specs=[WHOLE] * 2,
        compiler_params=params(12),
        cost_estimate=pl.CostEstimate(
            flops=16 * rows * n_owners * capacity, bytes_accessed=8 * rows, transcendentals=0
        ),
        name="place_codes",
    )(owner.reshape(1, rows), position.reshape(1, rows), time_embed)


def place_kernel(owner_ref, feat_ref, out_ref):
    n_owners, capacity, _ = out_ref.shape
    owner = owner_ref[...]
    rank = block_places(owner, n_owners)
    feat = feat_ref[...]
    for block in range(n_owners):
        out_ref[block] = dot(one_hot_rows(owner, rank, block, capacity), feat).astype(BF16)


def place_rows(owner, obs_feat, n_owners, capacity):
    rows, width = obs_feat.shape
    return pl.pallas_call(
        place_kernel,
        out_shape=jax.ShapeDtypeStruct((n_owners, capacity, width), BF16),
        in_specs=[WHOLE] * 2,
        out_specs=WHOLE,
        compiler_params=params(12),
        cost_estimate=pl.CostEstimate(
            flops=2 * rows * width * n_owners * capacity,
            bytes_accessed=2 * width * (rows + n_owners * capacity),
            transcendentals=0,
        ),
        name="place_rows",
    )(owner.reshape(1, rows), obs_feat)


def pool_kernel(capacity, slot_dev, slot_ref, embed_ref, code_ref, got_ref, keep_ref, send_ref):
    half = keep_ref.shape[0]
    places = 2 * half
    mine = slot_ref[0]
    total = jnp.zeros((places, keep_ref.shape[1]), F32)
    seen = jnp.zeros((places, capacity), F32)
    for block in range(got_ref.shape[0]):
        code = code_ref[block]
        turned = jnp.where(code >= half, code - half, code + half)
        code = jnp.where((code >= 0) & (mine == 1), turned, code)
        hot = (iota((places, capacity), 0) == code).astype(F32)
        seen += hot
        total += dot(hot.astype(BF16), got_ref[block])
    count = jnp.sum(seen, axis=1, keepdims=True)
    steps = embed_ref.shape[0]
    step_hot = iota((places, steps), 1) == iota((places, steps), 0) % slot_dev + mine * slot_dev
    embed = dot(step_hot.astype(F32).astype(BF16), embed_ref[...])
    tokens = (total / jnp.maximum(count, 1.0) + embed).astype(BF16)
    keep_ref[...] = tokens[:half]
    send_ref[...] = tokens[half:]


def pool_rows(my_slot, time_embed, codes, got, capacity, slot_dev):
    width = time_embed.shape[1]
    half = jax.ShapeDtypeStruct((CB * slot_dev // 2, width), BF16)
    return pl.pallas_call(
        functools.partial(pool_kernel, capacity, slot_dev),
        out_shape=[half, half],
        in_specs=[SCALARS] + [WHOLE] * 3,
        out_specs=[WHOLE] * 2,
        compiler_params=params(12),
        cost_estimate=pl.CostEstimate(
            flops=2 * CB * slot_dev * got.size, bytes_accessed=2 * got.size, transcendentals=0
        ),
        name="pool_rows",
    )(my_slot, time_embed, codes, got)


def weave_kernel(slot_dev, slot_ref, order_ref, keep_ref, got_ref, out_ref):
    rows, width = out_ref.shape
    half = keep_ref.shape[0]
    mine = slot_ref[0]
    row, col = iota((rows, half), 0), iota((rows, half), 1)
    source = col == row // TSTEPS * slot_dev + row % slot_dev
    own = row % TSTEPS // slot_dev == mine
    from_keep = (source & own).astype(F32).astype(BF16)
    from_got = (source & jnp.logical_not(own)).astype(F32).astype(BF16)
    tokens = (dot(from_keep, keep_ref[...]) + dot(from_got, got_ref[...])).astype(BF16)
    move = (iota((width, width), 0) == order_ref[...]).astype(F32).astype(BF16)
    out_ref[...] = dot(tokens, move).astype(BF16)


def weave_steps(my_slot, order, keep, got, slot_dev):
    rows, width = 2 * keep.shape[0], keep.shape[1]
    return pl.pallas_call(
        functools.partial(weave_kernel, slot_dev),
        out_shape=jax.ShapeDtypeStruct((rows, width), BF16),
        in_specs=[SCALARS] + [WHOLE] * 3,
        out_specs=WHOLE,
        compiler_params=params(12),
        cost_estimate=pl.CostEstimate(
            flops=2 * rows * width * (rows + width), bytes_accessed=4 * rows * width, transcendentals=0
        ),
        name="weave_steps",
    )(my_slot, order.reshape(1, width), keep, got)


def attention(normed, weight, heads_width, ctx_ref):
    rows = normed.shape[0]
    group = LANES
    lane = iota((1, LANES), 1)
    first = iota((group, LANES), 1) < HD
    masks = [(lane < HD).astype(F32).astype(BF16), (lane >= HD).astype(F32).astype(BF16)]
    ones = (iota((LANES, LANES), 0) // HD == iota((LANES, LANES), 1) // HD).astype(F32)
    mean = (ones * (1.0 / HD)).astype(BF16)
    ones = ones.astype(BF16)
    same_cell = iota((2 * group, group), 0) % group // TSTEPS == iota((2 * group, group), 1) // TSTEPS
    same_cell = same_cell.astype(F32).astype(BF16)
    count = jnp.ones((group, LANES), BF16)
    projected = dot(normed, weight)
    begins = range(0, rows, group)
    for at in range(0, heads_width, LANES):
        query = projected[:, at : at + LANES]
        key = projected[:, heads_width + at : heads_width + at + LANES]
        value = projected[:, 2 * heads_width + at : 2 * heads_width + at + LANES].astype(BF16)
        query_bf, key_bf = query.astype(BF16), key.astype(BF16)
        query = (query * lax.rsqrt(dot(query_bf * query_bf, ones) + HD * EPS)).astype(BF16)
        key = (key * lax.rsqrt(dot(key_bf * key_bf, mean) + EPS)).astype(BF16)
        left, right = query * masks[0], query * masks[1]
        scores = [
            dot_t(jnp.concatenate([left[at : at + group], right[at : at + group]], axis=0), key[at : at + group])
            for at in begins
        ]
        expos = [jnp.exp(score).astype(BF16) * same_cell for score in scores]
        mixed = [
            dot(expo, jnp.concatenate([value[at : at + group], count], axis=1)) for at, expo in zip(begins, expos)
        ]
        for begin, both in zip(begins, mixed):
            top, low = both[:group], both[group:]
            over = jnp.where(first, top[:, :LANES], low[:, :LANES])
            under = jnp.where(first, top[:, LANES:], low[:, LANES:])
            ctx_ref[begin : begin + group, at : at + LANES] = (over / under).astype(BF16)


def gated(normed, gate_w, up_w, down_w):
    gate = dot(normed, gate_w)
    up = dot(normed, up_w)
    hidden = (gate * (0.5 * jnp.tanh(0.5 * gate) + 0.5) * up).astype(BF16)
    return dot_t(hidden, down_w)


def put_rows_kernel(places, *refs):
    pieces, (out_ref, sems) = refs[:-2], refs[-2:]
    copies = []
    for number, ((row, at), piece) in enumerate(zip(places, pieces)):
        rows, columns = piece.shape
        target = out_ref.at[pl.ds(row, rows), pl.ds(at, columns)]
        copies.append(pltpu.make_async_copy(piece, target, sems.at[number]))
    for copy in copies:
        copy.start()
    for copy in copies:
        copy.wait()


def put_rows(pieces, rows, columns):
    return pl.pallas_call(
        functools.partial(put_rows_kernel, [(row, at) for _, row, at in pieces]),
        out_shape=jax.ShapeDtypeStruct((rows, columns), BF16),
        in_specs=[FAR] * len(pieces),
        out_specs=FAR,
        scratch_shapes=[pltpu.SemaphoreType.DMA((len(pieces),))],
        compiler_params=params(2),
        cost_estimate=pl.CostEstimate(flops=0, bytes_accessed=4 * rows * columns, transcendentals=0),
        name="put_rows",
    )(*[array for array, _, _ in pieces])


def layer_kernel(hidden_width, tok_ref, w_ref, out_ref, norm_ref, ctx_ref, acc_ref):
    heads_width = ctx_ref.shape[1]
    gate_at = 3 * heads_width
    up_at = gate_at + hidden_width
    out_at = up_at + hidden_width
    down_at = out_at + heads_width
    tokens = tok_ref[...].astype(F32)
    scale = lax.rsqrt(jnp.mean(tokens * tokens, axis=1, keepdims=True) + EPS)
    norm_ref[...] = (tokens * scale).astype(BF16)
    attention(norm_ref[...], w_ref[:, :gate_at], heads_width, ctx_ref)
    acc_ref[...] = dot_t(ctx_ref[...], w_ref[:, out_at:down_at])
    for begin in range(0, hidden_width, UNIT):
        gate_w, up_w, down_w = [w_ref[:, at + begin : at + begin + UNIT] for at in (gate_at, up_at, down_at)]
        add = gated(norm_ref[...], gate_w, up_w, down_w)
        if begin + UNIT < hidden_width:
            acc_ref[...] += add
        else:
            out_ref[...] = (acc_ref[...] + add).astype(out_ref.dtype)


def layer(tokens, weights, heads_width, hidden_width, out_type):
    rows, width = tokens.shape
    return pl.pallas_call(
        functools.partial(layer_kernel, hidden_width),
        out_shape=jax.ShapeDtypeStruct((rows, width), out_type),
        in_specs=[WHOLE] * 2,
        out_specs=WHOLE,
        scratch_shapes=[
            pltpu.VMEM((rows, width), BF16),
            pltpu.VMEM((rows, heads_width), BF16),
            pltpu.VMEM((rows, width), F32),
        ],
        compiler_params=params(26),
        cost_estimate=pl.CostEstimate(
            flops=2 * rows * width * weights.shape[1],
            bytes_accessed=2 * weights.size + 6 * rows * width,
            transcendentals=rows * hidden_width,
        ),
        name="layer",
    )(tokens, weights)


def finish_kernel(tok_ref, sum_ref, got_ref, order_ref, out_ref):
    width = out_ref.shape[1]
    mixed = (tok_ref[...].astype(F32) + sum_ref[...] + got_ref[...].astype(F32)).astype(BF16)
    move = (iota((width, width), 0) == order_ref[...]).astype(F32).astype(BF16)
    out_ref[...] = dot_t(mixed, move).astype(BF16)


def finish(tokens, sums, got, order):
    rows, width = tokens.shape
    return pl.pallas_call(
        finish_kernel,
        out_shape=jax.ShapeDtypeStruct((rows, width), BF16),
        in_specs=[WHOLE] * 4,
        out_specs=WHOLE,
        compiler_params=params(12),
        cost_estimate=pl.CostEstimate(
            flops=2 * rows * width * width, bytes_accessed=10 * rows * width, transcendentals=0
        ),
        name="finish",
    )(tokens, sums, got, order.reshape(1, width))


def side_by_side(w_qkv, w_out, w_gate_up, w_down):
    rows = w_qkv.shape[0]
    return jnp.concatenate([w_qkv.reshape(rows, -1), w_gate_up.reshape(rows, -1), w_out, w_down], axis=1)


def along_cells(values, distance):
    n_cells = lax.axis_size("cells")
    return lax.ppermute(values, "cells", [(j, (j - distance) % n_cells) for j in range(n_cells)])


def to_other_places(shares):
    n_slots = lax.axis_size("slots")
    n_share = lax.axis_size("groups") * n_slots
    places = [shares]
    for far in range(1, n_share):
        pairs = [(place, place ^ far) for place in range(n_share)]
        places.append(lax.ppermute(shares, ("groups", "slots"), pairs))
    return places


def to_other_places_by_halves(shares):
    swap = [(0, 1), (1, 0)]
    by_slot = lax.ppermute(shares, "slots", swap)
    by_group = lax.ppermute(shares, "groups", swap)
    cut = shares.shape[1] // 2
    left = lax.ppermute(by_slot[:, :cut], "groups", swap)
    right = lax.ppermute(by_group[:, cut:], "slots", swap)
    return [shares, by_slot, by_group, left, right]


def arrival_order(width, n_share):
    n_cells = lax.axis_size("cells")
    mine = lax.axis_index("cells")
    place = lax.axis_index("groups") * lax.axis_size("slots") + lax.axis_index("slots")
    rows = width // n_cells
    share = rows // n_share
    row = jnp.arange(width, dtype=jnp.int32)
    past = row - 2 * rows
    far = jnp.where(past < 0, row // share % n_share, past // (2 * share))
    distance = jnp.where(past < 0, n_cells - 1, 1 + past // share % 2)
    other = (mine + distance) % n_cells * rows + (far ^ place) * share + row % share
    return jnp.where(row < rows, mine * rows + row, other)


def tokens_by_exchanges(owner, position, obs_feat, time_embed, my_slot, capacity, slot_dev):
    n_slots = lax.axis_size("slots")
    n_owners = lax.axis_size("cells") * lax.axis_size("mp")
    rows, width = obs_feat.shape
    owners = jnp.arange(n_owners, dtype=jnp.int32)
    owner_hot = (owner[:, None] == owners[None, :]).astype(F32)
    row_ids = jnp.arange(rows, dtype=jnp.int32)
    lower = (row_ids[None, :] <= row_ids[:, None]).astype(BF16)
    running = dot(lower, owner_hot.astype(BF16))
    rank = jnp.sum(running * owner_hot, axis=1).astype(jnp.int32) - 1
    place = jnp.where(owner < n_owners, owner * capacity + rank, n_owners * capacity)
    place_ids = jnp.arange(n_owners * capacity, dtype=jnp.int32)
    taken = place_ids[:, None] == place[None, :]
    send_feat = dot(taken.astype(BF16), obs_feat).astype(BF16).reshape(n_owners, capacity, width)
    send_code = jnp.sum(jnp.where(taken, position[None, :] + 1, 0), axis=1).reshape(n_owners, capacity)
    axes = ("cells", "mp")
    got_feat = lax.all_to_all(send_feat, axes, split_axis=0, concat_axis=0, tiled=True).reshape(-1, width)
    got_code = lax.all_to_all(send_code, axes, split_axis=0, concat_axis=0, tiled=True).reshape(-1) - 1
    hot = (jnp.arange(CB * slot_dev, dtype=jnp.int32)[:, None] == got_code[None, :]).astype(BF16)
    count = jnp.sum(hot.astype(F32), axis=1)
    pooled = dot(hot, got_feat) / jnp.maximum(count, 1.0)[:, None]
    embed = lax.dynamic_slice_in_dim(time_embed, my_slot * slot_dev, slot_dev, 0).astype(F32)
    tokens = (pooled.reshape(CB, slot_dev, width) + embed[None]).astype(BF16)
    grid = tokens.reshape(n_slots, CB // n_slots, slot_dev, width)
    grid = lax.all_to_all(grid, "slots", split_axis=0, concat_axis=2, tiled=True)
    return grid.reshape(-1, width)


def on_device(obs_feat, obs_cell, obs_slot, obs_count, time_embed, w_qkv, w_out, w_gate_up, w_down):
    n_cells = lax.axis_size("cells")
    n_slots = lax.axis_size("slots")
    n_groups = lax.axis_size("groups")
    n_mp = lax.axis_size("mp")
    n_owners = n_cells * n_mp
    rows, width = obs_feat.shape
    capacity = 3 * rows // n_owners
    quarter = CB // n_slots
    slot_dev = TSTEPS // n_slots
    my_slot = lax.axis_index("slots")
    n_share = n_groups * n_slots
    share = w_qkv.shape[0] // n_share
    valid = jnp.arange(rows, dtype=jnp.int32) < obs_count[0]
    owner = obs_cell // (quarter * n_mp * n_slots) * n_mp + obs_cell // quarter % n_mp
    owner = jnp.where(valid, owner, n_owners)
    local = obs_cell // (quarter * n_mp) % n_slots * quarter + obs_cell % quarter
    position = local * slot_dev + obs_slot

    local_weights = (w_qkv, w_out.T, w_gate_up, w_down.T)
    which = lax.axis_index("groups") * n_slots + my_slot
    share_weights = [lax.dynamic_slice_in_dim(w, which * share, share, 0) for w in local_weights]
    share_rows = side_by_side(*share_weights)
    if n_slots == 2 and n_groups == 2 and n_cells == 4 and share % 16 == 0 and capacity % 16 == 0:
        order = arrival_order(width, n_share)
        below = along_cells(share_rows, -1)
        codes, embed = place_codes(owner, position, time_embed, n_owners, capacity)
        codes = lax.all_to_all(codes, ("cells", "mp"), split_axis=0, concat_axis=0, tiled=True)
        below, codes, share_rows = lax.optimization_barrier((below, codes, share_rows))
        first = to_other_places(below)
        blocks = place_rows(owner, obs_feat, n_owners, capacity)
        above, opposite = along_cells(share_rows, 1), along_cells(below, -1)
        blocks, above, opposite, first = lax.optimization_barrier((blocks, above, opposite, first))
        second = to_other_places_by_halves(jnp.concatenate([above, opposite], axis=0))
        shard = side_by_side(*local_weights)
        got = lax.all_to_all(blocks, ("cells", "mp"), split_axis=0, concat_axis=0, tiled=True)
        got, shard, second = lax.optimization_barrier((got, shard, second))
        keep, send = pool_rows(my_slot.reshape(1), embed, codes, got, capacity, slot_dev)
        other = lax.ppermute(send, "slots", [(0, 1), (1, 0)])
        pieces, row = [], 0
        for array in [shard] + first + second[:3]:
            pieces.append((array, row, 0))
            row += array.shape[0]
        pieces += [(second[3], row, 0), (second[4], row, second[3].shape[1])]
        tokens = weave_steps(my_slot.reshape(1), order, keep, other, slot_dev)
        tokens, arrays = lax.optimization_barrier((tokens, [array for array, _, _ in pieces]))
        weights = put_rows([(array, row, at) for array, (_, row, at) in zip(arrays, pieces)], width, shard.shape[1])
    else:
        order = jnp.arange(width, dtype=jnp.int32)
        weights = lax.all_gather(share_rows, ("cells", "groups", "slots"), axis=0, tiled=True)
        tokens = tokens_by_exchanges(owner, position, obs_feat, time_embed, my_slot, capacity, slot_dev)

    swap = [(0, 1), (1, 0)]
    heads_width, hidden_width = w_qkv.shape[2], w_gate_up.shape[2]
    partner = lax.ppermute(tokens, "mp", swap)
    for_partner = layer(partner, weights, heads_width, hidden_width, BF16)
    from_partner = lax.ppermute(for_partner, "mp", swap)
    own = layer(tokens, weights, heads_width, hidden_width, F32)
    return finish(tokens, own, from_partner, order).reshape(quarter, TSTEPS, width)


def solution(mesh):
    placed = (
        P(("groups", "cells", "slots", "mp"), None),
        P(("groups", "cells", "slots", "mp")),
        P(("groups", "cells", "slots", "mp")),
        P(("groups", "cells", "slots", "mp")),
        P(),
        P("cells", None, "mp"),
        P("mp", "cells"),
        P("cells", None, "mp"),
        P("mp", "cells"),
    )
    return jax.shard_map(
        on_device,
        mesh=mesh,
        in_specs=placed,
        out_specs=P(("groups", "cells", "slots", "mp"), None, None),
        check_vma=False,
    )
```

```python
import functools

import jax
import jax.numpy as jnp
from jax import lax
from jax.experimental import pallas as pl
from jax.experimental.pallas import tpu as pltpu
from jax.sharding import PartitionSpec as P

HD = 64
TSTEPS = 8
CB = 128
EPS = 1e-06

CODE = 32
UNIT = 512
LANES = 128
MIB = 1024 * 1024
F32 = jnp.float32
BF16 = jnp.bfloat16
WHOLE = pl.BlockSpec(memory_space=pltpu.VMEM)
SCALARS = pl.BlockSpec(memory_space=pltpu.SMEM)
FAR = pl.BlockSpec(memory_space=pl.ANY)


def iota(shape, axis):
    return lax.broadcasted_iota(jnp.int32, shape, axis)


def dot(left, right):
    return jnp.dot(left, right, preferred_element_type=F32)


def dot_t(left, right):
    return lax.dot_general(left, right, (((1,), (1,)), ((), ())), preferred_element_type=F32)


def params(mib):
    return pltpu.CompilerParams(vmem_limit_bytes=mib * MIB)


def block_places(owner, n_owners):
    rows = owner.shape[1]
    owner_hot = (iota((n_owners, rows), 0) == owner).astype(F32)
    upper = (iota((rows, rows), 0) <= iota((rows, rows), 1)).astype(BF16)
    running = dot(owner_hot.astype(BF16), upper)
    return jnp.sum(running * owner_hot, axis=0, keepdims=True).astype(jnp.int32) - 1


def one_hot_rows(owner, rank, block, capacity):
    place = jnp.where(owner == block, rank, -1)
    return (iota((capacity, owner.shape[1]), 0) == place).astype(F32).astype(BF16)


def code_kernel(owner_ref, position_ref, time_ref, code_ref, embed_ref):
    n_owners, _, capacity = code_ref.shape
    embed_ref[...] = time_ref[...]
    owner = owner_ref[...]
    rank = block_places(owner, n_owners)
    code = position_ref[...] + 1
    line = iota((8, owner.shape[1]), 0)
    digits = jnp.where(line == 0, code // CODE, jnp.where(line == 1, code % CODE, 0))
    digits = digits.astype(F32).astype(BF16)
    for block in range(n_owners):
        sent = dot_t(digits, one_hot_rows(owner, rank, block, capacity))
        code_ref[block] = (sent[0:1] * CODE + sent[1:2]).astype(jnp.int32) - 1


def place_codes(owner, position, time_embed, n_owners, capacity):
    rows = owner.shape[0]
    return pl.pallas_call(
        code_kernel,
        out_shape=[
            jax.ShapeDtypeStruct((n_owners, 1, capacity), jnp.int32),
            jax.ShapeDtypeStruct(time_embed.shape, BF16),
        ],
        in_specs=[WHOLE] * 3,
        out_specs=[WHOLE] * 2,
        compiler_params=params(12),
        cost_estimate=pl.CostEstimate(
            flops=16 * rows * n_owners * capacity, bytes_accessed=8 * rows, transcendentals=0
        ),
        name="place_codes",
    )(owner.reshape(1, rows), position.reshape(1, rows), time_embed)


def place_kernel(owner_ref, feat_ref, out_ref):
    n_owners, capacity, _ = out_ref.shape
    owner = owner_ref[...]
    rank = block_places(owner, n_owners)
    feat = feat_ref[...]
    for block in range(n_owners):
        out_ref[block] = dot(one_hot_rows(owner, rank, block, capacity), feat).astype(BF16)


def place_rows(owner, obs_feat, n_owners, capacity):
    rows, width = obs_feat.shape
    return pl.pallas_call(
        place_kernel,
        out_shape=jax.ShapeDtypeStruct((n_owners, capacity, width), BF16),
        in_specs=[WHOLE] * 2,
        out_specs=WHOLE,
        compiler_params=params(12),
        cost_estimate=pl.CostEstimate(
            flops=2 * rows * width * n_owners * capacity,
            bytes_accessed=2 * width * (rows + n_owners * capacity),
            transcendentals=0,
        ),
        name="place_rows",
    )(owner.reshape(1, rows), obs_feat)


def pool_kernel(capacity, slot_dev, slot_ref, embed_ref, code_ref, got_ref, keep_ref, send_ref):
    half = keep_ref.shape[0]
    places = 2 * half
    mine = slot_ref[0]
    total = jnp.zeros((places, keep_ref.shape[1]), F32)
    seen = jnp.zeros((places, capacity), F32)
    for block in range(got_ref.shape[0]):
        code = code_ref[block]
        turned = jnp.where(code >= half, code - half, code + half)
        code = jnp.where((code >= 0) & (mine == 1), turned, code)
        hot = (iota((places, capacity), 0) == code).astype(F32)
        seen += hot
        total += dot(hot.astype(BF16), got_ref[block])
    count = jnp.sum(seen, axis=1, keepdims=True)
    steps = embed_ref.shape[0]
    step_hot = iota((places, steps), 1) == iota((places, steps), 0) % slot_dev + mine * slot_dev
    embed = dot(step_hot.astype(F32).astype(BF16), embed_ref[...])
    tokens = (total / jnp.maximum(count, 1.0) + embed).astype(BF16)
    keep_ref[...] = tokens[:half]
    send_ref[...] = tokens[half:]


def pool_rows(my_slot, time_embed, codes, got, capacity, slot_dev):
    width = time_embed.shape[1]
    half = jax.ShapeDtypeStruct((CB * slot_dev // 2, width), BF16)
    return pl.pallas_call(
        functools.partial(pool_kernel, capacity, slot_dev),
        out_shape=[half, half],
        in_specs=[SCALARS] + [WHOLE] * 3,
        out_specs=[WHOLE] * 2,
        compiler_params=params(12),
        cost_estimate=pl.CostEstimate(
            flops=2 * CB * slot_dev * got.size, bytes_accessed=2 * got.size, transcendentals=0
        ),
        name="pool_rows",
    )(my_slot, time_embed, codes, got)


def weave_kernel(slot_dev, slot_ref, order_ref, keep_ref, got_ref, out_ref):
    rows, width = out_ref.shape
    half = keep_ref.shape[0]
    mine = slot_ref[0]
    row, col = iota((rows, half), 0), iota((rows, half), 1)
    source = col == row // TSTEPS * slot_dev + row % slot_dev
    own = row % TSTEPS // slot_dev == mine
    from_keep = (source & own).astype(F32).astype(BF16)
    from_got = (source & jnp.logical_not(own)).astype(F32).astype(BF16)
    tokens = (dot(from_keep, keep_ref[...]) + dot(from_got, got_ref[...])).astype(BF16)
    move = (iota((width, width), 0) == order_ref[...]).astype(F32).astype(BF16)
    out_ref[...] = dot(tokens, move).astype(BF16)


def weave_steps(my_slot, order, keep, got, slot_dev):
    rows, width = 2 * keep.shape[0], keep.shape[1]
    return pl.pallas_call(
        functools.partial(weave_kernel, slot_dev),
        out_shape=jax.ShapeDtypeStruct((rows, width), BF16),
        in_specs=[SCALARS] + [WHOLE] * 3,
        out_specs=WHOLE,
        compiler_params=params(12),
        cost_estimate=pl.CostEstimate(
            flops=2 * rows * width * (rows + width), bytes_accessed=4 * rows * width, transcendentals=0
        ),
        name="weave_steps",
    )(my_slot, order.reshape(1, width), keep, got)


def attention(normed, weight, heads_width, ctx_ref):
    rows = normed.shape[0]
    group = LANES
    lane = iota((1, LANES), 1)
    first = iota((group, LANES), 1) < HD
    masks = [(lane < HD).astype(F32).astype(BF16), (lane >= HD).astype(F32).astype(BF16)]
    ones = (iota((LANES, LANES), 0) // HD == iota((LANES, LANES), 1) // HD).astype(F32)
    mean = (ones * (1.0 / HD)).astype(BF16)
    ones = ones.astype(BF16)
    same_cell = iota((2 * group, group), 0) % group // TSTEPS == iota((2 * group, group), 1) // TSTEPS
    same_cell = same_cell.astype(F32).astype(BF16)
    count = jnp.ones((group, LANES), BF16)
    projected = dot(normed, weight)
    begins = range(0, rows, group)
    for at in range(0, heads_width, LANES):
        query = projected[:, at : at + LANES]
        key = projected[:, heads_width + at : heads_width + at + LANES]
        value = projected[:, 2 * heads_width + at : 2 * heads_width + at + LANES].astype(BF16)
        query_bf, key_bf = query.astype(BF16), key.astype(BF16)
        query = (query * lax.rsqrt(dot(query_bf * query_bf, ones) + HD * EPS)).astype(BF16)
        key = (key * lax.rsqrt(dot(key_bf * key_bf, mean) + EPS)).astype(BF16)
        left, right = query * masks[0], query * masks[1]
        scores = [
            dot_t(jnp.concatenate([left[at : at + group], right[at : at + group]], axis=0), key[at : at + group])
            for at in begins
        ]
        expos = [jnp.exp(score).astype(BF16) * same_cell for score in scores]
        mixed = [
            dot(expo, jnp.concatenate([value[at : at + group], count], axis=1)) for at, expo in zip(begins, expos)
        ]
        for begin, both in zip(begins, mixed):
            top, low = both[:group], both[group:]
            over = jnp.where(first, top[:, :LANES], low[:, :LANES])
            under = jnp.where(first, top[:, LANES:], low[:, LANES:])
            ctx_ref[begin : begin + group, at : at + LANES] = (over / under).astype(BF16)


def gated(normed, gate_w, up_w, down_w):
    gate = dot(normed, gate_w)
    up = dot(normed, up_w)
    hidden = (gate * (0.5 * jnp.tanh(0.5 * gate) + 0.5) * up).astype(BF16)
    return dot_t(hidden, down_w)


def put_rows_kernel(places, *refs):
    pieces, (out_ref, sems) = refs[:-2], refs[-2:]
    copies = []
    for number, ((row, at), piece) in enumerate(zip(places, pieces)):
        rows, columns = piece.shape
        target = out_ref.at[pl.ds(row, rows), pl.ds(at, columns)]
        copies.append(pltpu.make_async_copy(piece, target, sems.at[number]))
    for copy in copies:
        copy.start()
    for copy in copies:
        copy.wait()


def put_rows(pieces, rows, columns):
    return pl.pallas_call(
        functools.partial(put_rows_kernel, [(row, at) for _, row, at in pieces]),
        out_shape=jax.ShapeDtypeStruct((rows, columns), BF16),
        in_specs=[FAR] * len(pieces),
        out_specs=WHOLE,
        scratch_shapes=[pltpu.SemaphoreType.DMA((len(pieces),))],
        compiler_params=params(53),
        cost_estimate=pl.CostEstimate(flops=0, bytes_accessed=4 * rows * columns, transcendentals=0),
        name="put_rows",
    )(*[array for array, _, _ in pieces])


def layer_kernel(hidden_width, tok_ref, w_ref, out_ref, norm_ref, ctx_ref, acc_ref):
    heads_width = ctx_ref.shape[1]
    gate_at = 3 * heads_width
    up_at = gate_at + hidden_width
    out_at = up_at + hidden_width
    down_at = out_at + heads_width
    tokens = tok_ref[...].astype(F32)
    scale = lax.rsqrt(jnp.mean(tokens * tokens, axis=1, keepdims=True) + EPS)
    norm_ref[...] = (tokens * scale).astype(BF16)
    attention(norm_ref[...], w_ref[:, :gate_at], heads_width, ctx_ref)
    acc_ref[...] = dot_t(ctx_ref[...], w_ref[:, out_at:down_at])
    for begin in range(0, hidden_width, UNIT):
        gate_w, up_w, down_w = [w_ref[:, at + begin : at + begin + UNIT] for at in (gate_at, up_at, down_at)]
        add = gated(norm_ref[...], gate_w, up_w, down_w)
        if begin + UNIT < hidden_width:
            acc_ref[...] += add
        else:
            out_ref[...] = (acc_ref[...] + add).astype(out_ref.dtype)


def layer(tokens, weights, heads_width, hidden_width, out_type):
    rows, width = tokens.shape
    return pl.pallas_call(
        functools.partial(layer_kernel, hidden_width),
        out_shape=jax.ShapeDtypeStruct((rows, width), out_type),
        in_specs=[WHOLE] * 2,
        out_specs=WHOLE,
        scratch_shapes=[
            pltpu.VMEM((rows, width), BF16),
            pltpu.VMEM((rows, heads_width), BF16),
            pltpu.VMEM((rows, width), F32),
        ],
        compiler_params=params(26),
        cost_estimate=pl.CostEstimate(
            flops=2 * rows * width * weights.shape[1],
            bytes_accessed=2 * weights.size + 6 * rows * width,
            transcendentals=rows * hidden_width,
        ),
        name="layer",
    )(tokens, weights)


def finish_kernel(tok_ref, sum_ref, got_ref, order_ref, out_ref):
    width = out_ref.shape[1]
    mixed = (tok_ref[...].astype(F32) + sum_ref[...] + got_ref[...].astype(F32)).astype(BF16)
    move = (iota((width, width), 0) == order_ref[...]).astype(F32).astype(BF16)
    out_ref[...] = dot_t(mixed, move).astype(BF16)


def finish(tokens, sums, got, order):
    rows, width = tokens.shape
    return pl.pallas_call(
        finish_kernel,
        out_shape=jax.ShapeDtypeStruct((rows, width), BF16),
        in_specs=[WHOLE] * 4,
        out_specs=WHOLE,
        compiler_params=params(12),
        cost_estimate=pl.CostEstimate(
            flops=2 * rows * width * width, bytes_accessed=10 * rows * width, transcendentals=0
        ),
        name="finish",
    )(tokens, sums, got, order.reshape(1, width))


def side_by_side(w_qkv, w_out, w_gate_up, w_down):
    rows = w_qkv.shape[0]
    return jnp.concatenate([w_qkv.reshape(rows, -1), w_gate_up.reshape(rows, -1), w_out, w_down], axis=1)


def along_cells(values, distance):
    n_cells = lax.axis_size("cells")
    return lax.ppermute(values, "cells", [(j, (j - distance) % n_cells) for j in range(n_cells)])


def to_other_places(shares):
    n_slots = lax.axis_size("slots")
    n_share = lax.axis_size("groups") * n_slots
    places = [shares]
    for far in range(1, n_share):
        pairs = [(place, place ^ far) for place in range(n_share)]
        places.append(lax.ppermute(shares, ("groups", "slots"), pairs))
    return places


def to_other_places_by_halves(shares):
    swap = [(0, 1), (1, 0)]
    by_slot = lax.ppermute(shares, "slots", swap)
    by_group = lax.ppermute(shares, "groups", swap)
    cut = shares.shape[1] // 2
    left = lax.ppermute(by_slot[:, :cut], "groups", swap)
    right = lax.ppermute(by_group[:, cut:], "slots", swap)
    return [shares, by_slot, by_group, left, right]


def arrival_order(width, n_share):
    n_cells = lax.axis_size("cells")
    mine = lax.axis_index("cells")
    place = lax.axis_index("groups") * lax.axis_size("slots") + lax.axis_index("slots")
    rows = width // n_cells
    share = rows // n_share
    row = jnp.arange(width, dtype=jnp.int32)
    past = row - 2 * rows
    far = jnp.where(past < 0, row // share % n_share, past // (2 * share))
    distance = jnp.where(past < 0, n_cells - 1, 1 + past // share % 2)
    other = (mine + distance) % n_cells * rows + (far ^ place) * share + row % share
    return jnp.where(row < rows, mine * rows + row, other)


def tokens_by_exchanges(owner, position, obs_feat, time_embed, my_slot, capacity, slot_dev):
    n_slots = lax.axis_size("slots")
    n_owners = lax.axis_size("cells") * lax.axis_size("mp")
    rows, width = obs_feat.shape
    owners = jnp.arange(n_owners, dtype=jnp.int32)
    owner_hot = (owner[:, None] == owners[None, :]).astype(F32)
    row_ids = jnp.arange(rows, dtype=jnp.int32)
    lower = (row_ids[None, :] <= row_ids[:, None]).astype(BF16)
    running = dot(lower, owner_hot.astype(BF16))
    rank = jnp.sum(running * owner_hot, axis=1).astype(jnp.int32) - 1
    place = jnp.where(owner < n_owners, owner * capacity + rank, n_owners * capacity)
    place_ids = jnp.arange(n_owners * capacity, dtype=jnp.int32)
    taken = place_ids[:, None] == place[None, :]
    send_feat = dot(taken.astype(BF16), obs_feat).astype(BF16).reshape(n_owners, capacity, width)
    send_code = jnp.sum(jnp.where(taken, position[None, :] + 1, 0), axis=1).reshape(n_owners, capacity)
    axes = ("cells", "mp")
    got_feat = lax.all_to_all(send_feat, axes, split_axis=0, concat_axis=0, tiled=True).reshape(-1, width)
    got_code = lax.all_to_all(send_code, axes, split_axis=0, concat_axis=0, tiled=True).reshape(-1) - 1
    hot = (jnp.arange(CB * slot_dev, dtype=jnp.int32)[:, None] == got_code[None, :]).astype(BF16)
    count = jnp.sum(hot.astype(F32), axis=1)
    pooled = dot(hot, got_feat) / jnp.maximum(count, 1.0)[:, None]
    embed = lax.dynamic_slice_in_dim(time_embed, my_slot * slot_dev, slot_dev, 0).astype(F32)
    tokens = (pooled.reshape(CB, slot_dev, width) + embed[None]).astype(BF16)
    grid = tokens.reshape(n_slots, CB // n_slots, slot_dev, width)
    grid = lax.all_to_all(grid, "slots", split_axis=0, concat_axis=2, tiled=True)
    return grid.reshape(-1, width)


def on_device(obs_feat, obs_cell, obs_slot, obs_count, time_embed, w_qkv, w_out, w_gate_up, w_down):
    n_cells = lax.axis_size("cells")
    n_slots = lax.axis_size("slots")
    n_groups = lax.axis_size("groups")
    n_mp = lax.axis_size("mp")
    n_owners = n_cells * n_mp
    rows, width = obs_feat.shape
    capacity = 3 * rows // n_owners
    quarter = CB // n_slots
    slot_dev = TSTEPS // n_slots
    my_slot = lax.axis_index("slots")
    n_share = n_groups * n_slots
    share = w_qkv.shape[0] // n_share
    valid = jnp.arange(rows, dtype=jnp.int32) < obs_count[0]
    owner = obs_cell // (quarter * n_mp * n_slots) * n_mp + obs_cell // quarter % n_mp
    owner = jnp.where(valid, owner, n_owners)
    local = obs_cell // (quarter * n_mp) % n_slots * quarter + obs_cell % quarter
    position = local * slot_dev + obs_slot

    local_weights = (w_qkv, w_out.T, w_gate_up, w_down.T)
    which = lax.axis_index("groups") * n_slots + my_slot
    share_weights = [lax.dynamic_slice_in_dim(w, which * share, share, 0) for w in local_weights]
    share_rows = side_by_side(*share_weights)
    if n_slots == 2 and n_groups == 2 and n_cells == 4 and share % 16 == 0 and capacity % 16 == 0:
        order = arrival_order(width, n_share)
        below = along_cells(share_rows, -1)
        codes, embed = place_codes(owner, position, time_embed, n_owners, capacity)
        codes = lax.all_to_all(codes, ("cells", "mp"), split_axis=0, concat_axis=0, tiled=True)
        below, codes, share_rows = lax.optimization_barrier((below, codes, share_rows))
        first = to_other_places(below)
        blocks = place_rows(owner, obs_feat, n_owners, capacity)
        above, opposite = along_cells(share_rows, 1), along_cells(below, -1)
        blocks, above, opposite, first = lax.optimization_barrier((blocks, above, opposite, first))
        second = to_other_places_by_halves(jnp.concatenate([above, opposite], axis=0))
        shard = side_by_side(*local_weights)
        got = lax.all_to_all(blocks, ("cells", "mp"), split_axis=0, concat_axis=0, tiled=True)
        got, shard, second = lax.optimization_barrier((got, shard, second))
        keep, send = pool_rows(my_slot.reshape(1), embed, codes, got, capacity, slot_dev)
        other = lax.ppermute(send, "slots", [(0, 1), (1, 0)])
        pieces, row = [], 0
        for array in [shard] + first + second[:3]:
            pieces.append((array, row, 0))
            row += array.shape[0]
        pieces += [(second[3], row, 0), (second[4], row, second[3].shape[1])]
        tokens = weave_steps(my_slot.reshape(1), order, keep, other, slot_dev)
        tokens, arrays = lax.optimization_barrier((tokens, [array for array, _, _ in pieces]))
        weights = put_rows([(array, row, at) for array, (_, row, at) in zip(arrays, pieces)], width, shard.shape[1])
    else:
        order = jnp.arange(width, dtype=jnp.int32)
        weights = lax.all_gather(share_rows, ("cells", "groups", "slots"), axis=0, tiled=True)
        tokens = tokens_by_exchanges(owner, position, obs_feat, time_embed, my_slot, capacity, slot_dev)

    swap = [(0, 1), (1, 0)]
    heads_width, hidden_width = w_qkv.shape[2], w_gate_up.shape[2]
    partner = lax.ppermute(tokens, "mp", swap)
    for_partner = layer(partner, weights, heads_width, hidden_width, BF16)
    from_partner = lax.ppermute(for_partner, "mp", swap)
    own = layer(tokens, weights, heads_width, hidden_width, F32)
    return finish(tokens, own, from_partner, order).reshape(quarter, TSTEPS, width)


def solution(mesh):
    placed = (
        P(("groups", "cells", "slots", "mp"), None),
        P(("groups", "cells", "slots", "mp")),
        P(("groups", "cells", "slots", "mp")),
        P(("groups", "cells", "slots", "mp")),
        P(),
        P("cells", None, "mp"),
        P("mp", "cells"),
        P("cells", None, "mp"),
        P("mp", "cells"),
    )
    return jax.shard_map(
        on_device,
        mesh=mesh,
        in_specs=placed,
        out_specs=P(("groups", "cells", "slots", "mp"), None, None),
        check_vma=False,
    )
```

```python
import functools

import jax
import jax.numpy as jnp
from jax import lax
from jax.experimental import pallas as pl
from jax.experimental.pallas import tpu as pltpu
from jax.sharding import PartitionSpec as P

HD = 64
TSTEPS = 8
CB = 128
EPS = 1e-06

CODE = 32
UNIT = 512
LANES = 128
MIB = 1024 * 1024
F32 = jnp.float32
BF16 = jnp.bfloat16
WHOLE = pl.BlockSpec(memory_space=pltpu.VMEM)
SCALARS = pl.BlockSpec(memory_space=pltpu.SMEM)
FAR = pl.BlockSpec(memory_space=pl.ANY)


def iota(shape, axis):
    return lax.broadcasted_iota(jnp.int32, shape, axis)


def dot(left, right):
    return jnp.dot(left, right, preferred_element_type=F32)


def dot_t(left, right):
    return lax.dot_general(left, right, (((1,), (1,)), ((), ())), preferred_element_type=F32)


def params(mib):
    return pltpu.CompilerParams(vmem_limit_bytes=mib * MIB)


def block_places(owner, n_owners):
    rows = owner.shape[1]
    owner_hot = (iota((n_owners, rows), 0) == owner).astype(F32)
    upper = (iota((rows, rows), 0) <= iota((rows, rows), 1)).astype(BF16)
    running = dot(owner_hot.astype(BF16), upper)
    return jnp.sum(running * owner_hot, axis=0, keepdims=True).astype(jnp.int32) - 1


def one_hot_rows(owner, rank, block, capacity):
    place = jnp.where(owner == block, rank, -1)
    return (iota((capacity, owner.shape[1]), 0) == place).astype(F32).astype(BF16)


def code_kernel(owner_ref, position_ref, time_ref, code_ref, embed_ref):
    n_owners, _, capacity = code_ref.shape
    embed_ref[...] = time_ref[...]
    owner = owner_ref[...]
    rank = block_places(owner, n_owners)
    code = position_ref[...] + 1
    line = iota((8, owner.shape[1]), 0)
    digits = jnp.where(line == 0, code // CODE, jnp.where(line == 1, code % CODE, 0))
    digits = digits.astype(F32).astype(BF16)
    for block in range(n_owners):
        sent = dot_t(digits, one_hot_rows(owner, rank, block, capacity))
        code_ref[block] = (sent[0:1] * CODE + sent[1:2]).astype(jnp.int32) - 1


def place_codes(owner, position, time_embed, n_owners, capacity):
    rows = owner.shape[0]
    return pl.pallas_call(
        code_kernel,
        out_shape=[
            jax.ShapeDtypeStruct((n_owners, 1, capacity), jnp.int32),
            jax.ShapeDtypeStruct(time_embed.shape, BF16),
        ],
        in_specs=[WHOLE] * 3,
        out_specs=[WHOLE] * 2,
        compiler_params=params(12),
        cost_estimate=pl.CostEstimate(
            flops=16 * rows * n_owners * capacity, bytes_accessed=8 * rows, transcendentals=0
        ),
        name="place_codes",
    )(owner.reshape(1, rows), position.reshape(1, rows), time_embed)


def place_kernel(owner_ref, feat_ref, out_ref):
    n_owners, capacity, _ = out_ref.shape
    owner = owner_ref[...]
    rank = block_places(owner, n_owners)
    feat = feat_ref[...]
    for block in range(n_owners):
        out_ref[block] = dot(one_hot_rows(owner, rank, block, capacity), feat).astype(BF16)


def place_rows(owner, obs_feat, n_owners, capacity):
    rows, width = obs_feat.shape
    return pl.pallas_call(
        place_kernel,
        out_shape=jax.ShapeDtypeStruct((n_owners, capacity, width), BF16),
        in_specs=[WHOLE] * 2,
        out_specs=WHOLE,
        compiler_params=params(12),
        cost_estimate=pl.CostEstimate(
            flops=2 * rows * width * n_owners * capacity,
            bytes_accessed=2 * width * (rows + n_owners * capacity),
            transcendentals=0,
        ),
        name="place_rows",
    )(owner.reshape(1, rows), obs_feat)


def pool_kernel(capacity, slot_dev, slot_ref, embed_ref, code_ref, got_ref, keep_ref, send_ref):
    half = keep_ref.shape[0]
    places = 2 * half
    mine = slot_ref[0]
    total = jnp.zeros((places, keep_ref.shape[1]), F32)
    seen = jnp.zeros((places, capacity), F32)
    for block in range(got_ref.shape[0]):
        code = code_ref[block]
        turned = jnp.where(code >= half, code - half, code + half)
        code = jnp.where((code >= 0) & (mine == 1), turned, code)
        hot = (iota((places, capacity), 0) == code).astype(F32)
        seen += hot
        total += dot(hot.astype(BF16), got_ref[block])
    count = jnp.sum(seen, axis=1, keepdims=True)
    steps = embed_ref.shape[0]
    step_hot = iota((places, steps), 1) == iota((places, steps), 0) % slot_dev + mine * slot_dev
    embed = dot(step_hot.astype(F32).astype(BF16), embed_ref[...])
    tokens = (total / jnp.maximum(count, 1.0) + embed).astype(BF16)
    keep_ref[...] = tokens[:half]
    send_ref[...] = tokens[half:]


def pool_rows(my_slot, time_embed, codes, got, capacity, slot_dev):
    width = time_embed.shape[1]
    half = jax.ShapeDtypeStruct((CB * slot_dev // 2, width), BF16)
    return pl.pallas_call(
        functools.partial(pool_kernel, capacity, slot_dev),
        out_shape=[half, half],
        in_specs=[SCALARS] + [WHOLE] * 3,
        out_specs=[WHOLE] * 2,
        compiler_params=params(12),
        cost_estimate=pl.CostEstimate(
            flops=2 * CB * slot_dev * got.size, bytes_accessed=2 * got.size, transcendentals=0
        ),
        name="pool_rows",
    )(my_slot, time_embed, codes, got)


def weave_kernel(slot_dev, slot_ref, order_ref, keep_ref, got_ref, out_ref):
    rows, width = out_ref.shape
    half = keep_ref.shape[0]
    mine = slot_ref[0]
    row, col = iota((rows, half), 0), iota((rows, half), 1)
    source = col == row // TSTEPS * slot_dev + row % slot_dev
    own = row % TSTEPS // slot_dev == mine
    from_keep = (source & own).astype(F32).astype(BF16)
    from_got = (source & jnp.logical_not(own)).astype(F32).astype(BF16)
    tokens = (dot(from_keep, keep_ref[...]) + dot(from_got, got_ref[...])).astype(BF16)
    move = (iota((width, width), 0) == order_ref[...]).astype(F32).astype(BF16)
    out_ref[...] = dot(tokens, move).astype(BF16)


def weave_steps(my_slot, order, keep, got, slot_dev):
    rows, width = 2 * keep.shape[0], keep.shape[1]
    return pl.pallas_call(
        functools.partial(weave_kernel, slot_dev),
        out_shape=jax.ShapeDtypeStruct((rows, width), BF16),
        in_specs=[SCALARS] + [WHOLE] * 3,
        out_specs=WHOLE,
        compiler_params=params(12),
        cost_estimate=pl.CostEstimate(
            flops=2 * rows * width * (rows + width), bytes_accessed=4 * rows * width, transcendentals=0
        ),
        name="weave_steps",
    )(my_slot, order.reshape(1, width), keep, got)


def attention(normed, weight, heads_width, ctx_ref):
    rows = normed.shape[0]
    group = LANES
    lane = iota((1, LANES), 1)
    first = iota((group, LANES), 1) < HD
    masks = [(lane < HD).astype(F32).astype(BF16), (lane >= HD).astype(F32).astype(BF16)]
    ones = (iota((LANES, LANES), 0) // HD == iota((LANES, LANES), 1) // HD).astype(F32)
    mean = (ones * (1.0 / HD)).astype(BF16)
    ones = ones.astype(BF16)
    same_cell = iota((2 * group, group), 0) % group // TSTEPS == iota((2 * group, group), 1) // TSTEPS
    same_cell = same_cell.astype(F32).astype(BF16)
    count = jnp.ones((group, LANES), BF16)
    projected = dot(normed, weight)
    begins = range(0, rows, group)
    for at in range(0, heads_width, LANES):
        query = projected[:, at : at + LANES]
        key = projected[:, heads_width + at : heads_width + at + LANES]
        value = projected[:, 2 * heads_width + at : 2 * heads_width + at + LANES].astype(BF16)
        query_bf, key_bf = query.astype(BF16), key.astype(BF16)
        query = (query * lax.rsqrt(dot(query_bf * query_bf, ones) + HD * EPS)).astype(BF16)
        key = (key * lax.rsqrt(dot(key_bf * key_bf, mean) + EPS)).astype(BF16)
        left, right = query * masks[0], query * masks[1]
        scores = [
            dot_t(jnp.concatenate([left[at : at + group], right[at : at + group]], axis=0), key[at : at + group])
            for at in begins
        ]
        expos = [jnp.exp(score).astype(BF16) * same_cell for score in scores]
        mixed = [
            dot(expo, jnp.concatenate([value[at : at + group], count], axis=1)) for at, expo in zip(begins, expos)
        ]
        for begin, both in zip(begins, mixed):
            top, low = both[:group], both[group:]
            over = jnp.where(first, top[:, :LANES], low[:, :LANES])
            under = jnp.where(first, top[:, LANES:], low[:, LANES:])
            ctx_ref[begin : begin + group, at : at + LANES] = (over / under).astype(BF16)


def gated(normed, gate_w, up_w, down_w):
    gate = dot(normed, gate_w)
    up = dot(normed, up_w)
    hidden = (gate * (0.5 * jnp.tanh(0.5 * gate) + 0.5) * up).astype(BF16)
    return dot_t(hidden, down_w)


def put_rows_kernel(plan, *refs):
    sems, outs, pieces = refs[-1], refs[-3:-1], refs[:-3]
    copies = []
    for number, (piece, out, source, row, at, size) in enumerate(plan):
        rows = pieces[piece].shape[0]
        target = outs[out].at[pl.ds(row, rows), pl.ds(at, size)]
        copies.append(pltpu.make_async_copy(pieces[piece].at[:, pl.ds(source, size)], target, sems.at[number]))
    for copy in copies:
        copy.start()
    for copy in copies:
        copy.wait()


def put_rows(pieces, rows, heads_width, hidden_width):
    gate_at, out_at = 3 * heads_width, 3 * heads_width + 2 * hidden_width
    down_at = out_at + heads_width
    end = down_at + hidden_width
    runs = [(0, gate_at, 0, 0), (gate_at, out_at, 1, 0), (out_at, down_at, 0, gate_at), (down_at, end, 1, 2 * hidden_width)]
    plan = []
    for left, right, out, shift in runs:
        for number, (array, row, at) in enumerate(pieces):
            low, high = max(left, at), min(right, at + array.shape[1])
            if low < high:
                plan.append((number, out, low - at, row, shift + low - left, high - low))
    return pl.pallas_call(
        functools.partial(put_rows_kernel, plan),
        out_shape=[
            jax.ShapeDtypeStruct((rows, 4 * heads_width), BF16),
            jax.ShapeDtypeStruct((rows, 3 * hidden_width), BF16),
        ],
        in_specs=[FAR] * len(pieces),
        out_specs=[WHOLE] * 2,
        scratch_shapes=[pltpu.SemaphoreType.DMA((len(plan),))],
        compiler_params=params(53),
        cost_estimate=pl.CostEstimate(flops=0, bytes_accessed=4 * rows * end, transcendentals=0),
        name="put_rows",
    )(*[array for array, _, _ in pieces])


def layer_kernel(tok_ref, heads_ref, far_ref, out_ref, gated_ref, norm_ref, ctx_ref, acc_ref, sem):
    copy = pltpu.make_async_copy(far_ref, gated_ref, sem)
    copy.start()
    heads_width = ctx_ref.shape[1]
    hidden_width = gated_ref.shape[1] // 3
    tokens = tok_ref[...].astype(F32)
    scale = lax.rsqrt(jnp.mean(tokens * tokens, axis=1, keepdims=True) + EPS)
    norm_ref[...] = (tokens * scale).astype(BF16)
    attention(norm_ref[...], heads_ref[:, : 3 * heads_width], heads_width, ctx_ref)
    acc_ref[...] = dot_t(ctx_ref[...], heads_ref[:, 3 * heads_width :])
    copy.wait()
    for begin in range(0, hidden_width, UNIT):
        gate_w, up_w, down_w = [
            gated_ref[:, at + begin : at + begin + UNIT] for at in (0, hidden_width, 2 * hidden_width)
        ]
        add = gated(norm_ref[...], gate_w, up_w, down_w)
        if begin + UNIT < hidden_width:
            acc_ref[...] += add
        else:
            out_ref[...] = (acc_ref[...] + add).astype(out_ref.dtype)


def layer(tokens, heads, hiddens, out_type):
    rows, width = tokens.shape
    return pl.pallas_call(
        layer_kernel,
        out_shape=jax.ShapeDtypeStruct((rows, width), out_type),
        in_specs=[WHOLE, WHOLE, FAR],
        out_specs=WHOLE,
        scratch_shapes=[
            pltpu.VMEM(hiddens.shape, BF16),
            pltpu.VMEM((rows, width), BF16),
            pltpu.VMEM((rows, heads.shape[1] // 4), BF16),
            pltpu.VMEM((rows, width), F32),
            pltpu.SemaphoreType.DMA,
        ],
        compiler_params=params(36),
        cost_estimate=pl.CostEstimate(
            flops=2 * rows * (heads.size + hiddens.size),
            bytes_accessed=2 * (heads.size + hiddens.size) + 6 * rows * width,
            transcendentals=rows * hiddens.shape[1] // 3,
        ),
        name="layer",
    )(tokens, heads, hiddens)


def finish_kernel(tok_ref, sum_ref, got_ref, order_ref, out_ref):
    width = out_ref.shape[1]
    mixed = (tok_ref[...].astype(F32) + sum_ref[...] + got_ref[...].astype(F32)).astype(BF16)
    move = (iota((width, width), 0) == order_ref[...]).astype(F32).astype(BF16)
    out_ref[...] = dot_t(mixed, move).astype(BF16)


def finish(tokens, sums, got, order):
    rows, width = tokens.shape
    return pl.pallas_call(
        finish_kernel,
        out_shape=jax.ShapeDtypeStruct((rows, width), BF16),
        in_specs=[WHOLE] * 4,
        out_specs=WHOLE,
        compiler_params=params(12),
        cost_estimate=pl.CostEstimate(
            flops=2 * rows * width * width, bytes_accessed=10 * rows * width, transcendentals=0
        ),
        name="finish",
    )(tokens, sums, got, order.reshape(1, width))


def side_by_side(w_qkv, w_out, w_gate_up, w_down):
    rows = w_qkv.shape[0]
    return jnp.concatenate([w_qkv.reshape(rows, -1), w_gate_up.reshape(rows, -1), w_out, w_down], axis=1)


def along_cells(values, distance):
    n_cells = lax.axis_size("cells")
    return lax.ppermute(values, "cells", [(j, (j - distance) % n_cells) for j in range(n_cells)])


def to_other_places(shares):
    n_slots = lax.axis_size("slots")
    n_share = lax.axis_size("groups") * n_slots
    places = [shares]
    for far in range(1, n_share):
        pairs = [(place, place ^ far) for place in range(n_share)]
        places.append(lax.ppermute(shares, ("groups", "slots"), pairs))
    return places


def to_other_places_by_halves(shares):
    swap = [(0, 1), (1, 0)]
    by_slot = lax.ppermute(shares, "slots", swap)
    by_group = lax.ppermute(shares, "groups", swap)
    cut = shares.shape[1] // 2
    left = lax.ppermute(by_slot[:, :cut], "groups", swap)
    right = lax.ppermute(by_group[:, cut:], "slots", swap)
    return [shares, by_slot, by_group, left, right]


def arrival_order(width, n_share):
    n_cells = lax.axis_size("cells")
    mine = lax.axis_index("cells")
    place = lax.axis_index("groups") * lax.axis_size("slots") + lax.axis_index("slots")
    rows = width // n_cells
    share = rows // n_share
    row = jnp.arange(width, dtype=jnp.int32)
    past = row - 2 * rows
    far = jnp.where(past < 0, row // share % n_share, past // (2 * share))
    distance = jnp.where(past < 0, n_cells - 1, 1 + past // share % 2)
    other = (mine + distance) % n_cells * rows + (far ^ place) * share + row % share
    return jnp.where(row < rows, mine * rows + row, other)


def tokens_by_exchanges(owner, position, obs_feat, time_embed, my_slot, capacity, slot_dev):
    n_slots = lax.axis_size("slots")
    n_owners = lax.axis_size("cells") * lax.axis_size("mp")
    rows, width = obs_feat.shape
    owners = jnp.arange(n_owners, dtype=jnp.int32)
    owner_hot = (owner[:, None] == owners[None, :]).astype(F32)
    row_ids = jnp.arange(rows, dtype=jnp.int32)
    lower = (row_ids[None, :] <= row_ids[:, None]).astype(BF16)
    running = dot(lower, owner_hot.astype(BF16))
    rank = jnp.sum(running * owner_hot, axis=1).astype(jnp.int32) - 1
    place = jnp.where(owner < n_owners, owner * capacity + rank, n_owners * capacity)
    place_ids = jnp.arange(n_owners * capacity, dtype=jnp.int32)
    taken = place_ids[:, None] == place[None, :]
    send_feat = dot(taken.astype(BF16), obs_feat).astype(BF16).reshape(n_owners, capacity, width)
    send_code = jnp.sum(jnp.where(taken, position[None, :] + 1, 0), axis=1).reshape(n_owners, capacity)
    axes = ("cells", "mp")
    got_feat = lax.all_to_all(send_feat, axes, split_axis=0, concat_axis=0, tiled=True).reshape(-1, width)
    got_code = lax.all_to_all(send_code, axes, split_axis=0, concat_axis=0, tiled=True).reshape(-1) - 1
    hot = (jnp.arange(CB * slot_dev, dtype=jnp.int32)[:, None] == got_code[None, :]).astype(BF16)
    count = jnp.sum(hot.astype(F32), axis=1)
    pooled = dot(hot, got_feat) / jnp.maximum(count, 1.0)[:, None]
    embed = lax.dynamic_slice_in_dim(time_embed, my_slot * slot_dev, slot_dev, 0).astype(F32)
    tokens = (pooled.reshape(CB, slot_dev, width) + embed[None]).astype(BF16)
    grid = tokens.reshape(n_slots, CB // n_slots, slot_dev, width)
    grid = lax.all_to_all(grid, "slots", split_axis=0, concat_axis=2, tiled=True)
    return grid.reshape(-1, width)


def on_device(obs_feat, obs_cell, obs_slot, obs_count, time_embed, w_qkv, w_out, w_gate_up, w_down):
    n_cells = lax.axis_size("cells")
    n_slots = lax.axis_size("slots")
    n_groups = lax.axis_size("groups")
    n_mp = lax.axis_size("mp")
    n_owners = n_cells * n_mp
    rows, width = obs_feat.shape
    capacity = 3 * rows // n_owners
    quarter = CB // n_slots
    slot_dev = TSTEPS // n_slots
    my_slot = lax.axis_index("slots")
    n_share = n_groups * n_slots
    heads_width, hidden_width = w_qkv.shape[2], w_gate_up.shape[2]
    share = w_qkv.shape[0] // n_share
    valid = jnp.arange(rows, dtype=jnp.int32) < obs_count[0]
    owner = obs_cell // (quarter * n_mp * n_slots) * n_mp + obs_cell // quarter % n_mp
    owner = jnp.where(valid, owner, n_owners)
    local = obs_cell // (quarter * n_mp) % n_slots * quarter + obs_cell % quarter
    position = local * slot_dev + obs_slot

    local_weights = (w_qkv, w_out.T, w_gate_up, w_down.T)
    which = lax.axis_index("groups") * n_slots + my_slot
    share_weights = [lax.dynamic_slice_in_dim(w, which * share, share, 0) for w in local_weights]
    share_rows = side_by_side(*share_weights)
    if n_slots == 2 and n_groups == 2 and n_cells == 4 and share % 16 == 0 and capacity % 16 == 0:
        order = arrival_order(width, n_share)
        below = along_cells(share_rows, -1)
        codes, embed = place_codes(owner, position, time_embed, n_owners, capacity)
        codes = lax.all_to_all(codes, ("cells", "mp"), split_axis=0, concat_axis=0, tiled=True)
        below, codes, share_rows = lax.optimization_barrier((below, codes, share_rows))
        first = to_other_places(below)
        blocks = place_rows(owner, obs_feat, n_owners, capacity)
        above, opposite = along_cells(share_rows, 1), along_cells(below, -1)
        blocks, above, opposite, first = lax.optimization_barrier((blocks, above, opposite, first))
        second = to_other_places_by_halves(jnp.concatenate([above, opposite], axis=0))
        shard = side_by_side(*local_weights)
        got = lax.all_to_all(blocks, ("cells", "mp"), split_axis=0, concat_axis=0, tiled=True)
        got, shard, second = lax.optimization_barrier((got, shard, second))
        keep, send = pool_rows(my_slot.reshape(1), embed, codes, got, capacity, slot_dev)
        other = lax.ppermute(send, "slots", [(0, 1), (1, 0)])
        pieces, row = [], 0
        for array in [shard] + first + second[:3]:
            pieces.append((array, row, 0))
            row += array.shape[0]
        pieces += [(second[3], row, 0), (second[4], row, second[3].shape[1])]
        weights = put_rows(pieces, width, heads_width, hidden_width)
        other, weights = lax.optimization_barrier((other, weights))
        tokens = weave_steps(my_slot.reshape(1), order, keep, other, slot_dev)
    else:
        order = jnp.arange(width, dtype=jnp.int32)
        whole = lax.all_gather(share_rows, ("cells", "groups", "slots"), axis=0, tiled=True)
        weights = put_rows([(whole, 0, 0)], width, heads_width, hidden_width)
        tokens = tokens_by_exchanges(owner, position, obs_feat, time_embed, my_slot, capacity, slot_dev)

    swap = [(0, 1), (1, 0)]
    partner = lax.ppermute(tokens, "mp", swap)
    for_partner = layer(partner, *weights, BF16)
    from_partner = lax.ppermute(for_partner, "mp", swap)
    own = layer(tokens, *weights, F32)
    return finish(tokens, own, from_partner, order).reshape(quarter, TSTEPS, width)


def solution(mesh):
    placed = (
        P(("groups", "cells", "slots", "mp"), None),
        P(("groups", "cells", "slots", "mp")),
        P(("groups", "cells", "slots", "mp")),
        P(("groups", "cells", "slots", "mp")),
        P(),
        P("cells", None, "mp"),
        P("mp", "cells"),
        P("cells", None, "mp"),
        P("mp", "cells"),
    )
    return jax.shard_map(
        on_device,
        mesh=mesh,
        in_specs=placed,
        out_specs=P(("groups", "cells", "slots", "mp"), None, None),
        check_vma=False,
    )
```

```python
import functools

import jax
import jax.numpy as jnp
from jax import lax
from jax.experimental import pallas as pl
from jax.experimental.pallas import tpu as pltpu
from jax.sharding import PartitionSpec as P

HD = 64
TSTEPS = 8
CB = 128
EPS = 1e-06

CODE = 32
UNIT = 512
LANES = 128
MIB = 1024 * 1024
F32 = jnp.float32
BF16 = jnp.bfloat16
WHOLE = pl.BlockSpec(memory_space=pltpu.VMEM)
SCALARS = pl.BlockSpec(memory_space=pltpu.SMEM)
FAR = pl.BlockSpec(memory_space=pl.ANY)


def iota(shape, axis):
    return lax.broadcasted_iota(jnp.int32, shape, axis)


def dot(left, right):
    return jnp.dot(left, right, preferred_element_type=F32)


def dot_t(left, right):
    return lax.dot_general(left, right, (((1,), (1,)), ((), ())), preferred_element_type=F32)


def params(mib):
    return pltpu.CompilerParams(vmem_limit_bytes=mib * MIB)


def block_places(owner, n_owners):
    rows = owner.shape[1]
    owner_hot = (iota((n_owners, rows), 0) == owner).astype(F32)
    upper = (iota((rows, rows), 0) <= iota((rows, rows), 1)).astype(BF16)
    running = dot(owner_hot.astype(BF16), upper)
    return jnp.sum(running * owner_hot, axis=0, keepdims=True).astype(jnp.int32) - 1


def one_hot_rows(owner, rank, block, capacity):
    place = jnp.where(owner == block, rank, -1)
    return (iota((capacity, owner.shape[1]), 0) == place).astype(F32).astype(BF16)


def code_kernel(owner_ref, position_ref, time_ref, code_ref, embed_ref):
    n_owners, _, capacity = code_ref.shape
    embed_ref[...] = time_ref[...]
    owner = owner_ref[...]
    rank = block_places(owner, n_owners)
    code = position_ref[...] + 1
    line = iota((8, owner.shape[1]), 0)
    digits = jnp.where(line == 0, code // CODE, jnp.where(line == 1, code % CODE, 0))
    digits = digits.astype(F32).astype(BF16)
    for block in range(n_owners):
        sent = dot_t(digits, one_hot_rows(owner, rank, block, capacity))
        code_ref[block] = (sent[0:1] * CODE + sent[1:2]).astype(jnp.int32) - 1


def place_codes(owner, position, time_embed, n_owners, capacity):
    rows = owner.shape[0]
    return pl.pallas_call(
        code_kernel,
        out_shape=[
            jax.ShapeDtypeStruct((n_owners, 1, capacity), jnp.int32),
            jax.ShapeDtypeStruct(time_embed.shape, BF16),
        ],
        in_specs=[WHOLE] * 3,
        out_specs=[WHOLE] * 2,
        compiler_params=params(12),
        cost_estimate=pl.CostEstimate(
            flops=16 * rows * n_owners * capacity, bytes_accessed=8 * rows, transcendentals=0
        ),
        name="place_codes",
    )(owner.reshape(1, rows), position.reshape(1, rows), time_embed)


def place_kernel(owner_ref, feat_ref, out_ref):
    n_owners, capacity, _ = out_ref.shape
    owner = owner_ref[...]
    rank = block_places(owner, n_owners)
    feat = feat_ref[...]
    for block in range(n_owners):
        out_ref[block] = dot(one_hot_rows(owner, rank, block, capacity), feat).astype(BF16)


def place_rows(owner, obs_feat, n_owners, capacity):
    rows, width = obs_feat.shape
    return pl.pallas_call(
        place_kernel,
        out_shape=jax.ShapeDtypeStruct((n_owners, capacity, width), BF16),
        in_specs=[WHOLE] * 2,
        out_specs=WHOLE,
        compiler_params=params(12),
        cost_estimate=pl.CostEstimate(
            flops=2 * rows * width * n_owners * capacity,
            bytes_accessed=2 * width * (rows + n_owners * capacity),
            transcendentals=0,
        ),
        name="place_rows",
    )(owner.reshape(1, rows), obs_feat)


def pool_kernel(capacity, slot_dev, slot_ref, embed_ref, code_ref, got_ref, keep_ref, send_ref):
    half = keep_ref.shape[0]
    places = 2 * half
    mine = slot_ref[0]
    total = jnp.zeros((places, keep_ref.shape[1]), F32)
    seen = jnp.zeros((places, capacity), F32)
    for block in range(got_ref.shape[0]):
        code = code_ref[block]
        turned = jnp.where(code >= half, code - half, code + half)
        code = jnp.where((code >= 0) & (mine == 1), turned, code)
        hot = (iota((places, capacity), 0) == code).astype(F32)
        seen += hot
        total += dot(hot.astype(BF16), got_ref[block])
    count = jnp.sum(seen, axis=1, keepdims=True)
    steps = embed_ref.shape[0]
    step_hot = iota((places, steps), 1) == iota((places, steps), 0) % slot_dev + mine * slot_dev
    embed = dot(step_hot.astype(F32).astype(BF16), embed_ref[...])
    tokens = (total / jnp.maximum(count, 1.0) + embed).astype(BF16)
    keep_ref[...] = tokens[:half]
    send_ref[...] = tokens[half:]


def pool_rows(my_slot, time_embed, codes, got, capacity, slot_dev):
    width = time_embed.shape[1]
    half = jax.ShapeDtypeStruct((CB * slot_dev // 2, width), BF16)
    return pl.pallas_call(
        functools.partial(pool_kernel, capacity, slot_dev),
        out_shape=[half, half],
        in_specs=[SCALARS] + [WHOLE] * 3,
        out_specs=[WHOLE] * 2,
        compiler_params=params(12),
        cost_estimate=pl.CostEstimate(
            flops=2 * CB * slot_dev * got.size, bytes_accessed=2 * got.size, transcendentals=0
        ),
        name="pool_rows",
    )(my_slot, time_embed, codes, got)


def weave_kernel(slot_dev, slot_ref, order_ref, keep_ref, got_ref, out_ref):
    rows, width = out_ref.shape
    half = keep_ref.shape[0]
    mine = slot_ref[0]
    row, col = iota((rows, half), 0), iota((rows, half), 1)
    source = col == row // TSTEPS * slot_dev + row % slot_dev
    own = row % TSTEPS // slot_dev == mine
    from_keep = (source & own).astype(F32).astype(BF16)
    from_got = (source & jnp.logical_not(own)).astype(F32).astype(BF16)
    tokens = (dot(from_keep, keep_ref[...]) + dot(from_got, got_ref[...])).astype(BF16)
    move = (iota((width, width), 0) == order_ref[...]).astype(F32).astype(BF16)
    out_ref[...] = dot(tokens, move).astype(BF16)


def weave_steps(my_slot, order, keep, got, slot_dev):
    rows, width = 2 * keep.shape[0], keep.shape[1]
    return pl.pallas_call(
        functools.partial(weave_kernel, slot_dev),
        out_shape=jax.ShapeDtypeStruct((rows, width), BF16),
        in_specs=[SCALARS] + [WHOLE] * 3,
        out_specs=WHOLE,
        compiler_params=params(12),
        cost_estimate=pl.CostEstimate(
            flops=2 * rows * width * (rows + width), bytes_accessed=4 * rows * width, transcendentals=0
        ),
        name="weave_steps",
    )(my_slot, order.reshape(1, width), keep, got)


def attention(normed, weight, heads_width, ctx_ref):
    rows = normed.shape[0]
    group = LANES
    lane = iota((1, LANES), 1)
    first = iota((group, LANES), 1) < HD
    masks = [(lane < HD).astype(F32).astype(BF16), (lane >= HD).astype(F32).astype(BF16)]
    ones = (iota((LANES, LANES), 0) // HD == iota((LANES, LANES), 1) // HD).astype(F32)
    mean = (ones * (1.0 / HD)).astype(BF16)
    ones = ones.astype(BF16)
    same_cell = iota((2 * group, group), 0) % group // TSTEPS == iota((2 * group, group), 1) // TSTEPS
    same_cell = same_cell.astype(F32).astype(BF16)
    count = jnp.ones((group, LANES), BF16)
    projected = dot(normed, weight)
    begins = range(0, rows, group)
    for at in range(0, heads_width, LANES):
        query = projected[:, at : at + LANES]
        key = projected[:, heads_width + at : heads_width + at + LANES]
        value = projected[:, 2 * heads_width + at : 2 * heads_width + at + LANES].astype(BF16)
        query_bf, key_bf = query.astype(BF16), key.astype(BF16)
        query = (query * lax.rsqrt(dot(query_bf * query_bf, ones) + HD * EPS)).astype(BF16)
        key = (key * lax.rsqrt(dot(key_bf * key_bf, mean) + EPS)).astype(BF16)
        left, right = query * masks[0], query * masks[1]
        scores = [
            dot_t(jnp.concatenate([left[at : at + group], right[at : at + group]], axis=0), key[at : at + group])
            for at in begins
        ]
        expos = [jnp.exp(score).astype(BF16) * same_cell for score in scores]
        mixed = [
            dot(expo, jnp.concatenate([value[at : at + group], count], axis=1)) for at, expo in zip(begins, expos)
        ]
        for begin, both in zip(begins, mixed):
            top, low = both[:group], both[group:]
            over = jnp.where(first, top[:, :LANES], low[:, :LANES])
            under = jnp.where(first, top[:, LANES:], low[:, LANES:])
            ctx_ref[begin : begin + group, at : at + LANES] = (over / under).astype(BF16)


def gated(normed, gate_w, up_w, down_w):
    gate = dot(normed, gate_w)
    up = dot(normed, up_w)
    hidden = (gate * (0.5 * jnp.tanh(0.5 * gate) + 0.5) * up).astype(BF16)
    return dot_t(hidden, down_w)


def put_rows_kernel(plan, *refs):
    sems, outs, pieces = refs[-1], refs[-3:-1], refs[:-3]
    copies = []
    for number, (piece, out, source, row, at, size) in enumerate(plan):
        rows = pieces[piece].shape[0]
        target = outs[out].at[pl.ds(row, rows), pl.ds(at, size)]
        copies.append(pltpu.make_async_copy(pieces[piece].at[:, pl.ds(source, size)], target, sems.at[number]))
    for copy in copies:
        copy.start()
    for copy in copies:
        copy.wait()


def put_rows(pieces, rows, heads_width, hidden_width):
    gate_at, out_at = 3 * heads_width, 3 * heads_width + 2 * hidden_width
    down_at = out_at + heads_width
    end = down_at + hidden_width
    runs = [(0, gate_at, 0, 0), (gate_at, out_at, 1, 0), (out_at, down_at, 0, gate_at), (down_at, end, 1, 2 * hidden_width)]
    plan = []
    for left, right, out, shift in runs:
        for number, (array, row, at) in enumerate(pieces):
            low, high = max(left, at), min(right, at + array.shape[1])
            if low < high:
                plan.append((number, out, low - at, row, shift + low - left, high - low))
    return pl.pallas_call(
        functools.partial(put_rows_kernel, plan),
        out_shape=[
            jax.ShapeDtypeStruct((rows, 4 * heads_width), BF16),
            jax.ShapeDtypeStruct((rows, 3 * hidden_width), BF16),
        ],
        in_specs=[FAR] * len(pieces),
        out_specs=[WHOLE] * 2,
        scratch_shapes=[pltpu.SemaphoreType.DMA((len(plan),))],
        compiler_params=params(53),
        cost_estimate=pl.CostEstimate(flops=0, bytes_accessed=4 * rows * end, transcendentals=0),
        name="put_rows",
    )(*[array for array, _, _ in pieces])


def layer_kernel(tok_ref, heads_ref, far_ref, out_ref, gated_ref, norm_ref, ctx_ref, acc_ref, sem):
    copy = pltpu.make_async_copy(far_ref, gated_ref, sem)
    copy.start()
    heads_width = ctx_ref.shape[1]
    hidden_width = gated_ref.shape[1] // 3
    tokens = tok_ref[...].astype(F32)
    scale = lax.rsqrt(jnp.mean(tokens * tokens, axis=1, keepdims=True) + EPS)
    norm_ref[...] = (tokens * scale).astype(BF16)
    attention(norm_ref[...], heads_ref[:, : 3 * heads_width], heads_width, ctx_ref)
    acc_ref[...] = dot_t(ctx_ref[...], heads_ref[:, 3 * heads_width :])
    copy.wait()
    for begin in range(0, hidden_width, UNIT):
        gate_w, up_w, down_w = [
            gated_ref[:, at + begin : at + begin + UNIT] for at in (0, hidden_width, 2 * hidden_width)
        ]
        add = gated(norm_ref[...], gate_w, up_w, down_w)
        if begin + UNIT < hidden_width:
            acc_ref[...] += add
        else:
            out_ref[...] = (acc_ref[...] + add).astype(out_ref.dtype)


def layer(tokens, heads, hiddens, out_type):
    rows, width = tokens.shape
    return pl.pallas_call(
        layer_kernel,
        out_shape=jax.ShapeDtypeStruct((rows, width), out_type),
        in_specs=[WHOLE, WHOLE, FAR],
        out_specs=WHOLE,
        scratch_shapes=[
            pltpu.VMEM(hiddens.shape, BF16),
            pltpu.VMEM((rows, width), BF16),
            pltpu.VMEM((rows, heads.shape[1] // 4), BF16),
            pltpu.VMEM((rows, width), F32),
            pltpu.SemaphoreType.DMA,
        ],
        compiler_params=params(58),
        cost_estimate=pl.CostEstimate(
            flops=2 * rows * (heads.size + hiddens.size),
            bytes_accessed=2 * (heads.size + hiddens.size) + 6 * rows * width,
            transcendentals=rows * hiddens.shape[1] // 3,
        ),
        name="layer",
    )(tokens, heads, hiddens)


def finish_kernel(tok_ref, sum_ref, got_ref, order_ref, out_ref):
    width = out_ref.shape[1]
    mixed = (tok_ref[...].astype(F32) + sum_ref[...] + got_ref[...].astype(F32)).astype(BF16)
    move = (iota((width, width), 0) == order_ref[...]).astype(F32).astype(BF16)
    out_ref[...] = dot_t(mixed, move).astype(BF16)


def finish(tokens, sums, got, order):
    rows, width = tokens.shape
    return pl.pallas_call(
        finish_kernel,
        out_shape=jax.ShapeDtypeStruct((rows, width), BF16),
        in_specs=[WHOLE] * 4,
        out_specs=WHOLE,
        compiler_params=params(12),
        cost_estimate=pl.CostEstimate(
            flops=2 * rows * width * width, bytes_accessed=10 * rows * width, transcendentals=0
        ),
        name="finish",
    )(tokens, sums, got, order.reshape(1, width))


def side_by_side(w_qkv, w_out, w_gate_up, w_down):
    rows = w_qkv.shape[0]
    return jnp.concatenate([w_qkv.reshape(rows, -1), w_gate_up.reshape(rows, -1), w_out, w_down], axis=1)


def along_cells(values, distance):
    n_cells = lax.axis_size("cells")
    return lax.ppermute(values, "cells", [(j, (j - distance) % n_cells) for j in range(n_cells)])


def to_other_places(shares):
    n_slots = lax.axis_size("slots")
    n_share = lax.axis_size("groups") * n_slots
    places = [shares]
    for far in range(1, n_share):
        pairs = [(place, place ^ far) for place in range(n_share)]
        places.append(lax.ppermute(shares, ("groups", "slots"), pairs))
    return places


def to_other_places_by_halves(shares):
    swap = [(0, 1), (1, 0)]
    by_slot = lax.ppermute(shares, "slots", swap)
    by_group = lax.ppermute(shares, "groups", swap)
    cut = shares.shape[1] // 2
    left = lax.ppermute(by_slot[:, :cut], "groups", swap)
    right = lax.ppermute(by_group[:, cut:], "slots", swap)
    return [shares, by_slot, by_group, left, right]


def arrival_order(width, n_share):
    n_cells = lax.axis_size("cells")
    mine = lax.axis_index("cells")
    place = lax.axis_index("groups") * lax.axis_size("slots") + lax.axis_index("slots")
    rows = width // n_cells
    share = rows // n_share
    row = jnp.arange(width, dtype=jnp.int32)
    past = row - 2 * rows
    far = jnp.where(past < 0, row // share % n_share, past // (2 * share))
    distance = jnp.where(past < 0, n_cells - 1, 1 + past // share % 2)
    other = (mine + distance) % n_cells * rows + (far ^ place) * share + row % share
    return jnp.where(row < rows, mine * rows + row, other)


def tokens_by_exchanges(owner, position, obs_feat, time_embed, my_slot, capacity, slot_dev):
    n_slots = lax.axis_size("slots")
    n_owners = lax.axis_size("cells") * lax.axis_size("mp")
    rows, width = obs_feat.shape
    owners = jnp.arange(n_owners, dtype=jnp.int32)
    owner_hot = (owner[:, None] == owners[None, :]).astype(F32)
    row_ids = jnp.arange(rows, dtype=jnp.int32)
    lower = (row_ids[None, :] <= row_ids[:, None]).astype(BF16)
    running = dot(lower, owner_hot.astype(BF16))
    rank = jnp.sum(running * owner_hot, axis=1).astype(jnp.int32) - 1
    place = jnp.where(owner < n_owners, owner * capacity + rank, n_owners * capacity)
    place_ids = jnp.arange(n_owners * capacity, dtype=jnp.int32)
    taken = place_ids[:, None] == place[None, :]
    send_feat = dot(taken.astype(BF16), obs_feat).astype(BF16).reshape(n_owners, capacity, width)
    send_code = jnp.sum(jnp.where(taken, position[None, :] + 1, 0), axis=1).reshape(n_owners, capacity)
    axes = ("cells", "mp")
    got_feat = lax.all_to_all(send_feat, axes, split_axis=0, concat_axis=0, tiled=True).reshape(-1, width)
    got_code = lax.all_to_all(send_code, axes, split_axis=0, concat_axis=0, tiled=True).reshape(-1) - 1
    hot = (jnp.arange(CB * slot_dev, dtype=jnp.int32)[:, None] == got_code[None, :]).astype(BF16)
    count = jnp.sum(hot.astype(F32), axis=1)
    pooled = dot(hot, got_feat) / jnp.maximum(count, 1.0)[:, None]
    embed = lax.dynamic_slice_in_dim(time_embed, my_slot * slot_dev, slot_dev, 0).astype(F32)
    tokens = (pooled.reshape(CB, slot_dev, width) + embed[None]).astype(BF16)
    grid = tokens.reshape(n_slots, CB // n_slots, slot_dev, width)
    grid = lax.all_to_all(grid, "slots", split_axis=0, concat_axis=2, tiled=True)
    return grid.reshape(-1, width)


def on_device(obs_feat, obs_cell, obs_slot, obs_count, time_embed, w_qkv, w_out, w_gate_up, w_down):
    n_cells = lax.axis_size("cells")
    n_slots = lax.axis_size("slots")
    n_groups = lax.axis_size("groups")
    n_mp = lax.axis_size("mp")
    n_owners = n_cells * n_mp
    rows, width = obs_feat.shape
    capacity = 3 * rows // n_owners
    quarter = CB // n_slots
    slot_dev = TSTEPS // n_slots
    my_slot = lax.axis_index("slots")
    n_share = n_groups * n_slots
    heads_width, hidden_width = w_qkv.shape[2], w_gate_up.shape[2]
    share = w_qkv.shape[0] // n_share
    valid = jnp.arange(rows, dtype=jnp.int32) < obs_count[0]
    owner = obs_cell // (quarter * n_mp * n_slots) * n_mp + obs_cell // quarter % n_mp
    owner = jnp.where(valid, owner, n_owners)
    local = obs_cell // (quarter * n_mp) % n_slots * quarter + obs_cell % quarter
    position = local * slot_dev + obs_slot

    local_weights = (w_qkv, w_out.T, w_gate_up, w_down.T)
    which = lax.axis_index("groups") * n_slots + my_slot
    share_weights = [lax.dynamic_slice_in_dim(w, which * share, share, 0) for w in local_weights]
    share_rows = side_by_side(*share_weights)
    if n_slots == 2 and n_groups == 2 and n_cells == 4 and share % 16 == 0 and capacity % 16 == 0:
        order = arrival_order(width, n_share)
        below = along_cells(share_rows, -1)
        codes, embed = place_codes(owner, position, time_embed, n_owners, capacity)
        below, codes, share_rows = lax.optimization_barrier((below, codes, share_rows))
        codes = lax.all_to_all(codes, ("cells", "mp"), split_axis=0, concat_axis=0, tiled=True)
        first = to_other_places(below)
        blocks = place_rows(owner, obs_feat, n_owners, capacity)
        above, opposite = along_cells(share_rows, 1), along_cells(below, -1)
        blocks, codes, above, opposite, first = lax.optimization_barrier((blocks, codes, above, opposite, first))
        second = to_other_places_by_halves(jnp.concatenate([above, opposite], axis=0))
        shard = side_by_side(*local_weights)
        got = lax.all_to_all(blocks, ("cells", "mp"), split_axis=0, concat_axis=0, tiled=True)
        got, shard, second = lax.optimization_barrier((got, shard, second))
        keep, send = pool_rows(my_slot.reshape(1), embed, codes, got, capacity, slot_dev)
        other = lax.ppermute(send, "slots", [(0, 1), (1, 0)])
        pieces, row = [], 0
        for array in [shard] + first + second[:3]:
            pieces.append((array, row, 0))
            row += array.shape[0]
        pieces += [(second[3], row, 0), (second[4], row, second[3].shape[1])]
        weights = put_rows(pieces, width, heads_width, hidden_width)
        other, weights = lax.optimization_barrier((other, weights))
        tokens = weave_steps(my_slot.reshape(1), order, keep, other, slot_dev)
    else:
        order = jnp.arange(width, dtype=jnp.int32)
        whole = lax.all_gather(share_rows, ("cells", "groups", "slots"), axis=0, tiled=True)
        weights = put_rows([(whole, 0, 0)], width, heads_width, hidden_width)
        tokens = tokens_by_exchanges(owner, position, obs_feat, time_embed, my_slot, capacity, slot_dev)

    swap = [(0, 1), (1, 0)]
    partner = lax.ppermute(tokens, "mp", swap)
    for_partner = layer(partner, *weights, BF16)
    from_partner = lax.ppermute(for_partner, "mp", swap)
    own = layer(tokens, *weights, F32)
    return finish(tokens, own, from_partner, order).reshape(quarter, TSTEPS, width)


def solution(mesh):
    placed = (
        P(("groups", "cells", "slots", "mp"), None),
        P(("groups", "cells", "slots", "mp")),
        P(("groups", "cells", "slots", "mp")),
        P(("groups", "cells", "slots", "mp")),
        P(),
        P("cells", None, "mp"),
        P("mp", "cells"),
        P("cells", None, "mp"),
        P("mp", "cells"),
    )
    return jax.shard_map(
        on_device,
        mesh=mesh,
        in_specs=placed,
        out_specs=P(("groups", "cells", "slots", "mp"), None, None),
        check_vma=False,
    )
```

```python
import functools

import jax
import jax.numpy as jnp
from jax import lax
from jax.experimental import pallas as pl
from jax.experimental.pallas import tpu as pltpu
from jax.sharding import PartitionSpec as P

HD = 64
TSTEPS = 8
CB = 128
EPS = 1e-06

CODE = 32
UNIT = 512
LANES = 128
MIB = 1024 * 1024
F32 = jnp.float32
BF16 = jnp.bfloat16
WHOLE = pl.BlockSpec(memory_space=pltpu.VMEM)
SCALARS = pl.BlockSpec(memory_space=pltpu.SMEM)
FAR = pl.BlockSpec(memory_space=pl.ANY)


def iota(shape, axis):
    return lax.broadcasted_iota(jnp.int32, shape, axis)


def dot(left, right):
    return jnp.dot(left, right, preferred_element_type=F32)


def dot_t(left, right):
    return lax.dot_general(left, right, (((1,), (1,)), ((), ())), preferred_element_type=F32)


def params(mib):
    return pltpu.CompilerParams(vmem_limit_bytes=mib * MIB)


def block_places(owner, n_owners):
    rows = owner.shape[1]
    owner_hot = (iota((n_owners, rows), 0) == owner).astype(F32)
    upper = (iota((rows, rows), 0) <= iota((rows, rows), 1)).astype(BF16)
    running = dot(owner_hot.astype(BF16), upper)
    return jnp.sum(running * owner_hot, axis=0, keepdims=True).astype(jnp.int32) - 1


def one_hot_rows(owner, rank, block, capacity):
    place = jnp.where(owner == block, rank, -1)
    return (iota((capacity, owner.shape[1]), 0) == place).astype(F32).astype(BF16)


def code_kernel(owner_ref, position_ref, time_ref, code_ref, embed_ref):
    n_owners, _, capacity = code_ref.shape
    embed_ref[...] = time_ref[...]
    owner = owner_ref[...]
    rank = block_places(owner, n_owners)
    code = position_ref[...] + 1
    line = iota((8, owner.shape[1]), 0)
    digits = jnp.where(line == 0, code // CODE, jnp.where(line == 1, code % CODE, 0))
    digits = digits.astype(F32).astype(BF16)
    for block in range(n_owners):
        sent = dot_t(digits, one_hot_rows(owner, rank, block, capacity))
        code_ref[block] = (sent[0:1] * CODE + sent[1:2]).astype(jnp.int32) - 1


def place_codes(owner, position, time_embed, n_owners, capacity):
    rows = owner.shape[0]
    return pl.pallas_call(
        code_kernel,
        out_shape=[
            jax.ShapeDtypeStruct((n_owners, 1, capacity), jnp.int32),
            jax.ShapeDtypeStruct(time_embed.shape, BF16),
        ],
        in_specs=[WHOLE] * 3,
        out_specs=[WHOLE] * 2,
        compiler_params=params(12),
        cost_estimate=pl.CostEstimate(
            flops=16 * rows * n_owners * capacity, bytes_accessed=8 * rows, transcendentals=0
        ),
        name="place_codes",
    )(owner.reshape(1, rows), position.reshape(1, rows), time_embed)


def place_kernel(owner_ref, feat_ref, out_ref):
    n_owners, capacity, _ = out_ref.shape
    owner = owner_ref[...]
    rank = block_places(owner, n_owners)
    feat = feat_ref[...]
    for block in range(n_owners):
        out_ref[block] = dot(one_hot_rows(owner, rank, block, capacity), feat).astype(BF16)


def place_rows(owner, obs_feat, n_owners, capacity):
    rows, width = obs_feat.shape
    return pl.pallas_call(
        place_kernel,
        out_shape=jax.ShapeDtypeStruct((n_owners, capacity, width), BF16),
        in_specs=[WHOLE] * 2,
        out_specs=WHOLE,
        compiler_params=params(12),
        cost_estimate=pl.CostEstimate(
            flops=2 * rows * width * n_owners * capacity,
            bytes_accessed=2 * width * (rows + n_owners * capacity),
            transcendentals=0,
        ),
        name="place_rows",
    )(owner.reshape(1, rows), obs_feat)


def pool_kernel(capacity, slot_dev, slot_ref, embed_ref, code_ref, got_ref, keep_ref, send_ref):
    half = keep_ref.shape[0]
    places = 2 * half
    mine = slot_ref[0]
    total = jnp.zeros((places, keep_ref.shape[1]), F32)
    seen = jnp.zeros((places, capacity), F32)
    for block in range(got_ref.shape[0]):
        code = code_ref[block]
        turned = jnp.where(code >= half, code - half, code + half)
        code = jnp.where((code >= 0) & (mine == 1), turned, code)
        hot = (iota((places, capacity), 0) == code).astype(F32)
        seen += hot
        total += dot(hot.astype(BF16), got_ref[block])
    count = jnp.sum(seen, axis=1, keepdims=True)
    steps = embed_ref.shape[0]
    step_hot = iota((places, steps), 1) == iota((places, steps), 0) % slot_dev + mine * slot_dev
    embed = dot(step_hot.astype(F32).astype(BF16), embed_ref[...])
    tokens = (total / jnp.maximum(count, 1.0) + embed).astype(BF16)
    keep_ref[...] = tokens[:half]
    send_ref[...] = tokens[half:]


def pool_rows(my_slot, time_embed, codes, got, capacity, slot_dev):
    width = time_embed.shape[1]
    half = jax.ShapeDtypeStruct((CB * slot_dev // 2, width), BF16)
    return pl.pallas_call(
        functools.partial(pool_kernel, capacity, slot_dev),
        out_shape=[half, half],
        in_specs=[SCALARS] + [WHOLE] * 3,
        out_specs=[WHOLE] * 2,
        compiler_params=params(12),
        cost_estimate=pl.CostEstimate(
            flops=2 * CB * slot_dev * got.size, bytes_accessed=2 * got.size, transcendentals=0
        ),
        name="pool_rows",
    )(my_slot, time_embed, codes, got)


def weave_kernel(slot_dev, slot_ref, order_ref, keep_ref, got_ref, out_ref):
    rows, width = out_ref.shape
    half = keep_ref.shape[0]
    mine = slot_ref[0]
    row, col = iota((rows, half), 0), iota((rows, half), 1)
    source = col == row // TSTEPS * slot_dev + row % slot_dev
    own = row % TSTEPS // slot_dev == mine
    from_keep = (source & own).astype(F32).astype(BF16)
    from_got = (source & jnp.logical_not(own)).astype(F32).astype(BF16)
    tokens = (dot(from_keep, keep_ref[...]) + dot(from_got, got_ref[...])).astype(BF16)
    move = (iota((width, width), 0) == order_ref[...]).astype(F32).astype(BF16)
    out_ref[...] = dot(tokens, move).astype(BF16)


def weave_steps(my_slot, order, keep, got, slot_dev):
    rows, width = 2 * keep.shape[0], keep.shape[1]
    return pl.pallas_call(
        functools.partial(weave_kernel, slot_dev),
        out_shape=jax.ShapeDtypeStruct((rows, width), BF16),
        in_specs=[SCALARS] + [WHOLE] * 3,
        out_specs=WHOLE,
        compiler_params=params(12),
        cost_estimate=pl.CostEstimate(
            flops=2 * rows * width * (rows + width), bytes_accessed=4 * rows * width, transcendentals=0
        ),
        name="weave_steps",
    )(my_slot, order.reshape(1, width), keep, got)


def attention(normed, weight, heads_width, ctx_ref):
    rows = normed.shape[0]
    group = LANES
    lane = iota((1, LANES), 1)
    first = iota((group, LANES), 1) < HD
    masks = [(lane < HD).astype(F32).astype(BF16), (lane >= HD).astype(F32).astype(BF16)]
    ones = (iota((LANES, LANES), 0) // HD == iota((LANES, LANES), 1) // HD).astype(F32)
    mean = (ones * (1.0 / HD)).astype(BF16)
    ones = ones.astype(BF16)
    same_cell = iota((2 * group, group), 0) % group // TSTEPS == iota((2 * group, group), 1) // TSTEPS
    same_cell = same_cell.astype(F32).astype(BF16)
    count = jnp.ones((group, LANES), BF16)
    projected = dot(normed, weight)
    begins = range(0, rows, group)
    for at in range(0, heads_width, LANES):
        query = projected[:, at : at + LANES]
        key = projected[:, heads_width + at : heads_width + at + LANES]
        value = projected[:, 2 * heads_width + at : 2 * heads_width + at + LANES].astype(BF16)
        query_bf, key_bf = query.astype(BF16), key.astype(BF16)
        query = (query * lax.rsqrt(dot(query_bf * query_bf, ones) + HD * EPS)).astype(BF16)
        key = (key * lax.rsqrt(dot(key_bf * key_bf, mean) + EPS)).astype(BF16)
        left, right = query * masks[0], query * masks[1]
        scores = [
            dot_t(jnp.concatenate([left[at : at + group], right[at : at + group]], axis=0), key[at : at + group])
            for at in begins
        ]
        expos = [jnp.exp(score).astype(BF16) * same_cell for score in scores]
        mixed = [
            dot(expo, jnp.concatenate([value[at : at + group], count], axis=1)) for at, expo in zip(begins, expos)
        ]
        for begin, both in zip(begins, mixed):
            top, low = both[:group], both[group:]
            over = jnp.where(first, top[:, :LANES], low[:, :LANES])
            under = jnp.where(first, top[:, LANES:], low[:, LANES:])
            ctx_ref[begin : begin + group, at : at + LANES] = (over / under).astype(BF16)


def gated(normed, gate_w, up_w, down_w):
    gate = dot(normed, gate_w)
    up = dot(normed, up_w)
    hidden = (gate * (0.5 * jnp.tanh(0.5 * gate) + 0.5) * up).astype(BF16)
    return dot_t(hidden, down_w)


def put_rows_kernel(plan, *refs):
    sems, outs, pieces = refs[-1], refs[-4:-1], refs[:-4]
    copies = []
    for number, (piece, out, source, row, at, size) in enumerate(plan):
        rows = pieces[piece].shape[0]
        target = outs[out].at[pl.ds(row, rows), pl.ds(at, size)]
        copies.append(pltpu.make_async_copy(pieces[piece].at[:, pl.ds(source, size)], target, sems.at[number]))
    for copy in copies:
        copy.start()
    for copy in copies:
        copy.wait()


def put_rows(pieces, rows, heads_width, hidden_width):
    gate_at, out_at = 3 * heads_width, 3 * heads_width + 2 * hidden_width
    down_at = out_at + heads_width
    end = down_at + hidden_width
    runs = [(0, gate_at, 0, 0), (gate_at, out_at, 1, 0), (out_at, down_at, 0, gate_at), (down_at, end, 2, 0)]
    plan = []
    for left, right, out, shift in runs:
        for number, (array, row, at) in enumerate(pieces):
            low, high = max(left, at), min(right, at + array.shape[1])
            if low < high:
                plan.append((number, out, low - at, row, shift + low - left, high - low))
    return pl.pallas_call(
        functools.partial(put_rows_kernel, plan),
        out_shape=[
            jax.ShapeDtypeStruct((rows, 4 * heads_width), BF16),
            jax.ShapeDtypeStruct((rows, 2 * hidden_width), BF16),
            jax.ShapeDtypeStruct((rows, hidden_width), BF16),
        ],
        in_specs=[FAR] * len(pieces),
        out_specs=[WHOLE] * 3,
        scratch_shapes=[pltpu.SemaphoreType.DMA((len(plan),))],
        compiler_params=params(53),
        cost_estimate=pl.CostEstimate(flops=0, bytes_accessed=4 * rows * end, transcendentals=0),
        name="put_rows",
    )(*[array for array, _, _ in pieces])


def layer_kernel(tok_ref, heads_ref, gate_up_ref, down_ref, out_ref, norm_ref, ctx_ref, acc_ref):
    heads_width = ctx_ref.shape[1]
    hidden_width = down_ref.shape[1]
    tokens = tok_ref[...].astype(F32)
    scale = lax.rsqrt(jnp.mean(tokens * tokens, axis=1, keepdims=True) + EPS)
    norm_ref[...] = (tokens * scale).astype(BF16)
    attention(norm_ref[...], heads_ref[:, : 3 * heads_width], heads_width, ctx_ref)
    acc_ref[...] = dot_t(ctx_ref[...], heads_ref[:, 3 * heads_width :])
    for begin in range(0, hidden_width, UNIT):
        end = begin + UNIT
        gate_w, up_w = gate_up_ref[:, begin:end], gate_up_ref[:, hidden_width + begin : hidden_width + end]
        add = gated(norm_ref[...], gate_w, up_w, down_ref[:, begin:end])
        if end < hidden_width:
            acc_ref[...] += add
        else:
            out_ref[...] = (acc_ref[...] + add).astype(out_ref.dtype)


def layer(tokens, heads, gate_up, down, out_type):
    rows, width = tokens.shape
    size = heads.size + gate_up.size + down.size
    return pl.pallas_call(
        layer_kernel,
        out_shape=jax.ShapeDtypeStruct((rows, width), out_type),
        in_specs=[WHOLE] * 4,
        out_specs=WHOLE,
        scratch_shapes=[
            pltpu.VMEM((rows, width), BF16),
            pltpu.VMEM((rows, heads.shape[1] // 4), BF16),
            pltpu.VMEM((rows, width), F32),
        ],
        compiler_params=params(28),
        cost_estimate=pl.CostEstimate(
            flops=2 * rows * size,
            bytes_accessed=2 * size + 6 * rows * width,
            transcendentals=rows * down.shape[1],
        ),
        name="layer",
    )(tokens, heads, gate_up, down)


def finish_kernel(tok_ref, sum_ref, got_ref, order_ref, out_ref):
    width = out_ref.shape[1]
    mixed = (tok_ref[...].astype(F32) + sum_ref[...] + got_ref[...].astype(F32)).astype(BF16)
    move = (iota((width, width), 0) == order_ref[...]).astype(F32).astype(BF16)
    out_ref[...] = dot_t(mixed, move).astype(BF16)


def finish(tokens, sums, got, order):
    rows, width = tokens.shape
    return pl.pallas_call(
        finish_kernel,
        out_shape=jax.ShapeDtypeStruct((rows, width), BF16),
        in_specs=[WHOLE] * 4,
        out_specs=WHOLE,
        compiler_params=params(12),
        cost_estimate=pl.CostEstimate(
            flops=2 * rows * width * width, bytes_accessed=10 * rows * width, transcendentals=0
        ),
        name="finish",
    )(tokens, sums, got, order.reshape(1, width))


def side_by_side(w_qkv, w_out, w_gate_up, w_down):
    rows = w_qkv.shape[0]
    return jnp.concatenate([w_qkv.reshape(rows, -1), w_gate_up.reshape(rows, -1), w_out, w_down], axis=1)


def along_cells(values, distance):
    n_cells = lax.axis_size("cells")
    return lax.ppermute(values, "cells", [(j, (j - distance) % n_cells) for j in range(n_cells)])


def to_other_places(shares):
    n_slots = lax.axis_size("slots")
    n_share = lax.axis_size("groups") * n_slots
    places = [shares]
    for far in range(1, n_share):
        pairs = [(place, place ^ far) for place in range(n_share)]
        places.append(lax.ppermute(shares, ("groups", "slots"), pairs))
    return places


def to_other_places_by_halves(shares):
    swap = [(0, 1), (1, 0)]
    by_slot = lax.ppermute(shares, "slots", swap)
    by_group = lax.ppermute(shares, "groups", swap)
    cut = shares.shape[1] // 2
    left = lax.ppermute(by_slot[:, :cut], "groups", swap)
    right = lax.ppermute(by_group[:, cut:], "slots", swap)
    return [shares, by_slot, by_group, left, right]


def arrival_order(width, n_share):
    n_cells = lax.axis_size("cells")
    mine = lax.axis_index("cells")
    place = lax.axis_index("groups") * lax.axis_size("slots") + lax.axis_index("slots")
    rows = width // n_cells
    share = rows // n_share
    row = jnp.arange(width, dtype=jnp.int32)
    past = row - 2 * rows
    far = jnp.where(past < 0, row // share % n_share, past // (2 * share))
    distance = jnp.where(past < 0, n_cells - 1, 1 + past // share % 2)
    other = (mine + distance) % n_cells * rows + (far ^ place) * share + row % share
    return jnp.where(row < rows, mine * rows + row, other)


def tokens_by_exchanges(owner, position, obs_feat, time_embed, my_slot, capacity, slot_dev):
    n_slots = lax.axis_size("slots")
    n_owners = lax.axis_size("cells") * lax.axis_size("mp")
    rows, width = obs_feat.shape
    owners = jnp.arange(n_owners, dtype=jnp.int32)
    owner_hot = (owner[:, None] == owners[None, :]).astype(F32)
    row_ids = jnp.arange(rows, dtype=jnp.int32)
    lower = (row_ids[None, :] <= row_ids[:, None]).astype(BF16)
    running = dot(lower, owner_hot.astype(BF16))
    rank = jnp.sum(running * owner_hot, axis=1).astype(jnp.int32) - 1
    place = jnp.where(owner < n_owners, owner * capacity + rank, n_owners * capacity)
    place_ids = jnp.arange(n_owners * capacity, dtype=jnp.int32)
    taken = place_ids[:, None] == place[None, :]
    send_feat = dot(taken.astype(BF16), obs_feat).astype(BF16).reshape(n_owners, capacity, width)
    send_code = jnp.sum(jnp.where(taken, position[None, :] + 1, 0), axis=1).reshape(n_owners, capacity)
    axes = ("cells", "mp")
    got_feat = lax.all_to_all(send_feat, axes, split_axis=0, concat_axis=0, tiled=True).reshape(-1, width)
    got_code = lax.all_to_all(send_code, axes, split_axis=0, concat_axis=0, tiled=True).reshape(-1) - 1
    hot = (jnp.arange(CB * slot_dev, dtype=jnp.int32)[:, None] == got_code[None, :]).astype(BF16)
    count = jnp.sum(hot.astype(F32), axis=1)
    pooled = dot(hot, got_feat) / jnp.maximum(count, 1.0)[:, None]
    embed = lax.dynamic_slice_in_dim(time_embed, my_slot * slot_dev, slot_dev, 0).astype(F32)
    tokens = (pooled.reshape(CB, slot_dev, width) + embed[None]).astype(BF16)
    grid = tokens.reshape(n_slots, CB // n_slots, slot_dev, width)
    grid = lax.all_to_all(grid, "slots", split_axis=0, concat_axis=2, tiled=True)
    return grid.reshape(-1, width)


def on_device(obs_feat, obs_cell, obs_slot, obs_count, time_embed, w_qkv, w_out, w_gate_up, w_down):
    n_cells = lax.axis_size("cells")
    n_slots = lax.axis_size("slots")
    n_groups = lax.axis_size("groups")
    n_mp = lax.axis_size("mp")
    n_owners = n_cells * n_mp
    rows, width = obs_feat.shape
    capacity = 3 * rows // n_owners
    quarter = CB // n_slots
    slot_dev = TSTEPS // n_slots
    my_slot = lax.axis_index("slots")
    n_share = n_groups * n_slots
    heads_width, hidden_width = w_qkv.shape[2], w_gate_up.shape[2]
    share = w_qkv.shape[0] // n_share
    valid = jnp.arange(rows, dtype=jnp.int32) < obs_count[0]
    owner = obs_cell // (quarter * n_mp * n_slots) * n_mp + obs_cell // quarter % n_mp
    owner = jnp.where(valid, owner, n_owners)
    local = obs_cell // (quarter * n_mp) % n_slots * quarter + obs_cell % quarter
    position = local * slot_dev + obs_slot

    local_weights = (w_qkv, w_out.T, w_gate_up, w_down.T)
    which = lax.axis_index("groups") * n_slots + my_slot
    share_weights = [lax.dynamic_slice_in_dim(w, which * share, share, 0) for w in local_weights]
    share_rows = side_by_side(*share_weights)
    if n_slots == 2 and n_groups == 2 and n_cells == 4 and share % 16 == 0 and capacity % 16 == 0:
        order = arrival_order(width, n_share)
        below = along_cells(share_rows, -1)
        codes, embed = place_codes(owner, position, time_embed, n_owners, capacity)
        below, codes, share_rows = lax.optimization_barrier((below, codes, share_rows))
        codes = lax.all_to_all(codes, ("cells", "mp"), split_axis=0, concat_axis=0, tiled=True)
        first = to_other_places(below)
        blocks = place_rows(owner, obs_feat, n_owners, capacity)
        above, opposite = along_cells(share_rows, 1), along_cells(below, -1)
        blocks, codes, above, opposite, first = lax.optimization_barrier((blocks, codes, above, opposite, first))
        second = to_other_places_by_halves(jnp.concatenate([above, opposite], axis=0))
        shard = side_by_side(*local_weights)
        got = lax.all_to_all(blocks, ("cells", "mp"), split_axis=0, concat_axis=0, tiled=True)
        got, shard, second = lax.optimization_barrier((got, shard, second))
        keep, send = pool_rows(my_slot.reshape(1), embed, codes, got, capacity, slot_dev)
        other = lax.ppermute(send, "slots", [(0, 1), (1, 0)])
        pieces, row = [], 0
        for array in [shard] + first + second[:3]:
            pieces.append((array, row, 0))
            row += array.shape[0]
        pieces += [(second[3], row, 0), (second[4], row, second[3].shape[1])]
        weights = put_rows(pieces, width, heads_width, hidden_width)
        other, weights = lax.optimization_barrier((other, weights))
        tokens = weave_steps(my_slot.reshape(1), order, keep, other, slot_dev)
    else:
        order = jnp.arange(width, dtype=jnp.int32)
        whole = lax.all_gather(share_rows, ("cells", "groups", "slots"), axis=0, tiled=True)
        weights = put_rows([(whole, 0, 0)], width, heads_width, hidden_width)
        tokens = tokens_by_exchanges(owner, position, obs_feat, time_embed, my_slot, capacity, slot_dev)

    swap = [(0, 1), (1, 0)]
    partner = lax.ppermute(tokens, "mp", swap)
    for_partner = layer(partner, *weights, BF16)
    from_partner = lax.ppermute(for_partner, "mp", swap)
    own = layer(tokens, *weights, F32)
    return finish(tokens, own, from_partner, order).reshape(quarter, TSTEPS, width)


def solution(mesh):
    placed = (
        P(("groups", "cells", "slots", "mp"), None),
        P(("groups", "cells", "slots", "mp")),
        P(("groups", "cells", "slots", "mp")),
        P(("groups", "cells", "slots", "mp")),
        P(),
        P("cells", None, "mp"),
        P("mp", "cells"),
        P("cells", None, "mp"),
        P("mp", "cells"),
    )
    return jax.shard_map(
        on_device,
        mesh=mesh,
        in_specs=placed,
        out_specs=P(("groups", "cells", "slots", "mp"), None, None),
        check_vma=False,
    )
```

```python
import functools

import jax
import jax.numpy as jnp
from jax import lax
from jax.experimental import pallas as pl
from jax.experimental.pallas import tpu as pltpu
from jax.sharding import PartitionSpec as P

HD = 64
TSTEPS = 8
CB = 128
EPS = 1e-06

CODE = 32
UNIT = 512
LANES = 128
MIB = 1024 * 1024
F32 = jnp.float32
BF16 = jnp.bfloat16
WHOLE = pl.BlockSpec(memory_space=pltpu.VMEM)
SCALARS = pl.BlockSpec(memory_space=pltpu.SMEM)
FAR = pl.BlockSpec(memory_space=pl.ANY)


def iota(shape, axis):
    return lax.broadcasted_iota(jnp.int32, shape, axis)


def dot(left, right):
    return jnp.dot(left, right, preferred_element_type=F32)


def dot_t(left, right):
    return lax.dot_general(left, right, (((1,), (1,)), ((), ())), preferred_element_type=F32)


def params(mib):
    return pltpu.CompilerParams(vmem_limit_bytes=mib * MIB)


def block_places(owner, n_owners):
    rows = owner.shape[1]
    owner_hot = (iota((n_owners, rows), 0) == owner).astype(F32)
    upper = (iota((rows, rows), 0) <= iota((rows, rows), 1)).astype(BF16)
    running = dot(owner_hot.astype(BF16), upper)
    return jnp.sum(running * owner_hot, axis=0, keepdims=True).astype(jnp.int32) - 1


def one_hot_rows(owner, rank, block, capacity):
    place = jnp.where(owner == block, rank, -1)
    return (iota((capacity, owner.shape[1]), 0) == place).astype(F32).astype(BF16)


def code_kernel(owner_ref, position_ref, time_ref, code_ref, embed_ref):
    n_owners, _, capacity = code_ref.shape
    embed_ref[...] = time_ref[...]
    owner = owner_ref[...]
    rank = block_places(owner, n_owners)
    code = position_ref[...] + 1
    line = iota((8, owner.shape[1]), 0)
    digits = jnp.where(line == 0, code // CODE, jnp.where(line == 1, code % CODE, 0))
    digits = digits.astype(F32).astype(BF16)
    for block in range(n_owners):
        sent = dot_t(digits, one_hot_rows(owner, rank, block, capacity))
        code_ref[block] = (sent[0:1] * CODE + sent[1:2]).astype(jnp.int32) - 1


def place_codes(owner, position, time_embed, n_owners, capacity):
    rows = owner.shape[0]
    return pl.pallas_call(
        code_kernel,
        out_shape=[
            jax.ShapeDtypeStruct((n_owners, 1, capacity), jnp.int32),
            jax.ShapeDtypeStruct(time_embed.shape, BF16),
        ],
        in_specs=[WHOLE] * 3,
        out_specs=[WHOLE] * 2,
        compiler_params=params(12),
        cost_estimate=pl.CostEstimate(
            flops=16 * rows * n_owners * capacity, bytes_accessed=8 * rows, transcendentals=0
        ),
        name="place_codes",
    )(owner.reshape(1, rows), position.reshape(1, rows), time_embed)


def place_kernel(owner_ref, feat_ref, out_ref):
    n_owners, capacity, _ = out_ref.shape
    owner = owner_ref[...]
    rank = block_places(owner, n_owners)
    feat = feat_ref[...]
    for block in range(n_owners):
        out_ref[block] = dot(one_hot_rows(owner, rank, block, capacity), feat).astype(BF16)


def place_rows(owner, obs_feat, n_owners, capacity):
    rows, width = obs_feat.shape
    return pl.pallas_call(
        place_kernel,
        out_shape=jax.ShapeDtypeStruct((n_owners, capacity, width), BF16),
        in_specs=[WHOLE] * 2,
        out_specs=WHOLE,
        compiler_params=params(12),
        cost_estimate=pl.CostEstimate(
            flops=2 * rows * width * n_owners * capacity,
            bytes_accessed=2 * width * (rows + n_owners * capacity),
            transcendentals=0,
        ),
        name="place_rows",
    )(owner.reshape(1, rows), obs_feat)


def pool_kernel(capacity, slot_dev, slot_ref, embed_ref, code_ref, got_ref, keep_ref, send_ref):
    half = keep_ref.shape[0]
    places = 2 * half
    mine = slot_ref[0]
    total = jnp.zeros((places, keep_ref.shape[1]), F32)
    seen = jnp.zeros((places, capacity), F32)
    for block in range(got_ref.shape[0]):
        code = code_ref[block]
        turned = jnp.where(code >= half, code - half, code + half)
        code = jnp.where((code >= 0) & (mine == 1), turned, code)
        hot = (iota((places, capacity), 0) == code).astype(F32)
        seen += hot
        total += dot(hot.astype(BF16), got_ref[block])
    count = jnp.sum(seen, axis=1, keepdims=True)
    steps = embed_ref.shape[0]
    step_hot = iota((places, steps), 1) == iota((places, steps), 0) % slot_dev + mine * slot_dev
    embed = dot(step_hot.astype(F32).astype(BF16), embed_ref[...])
    tokens = (total / jnp.maximum(count, 1.0) + embed).astype(BF16)
    keep_ref[...] = tokens[:half]
    send_ref[...] = tokens[half:]


def pool_rows(my_slot, time_embed, codes, got, capacity, slot_dev):
    width = time_embed.shape[1]
    half = jax.ShapeDtypeStruct((CB * slot_dev // 2, width), BF16)
    return pl.pallas_call(
        functools.partial(pool_kernel, capacity, slot_dev),
        out_shape=[half, half],
        in_specs=[SCALARS] + [WHOLE] * 3,
        out_specs=[WHOLE] * 2,
        compiler_params=params(12),
        cost_estimate=pl.CostEstimate(
            flops=2 * CB * slot_dev * got.size, bytes_accessed=2 * got.size, transcendentals=0
        ),
        name="pool_rows",
    )(my_slot, time_embed, codes, got)


def weave_kernel(slot_dev, slot_ref, order_ref, keep_ref, got_ref, out_ref):
    rows, width = out_ref.shape
    half = keep_ref.shape[0]
    mine = slot_ref[0]
    row, col = iota((rows, half), 0), iota((rows, half), 1)
    source = col == row // TSTEPS * slot_dev + row % slot_dev
    own = row % TSTEPS // slot_dev == mine
    from_keep = (source & own).astype(F32).astype(BF16)
    from_got = (source & jnp.logical_not(own)).astype(F32).astype(BF16)
    tokens = (dot(from_keep, keep_ref[...]) + dot(from_got, got_ref[...])).astype(BF16)
    move = (iota((width, width), 0) == order_ref[...]).astype(F32).astype(BF16)
    out_ref[...] = dot(tokens, move).astype(BF16)


def weave_steps(my_slot, order, keep, got, slot_dev):
    rows, width = 2 * keep.shape[0], keep.shape[1]
    return pl.pallas_call(
        functools.partial(weave_kernel, slot_dev),
        out_shape=jax.ShapeDtypeStruct((rows, width), BF16),
        in_specs=[SCALARS] + [WHOLE] * 3,
        out_specs=WHOLE,
        compiler_params=params(12),
        cost_estimate=pl.CostEstimate(
            flops=2 * rows * width * (rows + width), bytes_accessed=4 * rows * width, transcendentals=0
        ),
        name="weave_steps",
    )(my_slot, order.reshape(1, width), keep, got)


def attention(normed, weight, heads_width, ctx_ref):
    rows = normed.shape[0]
    group = LANES
    lane = iota((1, LANES), 1)
    first = iota((group, LANES), 1) < HD
    masks = [(lane < HD).astype(F32).astype(BF16), (lane >= HD).astype(F32).astype(BF16)]
    ones = (iota((LANES, LANES), 0) // HD == iota((LANES, LANES), 1) // HD).astype(F32)
    mean = (ones * (1.0 / HD)).astype(BF16)
    ones = ones.astype(BF16)
    same_cell = iota((2 * group, group), 0) % group // TSTEPS == iota((2 * group, group), 1) // TSTEPS
    same_cell = same_cell.astype(F32).astype(BF16)
    count = jnp.ones((group, LANES), BF16)
    projected = dot(normed, weight)
    begins = range(0, rows, group)
    for at in range(0, heads_width, LANES):
        query = projected[:, at : at + LANES]
        key = projected[:, heads_width + at : heads_width + at + LANES]
        value = projected[:, 2 * heads_width + at : 2 * heads_width + at + LANES].astype(BF16)
        query_bf, key_bf = query.astype(BF16), key.astype(BF16)
        query = (query * lax.rsqrt(dot(query_bf * query_bf, ones) + HD * EPS)).astype(BF16)
        key = (key * lax.rsqrt(dot(key_bf * key_bf, mean) + EPS)).astype(BF16)
        left, right = query * masks[0], query * masks[1]
        scores = [
            dot_t(jnp.concatenate([left[at : at + group], right[at : at + group]], axis=0), key[at : at + group])
            for at in begins
        ]
        expos = [jnp.exp(score).astype(BF16) * same_cell for score in scores]
        mixed = [
            dot(expo, jnp.concatenate([value[at : at + group], count], axis=1)) for at, expo in zip(begins, expos)
        ]
        for begin, both in zip(begins, mixed):
            top, low = both[:group], both[group:]
            over = jnp.where(first, top[:, :LANES], low[:, :LANES])
            under = jnp.where(first, top[:, LANES:], low[:, LANES:])
            ctx_ref[begin : begin + group, at : at + LANES] = (over / under).astype(BF16)


def gated(normed, gate_w, up_w, down_w):
    gate = dot(normed, gate_w)
    up = dot(normed, up_w)
    hidden = (gate * (0.5 * jnp.tanh(0.5 * gate) + 0.5) * up).astype(BF16)
    return dot_t(hidden, down_w)


def put_rows_kernel(plan, *refs):
    sems, outs, pieces = refs[-1], refs[-4:-1], refs[:-4]
    copies = []
    for number, (piece, out, source, row, at, size) in enumerate(plan):
        rows = pieces[piece].shape[0]
        target = outs[out].at[pl.ds(row, rows), pl.ds(at, size)]
        copies.append(pltpu.make_async_copy(pieces[piece].at[:, pl.ds(source, size)], target, sems.at[number]))
    for copy in copies:
        copy.start()
    for copy in copies:
        copy.wait()


def put_rows(pieces, rows, heads_width, hidden_width):
    gate_at, out_at = 3 * heads_width, 3 * heads_width + 2 * hidden_width
    down_at = out_at + heads_width
    end = down_at + hidden_width
    runs = [(0, gate_at, 0, 0), (gate_at, out_at, 1, 0), (out_at, down_at, 0, gate_at), (down_at, end, 2, 0)]
    plan = []
    for left, right, out, shift in runs:
        for number, (array, row, at) in enumerate(pieces):
            low, high = max(left, at), min(right, at + array.shape[1])
            if low < high:
                plan.append((number, out, low - at, row, shift + low - left, high - low))
    return pl.pallas_call(
        functools.partial(put_rows_kernel, plan),
        out_shape=[
            jax.ShapeDtypeStruct((rows, 4 * heads_width), BF16),
            jax.ShapeDtypeStruct((rows, 2 * hidden_width), BF16),
            jax.ShapeDtypeStruct((rows, hidden_width), BF16),
        ],
        in_specs=[FAR] * len(pieces),
        out_specs=[WHOLE] * 3,
        scratch_shapes=[pltpu.SemaphoreType.DMA((len(plan),))],
        compiler_params=params(53),
        cost_estimate=pl.CostEstimate(flops=0, bytes_accessed=4 * rows * end, transcendentals=0),
        name="put_rows",
    )(*[array for array, _, _ in pieces])


def layer_kernel(tok_ref, heads_ref, gate_up_ref, down_ref, out_ref, norm_ref, ctx_ref, acc_ref):
    heads_width = ctx_ref.shape[1]
    hidden_width = down_ref.shape[1]
    tokens = tok_ref[...].astype(F32)
    scale = lax.rsqrt(jnp.mean(tokens * tokens, axis=1, keepdims=True) + EPS)
    norm_ref[...] = (tokens * scale).astype(BF16)
    attention(norm_ref[...], heads_ref[:, : 3 * heads_width], heads_width, ctx_ref)
    acc_ref[...] = dot_t(ctx_ref[...], heads_ref[:, 3 * heads_width :])
    for begin in range(0, hidden_width, UNIT):
        end = begin + UNIT
        gate_w, up_w = gate_up_ref[:, begin:end], gate_up_ref[:, hidden_width + begin : hidden_width + end]
        add = gated(norm_ref[...], gate_w, up_w, down_ref[:, begin:end])
        if end < hidden_width:
            acc_ref[...] += add
        else:
            out_ref[...] = (acc_ref[...] + add).astype(out_ref.dtype)


def layer(tokens, heads, gate_up, down, out_type):
    rows, width = tokens.shape
    size = heads.size + gate_up.size + down.size
    return pl.pallas_call(
        layer_kernel,
        out_shape=jax.ShapeDtypeStruct((rows, width), out_type),
        in_specs=[WHOLE] * 4,
        out_specs=WHOLE,
        scratch_shapes=[
            pltpu.VMEM((rows, width), BF16),
            pltpu.VMEM((rows, heads.shape[1] // 4), BF16),
            pltpu.VMEM((rows, width), F32),
        ],
        compiler_params=params(28),
        cost_estimate=pl.CostEstimate(
            flops=2 * rows * size,
            bytes_accessed=2 * size + 6 * rows * width,
            transcendentals=rows * down.shape[1],
        ),
        name="layer",
    )(tokens, heads, gate_up, down)


def finish_kernel(tok_ref, sum_ref, got_ref, order_ref, out_ref):
    width = out_ref.shape[1]
    mixed = (tok_ref[...].astype(F32) + sum_ref[...] + got_ref[...].astype(F32)).astype(BF16)
    move = (iota((width, width), 0) == order_ref[...]).astype(F32).astype(BF16)
    out_ref[...] = dot_t(mixed, move).astype(BF16)


def finish(tokens, sums, got, order):
    rows, width = tokens.shape
    return pl.pallas_call(
        finish_kernel,
        out_shape=jax.ShapeDtypeStruct((rows, width), BF16),
        in_specs=[WHOLE] * 4,
        out_specs=WHOLE,
        compiler_params=params(12),
        cost_estimate=pl.CostEstimate(
            flops=2 * rows * width * width, bytes_accessed=10 * rows * width, transcendentals=0
        ),
        name="finish",
    )(tokens, sums, got, order.reshape(1, width))


def side_by_side(w_qkv, w_out, w_gate_up, w_down):
    rows = w_qkv.shape[0]
    return jnp.concatenate([w_qkv.reshape(rows, -1), w_gate_up.reshape(rows, -1), w_out, w_down], axis=1)


def along_cells(values, distance):
    n_cells = lax.axis_size("cells")
    return lax.ppermute(values, "cells", [(j, (j - distance) % n_cells) for j in range(n_cells)])


def to_other_places(shares):
    swap = [(0, 1), (1, 0)]
    by_slot = lax.ppermute(shares, "slots", swap)
    by_group = lax.ppermute(shares, "groups", swap)
    cut = shares.shape[1] // 2
    left = lax.ppermute(by_slot[:, :cut], "groups", swap)
    right = lax.ppermute(by_group[:, cut:], "slots", swap)
    return [shares, by_slot, by_group, left, right]


def arrival_order(width, n_share):
    n_cells = lax.axis_size("cells")
    mine = lax.axis_index("cells")
    place = lax.axis_index("groups") * lax.axis_size("slots") + lax.axis_index("slots")
    rows = width // n_cells
    share = rows // n_share
    row = jnp.arange(width, dtype=jnp.int32)
    past = row - 2 * rows
    far = jnp.where(past < 0, row // share % n_share, past // (2 * share))
    distance = jnp.where(past < 0, n_cells - 1, 1 + past // share % 2)
    other = (mine + distance) % n_cells * rows + (far ^ place) * share + row % share
    return jnp.where(row < rows, mine * rows + row, other)


def tokens_by_exchanges(owner, position, obs_feat, time_embed, my_slot, capacity, slot_dev):
    n_slots = lax.axis_size("slots")
    n_owners = lax.axis_size("cells") * lax.axis_size("mp")
    rows, width = obs_feat.shape
    owners = jnp.arange(n_owners, dtype=jnp.int32)
    owner_hot = (owner[:, None] == owners[None, :]).astype(F32)
    row_ids = jnp.arange(rows, dtype=jnp.int32)
    lower = (row_ids[None, :] <= row_ids[:, None]).astype(BF16)
    running = dot(lower, owner_hot.astype(BF16))
    rank = jnp.sum(running * owner_hot, axis=1).astype(jnp.int32) - 1
    place = jnp.where(owner < n_owners, owner * capacity + rank, n_owners * capacity)
    place_ids = jnp.arange(n_owners * capacity, dtype=jnp.int32)
    taken = place_ids[:, None] == place[None, :]
    send_feat = dot(taken.astype(BF16), obs_feat).astype(BF16).reshape(n_owners, capacity, width)
    send_code = jnp.sum(jnp.where(taken, position[None, :] + 1, 0), axis=1).reshape(n_owners, capacity)
    axes = ("cells", "mp")
    got_feat = lax.all_to_all(send_feat, axes, split_axis=0, concat_axis=0, tiled=True).reshape(-1, width)
    got_code = lax.all_to_all(send_code, axes, split_axis=0, concat_axis=0, tiled=True).reshape(-1) - 1
    hot = (jnp.arange(CB * slot_dev, dtype=jnp.int32)[:, None] == got_code[None, :]).astype(BF16)
    count = jnp.sum(hot.astype(F32), axis=1)
    pooled = dot(hot, got_feat) / jnp.maximum(count, 1.0)[:, None]
    embed = lax.dynamic_slice_in_dim(time_embed, my_slot * slot_dev, slot_dev, 0).astype(F32)
    tokens = (pooled.reshape(CB, slot_dev, width) + embed[None]).astype(BF16)
    grid = tokens.reshape(n_slots, CB // n_slots, slot_dev, width)
    grid = lax.all_to_all(grid, "slots", split_axis=0, concat_axis=2, tiled=True)
    return grid.reshape(-1, width)


def on_device(obs_feat, obs_cell, obs_slot, obs_count, time_embed, w_qkv, w_out, w_gate_up, w_down):
    n_cells = lax.axis_size("cells")
    n_slots = lax.axis_size("slots")
    n_groups = lax.axis_size("groups")
    n_mp = lax.axis_size("mp")
    n_owners = n_cells * n_mp
    rows, width = obs_feat.shape
    capacity = 3 * rows // n_owners
    quarter = CB // n_slots
    slot_dev = TSTEPS // n_slots
    my_slot = lax.axis_index("slots")
    n_share = n_groups * n_slots
    heads_width, hidden_width = w_qkv.shape[2], w_gate_up.shape[2]
    share = w_qkv.shape[0] // n_share
    valid = jnp.arange(rows, dtype=jnp.int32) < obs_count[0]
    owner = obs_cell // (quarter * n_mp * n_slots) * n_mp + obs_cell // quarter % n_mp
    owner = jnp.where(valid, owner, n_owners)
    local = obs_cell // (quarter * n_mp) % n_slots * quarter + obs_cell % quarter
    position = local * slot_dev + obs_slot

    local_weights = (w_qkv, w_out.T, w_gate_up, w_down.T)
    which = lax.axis_index("groups") * n_slots + my_slot
    share_weights = [lax.dynamic_slice_in_dim(w, which * share, share, 0) for w in local_weights]
    share_rows = side_by_side(*share_weights)
    if n_slots == 2 and n_groups == 2 and n_cells == 4 and share % 16 == 0 and capacity % 16 == 0:
        order = arrival_order(width, n_share)
        below = along_cells(share_rows, -1)
        codes, embed = place_codes(owner, position, time_embed, n_owners, capacity)
        below, codes, share_rows = lax.optimization_barrier((below, codes, share_rows))
        codes = lax.all_to_all(codes, ("cells", "mp"), split_axis=0, concat_axis=0, tiled=True)
        first = to_other_places(below)
        blocks = place_rows(owner, obs_feat, n_owners, capacity)
        above, opposite = along_cells(share_rows, 1), along_cells(below, -1)
        blocks, codes, above, first = lax.optimization_barrier((blocks, codes, above, first))
        second = to_other_places(jnp.concatenate([above, opposite], axis=0))
        shard = side_by_side(*local_weights)
        got = lax.all_to_all(blocks, ("cells", "mp"), split_axis=0, concat_axis=0, tiled=True)
        got, shard, second = lax.optimization_barrier((got, shard, second))
        keep, send = pool_rows(my_slot.reshape(1), embed, codes, got, capacity, slot_dev)
        other = lax.ppermute(send, "slots", [(0, 1), (1, 0)])
        pieces, row = [(shard, 0, 0)], shard.shape[0]
        for own, by_slot, by_group, left, right in (first, second):
            for array in (own, by_slot, by_group):
                pieces.append((array, row, 0))
                row += array.shape[0]
            pieces += [(left, row, 0), (right, row, left.shape[1])]
            row += own.shape[0]
        weights = put_rows(pieces, width, heads_width, hidden_width)
        other, weights = lax.optimization_barrier((other, weights))
        tokens = weave_steps(my_slot.reshape(1), order, keep, other, slot_dev)
    else:
        order = jnp.arange(width, dtype=jnp.int32)
        whole = lax.all_gather(share_rows, ("cells", "groups", "slots"), axis=0, tiled=True)
        weights = put_rows([(whole, 0, 0)], width, heads_width, hidden_width)
        tokens = tokens_by_exchanges(owner, position, obs_feat, time_embed, my_slot, capacity, slot_dev)

    swap = [(0, 1), (1, 0)]
    partner = lax.ppermute(tokens, "mp", swap)
    for_partner = layer(partner, *weights, BF16)
    from_partner = lax.ppermute(for_partner, "mp", swap)
    own = layer(tokens, *weights, F32)
    return finish(tokens, own, from_partner, order).reshape(quarter, TSTEPS, width)


def solution(mesh):
    placed = (
        P(("groups", "cells", "slots", "mp"), None),
        P(("groups", "cells", "slots", "mp")),
        P(("groups", "cells", "slots", "mp")),
        P(("groups", "cells", "slots", "mp")),
        P(),
        P("cells", None, "mp"),
        P("mp", "cells"),
        P("cells", None, "mp"),
        P("mp", "cells"),
    )
    return jax.shard_map(
        on_device,
        mesh=mesh,
        in_specs=placed,
        out_specs=P(("groups", "cells", "slots", "mp"), None, None),
        check_vma=False,
    )
```

```python
import functools

import jax
import jax.numpy as jnp
from jax import lax
from jax.experimental import pallas as pl
from jax.experimental.pallas import tpu as pltpu
from jax.sharding import PartitionSpec as P

HD = 64
TSTEPS = 8
CB = 128
EPS = 1e-06

CODE = 32
UNIT = 512
LANES = 128
MIB = 1024 * 1024
F32 = jnp.float32
BF16 = jnp.bfloat16
WHOLE = pl.BlockSpec(memory_space=pltpu.VMEM)
SCALARS = pl.BlockSpec(memory_space=pltpu.SMEM)
FAR = pl.BlockSpec(memory_space=pl.ANY)


def iota(shape, axis):
    return lax.broadcasted_iota(jnp.int32, shape, axis)


def dot(left, right):
    return jnp.dot(left, right, preferred_element_type=F32)


def dot_t(left, right):
    return lax.dot_general(left, right, (((1,), (1,)), ((), ())), preferred_element_type=F32)


def params(mib):
    return pltpu.CompilerParams(vmem_limit_bytes=mib * MIB)


def block_places(owner, n_owners):
    rows = owner.shape[1]
    owner_hot = (iota((n_owners, rows), 0) == owner).astype(F32)
    upper = (iota((rows, rows), 0) <= iota((rows, rows), 1)).astype(BF16)
    running = dot(owner_hot.astype(BF16), upper)
    return jnp.sum(running * owner_hot, axis=0, keepdims=True).astype(jnp.int32) - 1


def one_hot_rows(owner, rank, block, capacity):
    place = jnp.where(owner == block, rank, -1)
    return (iota((capacity, owner.shape[1]), 0) == place).astype(F32).astype(BF16)


def code_kernel(owner_ref, position_ref, time_ref, code_ref, embed_ref):
    n_owners, _, capacity = code_ref.shape
    embed_ref[...] = time_ref[...]
    owner = owner_ref[...]
    rank = block_places(owner, n_owners)
    code = position_ref[...] + 1
    line = iota((8, owner.shape[1]), 0)
    digits = jnp.where(line == 0, code // CODE, jnp.where(line == 1, code % CODE, 0))
    digits = digits.astype(F32).astype(BF16)
    for block in range(n_owners):
        sent = dot_t(digits, one_hot_rows(owner, rank, block, capacity))
        code_ref[block] = (sent[0:1] * CODE + sent[1:2]).astype(jnp.int32) - 1


def place_codes(owner, position, time_embed, n_owners, capacity):
    rows = owner.shape[0]
    return pl.pallas_call(
        code_kernel,
        out_shape=[
            jax.ShapeDtypeStruct((n_owners, 1, capacity), jnp.int32),
            jax.ShapeDtypeStruct(time_embed.shape, BF16),
        ],
        in_specs=[WHOLE] * 3,
        out_specs=[WHOLE] * 2,
        compiler_params=params(12),
        cost_estimate=pl.CostEstimate(
            flops=16 * rows * n_owners * capacity, bytes_accessed=8 * rows, transcendentals=0
        ),
        name="place_codes",
    )(owner.reshape(1, rows), position.reshape(1, rows), time_embed)


def place_kernel(owner_ref, feat_ref, out_ref):
    n_owners, capacity, _ = out_ref.shape
    owner = owner_ref[...]
    rank = block_places(owner, n_owners)
    feat = feat_ref[...]
    for block in range(n_owners):
        out_ref[block] = dot(one_hot_rows(owner, rank, block, capacity), feat).astype(BF16)


def place_rows(owner, obs_feat, n_owners, capacity):
    rows, width = obs_feat.shape
    return pl.pallas_call(
        place_kernel,
        out_shape=jax.ShapeDtypeStruct((n_owners, capacity, width), BF16),
        in_specs=[WHOLE] * 2,
        out_specs=WHOLE,
        compiler_params=params(12),
        cost_estimate=pl.CostEstimate(
            flops=2 * rows * width * n_owners * capacity,
            bytes_accessed=2 * width * (rows + n_owners * capacity),
            transcendentals=0,
        ),
        name="place_rows",
    )(owner.reshape(1, rows), obs_feat)


def pool_kernel(capacity, slot_dev, slot_ref, embed_ref, code_ref, got_ref, keep_ref, send_ref):
    half = keep_ref.shape[0]
    places = 2 * half
    mine = slot_ref[0]
    total = jnp.zeros((places, keep_ref.shape[1]), F32)
    seen = jnp.zeros((places, capacity), F32)
    for block in range(got_ref.shape[0]):
        code = code_ref[block]
        turned = jnp.where(code >= half, code - half, code + half)
        code = jnp.where((code >= 0) & (mine == 1), turned, code)
        hot = (iota((places, capacity), 0) == code).astype(F32)
        seen += hot
        total += dot(hot.astype(BF16), got_ref[block])
    count = jnp.sum(seen, axis=1, keepdims=True)
    steps = embed_ref.shape[0]
    step_hot = iota((places, steps), 1) == iota((places, steps), 0) % slot_dev + mine * slot_dev
    embed = dot(step_hot.astype(F32).astype(BF16), embed_ref[...])
    tokens = (total / jnp.maximum(count, 1.0) + embed).astype(BF16)
    keep_ref[...] = tokens[:half]
    send_ref[...] = tokens[half:]


def pool_rows(my_slot, time_embed, codes, got, capacity, slot_dev):
    width = time_embed.shape[1]
    half = jax.ShapeDtypeStruct((CB * slot_dev // 2, width), BF16)
    return pl.pallas_call(
        functools.partial(pool_kernel, capacity, slot_dev),
        out_shape=[half, half],
        in_specs=[SCALARS] + [WHOLE] * 3,
        out_specs=[WHOLE] * 2,
        compiler_params=params(12),
        cost_estimate=pl.CostEstimate(
            flops=2 * CB * slot_dev * got.size, bytes_accessed=2 * got.size, transcendentals=0
        ),
        name="pool_rows",
    )(my_slot, time_embed, codes, got)


def weave_kernel(slot_dev, slot_ref, order_ref, keep_ref, got_ref, out_ref):
    rows, width = out_ref.shape
    half = keep_ref.shape[0]
    mine = slot_ref[0]
    row, col = iota((rows, half), 0), iota((rows, half), 1)
    source = col == row // TSTEPS * slot_dev + row % slot_dev
    own = row % TSTEPS // slot_dev == mine
    from_keep = (source & own).astype(F32).astype(BF16)
    from_got = (source & jnp.logical_not(own)).astype(F32).astype(BF16)
    tokens = (dot(from_keep, keep_ref[...]) + dot(from_got, got_ref[...])).astype(BF16)
    move = (iota((width, width), 0) == order_ref[...]).astype(F32).astype(BF16)
    out_ref[...] = dot(tokens, move).astype(BF16)


def weave_steps(my_slot, order, keep, got, slot_dev):
    rows, width = 2 * keep.shape[0], keep.shape[1]
    return pl.pallas_call(
        functools.partial(weave_kernel, slot_dev),
        out_shape=jax.ShapeDtypeStruct((rows, width), BF16),
        in_specs=[SCALARS] + [WHOLE] * 3,
        out_specs=WHOLE,
        compiler_params=params(12),
        cost_estimate=pl.CostEstimate(
            flops=2 * rows * width * (rows + width), bytes_accessed=4 * rows * width, transcendentals=0
        ),
        name="weave_steps",
    )(my_slot, order.reshape(1, width), keep, got)


def attention(normed, weight, heads_width, ctx_ref):
    rows = normed.shape[0]
    group = LANES
    lane = iota((1, LANES), 1)
    first = iota((group, LANES), 1) < HD
    masks = [(lane < HD).astype(F32).astype(BF16), (lane >= HD).astype(F32).astype(BF16)]
    ones = (iota((LANES, LANES), 0) // HD == iota((LANES, LANES), 1) // HD).astype(F32)
    mean = (ones * (1.0 / HD)).astype(BF16)
    ones = ones.astype(BF16)
    same_cell = iota((2 * group, group), 0) % group // TSTEPS == iota((2 * group, group), 1) // TSTEPS
    same_cell = same_cell.astype(F32).astype(BF16)
    count = jnp.ones((group, LANES), BF16)
    projected = dot(normed, weight)
    begins = range(0, rows, group)
    for at in range(0, heads_width, LANES):
        query = projected[:, at : at + LANES]
        key = projected[:, heads_width + at : heads_width + at + LANES]
        value = projected[:, 2 * heads_width + at : 2 * heads_width + at + LANES].astype(BF16)
        query_bf, key_bf = query.astype(BF16), key.astype(BF16)
        query = (query * lax.rsqrt(dot(query_bf * query_bf, ones) + HD * EPS)).astype(BF16)
        key = (key * lax.rsqrt(dot(key_bf * key_bf, mean) + EPS)).astype(BF16)
        left, right = query * masks[0], query * masks[1]
        scores = [
            dot_t(jnp.concatenate([left[at : at + group], right[at : at + group]], axis=0), key[at : at + group])
            for at in begins
        ]
        expos = [jnp.exp(score).astype(BF16) * same_cell for score in scores]
        mixed = [
            dot(expo, jnp.concatenate([value[at : at + group], count], axis=1)) for at, expo in zip(begins, expos)
        ]
        for begin, both in zip(begins, mixed):
            top, low = both[:group], both[group:]
            over = jnp.where(first, top[:, :LANES], low[:, :LANES])
            under = jnp.where(first, top[:, LANES:], low[:, LANES:])
            ctx_ref[begin : begin + group, at : at + LANES] = (over / under).astype(BF16)


def gated(normed, gate_w, up_w, down_w):
    gate = dot(normed, gate_w)
    up = dot(normed, up_w)
    hidden = (gate * (0.5 * jnp.tanh(0.5 * gate) + 0.5) * up).astype(BF16)
    return dot_t(hidden, down_w)


def put_rows_kernel(plan, *refs):
    sems, outs, pieces = refs[-1], refs[-5:-1], refs[:-5]
    copies = []
    for number, (piece, out, source, row, at, size) in enumerate(plan):
        rows = pieces[piece].shape[0]
        target = outs[out].at[pl.ds(row, rows), pl.ds(at, size)]
        copies.append(pltpu.make_async_copy(pieces[piece].at[:, pl.ds(source, size)], target, sems.at[number]))
    for copy in copies:
        copy.start()
    for copy in copies:
        copy.wait()


def put_rows(pieces, rows, heads_width, hidden_width):
    gate_at, out_at = 3 * heads_width, 3 * heads_width + 2 * hidden_width
    down_at = out_at + heads_width
    end = down_at + hidden_width
    up_at = gate_at + hidden_width
    runs = [(0, gate_at, 0, 0), (gate_at, up_at, 1, 0), (up_at, out_at, 2, 0)]
    runs += [(out_at, down_at, 0, gate_at), (down_at, end, 3, 0)]
    plan = []
    for left, right, out, shift in runs:
        for number, (array, row, at) in enumerate(pieces):
            low, high = max(left, at), min(right, at + array.shape[1])
            if low < high:
                plan.append((number, out, low - at, row, shift + low - left, high - low))
    return pl.pallas_call(
        functools.partial(put_rows_kernel, plan),
        out_shape=[
            jax.ShapeDtypeStruct((rows, columns), BF16)
            for columns in (4 * heads_width, hidden_width, hidden_width, hidden_width)
        ],
        in_specs=[FAR] * len(pieces),
        out_specs=[WHOLE] * 4,
        scratch_shapes=[pltpu.SemaphoreType.DMA((len(plan),))],
        compiler_params=params(53),
        cost_estimate=pl.CostEstimate(flops=0, bytes_accessed=4 * rows * end, transcendentals=0),
        name="put_rows",
    )(*[array for array, _, _ in pieces])


def layer_kernel(tok_ref, heads_ref, gate_ref, up_ref, down_ref, out_ref, norm_ref, ctx_ref, acc_ref):
    heads_width = ctx_ref.shape[1]
    hidden_width = down_ref.shape[1]
    tokens = tok_ref[...].astype(F32)
    scale = lax.rsqrt(jnp.mean(tokens * tokens, axis=1, keepdims=True) + EPS)
    norm_ref[...] = (tokens * scale).astype(BF16)
    attention(norm_ref[...], heads_ref[:, : 3 * heads_width], heads_width, ctx_ref)
    acc_ref[...] = dot_t(ctx_ref[...], heads_ref[:, 3 * heads_width :])
    for begin in range(0, hidden_width, UNIT):
        end = begin + UNIT
        add = gated(norm_ref[...], gate_ref[:, begin:end], up_ref[:, begin:end], down_ref[:, begin:end])
        if end < hidden_width:
            acc_ref[...] += add
        else:
            out_ref[...] = (acc_ref[...] + add).astype(out_ref.dtype)


def layer(tokens, heads, gate, up, down, out_type):
    rows, width = tokens.shape
    size = heads.size + 3 * down.size
    return pl.pallas_call(
        layer_kernel,
        out_shape=jax.ShapeDtypeStruct((rows, width), out_type),
        in_specs=[WHOLE] * 5,
        out_specs=WHOLE,
        scratch_shapes=[
            pltpu.VMEM((rows, width), BF16),
            pltpu.VMEM((rows, heads.shape[1] // 4), BF16),
            pltpu.VMEM((rows, width), F32),
        ],
        compiler_params=params(28),
        cost_estimate=pl.CostEstimate(
            flops=2 * rows * size,
            bytes_accessed=2 * size + 6 * rows * width,
            transcendentals=rows * down.shape[1],
        ),
        name="layer",
    )(tokens, heads, gate, up, down)


def finish_kernel(tok_ref, sum_ref, got_ref, order_ref, out_ref):
    width = out_ref.shape[1]
    mixed = (tok_ref[...].astype(F32) + sum_ref[...] + got_ref[...].astype(F32)).astype(BF16)
    move = (iota((width, width), 0) == order_ref[...]).astype(F32).astype(BF16)
    out_ref[...] = dot_t(mixed, move).astype(BF16)


def finish(tokens, sums, got, order):
    rows, width = tokens.shape
    return pl.pallas_call(
        finish_kernel,
        out_shape=jax.ShapeDtypeStruct((rows, width), BF16),
        in_specs=[WHOLE] * 4,
        out_specs=WHOLE,
        compiler_params=params(12),
        cost_estimate=pl.CostEstimate(
            flops=2 * rows * width * width, bytes_accessed=10 * rows * width, transcendentals=0
        ),
        name="finish",
    )(tokens, sums, got, order.reshape(1, width))


def side_by_side(w_qkv, w_out, w_gate_up, w_down):
    rows = w_qkv.shape[0]
    return jnp.concatenate([w_qkv.reshape(rows, -1), w_gate_up.reshape(rows, -1), w_out, w_down], axis=1)


def along_cells(values, distance):
    n_cells = lax.axis_size("cells")
    return lax.ppermute(values, "cells", [(j, (j - distance) % n_cells) for j in range(n_cells)])


def to_other_places(shares):
    swap = [(0, 1), (1, 0)]
    by_slot = lax.ppermute(shares, "slots", swap)
    by_group = lax.ppermute(shares, "groups", swap)
    cut = shares.shape[1] // 2
    left = lax.ppermute(by_slot[:, :cut], "groups", swap)
    right = lax.ppermute(by_group[:, cut:], "slots", swap)
    return [shares, by_slot, by_group, left, right]


def arrival_order(width, n_share):
    n_cells = lax.axis_size("cells")
    mine = lax.axis_index("cells")
    place = lax.axis_index("groups") * lax.axis_size("slots") + lax.axis_index("slots")
    rows = width // n_cells
    share = rows // n_share
    row = jnp.arange(width, dtype=jnp.int32)
    past = row - 2 * rows
    far = jnp.where(past < 0, row // share % n_share, past // (2 * share))
    distance = jnp.where(past < 0, n_cells - 1, 1 + past // share % 2)
    other = (mine + distance) % n_cells * rows + (far ^ place) * share + row % share
    return jnp.where(row < rows, mine * rows + row, other)


def tokens_by_exchanges(owner, position, obs_feat, time_embed, my_slot, capacity, slot_dev):
    n_slots = lax.axis_size("slots")
    n_owners = lax.axis_size("cells") * lax.axis_size("mp")
    rows, width = obs_feat.shape
    owners = jnp.arange(n_owners, dtype=jnp.int32)
    owner_hot = (owner[:, None] == owners[None, :]).astype(F32)
    row_ids = jnp.arange(rows, dtype=jnp.int32)
    lower = (row_ids[None, :] <= row_ids[:, None]).astype(BF16)
    running = dot(lower, owner_hot.astype(BF16))
    rank = jnp.sum(running * owner_hot, axis=1).astype(jnp.int32) - 1
    place = jnp.where(owner < n_owners, owner * capacity + rank, n_owners * capacity)
    place_ids = jnp.arange(n_owners * capacity, dtype=jnp.int32)
    taken = place_ids[:, None] == place[None, :]
    send_feat = dot(taken.astype(BF16), obs_feat).astype(BF16).reshape(n_owners, capacity, width)
    send_code = jnp.sum(jnp.where(taken, position[None, :] + 1, 0), axis=1).reshape(n_owners, capacity)
    axes = ("cells", "mp")
    got_feat = lax.all_to_all(send_feat, axes, split_axis=0, concat_axis=0, tiled=True).reshape(-1, width)
    got_code = lax.all_to_all(send_code, axes, split_axis=0, concat_axis=0, tiled=True).reshape(-1) - 1
    hot = (jnp.arange(CB * slot_dev, dtype=jnp.int32)[:, None] == got_code[None, :]).astype(BF16)
    count = jnp.sum(hot.astype(F32), axis=1)
    pooled = dot(hot, got_feat) / jnp.maximum(count, 1.0)[:, None]
    embed = lax.dynamic_slice_in_dim(time_embed, my_slot * slot_dev, slot_dev, 0).astype(F32)
    tokens = (pooled.reshape(CB, slot_dev, width) + embed[None]).astype(BF16)
    grid = tokens.reshape(n_slots, CB // n_slots, slot_dev, width)
    grid = lax.all_to_all(grid, "slots", split_axis=0, concat_axis=2, tiled=True)
    return grid.reshape(-1, width)


def on_device(obs_feat, obs_cell, obs_slot, obs_count, time_embed, w_qkv, w_out, w_gate_up, w_down):
    n_cells = lax.axis_size("cells")
    n_slots = lax.axis_size("slots")
    n_groups = lax.axis_size("groups")
    n_mp = lax.axis_size("mp")
    n_owners = n_cells * n_mp
    rows, width = obs_feat.shape
    capacity = 3 * rows // n_owners
    quarter = CB // n_slots
    slot_dev = TSTEPS // n_slots
    my_slot = lax.axis_index("slots")
    n_share = n_groups * n_slots
    heads_width, hidden_width = w_qkv.shape[2], w_gate_up.shape[2]
    share = w_qkv.shape[0] // n_share
    valid = jnp.arange(rows, dtype=jnp.int32) < obs_count[0]
    owner = obs_cell // (quarter * n_mp * n_slots) * n_mp + obs_cell // quarter % n_mp
    owner = jnp.where(valid, owner, n_owners)
    local = obs_cell // (quarter * n_mp) % n_slots * quarter + obs_cell % quarter
    position = local * slot_dev + obs_slot

    local_weights = (w_qkv, w_out.T, w_gate_up, w_down.T)
    which = lax.axis_index("groups") * n_slots + my_slot
    share_weights = [lax.dynamic_slice_in_dim(w, which * share, share, 0) for w in local_weights]
    share_rows = side_by_side(*share_weights)
    if n_slots == 2 and n_groups == 2 and n_cells == 4 and share % 16 == 0 and capacity % 16 == 0:
        order = arrival_order(width, n_share)
        below = along_cells(share_rows, -1)
        codes, embed = place_codes(owner, position, time_embed, n_owners, capacity)
        below, codes, share_rows = lax.optimization_barrier((below, codes, share_rows))
        codes = lax.all_to_all(codes, ("cells", "mp"), split_axis=0, concat_axis=0, tiled=True)
        first = to_other_places(below)
        blocks = place_rows(owner, obs_feat, n_owners, capacity)
        above, opposite = along_cells(share_rows, 1), along_cells(below, -1)
        blocks, codes, above, opposite, first = lax.optimization_barrier((blocks, codes, above, opposite, first))
        second = to_other_places(jnp.concatenate([above, opposite], axis=0))
        shard = side_by_side(*local_weights)
        got = lax.all_to_all(blocks, ("cells", "mp"), split_axis=0, concat_axis=0, tiled=True)
        got, shard, second = lax.optimization_barrier((got, shard, second))
        keep, send = pool_rows(my_slot.reshape(1), embed, codes, got, capacity, slot_dev)
        other = lax.ppermute(send, "slots", [(0, 1), (1, 0)])
        pieces, row = [(shard, 0, 0)], shard.shape[0]
        for own, by_slot, by_group, left, right in (first, second):
            for array in (own, by_slot, by_group):
                pieces.append((array, row, 0))
                row += array.shape[0]
            pieces += [(left, row, 0), (right, row, left.shape[1])]
            row += own.shape[0]
        weights = put_rows(pieces, width, heads_width, hidden_width)
        other, weights = lax.optimization_barrier((other, weights))
        tokens = weave_steps(my_slot.reshape(1), order, keep, other, slot_dev)
    else:
        order = jnp.arange(width, dtype=jnp.int32)
        whole = lax.all_gather(share_rows, ("cells", "groups", "slots"), axis=0, tiled=True)
        weights = put_rows([(whole, 0, 0)], width, heads_width, hidden_width)
        tokens = tokens_by_exchanges(owner, position, obs_feat, time_embed, my_slot, capacity, slot_dev)

    swap = [(0, 1), (1, 0)]
    partner = lax.ppermute(tokens, "mp", swap)
    for_partner = layer(partner, *weights, BF16)
    from_partner = lax.ppermute(for_partner, "mp", swap)
    own = layer(tokens, *weights, F32)
    return finish(tokens, own, from_partner, order).reshape(quarter, TSTEPS, width)


def solution(mesh):
    placed = (
        P(("groups", "cells", "slots", "mp"), None),
        P(("groups", "cells", "slots", "mp")),
        P(("groups", "cells", "slots", "mp")),
        P(("groups", "cells", "slots", "mp")),
        P(),
        P("cells", None, "mp"),
        P("mp", "cells"),
        P("cells", None, "mp"),
        P("mp", "cells"),
    )
    return jax.shard_map(
        on_device,
        mesh=mesh,
        in_specs=placed,
        out_specs=P(("groups", "cells", "slots", "mp"), None, None),
        check_vma=False,
    )
```

```python
import functools

import jax
import jax.numpy as jnp
from jax import lax
from jax.experimental import pallas as pl
from jax.experimental.pallas import tpu as pltpu
from jax.sharding import PartitionSpec as P

HD = 64
TSTEPS = 8
CB = 128
EPS = 1e-06

CODE = 32
UNIT = 512
LANES = 128
MIB = 1024 * 1024
F32 = jnp.float32
BF16 = jnp.bfloat16
WHOLE = pl.BlockSpec(memory_space=pltpu.VMEM)
SCALARS = pl.BlockSpec(memory_space=pltpu.SMEM)
FAR = pl.BlockSpec(memory_space=pl.ANY)


def iota(shape, axis):
    return lax.broadcasted_iota(jnp.int32, shape, axis)


def dot(left, right):
    return jnp.dot(left, right, preferred_element_type=F32)


def dot_t(left, right):
    return lax.dot_general(left, right, (((1,), (1,)), ((), ())), preferred_element_type=F32)


def params(mib):
    return pltpu.CompilerParams(vmem_limit_bytes=mib * MIB)


def block_places(owner, n_owners):
    rows = owner.shape[1]
    owner_hot = (iota((n_owners, rows), 0) == owner).astype(F32)
    upper = (iota((rows, rows), 0) <= iota((rows, rows), 1)).astype(BF16)
    running = dot(owner_hot.astype(BF16), upper)
    return jnp.sum(running * owner_hot, axis=0, keepdims=True).astype(jnp.int32) - 1


def one_hot_rows(owner, rank, block, capacity):
    place = jnp.where(owner == block, rank, -1)
    return (iota((capacity, owner.shape[1]), 0) == place).astype(F32).astype(BF16)


def code_kernel(owner_ref, position_ref, time_ref, code_ref, embed_ref):
    n_owners, _, capacity = code_ref.shape
    embed_ref[...] = time_ref[...]
    owner = owner_ref[...]
    rank = block_places(owner, n_owners)
    code = position_ref[...] + 1
    line = iota((8, owner.shape[1]), 0)
    digits = jnp.where(line == 0, code // CODE, jnp.where(line == 1, code % CODE, 0))
    digits = digits.astype(F32).astype(BF16)
    for block in range(n_owners):
        sent = dot_t(digits, one_hot_rows(owner, rank, block, capacity))
        code_ref[block] = (sent[0:1] * CODE + sent[1:2]).astype(jnp.int32) - 1


def place_codes(owner, position, time_embed, n_owners, capacity):
    rows = owner.shape[0]
    return pl.pallas_call(
        code_kernel,
        out_shape=[
            jax.ShapeDtypeStruct((n_owners, 1, capacity), jnp.int32),
            jax.ShapeDtypeStruct(time_embed.shape, BF16),
        ],
        in_specs=[WHOLE] * 3,
        out_specs=[WHOLE] * 2,
        compiler_params=params(12),
        cost_estimate=pl.CostEstimate(
            flops=16 * rows * n_owners * capacity, bytes_accessed=8 * rows, transcendentals=0
        ),
        name="place_codes",
    )(owner.reshape(1, rows), position.reshape(1, rows), time_embed)


def place_kernel(owner_ref, feat_ref, out_ref):
    n_owners, capacity, _ = out_ref.shape
    owner = owner_ref[...]
    rank = block_places(owner, n_owners)
    feat = feat_ref[...]
    for block in range(n_owners):
        out_ref[block] = dot(one_hot_rows(owner, rank, block, capacity), feat).astype(BF16)


def place_rows(owner, obs_feat, n_owners, capacity):
    rows, width = obs_feat.shape
    return pl.pallas_call(
        place_kernel,
        out_shape=jax.ShapeDtypeStruct((n_owners, capacity, width), BF16),
        in_specs=[WHOLE] * 2,
        out_specs=WHOLE,
        compiler_params=params(12),
        cost_estimate=pl.CostEstimate(
            flops=2 * rows * width * n_owners * capacity,
            bytes_accessed=2 * width * (rows + n_owners * capacity),
            transcendentals=0,
        ),
        name="place_rows",
    )(owner.reshape(1, rows), obs_feat)


def pool_kernel(capacity, slot_dev, slot_ref, embed_ref, code_ref, got_ref, keep_ref, send_ref):
    half = keep_ref.shape[0]
    places = 2 * half
    mine = slot_ref[0]
    total = jnp.zeros((places, keep_ref.shape[1]), F32)
    seen = jnp.zeros((places, capacity), F32)
    for block in range(got_ref.shape[0]):
        code = code_ref[block]
        turned = jnp.where(code >= half, code - half, code + half)
        code = jnp.where((code >= 0) & (mine == 1), turned, code)
        hot = (iota((places, capacity), 0) == code).astype(F32)
        seen += hot
        total += dot(hot.astype(BF16), got_ref[block])
    count = jnp.sum(seen, axis=1, keepdims=True)
    steps = embed_ref.shape[0]
    step_hot = iota((places, steps), 1) == iota((places, steps), 0) % slot_dev + mine * slot_dev
    embed = dot(step_hot.astype(F32).astype(BF16), embed_ref[...])
    tokens = (total / jnp.maximum(count, 1.0) + embed).astype(BF16)
    keep_ref[...] = tokens[:half]
    send_ref[...] = tokens[half:]


def pool_rows(my_slot, time_embed, codes, got, capacity, slot_dev):
    width = time_embed.shape[1]
    half = jax.ShapeDtypeStruct((CB * slot_dev // 2, width), BF16)
    return pl.pallas_call(
        functools.partial(pool_kernel, capacity, slot_dev),
        out_shape=[half, half],
        in_specs=[SCALARS] + [WHOLE] * 3,
        out_specs=[WHOLE] * 2,
        compiler_params=params(12),
        cost_estimate=pl.CostEstimate(
            flops=2 * CB * slot_dev * got.size, bytes_accessed=2 * got.size, transcendentals=0
        ),
        name="pool_rows",
    )(my_slot, time_embed, codes, got)


def weave_kernel(slot_dev, slot_ref, order_ref, keep_ref, got_ref, out_ref):
    rows, width = out_ref.shape
    half = keep_ref.shape[0]
    mine = slot_ref[0]
    row, col = iota((rows, half), 0), iota((rows, half), 1)
    source = col == row // TSTEPS * slot_dev + row % slot_dev
    own = row % TSTEPS // slot_dev == mine
    from_keep = (source & own).astype(F32).astype(BF16)
    from_got = (source & jnp.logical_not(own)).astype(F32).astype(BF16)
    tokens = (dot(from_keep, keep_ref[...]) + dot(from_got, got_ref[...])).astype(BF16)
    move = (iota((width, width), 0) == order_ref[...]).astype(F32).astype(BF16)
    out_ref[...] = dot(tokens, move).astype(BF16)


def weave_steps(my_slot, order, keep, got, slot_dev):
    rows, width = 2 * keep.shape[0], keep.shape[1]
    return pl.pallas_call(
        functools.partial(weave_kernel, slot_dev),
        out_shape=jax.ShapeDtypeStruct((rows, width), BF16),
        in_specs=[SCALARS] + [WHOLE] * 3,
        out_specs=WHOLE,
        compiler_params=params(12),
        cost_estimate=pl.CostEstimate(
            flops=2 * rows * width * (rows + width), bytes_accessed=4 * rows * width, transcendentals=0
        ),
        name="weave_steps",
    )(my_slot, order.reshape(1, width), keep, got)


def attention(normed, weight, heads_width, ctx_ref):
    rows = normed.shape[0]
    group = LANES
    lane = iota((1, LANES), 1)
    first = iota((group, LANES), 1) < HD
    masks = [(lane < HD).astype(F32).astype(BF16), (lane >= HD).astype(F32).astype(BF16)]
    ones = (iota((LANES, LANES), 0) // HD == iota((LANES, LANES), 1) // HD).astype(F32)
    mean = (ones * (1.0 / HD)).astype(BF16)
    ones = ones.astype(BF16)
    same_cell = iota((2 * group, group), 0) % group // TSTEPS == iota((2 * group, group), 1) // TSTEPS
    same_cell = same_cell.astype(F32).astype(BF16)
    count = jnp.ones((group, LANES), BF16)
    projected = dot(normed, weight)
    begins = range(0, rows, group)
    for at in range(0, heads_width, LANES):
        query = projected[:, at : at + LANES]
        key = projected[:, heads_width + at : heads_width + at + LANES]
        value = projected[:, 2 * heads_width + at : 2 * heads_width + at + LANES].astype(BF16)
        query_bf, key_bf = query.astype(BF16), key.astype(BF16)
        query = (query * lax.rsqrt(dot(query_bf * query_bf, ones) + HD * EPS)).astype(BF16)
        key = (key * lax.rsqrt(dot(key_bf * key_bf, mean) + EPS)).astype(BF16)
        left, right = query * masks[0], query * masks[1]
        scores = [
            dot_t(jnp.concatenate([left[at : at + group], right[at : at + group]], axis=0), key[at : at + group])
            for at in begins
        ]
        expos = [jnp.exp(score).astype(BF16) * same_cell for score in scores]
        mixed = [
            dot(expo, jnp.concatenate([value[at : at + group], count], axis=1)) for at, expo in zip(begins, expos)
        ]
        for begin, both in zip(begins, mixed):
            top, low = both[:group], both[group:]
            over = jnp.where(first, top[:, :LANES], low[:, :LANES])
            under = jnp.where(first, top[:, LANES:], low[:, LANES:])
            ctx_ref[begin : begin + group, at : at + LANES] = (over / under).astype(BF16)


def gated(normed, gate_w, up_w, down_w):
    gate = dot(normed, gate_w)
    up = dot(normed, up_w)
    hidden = (gate * (0.5 * jnp.tanh(0.5 * gate) + 0.5) * up).astype(BF16)
    return dot_t(hidden, down_w)


def put_rows_kernel(plan, *refs):
    sems, outs, pieces = refs[-1], refs[-4:-1], refs[:-4]
    copies = []
    for number, (piece, out, source, row, at, size) in enumerate(plan):
        rows = pieces[piece].shape[0]
        target = outs[out].at[pl.ds(row, rows), pl.ds(at, size)]
        copies.append(pltpu.make_async_copy(pieces[piece].at[:, pl.ds(source, size)], target, sems.at[number]))
    for copy in copies:
        copy.start()
    for copy in copies:
        copy.wait()


def put_rows(pieces, rows, heads_width, hidden_width):
    gate_at, out_at = 3 * heads_width, 3 * heads_width + 2 * hidden_width
    down_at = out_at + heads_width
    end = down_at + hidden_width
    runs = [(0, gate_at, 0, 0), (gate_at, out_at, 1, 0), (out_at, down_at, 0, gate_at), (down_at, end, 2, 0)]
    plan = []
    for left, right, out, shift in runs:
        for number, (array, row, at) in enumerate(pieces):
            low, high = max(left, at), min(right, at + array.shape[1])
            if low < high:
                plan.append((number, out, low - at, row, shift + low - left, high - low))
    return pl.pallas_call(
        functools.partial(put_rows_kernel, plan),
        out_shape=[
            jax.ShapeDtypeStruct((rows, 4 * heads_width), BF16),
            jax.ShapeDtypeStruct((rows, 2 * hidden_width), BF16),
            jax.ShapeDtypeStruct((rows, hidden_width), BF16),
        ],
        in_specs=[FAR] * len(pieces),
        out_specs=[WHOLE] * 3,
        scratch_shapes=[pltpu.SemaphoreType.DMA((len(plan),))],
        compiler_params=params(40),
        cost_estimate=pl.CostEstimate(flops=0, bytes_accessed=4 * rows * end, transcendentals=0),
        name="put_rows",
    )(*[array for array, _, _ in pieces])


def layer_kernel(tok_ref, heads_ref, gate_up_ref, down_ref, out_ref, norm_ref, ctx_ref, acc_ref):
    heads_width = ctx_ref.shape[1]
    hidden_width = down_ref.shape[1]
    tokens = tok_ref[...].astype(F32)
    scale = lax.rsqrt(jnp.mean(tokens * tokens, axis=1, keepdims=True) + EPS)
    norm_ref[...] = (tokens * scale).astype(BF16)
    attention(norm_ref[...], heads_ref[:, : 3 * heads_width], heads_width, ctx_ref)
    acc_ref[...] = dot_t(ctx_ref[...], heads_ref[:, 3 * heads_width :])
    for begin in range(0, hidden_width, UNIT):
        end = begin + UNIT
        gate_w, up_w = gate_up_ref[:, begin:end], gate_up_ref[:, hidden_width + begin : hidden_width + end]
        add = gated(norm_ref[...], gate_w, up_w, down_ref[:, begin:end])
        if end < hidden_width:
            acc_ref[...] += add
        else:
            out_ref[...] = (acc_ref[...] + add).astype(out_ref.dtype)


def layer(tokens, heads, gate_up, down, out_type):
    rows, width = tokens.shape
    size = heads.size + gate_up.size + down.size
    return pl.pallas_call(
        layer_kernel,
        out_shape=jax.ShapeDtypeStruct((rows, width), out_type),
        in_specs=[WHOLE] * 4,
        out_specs=WHOLE,
        scratch_shapes=[
            pltpu.VMEM((rows, width), BF16),
            pltpu.VMEM((rows, heads.shape[1] // 4), BF16),
            pltpu.VMEM((rows, width), F32),
        ],
        compiler_params=params(28),
        cost_estimate=pl.CostEstimate(
            flops=2 * rows * size,
            bytes_accessed=2 * size + 6 * rows * width,
            transcendentals=rows * down.shape[1],
        ),
        name="layer",
    )(tokens, heads, gate_up, down)


def finish_kernel(tok_ref, sum_ref, got_ref, order_ref, out_ref):
    width = out_ref.shape[1]
    mixed = (tok_ref[...].astype(F32) + sum_ref[...] + got_ref[...].astype(F32)).astype(BF16)
    move = (iota((width, width), 0) == order_ref[...]).astype(F32).astype(BF16)
    out_ref[...] = dot_t(mixed, move).astype(BF16)


def finish(tokens, sums, got, order):
    rows, width = tokens.shape
    return pl.pallas_call(
        finish_kernel,
        out_shape=jax.ShapeDtypeStruct((rows, width), BF16),
        in_specs=[WHOLE] * 4,
        out_specs=WHOLE,
        compiler_params=params(12),
        cost_estimate=pl.CostEstimate(
            flops=2 * rows * width * width, bytes_accessed=10 * rows * width, transcendentals=0
        ),
        name="finish",
    )(tokens, sums, got, order.reshape(1, width))


def side_by_side(w_qkv, w_out, w_gate_up, w_down):
    rows = w_qkv.shape[0]
    return jnp.concatenate([w_qkv.reshape(rows, -1), w_gate_up.reshape(rows, -1), w_out, w_down], axis=1)


def along_cells(values, distance):
    n_cells = lax.axis_size("cells")
    return lax.ppermute(values, "cells", [(j, (j - distance) % n_cells) for j in range(n_cells)])


def to_other_places(shares):
    n_slots = lax.axis_size("slots")
    n_share = lax.axis_size("groups") * n_slots
    places = [shares]
    for far in range(1, n_share):
        pairs = [(place, place ^ far) for place in range(n_share)]
        places.append(lax.ppermute(shares, ("groups", "slots"), pairs))
    return places


def to_other_places_by_halves(shares):
    swap = [(0, 1), (1, 0)]
    by_slot = lax.ppermute(shares, "slots", swap)
    by_group = lax.ppermute(shares, "groups", swap)
    cut = shares.shape[1] // 2
    left = lax.ppermute(by_slot[:, :cut], "groups", swap)
    right = lax.ppermute(by_group[:, cut:], "slots", swap)
    return [shares, by_slot, by_group, left, right]


def arrival_order(width, n_share):
    n_cells = lax.axis_size("cells")
    mine = lax.axis_index("cells")
    place = lax.axis_index("groups") * lax.axis_size("slots") + lax.axis_index("slots")
    rows = width // n_cells
    share = rows // n_share
    row = jnp.arange(width, dtype=jnp.int32)
    past = row - 2 * rows
    far = jnp.where(past < 0, row // share % n_share, past // (2 * share))
    distance = jnp.where(past < 0, n_cells - 1, 1 + past // share % 2)
    other = (mine + distance) % n_cells * rows + (far ^ place) * share + row % share
    return jnp.where(row < rows, mine * rows + row, other)


def tokens_by_exchanges(owner, position, obs_feat, time_embed, my_slot, capacity, slot_dev):
    n_slots = lax.axis_size("slots")
    n_owners = lax.axis_size("cells") * lax.axis_size("mp")
    rows, width = obs_feat.shape
    owners = jnp.arange(n_owners, dtype=jnp.int32)
    owner_hot = (owner[:, None] == owners[None, :]).astype(F32)
    row_ids = jnp.arange(rows, dtype=jnp.int32)
    lower = (row_ids[None, :] <= row_ids[:, None]).astype(BF16)
    running = dot(lower, owner_hot.astype(BF16))
    rank = jnp.sum(running * owner_hot, axis=1).astype(jnp.int32) - 1
    place = jnp.where(owner < n_owners, owner * capacity + rank, n_owners * capacity)
    place_ids = jnp.arange(n_owners * capacity, dtype=jnp.int32)
    taken = place_ids[:, None] == place[None, :]
    send_feat = dot(taken.astype(BF16), obs_feat).astype(BF16).reshape(n_owners, capacity, width)
    send_code = jnp.sum(jnp.where(taken, position[None, :] + 1, 0), axis=1).reshape(n_owners, capacity)
    axes = ("cells", "mp")
    got_feat = lax.all_to_all(send_feat, axes, split_axis=0, concat_axis=0, tiled=True).reshape(-1, width)
    got_code = lax.all_to_all(send_code, axes, split_axis=0, concat_axis=0, tiled=True).reshape(-1) - 1
    hot = (jnp.arange(CB * slot_dev, dtype=jnp.int32)[:, None] == got_code[None, :]).astype(BF16)
    count = jnp.sum(hot.astype(F32), axis=1)
    pooled = dot(hot, got_feat) / jnp.maximum(count, 1.0)[:, None]
    embed = lax.dynamic_slice_in_dim(time_embed, my_slot * slot_dev, slot_dev, 0).astype(F32)
    tokens = (pooled.reshape(CB, slot_dev, width) + embed[None]).astype(BF16)
    grid = tokens.reshape(n_slots, CB // n_slots, slot_dev, width)
    grid = lax.all_to_all(grid, "slots", split_axis=0, concat_axis=2, tiled=True)
    return grid.reshape(-1, width)


def on_device(obs_feat, obs_cell, obs_slot, obs_count, time_embed, w_qkv, w_out, w_gate_up, w_down):
    n_cells = lax.axis_size("cells")
    n_slots = lax.axis_size("slots")
    n_groups = lax.axis_size("groups")
    n_mp = lax.axis_size("mp")
    n_owners = n_cells * n_mp
    rows, width = obs_feat.shape
    capacity = 3 * rows // n_owners
    quarter = CB // n_slots
    slot_dev = TSTEPS // n_slots
    my_slot = lax.axis_index("slots")
    n_share = n_groups * n_slots
    heads_width, hidden_width = w_qkv.shape[2], w_gate_up.shape[2]
    share = w_qkv.shape[0] // n_share
    valid = jnp.arange(rows, dtype=jnp.int32) < obs_count[0]
    owner = obs_cell // (quarter * n_mp * n_slots) * n_mp + obs_cell // quarter % n_mp
    owner = jnp.where(valid, owner, n_owners)
    local = obs_cell // (quarter * n_mp) % n_slots * quarter + obs_cell % quarter
    position = local * slot_dev + obs_slot

    local_weights = (w_qkv, w_out.T, w_gate_up, w_down.T)
    which = lax.axis_index("groups") * n_slots + my_slot
    share_weights = [lax.dynamic_slice_in_dim(w, which * share, share, 0) for w in local_weights]
    share_rows = side_by_side(*share_weights)
    if n_slots == 2 and n_groups == 2 and n_cells == 4 and share % 16 == 0 and capacity % 16 == 0:
        order = arrival_order(width, n_share)
        below = along_cells(share_rows, -1)
        codes, embed = place_codes(owner, position, time_embed, n_owners, capacity)
        below, codes, share_rows = lax.optimization_barrier((below, codes, share_rows))
        codes = lax.all_to_all(codes, ("cells", "mp"), split_axis=0, concat_axis=0, tiled=True)
        first = to_other_places(below)
        blocks = place_rows(owner, obs_feat, n_owners, capacity)
        above, opposite = along_cells(share_rows, 1), along_cells(below, -1)
        blocks, codes, above, opposite, first = lax.optimization_barrier((blocks, codes, above, opposite, first))
        second = to_other_places_by_halves(jnp.concatenate([above, opposite], axis=0))
        shard = side_by_side(*local_weights)
        got = lax.all_to_all(blocks, ("cells", "mp"), split_axis=0, concat_axis=0, tiled=True)
        got, shard, second = lax.optimization_barrier((got, shard, second))
        keep, send = pool_rows(my_slot.reshape(1), embed, codes, got, capacity, slot_dev)
        other = lax.ppermute(send, "slots", [(0, 1), (1, 0)])
        pieces, row = [], 0
        for array in [shard] + first + second[:3]:
            pieces.append((array, row, 0))
            row += array.shape[0]
        pieces += [(second[3], row, 0), (second[4], row, second[3].shape[1])]
        weights = put_rows(pieces, width, heads_width, hidden_width)
        other, weights = lax.optimization_barrier((other, weights))
        tokens = weave_steps(my_slot.reshape(1), order, keep, other, slot_dev)
    else:
        order = jnp.arange(width, dtype=jnp.int32)
        whole = lax.all_gather(share_rows, ("cells", "groups", "slots"), axis=0, tiled=True)
        weights = put_rows([(whole, 0, 0)], width, heads_width, hidden_width)
        tokens = tokens_by_exchanges(owner, position, obs_feat, time_embed, my_slot, capacity, slot_dev)

    swap = [(0, 1), (1, 0)]
    partner = lax.ppermute(tokens, "mp", swap)
    for_partner = layer(partner, *weights, BF16)
    from_partner = lax.ppermute(for_partner, "mp", swap)
    own = layer(tokens, *weights, F32)
    return finish(tokens, own, from_partner, order).reshape(quarter, TSTEPS, width)


def solution(mesh):
    placed = (
        P(("groups", "cells", "slots", "mp"), None),
        P(("groups", "cells", "slots", "mp")),
        P(("groups", "cells", "slots", "mp")),
        P(("groups", "cells", "slots", "mp")),
        P(),
        P("cells", None, "mp"),
        P("mp", "cells"),
        P("cells", None, "mp"),
        P("mp", "cells"),
    )
    return jax.shard_map(
        on_device,
        mesh=mesh,
        in_specs=placed,
        out_specs=P(("groups", "cells", "slots", "mp"), None, None),
        check_vma=False,
    )
```

```python
import functools

import jax
import jax.numpy as jnp
from jax import lax
from jax.experimental import pallas as pl
from jax.experimental.pallas import tpu as pltpu
from jax.sharding import PartitionSpec as P

HD = 64
TSTEPS = 8
CB = 128
EPS = 1e-06

CODE = 32
UNIT = 512
LANES = 128
MIB = 1024 * 1024
F32 = jnp.float32
BF16 = jnp.bfloat16
WHOLE = pl.BlockSpec(memory_space=pltpu.VMEM)
SCALARS = pl.BlockSpec(memory_space=pltpu.SMEM)
FAR = pl.BlockSpec(memory_space=pl.ANY)


def iota(shape, axis):
    return lax.broadcasted_iota(jnp.int32, shape, axis)


def dot(left, right):
    return jnp.dot(left, right, preferred_element_type=F32)


def dot_t(left, right):
    return lax.dot_general(left, right, (((1,), (1,)), ((), ())), preferred_element_type=F32)


def params(mib):
    return pltpu.CompilerParams(vmem_limit_bytes=mib * MIB)


def block_places(owner, n_owners):
    rows = owner.shape[1]
    owner_hot = (iota((n_owners, rows), 0) == owner).astype(F32)
    upper = (iota((rows, rows), 0) <= iota((rows, rows), 1)).astype(BF16)
    running = dot(owner_hot.astype(BF16), upper)
    return jnp.sum(running * owner_hot, axis=0, keepdims=True).astype(jnp.int32) - 1


def one_hot_rows(owner, rank, block, capacity):
    place = jnp.where(owner == block, rank, -1)
    return (iota((capacity, owner.shape[1]), 0) == place).astype(F32).astype(BF16)


def code_kernel(owner_ref, position_ref, time_ref, code_ref, embed_ref):
    n_owners, _, capacity = code_ref.shape
    embed_ref[...] = time_ref[...]
    owner = owner_ref[...]
    rank = block_places(owner, n_owners)
    code = position_ref[...] + 1
    line = iota((8, owner.shape[1]), 0)
    digits = jnp.where(line == 0, code // CODE, jnp.where(line == 1, code % CODE, 0))
    digits = digits.astype(F32).astype(BF16)
    for block in range(n_owners):
        sent = dot_t(digits, one_hot_rows(owner, rank, block, capacity))
        code_ref[block] = (sent[0:1] * CODE + sent[1:2]).astype(jnp.int32) - 1


def place_codes(owner, position, time_embed, n_owners, capacity):
    rows = owner.shape[0]
    return pl.pallas_call(
        code_kernel,
        out_shape=[
            jax.ShapeDtypeStruct((n_owners, 1, capacity), jnp.int32),
            jax.ShapeDtypeStruct(time_embed.shape, BF16),
        ],
        in_specs=[WHOLE] * 3,
        out_specs=[WHOLE] * 2,
        compiler_params=params(12),
        cost_estimate=pl.CostEstimate(
            flops=16 * rows * n_owners * capacity, bytes_accessed=8 * rows, transcendentals=0
        ),
        name="place_codes",
    )(owner.reshape(1, rows), position.reshape(1, rows), time_embed)


def place_kernel(owner_ref, feat_ref, out_ref):
    n_owners, capacity, _ = out_ref.shape
    owner = owner_ref[...]
    rank = block_places(owner, n_owners)
    feat = feat_ref[...]
    for block in range(n_owners):
        out_ref[block] = dot(one_hot_rows(owner, rank, block, capacity), feat).astype(BF16)


def place_rows(owner, obs_feat, n_owners, capacity):
    rows, width = obs_feat.shape
    return pl.pallas_call(
        place_kernel,
        out_shape=jax.ShapeDtypeStruct((n_owners, capacity, width), BF16),
        in_specs=[WHOLE] * 2,
        out_specs=WHOLE,
        compiler_params=params(12),
        cost_estimate=pl.CostEstimate(
            flops=2 * rows * width * n_owners * capacity,
            bytes_accessed=2 * width * (rows + n_owners * capacity),
            transcendentals=0,
        ),
        name="place_rows",
    )(owner.reshape(1, rows), obs_feat)


def pool_kernel(capacity, slot_dev, slot_ref, embed_ref, code_ref, got_ref, keep_ref, send_ref):
    half = keep_ref.shape[0]
    places = 2 * half
    mine = slot_ref[0]
    total = jnp.zeros((places, keep_ref.shape[1]), F32)
    seen = jnp.zeros((places, capacity), F32)
    for block in range(got_ref.shape[0]):
        code = code_ref[block]
        turned = jnp.where(code >= half, code - half, code + half)
        code = jnp.where((code >= 0) & (mine == 1), turned, code)
        hot = (iota((places, capacity), 0) == code).astype(F32)
        seen += hot
        total += dot(hot.astype(BF16), got_ref[block])
    count = jnp.sum(seen, axis=1, keepdims=True)
    steps = embed_ref.shape[0]
    step_hot = iota((places, steps), 1) == iota((places, steps), 0) % slot_dev + mine * slot_dev
    embed = dot(step_hot.astype(F32).astype(BF16), embed_ref[...])
    tokens = (total / jnp.maximum(count, 1.0) + embed).astype(BF16)
    keep_ref[...] = tokens[:half]
    send_ref[...] = tokens[half:]


def pool_rows(my_slot, time_embed, codes, got, capacity, slot_dev):
    width = time_embed.shape[1]
    half = jax.ShapeDtypeStruct((CB * slot_dev // 2, width), BF16)
    return pl.pallas_call(
        functools.partial(pool_kernel, capacity, slot_dev),
        out_shape=[half, half],
        in_specs=[SCALARS] + [WHOLE] * 3,
        out_specs=[WHOLE] * 2,
        compiler_params=params(12),
        cost_estimate=pl.CostEstimate(
            flops=2 * CB * slot_dev * got.size, bytes_accessed=2 * got.size, transcendentals=0
        ),
        name="pool_rows",
    )(my_slot, time_embed, codes, got)


def weave_kernel(slot_dev, slot_ref, order_ref, keep_ref, got_ref, out_ref):
    rows, width = out_ref.shape
    half = keep_ref.shape[0]
    mine = slot_ref[0]
    row, col = iota((rows, half), 0), iota((rows, half), 1)
    source = col == row // TSTEPS * slot_dev + row % slot_dev
    own = row % TSTEPS // slot_dev == mine
    from_keep = (source & own).astype(F32).astype(BF16)
    from_got = (source & jnp.logical_not(own)).astype(F32).astype(BF16)
    tokens = (dot(from_keep, keep_ref[...]) + dot(from_got, got_ref[...])).astype(BF16)
    move = (iota((width, width), 0) == order_ref[...]).astype(F32).astype(BF16)
    out_ref[...] = dot(tokens, move).astype(BF16)


def weave_steps(my_slot, order, keep, got, slot_dev):
    rows, width = 2 * keep.shape[0], keep.shape[1]
    return pl.pallas_call(
        functools.partial(weave_kernel, slot_dev),
        out_shape=jax.ShapeDtypeStruct((rows, width), BF16),
        in_specs=[SCALARS] + [WHOLE] * 3,
        out_specs=WHOLE,
        compiler_params=params(12),
        cost_estimate=pl.CostEstimate(
            flops=16 * rows * width * (rows + width), bytes_accessed=4 * rows * width, transcendentals=0
        ),
        name="weave_steps",
    )(my_slot, order.reshape(1, width), keep, got)


def attention(normed, weight, heads_width, ctx_ref):
    rows = normed.shape[0]
    group = LANES
    lane = iota((1, LANES), 1)
    first = iota((group, LANES), 1) < HD
    masks = [(lane < HD).astype(F32).astype(BF16), (lane >= HD).astype(F32).astype(BF16)]
    ones = (iota((LANES, LANES), 0) // HD == iota((LANES, LANES), 1) // HD).astype(F32)
    mean = (ones * (1.0 / HD)).astype(BF16)
    ones = ones.astype(BF16)
    same_cell = iota((2 * group, group), 0) % group // TSTEPS == iota((2 * group, group), 1) // TSTEPS
    same_cell = same_cell.astype(F32).astype(BF16)
    count = jnp.ones((group, LANES), BF16)
    projected = dot(normed, weight)
    begins = range(0, rows, group)
    for at in range(0, heads_width, LANES):
        query = projected[:, at : at + LANES]
        key = projected[:, heads_width + at : heads_width + at + LANES]
        value = projected[:, 2 * heads_width + at : 2 * heads_width + at + LANES].astype(BF16)
        query_bf, key_bf = query.astype(BF16), key.astype(BF16)
        query = (query * lax.rsqrt(dot(query_bf * query_bf, ones) + HD * EPS)).astype(BF16)
        key = (key * lax.rsqrt(dot(key_bf * key_bf, mean) + EPS)).astype(BF16)
        left, right = query * masks[0], query * masks[1]
        scores = [
            dot_t(jnp.concatenate([left[at : at + group], right[at : at + group]], axis=0), key[at : at + group])
            for at in begins
        ]
        expos = [jnp.exp(score).astype(BF16) * same_cell for score in scores]
        mixed = [
            dot(expo, jnp.concatenate([value[at : at + group], count], axis=1)) for at, expo in zip(begins, expos)
        ]
        for begin, both in zip(begins, mixed):
            top, low = both[:group], both[group:]
            over = jnp.where(first, top[:, :LANES], low[:, :LANES])
            under = jnp.where(first, top[:, LANES:], low[:, LANES:])
            ctx_ref[begin : begin + group, at : at + LANES] = (over / under).astype(BF16)


def gated(normed, gate_w, up_w, down_w):
    gate = dot(normed, gate_w)
    up = dot(normed, up_w)
    hidden = (gate * (0.5 * jnp.tanh(0.5 * gate) + 0.5) * up).astype(BF16)
    return dot_t(hidden, down_w)


def put_rows_kernel(plan, *refs):
    sems, outs, pieces = refs[-1], refs[-4:-1], refs[:-4]
    copies = []
    for number, (piece, out, source, row, at, size) in enumerate(plan):
        rows = pieces[piece].shape[0]
        target = outs[out].at[pl.ds(row, rows), pl.ds(at, size)]
        copies.append(pltpu.make_async_copy(pieces[piece].at[:, pl.ds(source, size)], target, sems.at[number]))
    for copy in copies:
        copy.start()
    for copy in copies:
        copy.wait()


def put_rows(pieces, rows, heads_width, hidden_width):
    gate_at, out_at = 3 * heads_width, 3 * heads_width + 2 * hidden_width
    down_at = out_at + heads_width
    end = down_at + hidden_width
    runs = [(0, gate_at, 0, 0), (gate_at, out_at, 1, 0), (out_at, down_at, 0, gate_at), (down_at, end, 2, 0)]
    plan = []
    for left, right, out, shift in runs:
        for number, (array, row, at) in enumerate(pieces):
            low, high = max(left, at), min(right, at + array.shape[1])
            if low < high:
                plan.append((number, out, low - at, row, shift + low - left, high - low))
    return pl.pallas_call(
        functools.partial(put_rows_kernel, plan),
        out_shape=[
            jax.ShapeDtypeStruct((rows, 4 * heads_width), BF16),
            jax.ShapeDtypeStruct((rows, 2 * hidden_width), BF16),
            jax.ShapeDtypeStruct((rows, hidden_width), BF16),
        ],
        in_specs=[FAR] * len(pieces),
        out_specs=[WHOLE] * 3,
        scratch_shapes=[pltpu.SemaphoreType.DMA((len(plan),))],
        compiler_params=params(53),
        cost_estimate=pl.CostEstimate(flops=0, bytes_accessed=4 * rows * end, transcendentals=0),
        name="put_rows",
    )(*[array for array, _, _ in pieces])


def layer_kernel(tok_ref, heads_ref, gate_up_ref, down_ref, out_ref, norm_ref, ctx_ref, acc_ref):
    heads_width = ctx_ref.shape[1]
    hidden_width = down_ref.shape[1]
    tokens = tok_ref[...].astype(F32)
    scale = lax.rsqrt(jnp.mean(tokens * tokens, axis=1, keepdims=True) + EPS)
    norm_ref[...] = (tokens * scale).astype(BF16)
    attention(norm_ref[...], heads_ref[:, : 3 * heads_width], heads_width, ctx_ref)
    acc_ref[...] = dot_t(ctx_ref[...], heads_ref[:, 3 * heads_width :])
    for begin in range(0, hidden_width, UNIT):
        end = begin + UNIT
        gate_w, up_w = gate_up_ref[:, begin:end], gate_up_ref[:, hidden_width + begin : hidden_width + end]
        add = gated(norm_ref[...], gate_w, up_w, down_ref[:, begin:end])
        if end < hidden_width:
            acc_ref[...] += add
        else:
            out_ref[...] = (acc_ref[...] + add).astype(out_ref.dtype)


def layer(tokens, heads, gate_up, down, out_type):
    rows, width = tokens.shape
    size = heads.size + gate_up.size + down.size
    return pl.pallas_call(
        layer_kernel,
        out_shape=jax.ShapeDtypeStruct((rows, width), out_type),
        in_specs=[WHOLE] * 4,
        out_specs=WHOLE,
        scratch_shapes=[
            pltpu.VMEM((rows, width), BF16),
            pltpu.VMEM((rows, heads.shape[1] // 4), BF16),
            pltpu.VMEM((rows, width), F32),
        ],
        compiler_params=params(28),
        cost_estimate=pl.CostEstimate(
            flops=2 * rows * size,
            bytes_accessed=2 * size + 6 * rows * width,
            transcendentals=rows * down.shape[1],
        ),
        name="layer",
    )(tokens, heads, gate_up, down)


def finish_kernel(tok_ref, sum_ref, got_ref, order_ref, out_ref):
    width = out_ref.shape[1]
    mixed = (tok_ref[...].astype(F32) + sum_ref[...] + got_ref[...].astype(F32)).astype(BF16)
    move = (iota((width, width), 0) == order_ref[...]).astype(F32).astype(BF16)
    out_ref[...] = dot_t(mixed, move).astype(BF16)


def finish(tokens, sums, got, order):
    rows, width = tokens.shape
    return pl.pallas_call(
        finish_kernel,
        out_shape=jax.ShapeDtypeStruct((rows, width), BF16),
        in_specs=[WHOLE] * 4,
        out_specs=WHOLE,
        compiler_params=params(12),
        cost_estimate=pl.CostEstimate(
            flops=2 * rows * width * width, bytes_accessed=10 * rows * width, transcendentals=0
        ),
        name="finish",
    )(tokens, sums, got, order.reshape(1, width))


def side_by_side(w_qkv, w_out, w_gate_up, w_down):
    rows = w_qkv.shape[0]
    return jnp.concatenate([w_qkv.reshape(rows, -1), w_gate_up.reshape(rows, -1), w_out, w_down], axis=1)


def along_cells(values, distance):
    n_cells = lax.axis_size("cells")
    return lax.ppermute(values, "cells", [(j, (j - distance) % n_cells) for j in range(n_cells)])


def to_other_places(shares):
    swap = [(0, 1), (1, 0)]
    by_slot = lax.ppermute(shares, "slots", swap)
    by_group = lax.ppermute(shares, "groups", swap)
    cut = shares.shape[1] // 2
    left = lax.ppermute(by_slot[:, :cut], "groups", swap)
    right = lax.ppermute(by_group[:, cut:], "slots", swap)
    return [shares, by_slot, by_group, left, right]


def arrival_order(width, n_share):
    n_cells = lax.axis_size("cells")
    mine = lax.axis_index("cells")
    place = lax.axis_index("groups") * lax.axis_size("slots") + lax.axis_index("slots")
    rows = width // n_cells
    share = rows // n_share
    row = jnp.arange(width, dtype=jnp.int32)
    past = row - 2 * rows
    far = jnp.where(past < 0, row // share % n_share, past // (2 * share))
    distance = jnp.where(past < 0, n_cells - 1, 1 + past // share % 2)
    other = (mine + distance) % n_cells * rows + (far ^ place) * share + row % share
    return jnp.where(row < rows, mine * rows + row, other)


def tokens_by_exchanges(owner, position, obs_feat, time_embed, my_slot, capacity, slot_dev):
    n_slots = lax.axis_size("slots")
    n_owners = lax.axis_size("cells") * lax.axis_size("mp")
    rows, width = obs_feat.shape
    owners = jnp.arange(n_owners, dtype=jnp.int32)
    owner_hot = (owner[:, None] == owners[None, :]).astype(F32)
    row_ids = jnp.arange(rows, dtype=jnp.int32)
    lower = (row_ids[None, :] <= row_ids[:, None]).astype(BF16)
    running = dot(lower, owner_hot.astype(BF16))
    rank = jnp.sum(running * owner_hot, axis=1).astype(jnp.int32) - 1
    place = jnp.where(owner < n_owners, owner * capacity + rank, n_owners * capacity)
    place_ids = jnp.arange(n_owners * capacity, dtype=jnp.int32)
    taken = place_ids[:, None] == place[None, :]
    send_feat = dot(taken.astype(BF16), obs_feat).astype(BF16).reshape(n_owners, capacity, width)
    send_code = jnp.sum(jnp.where(taken, position[None, :] + 1, 0), axis=1).reshape(n_owners, capacity)
    axes = ("cells", "mp")
    got_feat = lax.all_to_all(send_feat, axes, split_axis=0, concat_axis=0, tiled=True).reshape(-1, width)
    got_code = lax.all_to_all(send_code, axes, split_axis=0, concat_axis=0, tiled=True).reshape(-1) - 1
    hot = (jnp.arange(CB * slot_dev, dtype=jnp.int32)[:, None] == got_code[None, :]).astype(BF16)
    count = jnp.sum(hot.astype(F32), axis=1)
    pooled = dot(hot, got_feat) / jnp.maximum(count, 1.0)[:, None]
    embed = lax.dynamic_slice_in_dim(time_embed, my_slot * slot_dev, slot_dev, 0).astype(F32)
    tokens = (pooled.reshape(CB, slot_dev, width) + embed[None]).astype(BF16)
    grid = tokens.reshape(n_slots, CB // n_slots, slot_dev, width)
    grid = lax.all_to_all(grid, "slots", split_axis=0, concat_axis=2, tiled=True)
    return grid.reshape(-1, width)


def on_device(obs_feat, obs_cell, obs_slot, obs_count, time_embed, w_qkv, w_out, w_gate_up, w_down):
    n_cells = lax.axis_size("cells")
    n_slots = lax.axis_size("slots")
    n_groups = lax.axis_size("groups")
    n_mp = lax.axis_size("mp")
    n_owners = n_cells * n_mp
    rows, width = obs_feat.shape
    capacity = 3 * rows // n_owners
    quarter = CB // n_slots
    slot_dev = TSTEPS // n_slots
    my_slot = lax.axis_index("slots")
    n_share = n_groups * n_slots
    heads_width, hidden_width = w_qkv.shape[2], w_gate_up.shape[2]
    share = w_qkv.shape[0] // n_share
    valid = jnp.arange(rows, dtype=jnp.int32) < obs_count[0]
    owner = obs_cell // (quarter * n_mp * n_slots) * n_mp + obs_cell // quarter % n_mp
    owner = jnp.where(valid, owner, n_owners)
    local = obs_cell // (quarter * n_mp) % n_slots * quarter + obs_cell % quarter
    position = local * slot_dev + obs_slot

    local_weights = (w_qkv, w_out.T, w_gate_up, w_down.T)
    which = lax.axis_index("groups") * n_slots + my_slot
    share_weights = [lax.dynamic_slice_in_dim(w, which * share, share, 0) for w in local_weights]
    share_rows = side_by_side(*share_weights)
    if n_slots == 2 and n_groups == 2 and n_cells == 4 and share % 16 == 0 and capacity % 16 == 0:
        order = arrival_order(width, n_share)
        below = along_cells(share_rows, -1)
        codes, embed = place_codes(owner, position, time_embed, n_owners, capacity)
        below, codes, share_rows = lax.optimization_barrier((below, codes, share_rows))
        codes = lax.all_to_all(codes, ("cells", "mp"), split_axis=0, concat_axis=0, tiled=True)
        first = to_other_places(below)
        blocks = place_rows(owner, obs_feat, n_owners, capacity)
        above, opposite = along_cells(share_rows, 1), along_cells(below, -1)
        blocks, codes, above, opposite, first = lax.optimization_barrier((blocks, codes, above, opposite, first))
        second = to_other_places(jnp.concatenate([above, opposite], axis=0))
        shard = side_by_side(*local_weights)
        got = lax.all_to_all(blocks, ("cells", "mp"), split_axis=0, concat_axis=0, tiled=True)
        got, shard, second = lax.optimization_barrier((got, shard, second))
        keep, send = pool_rows(my_slot.reshape(1), embed, codes, got, capacity, slot_dev)
        other = lax.ppermute(send, "slots", [(0, 1), (1, 0)])
        pieces, row = [(shard, 0, 0)], shard.shape[0]
        for own, by_slot, by_group, left, right in (first, second):
            for array in (own, by_slot, by_group):
                pieces.append((array, row, 0))
                row += array.shape[0]
            pieces += [(left, row, 0), (right, row, left.shape[1])]
            row += own.shape[0]
        weights = put_rows(pieces, width, heads_width, hidden_width)
        other, weights = lax.optimization_barrier((other, weights))
        tokens = weave_steps(my_slot.reshape(1), order, keep, other, slot_dev)
    else:
        order = jnp.arange(width, dtype=jnp.int32)
        whole = lax.all_gather(share_rows, ("cells", "groups", "slots"), axis=0, tiled=True)
        weights = put_rows([(whole, 0, 0)], width, heads_width, hidden_width)
        tokens = tokens_by_exchanges(owner, position, obs_feat, time_embed, my_slot, capacity, slot_dev)

    swap = [(0, 1), (1, 0)]
    partner = lax.ppermute(tokens, "mp", swap)
    for_partner = layer(partner, *weights, BF16)
    from_partner = lax.ppermute(for_partner, "mp", swap)
    own = layer(tokens, *weights, F32)
    return finish(tokens, own, from_partner, order).reshape(quarter, TSTEPS, width)


def solution(mesh):
    placed = (
        P(("groups", "cells", "slots", "mp"), None),
        P(("groups", "cells", "slots", "mp")),
        P(("groups", "cells", "slots", "mp")),
        P(("groups", "cells", "slots", "mp")),
        P(),
        P("cells", None, "mp"),
        P("mp", "cells"),
        P("cells", None, "mp"),
        P("mp", "cells"),
    )
    return jax.shard_map(
        on_device,
        mesh=mesh,
        in_specs=placed,
        out_specs=P(("groups", "cells", "slots", "mp"), None, None),
        check_vma=False,
    )
```

```python
import functools

import jax
import jax.numpy as jnp
from jax import lax
from jax.experimental import pallas as pl
from jax.experimental.pallas import tpu as pltpu
from jax.sharding import PartitionSpec as P

HD = 64
TSTEPS = 8
CB = 128
EPS = 1e-06

CODE = 32
UNIT = 768
LANES = 128
MIB = 1024 * 1024
F32 = jnp.float32
BF16 = jnp.bfloat16
WHOLE = pl.BlockSpec(memory_space=pltpu.VMEM)
SCALARS = pl.BlockSpec(memory_space=pltpu.SMEM)
FAR = pl.BlockSpec(memory_space=pl.ANY)


def iota(shape, axis):
    return lax.broadcasted_iota(jnp.int32, shape, axis)


def dot(left, right):
    return jnp.dot(left, right, preferred_element_type=F32)


def dot_t(left, right):
    return lax.dot_general(left, right, (((1,), (1,)), ((), ())), preferred_element_type=F32)


def params(mib):
    return pltpu.CompilerParams(vmem_limit_bytes=mib * MIB)


def block_places(owner, n_owners):
    rows = owner.shape[1]
    owner_hot = (iota((n_owners, rows), 0) == owner).astype(F32)
    upper = (iota((rows, rows), 0) <= iota((rows, rows), 1)).astype(BF16)
    running = dot(owner_hot.astype(BF16), upper)
    return jnp.sum(running * owner_hot, axis=0, keepdims=True).astype(jnp.int32) - 1


def one_hot_rows(owner, rank, block, capacity):
    place = jnp.where(owner == block, rank, -1)
    return (iota((capacity, owner.shape[1]), 0) == place).astype(F32).astype(BF16)


def code_kernel(owner_ref, position_ref, time_ref, code_ref, embed_ref):
    n_owners, _, capacity = code_ref.shape
    embed_ref[...] = time_ref[...]
    owner = owner_ref[...]
    rank = block_places(owner, n_owners)
    code = position_ref[...] + 1
    line = iota((8, owner.shape[1]), 0)
    digits = jnp.where(line == 0, code // CODE, jnp.where(line == 1, code % CODE, 0))
    digits = digits.astype(F32).astype(BF16)
    for block in range(n_owners):
        sent = dot_t(digits, one_hot_rows(owner, rank, block, capacity))
        code_ref[block] = (sent[0:1] * CODE + sent[1:2]).astype(jnp.int32) - 1


def place_codes(owner, position, time_embed, n_owners, capacity):
    rows = owner.shape[0]
    return pl.pallas_call(
        code_kernel,
        out_shape=[
            jax.ShapeDtypeStruct((n_owners, 1, capacity), jnp.int32),
            jax.ShapeDtypeStruct(time_embed.shape, BF16),
        ],
        in_specs=[WHOLE] * 3,
        out_specs=[WHOLE] * 2,
        compiler_params=params(12),
        cost_estimate=pl.CostEstimate(
            flops=16 * rows * n_owners * capacity, bytes_accessed=8 * rows, transcendentals=0
        ),
        name="place_codes",
    )(owner.reshape(1, rows), position.reshape(1, rows), time_embed)


def place_kernel(owner_ref, feat_ref, out_ref):
    n_owners, capacity, _ = out_ref.shape
    owner = owner_ref[...]
    rank = block_places(owner, n_owners)
    feat = feat_ref[...]
    for block in range(n_owners):
        out_ref[block] = dot(one_hot_rows(owner, rank, block, capacity), feat).astype(BF16)


def place_rows(owner, obs_feat, n_owners, capacity):
    rows, width = obs_feat.shape
    return pl.pallas_call(
        place_kernel,
        out_shape=jax.ShapeDtypeStruct((n_owners, capacity, width), BF16),
        in_specs=[WHOLE] * 2,
        out_specs=WHOLE,
        compiler_params=params(12),
        cost_estimate=pl.CostEstimate(
            flops=2 * rows * width * n_owners * capacity,
            bytes_accessed=2 * width * (rows + n_owners * capacity),
            transcendentals=0,
        ),
        name="place_rows",
    )(owner.reshape(1, rows), obs_feat)


def pool_kernel(capacity, slot_dev, slot_ref, embed_ref, code_ref, got_ref, keep_ref, send_ref):
    half = keep_ref.shape[0]
    places = 2 * half
    mine = slot_ref[0]
    total = jnp.zeros((places, keep_ref.shape[1]), F32)
    seen = jnp.zeros((places, capacity), F32)
    for block in range(got_ref.shape[0]):
        code = code_ref[block]
        turned = jnp.where(code >= half, code - half, code + half)
        code = jnp.where((code >= 0) & (mine == 1), turned, code)
        hot = (iota((places, capacity), 0) == code).astype(F32)
        seen += hot
        total += dot(hot.astype(BF16), got_ref[block])
    count = jnp.sum(seen, axis=1, keepdims=True)
    steps = embed_ref.shape[0]
    step_hot = iota((places, steps), 1) == iota((places, steps), 0) % slot_dev + mine * slot_dev
    embed = dot(step_hot.astype(F32).astype(BF16), embed_ref[...])
    tokens = (total / jnp.maximum(count, 1.0) + embed).astype(BF16)
    keep_ref[...] = tokens[:half]
    send_ref[...] = tokens[half:]


def pool_rows(my_slot, time_embed, codes, got, capacity, slot_dev):
    width = time_embed.shape[1]
    half = jax.ShapeDtypeStruct((CB * slot_dev // 2, width), BF16)
    return pl.pallas_call(
        functools.partial(pool_kernel, capacity, slot_dev),
        out_shape=[half, half],
        in_specs=[SCALARS] + [WHOLE] * 3,
        out_specs=[WHOLE] * 2,
        compiler_params=params(12),
        cost_estimate=pl.CostEstimate(
            flops=2 * CB * slot_dev * got.size, bytes_accessed=2 * got.size, transcendentals=0
        ),
        name="pool_rows",
    )(my_slot, time_embed, codes, got)


def weave_kernel(slot_dev, slot_ref, order_ref, keep_ref, got_ref, out_ref):
    rows, width = out_ref.shape
    half = keep_ref.shape[0]
    mine = slot_ref[0]
    row, col = iota((rows, half), 0), iota((rows, half), 1)
    source = col == row // TSTEPS * slot_dev + row % slot_dev
    own = row % TSTEPS // slot_dev == mine
    from_keep = (source & own).astype(F32).astype(BF16)
    from_got = (source & jnp.logical_not(own)).astype(F32).astype(BF16)
    tokens = (dot(from_keep, keep_ref[...]) + dot(from_got, got_ref[...])).astype(BF16)
    move = (iota((width, width), 0) == order_ref[...]).astype(F32).astype(BF16)
    out_ref[...] = dot(tokens, move).astype(BF16)


def weave_steps(my_slot, order, keep, got, slot_dev):
    rows, width = 2 * keep.shape[0], keep.shape[1]
    return pl.pallas_call(
        functools.partial(weave_kernel, slot_dev),
        out_shape=jax.ShapeDtypeStruct((rows, width), BF16),
        in_specs=[SCALARS] + [WHOLE] * 3,
        out_specs=WHOLE,
        compiler_params=params(12),
        cost_estimate=pl.CostEstimate(
            flops=16 * rows * width * (rows + width), bytes_accessed=4 * rows * width, transcendentals=0
        ),
        name="weave_steps",
    )(my_slot, order.reshape(1, width), keep, got)


def attention(normed, weight, heads_width, ctx_ref):
    rows = normed.shape[0]
    group = LANES
    lane = iota((1, LANES), 1)
    first = iota((group, LANES), 1) < HD
    masks = [(lane < HD).astype(F32).astype(BF16), (lane >= HD).astype(F32).astype(BF16)]
    ones = (iota((LANES, LANES), 0) // HD == iota((LANES, LANES), 1) // HD).astype(F32)
    mean = (ones * (1.0 / HD)).astype(BF16)
    ones = ones.astype(BF16)
    same_cell = iota((2 * group, group), 0) % group // TSTEPS == iota((2 * group, group), 1) // TSTEPS
    same_cell = same_cell.astype(F32).astype(BF16)
    count = jnp.ones((group, LANES), BF16)
    projected = dot(normed, weight)
    begins = range(0, rows, group)
    for at in range(0, heads_width, LANES):
        query = projected[:, at : at + LANES]
        key = projected[:, heads_width + at : heads_width + at + LANES]
        value = projected[:, 2 * heads_width + at : 2 * heads_width + at + LANES].astype(BF16)
        query_bf, key_bf = query.astype(BF16), key.astype(BF16)
        query = (query * lax.rsqrt(dot(query_bf * query_bf, ones) + HD * EPS)).astype(BF16)
        key = (key * lax.rsqrt(dot(key_bf * key_bf, mean) + EPS)).astype(BF16)
        left, right = query * masks[0], query * masks[1]
        scores = [
            dot_t(jnp.concatenate([left[at : at + group], right[at : at + group]], axis=0), key[at : at + group])
            for at in begins
        ]
        expos = [jnp.exp(score).astype(BF16) * same_cell for score in scores]
        mixed = [
            dot(expo, jnp.concatenate([value[at : at + group], count], axis=1)) for at, expo in zip(begins, expos)
        ]
        for begin, both in zip(begins, mixed):
            top, low = both[:group], both[group:]
            over = jnp.where(first, top[:, :LANES], low[:, :LANES])
            under = jnp.where(first, top[:, LANES:], low[:, LANES:])
            ctx_ref[begin : begin + group, at : at + LANES] = (over / under).astype(BF16)


def gated(normed, gate_w, up_w, down_w):
    gate = dot(normed, gate_w)
    up = dot(normed, up_w)
    hidden = (gate * (0.5 * jnp.tanh(0.5 * gate) + 0.5) * up).astype(BF16)
    return dot_t(hidden, down_w)


def put_rows_kernel(plan, *refs):
    sems, outs, pieces = refs[-1], refs[-4:-1], refs[:-4]
    copies = []
    for number, (piece, out, source, row, at, size) in enumerate(plan):
        rows = pieces[piece].shape[0]
        target = outs[out].at[pl.ds(row, rows), pl.ds(at, size)]
        copies.append(pltpu.make_async_copy(pieces[piece].at[:, pl.ds(source, size)], target, sems.at[number]))
    for copy in copies:
        copy.start()
    for copy in copies:
        copy.wait()


def put_rows(pieces, rows, heads_width, hidden_width):
    gate_at, out_at = 3 * heads_width, 3 * heads_width + 2 * hidden_width
    down_at = out_at + heads_width
    end = down_at + hidden_width
    runs = [(0, gate_at, 0, 0), (gate_at, out_at, 1, 0), (out_at, down_at, 0, gate_at), (down_at, end, 2, 0)]
    plan = []
    for left, right, out, shift in runs:
        for number, (array, row, at) in enumerate(pieces):
            low, high = max(left, at), min(right, at + array.shape[1])
            if low < high:
                plan.append((number, out, low - at, row, shift + low - left, high - low))
    return pl.pallas_call(
        functools.partial(put_rows_kernel, plan),
        out_shape=[
            jax.ShapeDtypeStruct((rows, 4 * heads_width), BF16),
            jax.ShapeDtypeStruct((rows, 2 * hidden_width), BF16),
            jax.ShapeDtypeStruct((rows, hidden_width), BF16),
        ],
        in_specs=[FAR] * len(pieces),
        out_specs=[WHOLE] * 3,
        scratch_shapes=[pltpu.SemaphoreType.DMA((len(plan),))],
        compiler_params=params(53),
        cost_estimate=pl.CostEstimate(flops=0, bytes_accessed=4 * rows * end, transcendentals=0),
        name="put_rows",
    )(*[array for array, _, _ in pieces])


def layer_kernel(tok_ref, heads_ref, gate_up_ref, down_ref, out_ref, norm_ref, ctx_ref, acc_ref):
    heads_width = ctx_ref.shape[1]
    hidden_width = down_ref.shape[1]
    tokens = tok_ref[...].astype(F32)
    scale = lax.rsqrt(jnp.mean(tokens * tokens, axis=1, keepdims=True) + EPS)
    norm_ref[...] = (tokens * scale).astype(BF16)
    attention(norm_ref[...], heads_ref[:, : 3 * heads_width], heads_width, ctx_ref)
    acc_ref[...] = dot_t(ctx_ref[...], heads_ref[:, 3 * heads_width :])
    for begin in range(0, hidden_width, UNIT):
        end = begin + UNIT
        gate_w, up_w = gate_up_ref[:, begin:end], gate_up_ref[:, hidden_width + begin : hidden_width + end]
        add = gated(norm_ref[...], gate_w, up_w, down_ref[:, begin:end])
        if end < hidden_width:
            acc_ref[...] += add
        else:
            out_ref[...] = (acc_ref[...] + add).astype(out_ref.dtype)


def layer(tokens, heads, gate_up, down, out_type):
    rows, width = tokens.shape
    size = heads.size + gate_up.size + down.size
    return pl.pallas_call(
        layer_kernel,
        out_shape=jax.ShapeDtypeStruct((rows, width), out_type),
        in_specs=[WHOLE] * 4,
        out_specs=WHOLE,
        scratch_shapes=[
            pltpu.VMEM((rows, width), BF16),
            pltpu.VMEM((rows, heads.shape[1] // 4), BF16),
            pltpu.VMEM((rows, width), F32),
        ],
        compiler_params=params(28),
        cost_estimate=pl.CostEstimate(
            flops=2 * rows * size,
            bytes_accessed=2 * size + 6 * rows * width,
            transcendentals=rows * down.shape[1],
        ),
        name="layer",
    )(tokens, heads, gate_up, down)


def finish_kernel(tok_ref, sum_ref, got_ref, order_ref, out_ref):
    width = out_ref.shape[1]
    mixed = (tok_ref[...].astype(F32) + sum_ref[...] + got_ref[...].astype(F32)).astype(BF16)
    move = (iota((width, width), 0) == order_ref[...]).astype(F32).astype(BF16)
    out_ref[...] = dot_t(mixed, move).astype(BF16)


def finish(tokens, sums, got, order):
    rows, width = tokens.shape
    return pl.pallas_call(
        finish_kernel,
        out_shape=jax.ShapeDtypeStruct((rows, width), BF16),
        in_specs=[WHOLE] * 4,
        out_specs=WHOLE,
        compiler_params=params(12),
        cost_estimate=pl.CostEstimate(
            flops=2 * rows * width * width, bytes_accessed=10 * rows * width, transcendentals=0
        ),
        name="finish",
    )(tokens, sums, got, order.reshape(1, width))


def side_by_side(w_qkv, w_out, w_gate_up, w_down):
    rows = w_qkv.shape[0]
    return jnp.concatenate([w_qkv.reshape(rows, -1), w_gate_up.reshape(rows, -1), w_out, w_down], axis=1)


def along_cells(values, distance):
    n_cells = lax.axis_size("cells")
    return lax.ppermute(values, "cells", [(j, (j - distance) % n_cells) for j in range(n_cells)])


def to_other_places(shares):
    swap = [(0, 1), (1, 0)]
    by_slot = lax.ppermute(shares, "slots", swap)
    by_group = lax.ppermute(shares, "groups", swap)
    cut = shares.shape[1] // 2
    left = lax.ppermute(by_slot[:, :cut], "groups", swap)
    right = lax.ppermute(by_group[:, cut:], "slots", swap)
    return [shares, by_slot, by_group, left, right]


def arrival_order(width, n_share):
    n_cells = lax.axis_size("cells")
    mine = lax.axis_index("cells")
    place = lax.axis_index("groups") * lax.axis_size("slots") + lax.axis_index("slots")
    rows = width // n_cells
    share = rows // n_share
    row = jnp.arange(width, dtype=jnp.int32)
    past = row - 2 * rows
    far = jnp.where(past < 0, row // share % n_share, past // (2 * share))
    distance = jnp.where(past < 0, n_cells - 1, 1 + past // share % 2)
    other = (mine + distance) % n_cells * rows + (far ^ place) * share + row % share
    return jnp.where(row < rows, mine * rows + row, other)


def tokens_by_exchanges(owner, position, obs_feat, time_embed, my_slot, capacity, slot_dev):
    n_slots = lax.axis_size("slots")
    n_owners = lax.axis_size("cells") * lax.axis_size("mp")
    rows, width = obs_feat.shape
    owners = jnp.arange(n_owners, dtype=jnp.int32)
    owner_hot = (owner[:, None] == owners[None, :]).astype(F32)
    row_ids = jnp.arange(rows, dtype=jnp.int32)
    lower = (row_ids[None, :] <= row_ids[:, None]).astype(BF16)
    running = dot(lower, owner_hot.astype(BF16))
    rank = jnp.sum(running * owner_hot, axis=1).astype(jnp.int32) - 1
    place = jnp.where(owner < n_owners, owner * capacity + rank, n_owners * capacity)
    place_ids = jnp.arange(n_owners * capacity, dtype=jnp.int32)
    taken = place_ids[:, None] == place[None, :]
    send_feat = dot(taken.astype(BF16), obs_feat).astype(BF16).reshape(n_owners, capacity, width)
    send_code = jnp.sum(jnp.where(taken, position[None, :] + 1, 0), axis=1).reshape(n_owners, capacity)
    axes = ("cells", "mp")
    got_feat = lax.all_to_all(send_feat, axes, split_axis=0, concat_axis=0, tiled=True).reshape(-1, width)
    got_code = lax.all_to_all(send_code, axes, split_axis=0, concat_axis=0, tiled=True).reshape(-1) - 1
    hot = (jnp.arange(CB * slot_dev, dtype=jnp.int32)[:, None] == got_code[None, :]).astype(BF16)
    count = jnp.sum(hot.astype(F32), axis=1)
    pooled = dot(hot, got_feat) / jnp.maximum(count, 1.0)[:, None]
    embed = lax.dynamic_slice_in_dim(time_embed, my_slot * slot_dev, slot_dev, 0).astype(F32)
    tokens = (pooled.reshape(CB, slot_dev, width) + embed[None]).astype(BF16)
    grid = tokens.reshape(n_slots, CB // n_slots, slot_dev, width)
    grid = lax.all_to_all(grid, "slots", split_axis=0, concat_axis=2, tiled=True)
    return grid.reshape(-1, width)


def on_device(obs_feat, obs_cell, obs_slot, obs_count, time_embed, w_qkv, w_out, w_gate_up, w_down):
    n_cells = lax.axis_size("cells")
    n_slots = lax.axis_size("slots")
    n_groups = lax.axis_size("groups")
    n_mp = lax.axis_size("mp")
    n_owners = n_cells * n_mp
    rows, width = obs_feat.shape
    capacity = 3 * rows // n_owners
    quarter = CB // n_slots
    slot_dev = TSTEPS // n_slots
    my_slot = lax.axis_index("slots")
    n_share = n_groups * n_slots
    heads_width, hidden_width = w_qkv.shape[2], w_gate_up.shape[2]
    share = w_qkv.shape[0] // n_share
    valid = jnp.arange(rows, dtype=jnp.int32) < obs_count[0]
    owner = obs_cell // (quarter * n_mp * n_slots) * n_mp + obs_cell // quarter % n_mp
    owner = jnp.where(valid, owner, n_owners)
    local = obs_cell // (quarter * n_mp) % n_slots * quarter + obs_cell % quarter
    position = local * slot_dev + obs_slot

    local_weights = (w_qkv, w_out.T, w_gate_up, w_down.T)
    which = lax.axis_index("groups") * n_slots + my_slot
    share_weights = [lax.dynamic_slice_in_dim(w, which * share, share, 0) for w in local_weights]
    share_rows = side_by_side(*share_weights)
    if n_slots == 2 and n_groups == 2 and n_cells == 4 and share % 16 == 0 and capacity % 16 == 0:
        order = arrival_order(width, n_share)
        below = along_cells(share_rows, -1)
        codes, embed = place_codes(owner, position, time_embed, n_owners, capacity)
        below, codes, share_rows = lax.optimization_barrier((below, codes, share_rows))
        codes = lax.all_to_all(codes, ("cells", "mp"), split_axis=0, concat_axis=0, tiled=True)
        first = to_other_places(below)
        blocks = place_rows(owner, obs_feat, n_owners, capacity)
        above, opposite = along_cells(share_rows, 1), along_cells(below, -1)
        blocks, codes, above, opposite, first = lax.optimization_barrier((blocks, codes, above, opposite, first))
        second = to_other_places(jnp.concatenate([above, opposite], axis=0))
        shard = side_by_side(*local_weights)
        got = lax.all_to_all(blocks, ("cells", "mp"), split_axis=0, concat_axis=0, tiled=True)
        got, shard, second = lax.optimization_barrier((got, shard, second))
        keep, send = pool_rows(my_slot.reshape(1), embed, codes, got, capacity, slot_dev)
        other = lax.ppermute(send, "slots", [(0, 1), (1, 0)])
        pieces, row = [(shard, 0, 0)], shard.shape[0]
        for own, by_slot, by_group, left, right in (first, second):
            for array in (own, by_slot, by_group):
                pieces.append((array, row, 0))
                row += array.shape[0]
            pieces += [(left, row, 0), (right, row, left.shape[1])]
            row += own.shape[0]
        weights = put_rows(pieces, width, heads_width, hidden_width)
        other, weights = lax.optimization_barrier((other, weights))
        tokens = weave_steps(my_slot.reshape(1), order, keep, other, slot_dev)
    else:
        order = jnp.arange(width, dtype=jnp.int32)
        whole = lax.all_gather(share_rows, ("cells", "groups", "slots"), axis=0, tiled=True)
        weights = put_rows([(whole, 0, 0)], width, heads_width, hidden_width)
        tokens = tokens_by_exchanges(owner, position, obs_feat, time_embed, my_slot, capacity, slot_dev)

    swap = [(0, 1), (1, 0)]
    partner = lax.ppermute(tokens, "mp", swap)
    for_partner = layer(partner, *weights, BF16)
    from_partner = lax.ppermute(for_partner, "mp", swap)
    own = layer(tokens, *weights, F32)
    return finish(tokens, own, from_partner, order).reshape(quarter, TSTEPS, width)


def solution(mesh):
    placed = (
        P(("groups", "cells", "slots", "mp"), None),
        P(("groups", "cells", "slots", "mp")),
        P(("groups", "cells", "slots", "mp")),
        P(("groups", "cells", "slots", "mp")),
        P(),
        P("cells", None, "mp"),
        P("mp", "cells"),
        P("cells", None, "mp"),
        P("mp", "cells"),
    )
    return jax.shard_map(
        on_device,
        mesh=mesh,
        in_specs=placed,
        out_specs=P(("groups", "cells", "slots", "mp"), None, None),
        check_vma=False,
    )
```

```python
import functools

import jax
import jax.numpy as jnp
from jax import lax
from jax.experimental import pallas as pl
from jax.experimental.pallas import tpu as pltpu
from jax.sharding import PartitionSpec as P

HD = 64
TSTEPS = 8
CB = 128
EPS = 1e-06

CODE = 32
UNIT = 1536
LANES = 128
MIB = 1024 * 1024
F32 = jnp.float32
BF16 = jnp.bfloat16
WHOLE = pl.BlockSpec(memory_space=pltpu.VMEM)
SCALARS = pl.BlockSpec(memory_space=pltpu.SMEM)
FAR = pl.BlockSpec(memory_space=pl.ANY)


def iota(shape, axis):
    return lax.broadcasted_iota(jnp.int32, shape, axis)


def dot(left, right):
    return jnp.dot(left, right, preferred_element_type=F32)


def dot_t(left, right):
    return lax.dot_general(left, right, (((1,), (1,)), ((), ())), preferred_element_type=F32)


def params(mib):
    return pltpu.CompilerParams(vmem_limit_bytes=mib * MIB)


def block_places(owner, n_owners):
    rows = owner.shape[1]
    owner_hot = (iota((n_owners, rows), 0) == owner).astype(F32)
    upper = (iota((rows, rows), 0) <= iota((rows, rows), 1)).astype(BF16)
    running = dot(owner_hot.astype(BF16), upper)
    return jnp.sum(running * owner_hot, axis=0, keepdims=True).astype(jnp.int32) - 1


def one_hot_rows(owner, rank, block, capacity):
    place = jnp.where(owner == block, rank, -1)
    return (iota((capacity, owner.shape[1]), 0) == place).astype(F32).astype(BF16)


def code_kernel(owner_ref, position_ref, time_ref, code_ref, embed_ref):
    n_owners, _, capacity = code_ref.shape
    embed_ref[...] = time_ref[...]
    owner = owner_ref[...]
    rank = block_places(owner, n_owners)
    code = position_ref[...] + 1
    line = iota((8, owner.shape[1]), 0)
    digits = jnp.where(line == 0, code // CODE, jnp.where(line == 1, code % CODE, 0))
    digits = digits.astype(F32).astype(BF16)
    for block in range(n_owners):
        sent = dot_t(digits, one_hot_rows(owner, rank, block, capacity))
        code_ref[block] = (sent[0:1] * CODE + sent[1:2]).astype(jnp.int32) - 1


def place_codes(owner, position, time_embed, n_owners, capacity):
    rows = owner.shape[0]
    return pl.pallas_call(
        code_kernel,
        out_shape=[
            jax.ShapeDtypeStruct((n_owners, 1, capacity), jnp.int32),
            jax.ShapeDtypeStruct(time_embed.shape, BF16),
        ],
        in_specs=[WHOLE] * 3,
        out_specs=[WHOLE] * 2,
        compiler_params=params(12),
        cost_estimate=pl.CostEstimate(
            flops=16 * rows * n_owners * capacity, bytes_accessed=8 * rows, transcendentals=0
        ),
        name="place_codes",
    )(owner.reshape(1, rows), position.reshape(1, rows), time_embed)


def place_kernel(owner_ref, feat_ref, out_ref):
    n_owners, capacity, _ = out_ref.shape
    owner = owner_ref[...]
    rank = block_places(owner, n_owners)
    feat = feat_ref[...]
    for block in range(n_owners):
        out_ref[block] = dot(one_hot_rows(owner, rank, block, capacity), feat).astype(BF16)


def place_rows(owner, obs_feat, n_owners, capacity):
    rows, width = obs_feat.shape
    return pl.pallas_call(
        place_kernel,
        out_shape=jax.ShapeDtypeStruct((n_owners, capacity, width), BF16),
        in_specs=[WHOLE] * 2,
        out_specs=WHOLE,
        compiler_params=params(12),
        cost_estimate=pl.CostEstimate(
            flops=2 * rows * width * n_owners * capacity,
            bytes_accessed=2 * width * (rows + n_owners * capacity),
            transcendentals=0,
        ),
        name="place_rows",
    )(owner.reshape(1, rows), obs_feat)


def pool_kernel(capacity, slot_dev, slot_ref, embed_ref, code_ref, got_ref, keep_ref, send_ref):
    half = keep_ref.shape[0]
    places = 2 * half
    mine = slot_ref[0]
    total = jnp.zeros((places, keep_ref.shape[1]), F32)
    seen = jnp.zeros((places, capacity), F32)
    for block in range(got_ref.shape[0]):
        code = code_ref[block]
        turned = jnp.where(code >= half, code - half, code + half)
        code = jnp.where((code >= 0) & (mine == 1), turned, code)
        hot = (iota((places, capacity), 0) == code).astype(F32)
        seen += hot
        total += dot(hot.astype(BF16), got_ref[block])
    count = jnp.sum(seen, axis=1, keepdims=True)
    steps = embed_ref.shape[0]
    step_hot = iota((places, steps), 1) == iota((places, steps), 0) % slot_dev + mine * slot_dev
    embed = dot(step_hot.astype(F32).astype(BF16), embed_ref[...])
    tokens = (total / jnp.maximum(count, 1.0) + embed).astype(BF16)
    keep_ref[...] = tokens[:half]
    send_ref[...] = tokens[half:]


def pool_rows(my_slot, time_embed, codes, got, capacity, slot_dev):
    width = time_embed.shape[1]
    half = jax.ShapeDtypeStruct((CB * slot_dev // 2, width), BF16)
    return pl.pallas_call(
        functools.partial(pool_kernel, capacity, slot_dev),
        out_shape=[half, half],
        in_specs=[SCALARS] + [WHOLE] * 3,
        out_specs=[WHOLE] * 2,
        compiler_params=params(12),
        cost_estimate=pl.CostEstimate(
            flops=2 * CB * slot_dev * got.size, bytes_accessed=2 * got.size, transcendentals=0
        ),
        name="pool_rows",
    )(my_slot, time_embed, codes, got)


def weave_kernel(slot_dev, slot_ref, order_ref, keep_ref, got_ref, out_ref):
    rows, width = out_ref.shape
    half = keep_ref.shape[0]
    mine = slot_ref[0]
    row, col = iota((rows, half), 0), iota((rows, half), 1)
    source = col == row // TSTEPS * slot_dev + row % slot_dev
    own = row % TSTEPS // slot_dev == mine
    from_keep = (source & own).astype(F32).astype(BF16)
    from_got = (source & jnp.logical_not(own)).astype(F32).astype(BF16)
    tokens = (dot(from_keep, keep_ref[...]) + dot(from_got, got_ref[...])).astype(BF16)
    move = (iota((width, width), 0) == order_ref[...]).astype(F32).astype(BF16)
    out_ref[...] = dot(tokens, move).astype(BF16)


def weave_steps(my_slot, order, keep, got, slot_dev):
    rows, width = 2 * keep.shape[0], keep.shape[1]
    return pl.pallas_call(
        functools.partial(weave_kernel, slot_dev),
        out_shape=jax.ShapeDtypeStruct((rows, width), BF16),
        in_specs=[SCALARS] + [WHOLE] * 3,
        out_specs=WHOLE,
        compiler_params=params(12),
        cost_estimate=pl.CostEstimate(
            flops=16 * rows * width * (rows + width), bytes_accessed=4 * rows * width, transcendentals=0
        ),
        name="weave_steps",
    )(my_slot, order.reshape(1, width), keep, got)


def attention(normed, weight, heads_width, ctx_ref):
    rows = normed.shape[0]
    group = LANES
    lane = iota((1, LANES), 1)
    first = iota((group, LANES), 1) < HD
    masks = [(lane < HD).astype(F32).astype(BF16), (lane >= HD).astype(F32).astype(BF16)]
    ones = (iota((LANES, LANES), 0) // HD == iota((LANES, LANES), 1) // HD).astype(F32)
    mean = (ones * (1.0 / HD)).astype(BF16)
    ones = ones.astype(BF16)
    same_cell = iota((2 * group, group), 0) % group // TSTEPS == iota((2 * group, group), 1) // TSTEPS
    same_cell = same_cell.astype(F32).astype(BF16)
    count = jnp.ones((group, LANES), BF16)
    projected = dot(normed, weight)
    begins = range(0, rows, group)
    for at in range(0, heads_width, LANES):
        query = projected[:, at : at + LANES]
        key = projected[:, heads_width + at : heads_width + at + LANES]
        value = projected[:, 2 * heads_width + at : 2 * heads_width + at + LANES].astype(BF16)
        query_bf, key_bf = query.astype(BF16), key.astype(BF16)
        query = (query * lax.rsqrt(dot(query_bf * query_bf, ones) + HD * EPS)).astype(BF16)
        key = (key * lax.rsqrt(dot(key_bf * key_bf, mean) + EPS)).astype(BF16)
        left, right = query * masks[0], query * masks[1]
        scores = [
            dot_t(jnp.concatenate([left[at : at + group], right[at : at + group]], axis=0), key[at : at + group])
            for at in begins
        ]
        expos = [jnp.exp(score).astype(BF16) * same_cell for score in scores]
        mixed = [
            dot(expo, jnp.concatenate([value[at : at + group], count], axis=1)) for at, expo in zip(begins, expos)
        ]
        for begin, both in zip(begins, mixed):
            top, low = both[:group], both[group:]
            over = jnp.where(first, top[:, :LANES], low[:, :LANES])
            under = jnp.where(first, top[:, LANES:], low[:, LANES:])
            ctx_ref[begin : begin + group, at : at + LANES] = (over / under).astype(BF16)


def gated(normed, gate_w, up_w, down_w):
    gate = dot(normed, gate_w)
    up = dot(normed, up_w)
    hidden = (gate * (0.5 * jnp.tanh(0.5 * gate) + 0.5) * up).astype(BF16)
    return dot_t(hidden, down_w)


def put_rows_kernel(plan, *refs):
    sems, outs, pieces = refs[-1], refs[-4:-1], refs[:-4]
    copies = []
    for number, (piece, out, source, row, at, size) in enumerate(plan):
        rows = pieces[piece].shape[0]
        target = outs[out].at[pl.ds(row, rows), pl.ds(at, size)]
        copies.append(pltpu.make_async_copy(pieces[piece].at[:, pl.ds(source, size)], target, sems.at[number]))
    for copy in copies:
        copy.start()
    for copy in copies:
        copy.wait()


def put_rows(pieces, rows, heads_width, hidden_width):
    gate_at, out_at = 3 * heads_width, 3 * heads_width + 2 * hidden_width
    down_at = out_at + heads_width
    end = down_at + hidden_width
    runs = [(0, gate_at, 0, 0), (gate_at, out_at, 1, 0), (out_at, down_at, 0, gate_at), (down_at, end, 2, 0)]
    plan = []
    for left, right, out, shift in runs:
        for number, (array, row, at) in enumerate(pieces):
            low, high = max(left, at), min(right, at + array.shape[1])
            if low < high:
                plan.append((number, out, low - at, row, shift + low - left, high - low))
    return pl.pallas_call(
        functools.partial(put_rows_kernel, plan),
        out_shape=[
            jax.ShapeDtypeStruct((rows, 4 * heads_width), BF16),
            jax.ShapeDtypeStruct((rows, 2 * hidden_width), BF16),
            jax.ShapeDtypeStruct((rows, hidden_width), BF16),
        ],
        in_specs=[FAR] * len(pieces),
        out_specs=[WHOLE] * 3,
        scratch_shapes=[pltpu.SemaphoreType.DMA((len(plan),))],
        compiler_params=params(53),
        cost_estimate=pl.CostEstimate(flops=0, bytes_accessed=4 * rows * end, transcendentals=0),
        name="put_rows",
    )(*[array for array, _, _ in pieces])


def layer_kernel(tok_ref, heads_ref, gate_up_ref, down_ref, out_ref, norm_ref, ctx_ref, acc_ref):
    heads_width = ctx_ref.shape[1]
    hidden_width = down_ref.shape[1]
    tokens = tok_ref[...].astype(F32)
    scale = lax.rsqrt(jnp.mean(tokens * tokens, axis=1, keepdims=True) + EPS)
    norm_ref[...] = (tokens * scale).astype(BF16)
    attention(norm_ref[...], heads_ref[:, : 3 * heads_width], heads_width, ctx_ref)
    acc_ref[...] = dot_t(ctx_ref[...], heads_ref[:, 3 * heads_width :])
    for begin in range(0, hidden_width, UNIT):
        end = begin + UNIT
        gate_w, up_w = gate_up_ref[:, begin:end], gate_up_ref[:, hidden_width + begin : hidden_width + end]
        add = gated(norm_ref[...], gate_w, up_w, down_ref[:, begin:end])
        if end < hidden_width:
            acc_ref[...] += add
        else:
            out_ref[...] = (acc_ref[...] + add).astype(out_ref.dtype)


def layer(tokens, heads, gate_up, down, out_type):
    rows, width = tokens.shape
    size = heads.size + gate_up.size + down.size
    return pl.pallas_call(
        layer_kernel,
        out_shape=jax.ShapeDtypeStruct((rows, width), out_type),
        in_specs=[WHOLE] * 4,
        out_specs=WHOLE,
        scratch_shapes=[
            pltpu.VMEM((rows, width), BF16),
            pltpu.VMEM((rows, heads.shape[1] // 4), BF16),
            pltpu.VMEM((rows, width), F32),
        ],
        compiler_params=params(28),
        cost_estimate=pl.CostEstimate(
            flops=2 * rows * size,
            bytes_accessed=2 * size + 6 * rows * width,
            transcendentals=rows * down.shape[1],
        ),
        name="layer",
    )(tokens, heads, gate_up, down)


def finish_kernel(tok_ref, sum_ref, got_ref, order_ref, out_ref):
    width = out_ref.shape[1]
    mixed = (tok_ref[...].astype(F32) + sum_ref[...] + got_ref[...].astype(F32)).astype(BF16)
    move = (iota((width, width), 0) == order_ref[...]).astype(F32).astype(BF16)
    out_ref[...] = dot_t(mixed, move).astype(BF16)


def finish(tokens, sums, got, order):
    rows, width = tokens.shape
    return pl.pallas_call(
        finish_kernel,
        out_shape=jax.ShapeDtypeStruct((rows, width), BF16),
        in_specs=[WHOLE] * 4,
        out_specs=WHOLE,
        compiler_params=params(12),
        cost_estimate=pl.CostEstimate(
            flops=2 * rows * width * width, bytes_accessed=10 * rows * width, transcendentals=0
        ),
        name="finish",
    )(tokens, sums, got, order.reshape(1, width))


def side_by_side(w_qkv, w_out, w_gate_up, w_down):
    rows = w_qkv.shape[0]
    return jnp.concatenate([w_qkv.reshape(rows, -1), w_gate_up.reshape(rows, -1), w_out, w_down], axis=1)


def along_cells(values, distance):
    n_cells = lax.axis_size("cells")
    return lax.ppermute(values, "cells", [(j, (j - distance) % n_cells) for j in range(n_cells)])


def to_other_places(shares):
    swap = [(0, 1), (1, 0)]
    by_slot = lax.ppermute(shares, "slots", swap)
    by_group = lax.ppermute(shares, "groups", swap)
    cut = shares.shape[1] // 2
    left = lax.ppermute(by_slot[:, :cut], "groups", swap)
    right = lax.ppermute(by_group[:, cut:], "slots", swap)
    return [shares, by_slot, by_group, left, right]


def arrival_order(width, n_share):
    n_cells = lax.axis_size("cells")
    mine = lax.axis_index("cells")
    place = lax.axis_index("groups") * lax.axis_size("slots") + lax.axis_index("slots")
    rows = width // n_cells
    share = rows // n_share
    row = jnp.arange(width, dtype=jnp.int32)
    past = row - 2 * rows
    far = jnp.where(past < 0, row // share % n_share, past // (2 * share))
    distance = jnp.where(past < 0, n_cells - 1, 1 + past // share % 2)
    other = (mine + distance) % n_cells * rows + (far ^ place) * share + row % share
    return jnp.where(row < rows, mine * rows + row, other)


def tokens_by_exchanges(owner, position, obs_feat, time_embed, my_slot, capacity, slot_dev):
    n_slots = lax.axis_size("slots")
    n_owners = lax.axis_size("cells") * lax.axis_size("mp")
    rows, width = obs_feat.shape
    owners = jnp.arange(n_owners, dtype=jnp.int32)
    owner_hot = (owner[:, None] == owners[None, :]).astype(F32)
    row_ids = jnp.arange(rows, dtype=jnp.int32)
    lower = (row_ids[None, :] <= row_ids[:, None]).astype(BF16)
    running = dot(lower, owner_hot.astype(BF16))
    rank = jnp.sum(running * owner_hot, axis=1).astype(jnp.int32) - 1
    place = jnp.where(owner < n_owners, owner * capacity + rank, n_owners * capacity)
    place_ids = jnp.arange(n_owners * capacity, dtype=jnp.int32)
    taken = place_ids[:, None] == place[None, :]
    send_feat = dot(taken.astype(BF16), obs_feat).astype(BF16).reshape(n_owners, capacity, width)
    send_code = jnp.sum(jnp.where(taken, position[None, :] + 1, 0), axis=1).reshape(n_owners, capacity)
    axes = ("cells", "mp")
    got_feat = lax.all_to_all(send_feat, axes, split_axis=0, concat_axis=0, tiled=True).reshape(-1, width)
    got_code = lax.all_to_all(send_code, axes, split_axis=0, concat_axis=0, tiled=True).reshape(-1) - 1
    hot = (jnp.arange(CB * slot_dev, dtype=jnp.int32)[:, None] == got_code[None, :]).astype(BF16)
    count = jnp.sum(hot.astype(F32), axis=1)
    pooled = dot(hot, got_feat) / jnp.maximum(count, 1.0)[:, None]
    embed = lax.dynamic_slice_in_dim(time_embed, my_slot * slot_dev, slot_dev, 0).astype(F32)
    tokens = (pooled.reshape(CB, slot_dev, width) + embed[None]).astype(BF16)
    grid = tokens.reshape(n_slots, CB // n_slots, slot_dev, width)
    grid = lax.all_to_all(grid, "slots", split_axis=0, concat_axis=2, tiled=True)
    return grid.reshape(-1, width)


def on_device(obs_feat, obs_cell, obs_slot, obs_count, time_embed, w_qkv, w_out, w_gate_up, w_down):
    n_cells = lax.axis_size("cells")
    n_slots = lax.axis_size("slots")
    n_groups = lax.axis_size("groups")
    n_mp = lax.axis_size("mp")
    n_owners = n_cells * n_mp
    rows, width = obs_feat.shape
    capacity = 3 * rows // n_owners
    quarter = CB // n_slots
    slot_dev = TSTEPS // n_slots
    my_slot = lax.axis_index("slots")
    n_share = n_groups * n_slots
    heads_width, hidden_width = w_qkv.shape[2], w_gate_up.shape[2]
    share = w_qkv.shape[0] // n_share
    valid = jnp.arange(rows, dtype=jnp.int32) < obs_count[0]
    owner = obs_cell // (quarter * n_mp * n_slots) * n_mp + obs_cell // quarter % n_mp
    owner = jnp.where(valid, owner, n_owners)
    local = obs_cell // (quarter * n_mp) % n_slots * quarter + obs_cell % quarter
    position = local * slot_dev + obs_slot

    local_weights = (w_qkv, w_out.T, w_gate_up, w_down.T)
    which = lax.axis_index("groups") * n_slots + my_slot
    share_weights = [lax.dynamic_slice_in_dim(w, which * share, share, 0) for w in local_weights]
    share_rows = side_by_side(*share_weights)
    if n_slots == 2 and n_groups == 2 and n_cells == 4 and share % 16 == 0 and capacity % 16 == 0:
        order = arrival_order(width, n_share)
        below = along_cells(share_rows, -1)
        codes, embed = place_codes(owner, position, time_embed, n_owners, capacity)
        below, codes, share_rows = lax.optimization_barrier((below, codes, share_rows))
        codes = lax.all_to_all(codes, ("cells", "mp"), split_axis=0, concat_axis=0, tiled=True)
        first = to_other_places(below)
        blocks = place_rows(owner, obs_feat, n_owners, capacity)
        above, opposite = along_cells(share_rows, 1), along_cells(below, -1)
        blocks, codes, above, opposite, first = lax.optimization_barrier((blocks, codes, above, opposite, first))
        second = to_other_places(jnp.concatenate([above, opposite], axis=0))
        shard = side_by_side(*local_weights)
        got = lax.all_to_all(blocks, ("cells", "mp"), split_axis=0, concat_axis=0, tiled=True)
        got, shard, second = lax.optimization_barrier((got, shard, second))
        keep, send = pool_rows(my_slot.reshape(1), embed, codes, got, capacity, slot_dev)
        other = lax.ppermute(send, "slots", [(0, 1), (1, 0)])
        pieces, row = [(shard, 0, 0)], shard.shape[0]
        for own, by_slot, by_group, left, right in (first, second):
            for array in (own, by_slot, by_group):
                pieces.append((array, row, 0))
                row += array.shape[0]
            pieces += [(left, row, 0), (right, row, left.shape[1])]
            row += own.shape[0]
        weights = put_rows(pieces, width, heads_width, hidden_width)
        other, weights = lax.optimization_barrier((other, weights))
        tokens = weave_steps(my_slot.reshape(1), order, keep, other, slot_dev)
    else:
        order = jnp.arange(width, dtype=jnp.int32)
        whole = lax.all_gather(share_rows, ("cells", "groups", "slots"), axis=0, tiled=True)
        weights = put_rows([(whole, 0, 0)], width, heads_width, hidden_width)
        tokens = tokens_by_exchanges(owner, position, obs_feat, time_embed, my_slot, capacity, slot_dev)

    swap = [(0, 1), (1, 0)]
    partner = lax.ppermute(tokens, "mp", swap)
    for_partner = layer(partner, *weights, BF16)
    from_partner = lax.ppermute(for_partner, "mp", swap)
    own = layer(tokens, *weights, F32)
    return finish(tokens, own, from_partner, order).reshape(quarter, TSTEPS, width)


def solution(mesh):
    placed = (
        P(("groups", "cells", "slots", "mp"), None),
        P(("groups", "cells", "slots", "mp")),
        P(("groups", "cells", "slots", "mp")),
        P(("groups", "cells", "slots", "mp")),
        P(),
        P("cells", None, "mp"),
        P("mp", "cells"),
        P("cells", None, "mp"),
        P("mp", "cells"),
    )
    return jax.shard_map(
        on_device,
        mesh=mesh,
        in_specs=placed,
        out_specs=P(("groups", "cells", "slots", "mp"), None, None),
        check_vma=False,
    )
```
